128 devices in a mesh: dp: 4 (over z), head: 4 (over y_hi, core), blk: 8 (over y_lo, x).
Axes of the slice: x: 4, y: 4 (y_hi: 2, y_lo: 2; y = y_hi * 2 + y_lo), z: 4, core: 2. Of those that a mesh axis runs over, the one named last changes fastest.
Arguments:
- tokens: bfloat16 [16384, 2048], P(('dp', 'head', 'blk')), may hold values from -6 to 6
- segment_ids: int32 [4, 4096], P('dp'), may hold values from 0 to 9, never falling along the last dimension, each value on 1 to 2000 neighbouring positions
- valid_mask: int32 [4, 4096], P('dp'), may hold values 0 or 1
- routes: int32 [16384, 8], P(('dp', 'head', 'blk')), may hold values from 0 to 63, all different within a row; in each aligned block of 128 rows (0 to 127, 128 to 255, ...) at most 24 rows name the same one
- attn_gain: float32 [2048], replicated, may hold values from 0.5 to 1.5
- w_query: bfloat16 [2048, 2048], P(('dp', 'blk'), 'head'), may hold values from -0.125 to 0.125
- w_key: bfloat16 [2048, 2048], P(('dp', 'blk'), 'head'), may hold values from -0.125 to 0.125
- w_value: bfloat16 [2048, 2048], P(('dp', 'blk'), 'head'), may hold values from -0.125 to 0.125
- w_out: bfloat16 [2048, 2048], P(('dp', 'blk'), 'head'), may hold values from -2 to 2
- query_gain: float32 [128], replicated, may hold values from 0.5 to 1.5
- key_gain: float32 [128], replicated, may hold values from 0.5 to 1.5
- ffn_gain: float32 [2048], replicated, may hold values from 0.5 to 1.5
- router: bfloat16 [2048, 64], replicated, may hold values from -0.0625 to 0.0625
- expert_in: bfloat16 [2048, 64, 2048], P('dp', ('head', 'blk')), may hold values from -0.125 to 0.125
- expert_out: bfloat16 [2048, 64, 1024], P('dp', ('head', 'blk')), may hold values from -1 to 1
- cotangent: bfloat16 [16384, 2048], P(('dp', 'head', 'blk')), may hold values from -6 to 6
Outputs:
- output: bfloat16 [16384, 2048], P(('dp', 'head', 'blk'))
- input_grad: float32 [16384, 2048], P(('dp', 'head', 'blk'))
- attn_gain_grad: float32 [2048], replicated
- w_query_grad: float32 [2048, 2048], P(('dp', 'blk'), 'head')
- w_key_grad: float32 [2048, 2048], P(('dp', 'blk'), 'head')
- w_value_grad: float32 [2048, 2048], P(('dp', 'blk'), 'head')
- w_out_grad: float32 [2048, 2048], P(('dp', 'blk'), 'head')
- query_gain_grad: float32 [128], replicated
- key_gain_grad: float32 [128], replicated
- ffn_gain_grad: float32 [2048], replicated
- router_grad: float32 [2048, 64], replicated
- expert_in_grad: float32 [2048, 64, 2048], P('dp', ('head', 'blk'))
- expert_out_grad: float32 [2048, 64, 1024], P('dp', ('head', 'blk'))
The draws below stay inside these ranges and needn't reach their ends.
Inputs may be any that keep to these rules, and one draw needn't show every extreme that they name: `routes`: each row names 8 different experts. In each aligned block of 128 rows (the rows of one device) no expert is named by more than 24 rows, a bound that some block reaches. `segment_ids`: segment numbers never fall along a sequence; a document has at most 2000 tokens, and one has exactly that many.
All inputs are finite; a program needn't handle non-finite values. No bound on the sum of `valid_mask` on one device may be relied on, other than what follows from the above.
Results may differ from the reference program's by a relative error of at most 0.033.
Values may be sent and summed in bfloat16 or wider, within the bound.
A program may use at most 256 MiB of HBM per device.

```python
import math
import jax
import jax.numpy as jnp
import numpy as np
from jax import lax

D = 2048
HEADS = 16
HD = 128
FF = 1024
TOPK = 8
TOK_DEV = 128
EXPERTS = 64
SEQ = 4096
TOKENS = 16384
CAP = 24
DOCS = 10
DOC_MOST = 2000
N_DP = 4


def set_ends(drawn, own_key, smallest, high):
    longest = drawn.shape.index(max(drawn.shape))
    spots = []
    for shift in (0, 1):
        where = [jax.random.randint(jax.random.fold_in(own_key, axis), (), 0, length) for axis, length in enumerate(drawn.shape)]
        where[longest] = (where[longest] + shift) % drawn.shape[longest]
        spots.append(tuple(where))
    return drawn.at[spots[0]].set(smallest).at[spots[1]].set(high)


def block_levels(rng, dims, split, low, top_value):
    factor_of, own = 1.0, jax.random.fold_in(rng, 6)
    for axis_at, parts in split:
        draws = jnp.exp(jax.random.uniform(jax.random.fold_in(own, axis_at), (parts,), jnp.float32, low / len(split), top_value / len(split)))
        factor_of = factor_of * jnp.repeat(draws, dims[axis_at] // parts).reshape([-1 if axis == axis_at else 1 for axis in range(len(dims))])
    return factor_of


def length_profile(amount, total, bound, skew):
    portions = [(1 << 20) // math.isqrt(standing ** skew) + 1 for standing in range(2, amount + 1)]
    surplus, counts = total - bound - (amount - 1), [1] * (amount - 1)
    while surplus > 0:
        candidates = [i for i in range(amount - 1) if counts[i] < bound]
        pool, left = sum([portions[i] for i in candidates]), surplus
        for i in candidates:
            more = min(bound - counts[i], max(1, left * portions[i] // pool), surplus)
            counts[i] = counts[i] + more
            surplus = surplus - more
    return np.array([bound] + counts)


def uneven(rng, count, total, reach, lean):
    if count == 2:
        one = jax.random.randint(rng, (), max(1, total - reach), min(reach, total - 1) + 1)
        return jnp.stack([one, total - one])
    sizes = jnp.asarray(length_profile(count, total, reach, lean), jnp.int32)
    twos = (count - 1) // 2
    source_of, taker = sizes[1:1 + 2 * twos:2], sizes[2:2 + 2 * twos:2]
    margin = jnp.minimum(source_of - 1, reach - taker)
    moved = jax.random.randint(jax.random.fold_in(rng, 1), (twos,), 0, 1 << 20) % (margin + 1)
    sizes = sizes.at[1:1 + 2 * twos:2].set(source_of - moved).at[2:2 + 2 * twos:2].set(taker + moved)
    return sizes[jax.random.permutation(jax.random.fold_in(rng, 2), count)]


def deal_out(own_key, own, number, rows, count, top, reach, slope):
    ranking = jax.random.permutation(own_key, count)
    crowded, common = shares(count, rows * top, reach, slope, True), shares(count, rows * top, reach, slope, False)
    places = jnp.arange(count)

    def named(tallies, offset_by):
        used = int((tallies > 0).sum())
        fixed = max(1, used // 4)
        passed = fixed + (places - fixed + offset_by * (used - fixed)) % max(1, count - fixed)
        return jnp.zeros((count,), jnp.int32).at[ranking[jnp.where(places < fixed, places, passed)]].set(jnp.asarray(tallies, jnp.int32))

    tallies = jnp.where(number % 4 == 0, named(crowded, number // 4), named(common, number - number // 4 - 1))
    mixed = jax.random.permutation(jax.random.fold_in(own, 3), count)
    source_of, taker = mixed[0:count // 2 * 2:2], mixed[1:count // 2 * 2:2]
    room = jnp.minimum(tallies[source_of] - 1, reach - tallies[taker]) // 2
    room = jnp.where((source_of == ranking[0]) | (taker == ranking[0]) | (tallies[taker] == 0), 0, jnp.maximum(room, 0))
    passed = jax.random.randint(jax.random.fold_in(own, 4), (count // 2,), 0, 1 << 20) % (room + 1)
    tallies = tallies.at[source_of].add(-passed).at[taker].add(passed)
    labels = jnp.searchsorted(jnp.cumsum(tallies), jnp.arange(rows * top), side="right").astype(jnp.int32)
    grid = labels.reshape(top, rows).T
    grid = grid[jax.random.permutation(jax.random.fold_in(own, 1), rows)]
    offset_by = jax.random.randint(jax.random.fold_in(own, 2), (rows, 1), 0, top)
    return jnp.take_along_axis(grid, (jnp.arange(top)[None, :] + offset_by) % top, axis=1)


def shares(amount, total, most, skew, full):
    weights = [(1 << 20) // math.isqrt(rank ** skew) + 1 for rank in range(1, amount + 1)]
    largest = most if full else min(most, max(-(-total // amount), total * weights[0] // sum(weights)))
    least = 1 if total - largest >= amount - 1 else 0
    holding, spare = [largest] + [least] * (amount - 1), total - largest - least * (amount - 1)
    while spare > 0:
        candidates = [i for i in range(1, amount) if holding[i] < largest] or [i for i in range(1, amount) if holding[i] < most]
        whole, budget = sum([weights[i] for i in candidates]), spare
        for i in candidates:
            more = min(most - holding[i], max(1, budget * weights[i] // whole), spare)
            holding[i] = holding[i] + more
            spare = spare - more
    return np.array(holding)


def centred(own_key, extent, width, limit, cuts=(), held_as=jnp.bfloat16):
    level = block_levels(own_key, extent, cuts, -0.22, 0.18) if cuts else 1.0
    drawn = jax.random.normal(own_key, extent, jnp.float32) * width * level
    return jnp.minimum(jnp.maximum(drawn, -limit), limit).astype(held_as)


def setup_inputs(seed: int = 0) -> dict:
    seeds = jax.random.split(jax.random.key(seed), 17)
    tokens = centred(seeds[0], (TOKENS, D), 1.0, 6.0, ((0, 128),))
    segment_ids = jax.vmap(lambda own: jnp.searchsorted(jnp.cumsum(uneven(own, DOCS, SEQ, DOC_MOST, 2)), jnp.arange(SEQ), side="right"))(jax.random.split(seeds[1], N_DP)).reshape((N_DP, SEQ)).astype(jnp.int32)
    valid_mask = set_ends((jax.random.randint(seeds[2], (N_DP, SEQ), 0, 8) < 7).astype(jnp.int32), jax.random.fold_in(seeds[2], 1), 0, 1)
    routes_keys = jax.random.split(jax.random.fold_in(seeds[3], 1), TOKENS // TOK_DEV)
    routes_turns = jax.random.permutation(jax.random.fold_in(seeds[3], 3), TOKENS // TOK_DEV)
    routes = jax.vmap(lambda own, number: deal_out(jax.random.fold_in(seeds[3], 2), own, number, TOK_DEV, EXPERTS, TOPK, CAP, 1))(routes_keys, routes_turns).reshape((TOKENS, TOPK))
    attn_gain = jnp.clip(jax.random.uniform(seeds[4], (D,), jnp.float32, 0.5, 1.5), 0.5, 1.5)
    w_query = centred(seeds[5], (D, D), D ** -0.5, 0.125, ((0, 32), (1, 4)))
    w_key = centred(seeds[6], (D, D), D ** -0.5, 0.125, ((0, 32), (1, 4)))
    w_value = centred(seeds[7], (D, D), D ** -0.5, 0.125, ((0, 32), (1, 4)))
    w_out = centred(seeds[8], (D, D), (max(D // 256, 4)) ** -0.5, 2.0, ((0, 32), (1, 4)))
    query_gain = jnp.clip(jax.random.uniform(seeds[9], (HD,), jnp.float32, 0.5, 1.5), 0.5, 1.5)
    key_gain = jnp.clip(jax.random.uniform(seeds[10], (HD,), jnp.float32, 0.5, 1.5), 0.5, 1.5)
    ffn_gain = jnp.clip(jax.random.uniform(seeds[11], (D,), jnp.float32, 0.5, 1.5), 0.5, 1.5)
    router = centred(seeds[12], (D, EXPERTS), (4 * D) ** -0.5, 0.0625)
    expert_in = centred(seeds[13], (D, EXPERTS, 2 * FF), D ** -0.5, 0.125, ((0, 4), (1, 32)))
    expert_out = centred(seeds[14], (D, EXPERTS, FF), (FF // 32) ** -0.5, 1.0, ((0, 4), (1, 32)))
    cotangent = centred(seeds[15], (TOKENS, D), 1.0, 6.0, ((0, 128),))
    return dict(tokens=tokens, segment_ids=segment_ids, valid_mask=valid_mask, routes=routes, attn_gain=attn_gain, w_query=w_query, w_key=w_key, w_value=w_value, w_out=w_out, query_gain=query_gain, key_gain=key_gain, ffn_gain=ffn_gain, router=router, expert_in=expert_in, expert_out=expert_out, cotangent=cotangent)


@jax.custom_vjp
def low(v):
    return lax.optimization_barrier(v.astype(jnp.bfloat16)).astype(jnp.float32)

@jax.custom_vjp
def low_back(v):
    return v

def low_keep(v):
    return (low(v), None)

def low_pass(kept, grad):
    return (grad,)

def back_keep(v):
    return (v, None)

def back_low(kept, grad):
    return (low(grad),)
low.defvjp(low_keep, low_pass)
low_back.defvjp(back_keep, back_low)
epsilon = 1e-06
rope_base = 50000.0
masked_score = -1e+30
highest = lax.Precision.HIGHEST

def rms_scale(values, gain_vec):
    inverse = lax.rsqrt(lax.optimization_barrier(jnp.mean(values * values, axis=-1, keepdims=True)) + epsilon)
    return values * inverse * gain_vec

def rotary(values, positions, turning):
    half_dim = values.shape[-1] // 2
    frequency = rope_base ** (-jnp.arange(half_dim, dtype=jnp.float32) / half_dim)
    angles = positions.astype(jnp.float32)[:, None] * frequency[None, :]
    cosine = jnp.cos(angles)[:, None, :]
    sine_part = turning * jnp.sin(angles)[:, None, :]
    first_half = values[..., :half_dim]
    second = values[..., half_dim:]
    return jnp.concatenate([first_half * cosine - second * sine_part, second * cosine + first_half * sine_part], axis=-1)

def attention(queries, keys_all, values_all, segment, valid):
    length = queries.shape[0]
    row_count = math.gcd(512, length)
    score_scale = HD ** (-0.5)
    key_ids = jnp.arange(length, dtype=jnp.int32)

    def one_block(block_idx):
        first_row = block_idx * row_count
        query_rows = lax.dynamic_slice_in_dim(queries, first_row, row_count, 0)
        query_seg = lax.dynamic_slice_in_dim(segment, first_row, row_count, 0)
        query_ids = first_row + jnp.arange(row_count, dtype=jnp.int32)
        scores = low_back(jnp.einsum('qhd,khd->hqk', query_rows, keys_all, precision=highest) * score_scale)
        allowed = (query_seg[:, None] == segment[None, :]) & ((valid[None, :] > 0) | (query_ids[:, None] == key_ids[None, :]))
        scores = jnp.where(allowed[None], scores, masked_score)
        row_peak = lax.optimization_barrier(jnp.max(scores, axis=-1, keepdims=True))
        weights = jnp.exp(scores - row_peak)
        probabilities = weights / lax.optimization_barrier(jnp.sum(weights, axis=-1, keepdims=True))
        return jnp.einsum('hqk,khd->qhd', low(probabilities), values_all, precision=highest)
    blocks = lax.map(jax.checkpoint(one_block), jnp.arange(length // row_count, dtype=jnp.int32))
    return blocks.reshape(length, HEADS, HD)

def block_layer(weights, inputs, segment, valid, picked_ids):
    attn_gain, w_query, w_key, w_value, w_out, query_gain, key_gain, ffn_gain, router, moved_in, moved_out = weights
    length = inputs.shape[0]
    positions = jnp.arange(length, dtype=jnp.int32)
    normed = low(rms_scale(inputs, attn_gain))
    query_proj = low_back(jnp.dot(normed, w_query, precision=highest)).reshape(length, HEADS, HD)
    key_proj = low_back(jnp.dot(normed, w_key, precision=highest)).reshape(length, HEADS, HD)
    value_heads = low(low_back(jnp.dot(normed, w_value, precision=highest))).reshape(length, HEADS, HD)
    queries = low(low_back(rotary(rms_scale(query_proj, query_gain), positions, 1.0)))
    keys_all = low(low_back(rotary(rms_scale(key_proj, key_gain), positions, 1.0)))
    attended = low(low_back(attention(queries, keys_all, value_heads, segment, valid))).reshape(length, D)
    branch = low_back(jnp.dot(attended, w_out.T, precision=highest))
    middle = inputs + branch
    normed_ffn = low(rms_scale(middle, ffn_gain))
    logits = jnp.dot(normed_ffn, router, precision=highest)
    probabilities = jax.nn.softmax(logits, axis=-1)
    chosen = jnp.take_along_axis(probabilities, picked_ids, axis=1)
    gate_weights = chosen / lax.optimization_barrier(jnp.sum(chosen, axis=-1, keepdims=True))
    blocks_seq = length // TOK_DEV
    expert_ids = jnp.arange(EXPERTS, dtype=jnp.int32)
    chosen_hot = (picked_ids[..., None] == expert_ids).astype(jnp.int32)
    grouped = chosen_hot.reshape(blocks_seq, TOK_DEV * TOPK, EXPERTS)
    before = jnp.cumsum(grouped, axis=1, dtype=jnp.int32) - grouped
    slot_ids = lax.optimization_barrier(jnp.sum(before * grouped, axis=-1, dtype=jnp.int32)).reshape(length, TOPK)
    places = (positions // TOK_DEV)[:, None] * CAP + slot_ids
    rows_per = blocks_seq * CAP
    token_grid = jnp.broadcast_to(positions[:, None], (length, TOPK))
    sources = jnp.zeros((EXPERTS, rows_per), jnp.int32).at[picked_ids, places].set(token_grid)
    filled = jnp.zeros((EXPERTS, rows_per), jnp.float32).at[picked_ids, places].set(1.0)

    def run_expert(pieces):
        source_rows, fill_rows, weight_in, weight_back = pieces
        expert_rows = low_back(normed_ffn[source_rows] * fill_rows[:, None])
        gate_up = low_back(jnp.dot(expert_rows, weight_in, precision=highest))
        hidden = low(jax.nn.silu(gate_up[:, :FF]) * gate_up[:, FF:])
        return low(low_back(jnp.dot(hidden, weight_back.T, precision=highest)))
    outputs = lax.map(jax.checkpoint(run_expert), (sources, filled, moved_in, moved_out))
    picked = outputs[picked_ids, places]
    mixture = lax.optimization_barrier(jnp.sum(gate_weights[..., None] * picked, axis=1))
    return middle + mixture

def reference(tokens, segment_ids, valid_mask, routes, attn_gain, w_query, w_key, w_value, w_out, query_gain, key_gain, ffn_gain, router, expert_in, expert_out, cotangent):
    params = tuple((weight_arg.astype(jnp.float32) for weight_arg in (attn_gain, w_query, w_key, w_value, w_out, query_gain, key_gain, ffn_gain, router, expert_in, expert_out)))
    inputs = tokens.astype(jnp.float32)
    route_seq = routes.reshape(N_DP, SEQ, TOPK)

    def forward(layer_in, *weights):
        prepared = tuple(weights[:9]) + (jnp.moveaxis(weights[9], 1, 0), jnp.moveaxis(weights[10], 1, 0))

        def per_sequence(running, pieces):
            seq_in, seq_seg, seq_valid, seq_picks = pieces
            return (running, block_layer(prepared, seq_in, seq_seg, seq_valid, seq_picks))
        _, result = lax.scan(jax.checkpoint(per_sequence), jnp.zeros((), jnp.float32), (layer_in.reshape(N_DP, SEQ, D), segment_ids, valid_mask, route_seq))
        return result.reshape(TOKENS, D)
    result, pullback = jax.vjp(forward, inputs, *params)
    gradients = pullback(cotangent.astype(jnp.float32))
    return (result.astype(jnp.bfloat16), gradients[0], gradients[1], gradients[2], gradients[3], gradients[4], gradients[5], gradients[6], gradients[7], gradients[8], gradients[9], gradients[10], gradients[11])
```

```python
import functools
import math

import jax
import jax.numpy as jnp
from jax import lax
from jax.experimental import pallas as pl
from jax.experimental.pallas import tpu as pltpu
from jax.sharding import PartitionSpec as P

HEADS = 16
HD = 128
FF = 1024
TOPK = 8
EXP_DEV = 2
CAP = 24
EXPERTS = 64

epsilon = 1e-06
rope_base = 50000.0
highest = lax.Precision.HIGHEST
f32 = jnp.float32
bf16 = jnp.bfloat16
i32 = jnp.int32
MESH = pl.DeviceIdType.MESH
ANY = pl.BlockSpec(memory_space=pl.ANY)
VMEM = pl.BlockSpec(memory_space=pltpu.VMEM)
SMEM = pl.BlockSpec(memory_space=pltpu.SMEM)
DMA = pltpu.SemaphoreType.DMA


def rms_rows(values):
    return lax.rsqrt(jnp.mean(values * values, axis=-1, keepdims=True) + epsilon)


def rms_back(values, inverse, grad_scaled):
    inner_mean = jnp.mean(grad_scaled * values, axis=-1, keepdims=True)
    return inverse * grad_scaled - values * inverse * inverse * inverse * inner_mean


def wrap4(value):
    return lax.rem(value + 4, 4)


class Place:
    def __init__(self):
        head, blk = lax.axis_index("head"), lax.axis_index("blk")
        self.dp = lax.axis_index("dp")
        self.yh, self.co = head // 2, lax.rem(head, 2)
        self.yl, self.x = blk // 4, lax.rem(blk, 4)
        self.head = head
        self.zr, self.zl, self.zo = (wrap4(self.dp + s) for s in (1, -1, 2))
        self.xr, self.xl, self.xo = (wrap4(self.x + s) for s in (1, -1, 2))
        y = self.yh * 2 + self.yl
        self.yr, self.ylf, self.yo = (wrap4(y + s) for s in (1, -1, 2))
        self.ZR, self.ZL = {"dp": self.zr}, {"dp": self.zl}
        self.XR, self.XL, self.XO = (self.to_x(v) for v in (self.xr, self.xl, self.xo))
        self.Y = {"blk": (1 - self.yl) * 4 + self.x}
        self.C = {"head": self.yh * 2 + (1 - self.co)}
        self.H = {"head": (1 - self.yh) * 2 + self.co}
        self.YR, self.YL = self.to_y(self.yr), self.to_y(self.ylf)

    def to_x(self, x):
        return {"blk": self.yl * 4 + x}

    def to_y(self, y):
        return {"head": (y // 2) * 2 + self.co, "blk": lax.rem(y, 2) * 4 + self.x}


def greet(devices):
    barrier = pltpu.get_barrier_semaphore()
    for device in devices:
        pl.semaphore_signal(barrier, inc=1, device_id=device, device_id_type=MESH)
    pl.semaphore_wait(barrier, len(devices))


class Wire:
    def __init__(self, send_sem, recv_sem):
        self.send_sem, self.recv_sem, self.started = send_sem, recv_sem, []

    def send(self, src, dst, device):
        at = len(self.started)
        copy = pltpu.make_async_remote_copy(
            src_ref=src,
            dst_ref=dst,
            send_sem=self.send_sem.at[at],
            recv_sem=self.recv_sem.at[at],
            device_id=device,
            device_id_type=MESH,
        )
        copy.start()
        self.started.append(copy)
        return copy

    def drain(self):
        for copy in self.started:
            copy.wait_send()


def local(src, dst, sem):
    copy = pltpu.make_async_copy(src, dst, sem)
    copy.start()
    return copy


def remote_call(body, name, cid, sends, locals_, ins, outs, out_shape, scratch=(), vmem=None):
    return pl.pallas_call(
        body,
        name=name,
        out_shape=out_shape,
        in_specs=ins,
        out_specs=outs,
        scratch_shapes=[DMA((sends,)), DMA((sends,)), DMA((max(locals_, 1),)), *scratch],
        compiler_params=pltpu.CompilerParams(
            collective_id=cid, has_side_effects=True, vmem_limit_bytes=vmem
        ),
    )


def shaped(shape, dtype=bf16):
    return jax.ShapeDtypeStruct(shape, dtype)


def weights_kernel(w, wo, n, g, go, m, ss, rs, ls):
    p = Place()
    dp, yl, x = p.dp, p.yl, p.x
    own = [
        local(w, g.at[:, dp, yl, x], ls.at[0]),
        local(n, m.at[p.head], ls.at[1]),
        local(wo, go.at[dp], ls.at[2]),
    ]
    greet([p.ZR, p.ZL, p.XR, p.XL, p.Y, p.C, p.H])
    wire = Wire(ss, rs)
    n_c = wire.send(n, m.at[p.head], p.C)
    z1 = wire.send(w, g.at[:, dp, yl, x], p.ZR)
    z2 = wire.send(w, g.at[:, dp, yl, x], p.ZL)
    n_h = wire.send(n, m.at[p.head], p.H)
    o1 = wire.send(wo, go.at[dp], p.ZR)
    o2 = wire.send(wo, go.at[dp], p.ZL)
    z1.wait_recv()
    z3 = wire.send(g.at[0:2, p.zl, yl, x], g.at[0:2, p.zl, yl, x], p.ZR)
    z2.wait_recv()
    z4 = wire.send(g.at[2, p.zr, yl, x], g.at[2, p.zr, yl, x], p.ZL)
    own[0].wait()
    z3.wait_recv()
    z4.wait_recv()
    b1 = wire.send(g.at[2, :, yl, x], g.at[2, :, yl, x], p.XR)
    b2 = wire.send(g.at[2, :, yl, x], g.at[2, :, yl, x], p.XL)
    a1 = wire.send(g.at[0:2, :, yl, x], g.at[0:2, :, yl, x], p.Y)
    c1 = wire.send(g.at[2, :, yl, x], g.at[2, :, yl, x], p.Y)
    o1.wait_recv()
    o3 = wire.send(go.at[p.zl, 0:32], go.at[p.zl, 0:32], p.ZR)
    o2.wait_recv()
    o4 = wire.send(go.at[p.zr, 32:64], go.at[p.zr, 32:64], p.ZL)
    n_h.wait_recv()
    other = (1 - p.yh) * 2 + p.co
    n_f = wire.send(m.at[other], m.at[other], p.C)
    b1.wait_recv()
    b3 = wire.send(g.at[2, 0:2, yl, p.xl], g.at[2, 0:2, yl, p.xl], p.XR)
    c2 = wire.send(g.at[2, :, yl, p.xl], g.at[2, :, yl, p.xl], p.Y)
    b2.wait_recv()
    b4 = wire.send(g.at[2, 2:4, yl, p.xr], g.at[2, 2:4, yl, p.xr], p.XL)
    c3 = wire.send(g.at[2, :, yl, p.xr], g.at[2, :, yl, p.xr], p.Y)
    a1.wait_recv()
    a2 = wire.send(g.at[0:2, :, :, x], g.at[0:2, :, :, x], p.XR)
    a3 = wire.send(g.at[0:2, :, :, x], g.at[0:2, :, :, x], p.XL)
    b3.wait_recv()
    b4.wait_recv()
    c4 = wire.send(g.at[2, :, yl, p.xo], g.at[2, :, yl, p.xo], p.Y)
    a2.wait_recv()
    a4 = wire.send(g.at[0, :, :, p.xl], g.at[0, :, :, p.xl], p.XR)
    a3.wait_recv()
    a5 = wire.send(g.at[1, :, :, p.xr], g.at[1, :, :, p.xr], p.XL)
    for copy in (n_c, n_f, o3, o4, c1, c2, c3, c4, a4, a5):
        copy.wait_recv()
    own[1].wait()
    own[2].wait()
    wire.drain()


def gather_weights(w, wo, n):
    return remote_call(
        weights_kernel,
        "gather_weights",
        1,
        24,
        3,
        [ANY] * 3,
        [ANY] * 3,
        (shaped((3, 4, 2, 4, 64, 512)), shaped((4, 64, 512)), shaped((4, 128, 2048))),
    )(w, wo, n)


def rows_kernel(n, m, ss, rs, ls):
    p = Place()
    own = local(n, m.at[p.head], ls.at[0])
    greet([p.C, p.H])
    wire = Wire(ss, rs)
    n_h = wire.send(n, m.at[p.head], p.H)
    n_c = wire.send(n, m.at[p.head], p.C)
    n_h.wait_recv()
    other = (1 - p.yh) * 2 + p.co
    n_f = wire.send(m.at[other], m.at[other], p.C)
    n_c.wait_recv()
    n_f.wait_recv()
    own.wait()
    wire.drain()


def gather_rows(n):
    return remote_call(
        rows_kernel, "gather_rows", 2, 3, 1, [ANY], [ANY], (shaped((4, 128, 2048)),)
    )(n)[0]


def sum_kernel(part, out, ss, rs, ls, got_c, got_h, half):
    p = Place()
    greet([p.C, p.H])
    wire = Wire(ss, rs)
    far = wire.send(part.at[1 - p.yh, 1 - p.co], got_c.at[0], p.C)
    near = wire.send(part.at[p.yh, 1 - p.co], got_c.at[1], p.C)
    far.wait_recv()

    def add_far(i, carry):
        rows = pl.ds(pl.multiple_of(i * 16, 16), 16)
        half[rows] = (
            part[1 - p.yh, p.co, rows].astype(f32) + got_c[0, rows].astype(f32)
        ).astype(bf16)
        return carry

    lax.fori_loop(0, 8, add_far, 0)
    over = wire.send(half, got_h, p.H)
    near.wait_recv()
    over.wait_recv()

    def add_near(i, carry):
        rows = pl.ds(pl.multiple_of(i * 16, 16), 16)
        out[rows] = (
            part[p.yh, p.co, rows].astype(f32)
            + got_c[1, rows].astype(f32)
            + got_h[rows].astype(f32)
        )
        return carry

    lax.fori_loop(0, 8, add_near, 0)
    wire.drain()


def sum_rows(part, cid):
    return remote_call(
        sum_kernel,
        "sum_rows",
        cid,
        3,
        1,
        [VMEM],
        [VMEM],
        (shaped((128, 2048), f32),),
        scratch=[
            pltpu.VMEM((2, 128, 2048), bf16),
            pltpu.VMEM((128, 2048), bf16),
            pltpu.VMEM((128, 2048), bf16),
        ],
        vmem=16 << 20,
    )(part.reshape(2, 2, 128, 2048))[0]


def heads_kernel(q, k, v, go, qd, kd, vd, gd, ss, rs, ls):
    p = Place()
    yl, x = p.yl, p.x
    own = [
        local(q.at[x], qd.at[:, x], ls.at[0]),
        local(k.at[x], kd.at[:, yl, x], ls.at[1]),
        local(v.at[x], vd.at[:, yl, x], ls.at[2]),
        local(go, gd.at[:, yl, x], ls.at[3]),
    ]
    greet([p.Y, p.XR, p.XL, p.XO])
    wire = Wire(ss, rs)
    done = [
        wire.send(k.at[x], kd.at[:, yl, x], p.Y),
        wire.send(v.at[x], vd.at[:, yl, x], p.Y),
    ]
    w1 = wire.send(go, gd.at[:, yl, x], p.Y)
    moved = []
    for there, came, device in ((p.xo, p.xo, p.XO), (p.xr, p.xl, p.XR), (p.xl, p.xr, p.XL)):
        ks = wire.send(k.at[there], kd.at[:, yl, x], device)
        vs = wire.send(v.at[there], vd.at[:, yl, x], device)
        moved.append((came, ks, vs))
    for there, device in ((p.xo, p.XO), (p.xr, p.XR), (p.xl, p.XL)):
        done.append(wire.send(q.at[there], qd.at[:, x], device))
    for came, ks, vs in moved[1:] + moved[:1]:
        ks.wait_recv()
        done.append(wire.send(kd.at[:, yl, came], kd.at[:, yl, came], p.Y))
        vs.wait_recv()
        done.append(wire.send(vd.at[:, yl, came], vd.at[:, yl, came], p.Y))
    own[3].wait()
    w1.wait_recv()
    w2 = wire.send(gd.at[:, :, x], gd.at[:, :, x], p.XR)
    w3 = wire.send(gd.at[:, :, x], gd.at[:, :, x], p.XL)
    w2.wait_recv()
    done.append(wire.send(gd.at[0:2, :, p.xl], gd.at[0:2, :, p.xl], p.XR))
    w3.wait_recv()
    done.append(wire.send(gd.at[2:4, :, p.xr], gd.at[2:4, :, p.xr], p.XL))
    for copy in done:
        copy.wait_recv()
    for copy in own[:3]:
        copy.wait()
    wire.drain()


def heads_over_x(q, k, v, go):
    return remote_call(
        heads_kernel,
        "heads_over_x",
        3,
        22,
        4,
        [ANY] * 4,
        [ANY] * 4,
        (
            shaped((4, 4, 128, 128)),
            shaped((4, 2, 4, 128, 128)),
            shaped((4, 2, 4, 128, 128)),
            shaped((4, 2, 4, 64, 512)),
        ),
    )(q, k, v, go)


def back_x_kernel(o, att, ss, rs, ls):
    p = Place()
    own = local(o.at[:, p.x], att.at[p.x], ls.at[0])
    greet([p.XR, p.XL, p.XO])
    wire = Wire(ss, rs)
    for there, device in ((p.xo, p.XO), (p.xr, p.XR), (p.xl, p.XL)):
        wire.send(o.at[:, there], att.at[p.x], device)
    for copy in wire.started:
        copy.wait_recv()
    own.wait()
    wire.drain()


def back_over_x(o):
    return remote_call(
        back_x_kernel, "back_over_x", 4, 3, 1, [ANY], [ANY], (shaped((4, 4, 128, 128)),)
    )(o)[0]


def go_x_kernel(o, d, ss, rs, ls):
    p = Place()
    own = local(o.at[p.x], d.at[:, p.x], ls.at[0])
    greet([p.XR, p.XL, p.XO])
    wire = Wire(ss, rs)
    for there, device in ((p.xo, p.XO), (p.xr, p.XR), (p.xl, p.XL)):
        wire.send(o.at[there], d.at[:, p.x], device)
    for copy in wire.started:
        copy.wait_recv()
    own.wait()
    wire.drain()


def go_over_x(o):
    return remote_call(
        go_x_kernel, "go_over_x", 5, 3, 1, [ANY], [ANY], (shaped((4, 4, 128, 128)),)
    )(o)[0]


def grads_x_kernel(dq, dk, dv, qd, kd, vd, ss, rs, ls, gk, gv, sk, sv):
    p = Place()
    x, yl = p.x, p.yl
    own = local(dq.at[:, x], qd.at[x], ls.at[0])
    greet([p.Y, p.XR, p.XL, p.XO])
    wire = Wire(ss, rs)
    order = ((p.xo, p.XO), (p.xr, p.XR), (p.xl, p.XL), (x, None))
    pairs = []
    for i, (there, device) in enumerate(order):
        pairs.append(
            (
                wire.send(dk.at[:, 1 - yl, there], gk.at[i], p.Y),
                wire.send(dv.at[:, 1 - yl, there], gv.at[i], p.Y),
            )
        )
    last = []
    for there, device in order[:3]:
        last.append(wire.send(dq.at[:, there], qd.at[x], device))
    for i, (there, device) in enumerate(order):
        for grads, got, summed, out, arrived in (
            (dk, gk, sk, kd, pairs[i][0]),
            (dv, gv, sv, vd, pairs[i][1]),
        ):
            arrived.wait_recv()
            for run in range(4):
                total = grads[run, yl, there].astype(f32) + got[i, run].astype(f32)
                if device is None:
                    out[x, run] = total.astype(bf16)
                else:
                    summed[i, run] = total.astype(bf16)
            if device is not None:
                last.append(wire.send(summed.at[i], out.at[x], device))
    for copy in last:
        copy.wait_recv()
    own.wait()
    wire.drain()


def grads_over_x(dq, dk, dv):
    return remote_call(
        grads_x_kernel,
        "grads_over_x",
        6,
        17,
        1,
        [ANY, VMEM, VMEM],
        [ANY, VMEM, VMEM],
        (shaped((4, 4, 128, 128)),) * 3,
        scratch=[
            pltpu.VMEM((4, 4, 128, 128), bf16),
            pltpu.VMEM((4, 4, 128, 128), bf16),
            pltpu.VMEM((3, 4, 128, 128), bf16),
            pltpu.VMEM((3, 4, 128, 128), bf16),
        ],
        vmem=16 << 20,
    )(dq, dk, dv)


QB = 256
KB = 512
SCALE = HD**-0.5
SCALE2 = SCALE * math.log2(math.e)


def attend_kernel(lim, q, k, v, qseg, qpos, kseg, o_low, o, linv, vext):
    rows = k.shape[0]
    ones = (lax.broadcasted_iota(i32, (KB, HD), 1) == 0).astype(bf16)

    def fill(i, carry):
        at = pl.ds(pl.multiple_of(i * KB, KB), KB)
        vext[at, :HD] = v[at]
        vext[at, HD:] = ones
        return carry

    lax.fori_loop(0, rows // KB, fill, 0)

    def one_query(b, carry):
        at = pl.ds(pl.multiple_of(b * QB, QB), QB)
        query, seg, pos = q[at], qseg[at], qpos[at]

        def one_key(j, acc):
            keys = pl.ds(pl.multiple_of(j * KB, KB), KB)
            score = lax.dot_general(
                query, k[keys], (((1,), (1,)), ((), ())), preferred_element_type=f32
            )
            key_pos = j * KB + lax.broadcasted_iota(i32, (1, KB), 1)
            allowed = (seg == kseg[:, keys]) | (pos == key_pos)
            weight = jnp.where(allowed, jnp.exp2(score * SCALE2), 0.0).astype(bf16)
            return acc + jnp.dot(weight, vext[keys], preferred_element_type=f32)

        acc = lax.fori_loop(lim[0, b], lim[1, b], one_key, jnp.zeros((QB, 2 * HD), f32))
        inverse = 1.0 / acc[:, HD : HD + 1]
        result = acc[:, :HD] * inverse
        o[at] = result
        o_low[at] = result.astype(bf16)
        linv[at] = jnp.broadcast_to(inverse, (QB, HD))
        return carry

    lax.fori_loop(0, q.shape[0] // QB, one_query, 0)


def attend(lim, q, k, v, qseg, qpos, kseg):
    n = q.shape[0]
    return pl.pallas_call(
        attend_kernel,
        name="attend",
        out_shape=(shaped((n, HD)), shaped((n, HD), f32), shaped((n, HD), f32)),
        in_specs=[SMEM] + [VMEM] * 6,
        out_specs=[VMEM] * 3,
        scratch_shapes=[pltpu.VMEM((k.shape[0], 2 * HD), bf16)],
        compiler_params=pltpu.CompilerParams(vmem_limit_bytes=32 << 20),
    )(lim, q, k, v, qseg[:, None], qpos[:, None], kseg[None])


def attend_back_kernel(
    lim, q, k, v, g, qseg, qpos, kseg, linv, delta, dq, dk, dv, kt, dk_acc, dv_acc
):
    rows = k.shape[0]

    def fill(i, carry):
        at = pl.ds(pl.multiple_of(i * KB, KB), KB)
        kt[:, at] = k[at].astype(f32).T.astype(bf16)
        dk_acc[at] = jnp.zeros((KB, HD), f32)
        dv_acc[at] = jnp.zeros((KB, HD), f32)
        return carry

    lax.fori_loop(0, rows // KB, fill, 0)
    across = (((1,), (1,)), ((), ()))

    def one_query(b, carry):
        at = pl.ds(pl.multiple_of(b * QB, QB), QB)
        query, grad = q[at], g[at]
        seg, pos, inverse, shift = qseg[:, at], qpos[:, at], linv[:, at], delta[:, at]

        def one_key(j, acc):
            keys = pl.ds(pl.multiple_of(j * KB, KB), KB)
            key = k[keys]
            score = lax.dot_general(key, query, across, preferred_element_type=f32)
            key_pos = j * KB + lax.broadcasted_iota(i32, (KB, 1), 0)
            allowed = (kseg[keys] == seg) | (key_pos == pos)
            prob = jnp.where(allowed, jnp.exp2(score * SCALE2), 0.0) * inverse
            grad_prob = lax.dot_general(v[keys], grad, across, preferred_element_type=f32)
            grad_score = (prob * (grad_prob - shift)).astype(bf16)
            dv_acc[keys] += jnp.dot(prob.astype(bf16), grad, preferred_element_type=f32)
            dk_acc[keys] += jnp.dot(grad_score, query, preferred_element_type=f32)
            return acc + jnp.dot(kt[:, keys], grad_score, preferred_element_type=f32)

        acc = lax.fori_loop(lim[0, b], lim[1, b], one_key, jnp.zeros((HD, QB), f32))
        dq[at] = (acc * SCALE).T.astype(bf16)
        return carry

    lax.fori_loop(0, q.shape[0] // QB, one_query, 0)

    def finish(i, carry):
        at = pl.ds(pl.multiple_of(i * KB, KB), KB)
        dk[at] = (dk_acc[at] * SCALE).astype(bf16)
        dv[at] = dv_acc[at].astype(bf16)
        return carry

    lax.fori_loop(0, rows // KB, finish, 0)


def attend_back(lim, q, k, v, g, qseg, qpos, kseg, linv, delta):
    n, rows = q.shape[0], k.shape[0]
    return pl.pallas_call(
        attend_back_kernel,
        name="attend_back",
        out_shape=(shaped((n, HD)), shaped((rows, HD)), shaped((rows, HD))),
        in_specs=[SMEM] + [VMEM] * 9,
        out_specs=[VMEM] * 3,
        scratch_shapes=[
            pltpu.VMEM((HD, rows), bf16),
            pltpu.VMEM((rows, HD), f32),
            pltpu.VMEM((rows, HD), f32),
        ],
        compiler_params=pltpu.CompilerParams(vmem_limit_bytes=40 << 20),
    )(lim, q, k, v, g, qseg[None], qpos[None], kseg[:, None], linv[None], delta[None])


def spread_kernel(src, dst, ss, rs, ls):
    p = Place()
    yh, co, yl, x = p.yh, p.co, p.yl, p.x
    own = local(src, dst.at[yh, co, yl, x], ls.at[0])
    greet([p.XR, p.XL, p.YR, p.YL, p.C])
    wire = Wire(ss, rs)
    A, A1, A2 = pl.ds(0, 64), pl.ds(0, 32), pl.ds(32, 32)
    B, B1, B2 = pl.ds(64, 64), pl.ds(64, 32), pl.ds(96, 32)

    def at_y(y, rows):
        return dst.at[y // 2, co, lax.rem(y, 2), :, rows]

    def at_x(xx, rows):
        return dst.at[:, co, :, xx, rows]

    def both(ref, device):
        return wire.send(ref, ref, device)

    y = yh * 2 + yl
    me = dst.at[yh, co, yl]
    a1 = wire.send(src.at[A], me.at[x, A], p.XR)
    b1 = wire.send(src.at[B], me.at[x, B], p.YR)
    a2 = wire.send(src.at[A], me.at[x, A], p.XL)
    b2 = wire.send(src.at[B], me.at[x, B], p.YL)
    a1.wait_recv()
    a3 = both(me.at[p.xl, A1], p.XR)
    a2.wait_recv()
    a4 = both(me.at[p.xr, A2], p.XL)
    yr, ylf, yo = p.yr, p.ylf, p.yo

    def block(yy, rows):
        return dst.at[yy // 2, co, lax.rem(yy, 2), x, rows]

    b1.wait_recv()
    b3 = both(block(ylf, B1), p.YR)
    b2.wait_recv()
    b4 = both(block(yr, B2), p.YL)
    own.wait()
    a3.wait_recv()
    a4.wait_recv()
    a5 = both(at_y(y, A), p.YR)
    a6 = both(at_y(y, A), p.YL)
    b3.wait_recv()
    b4.wait_recv()
    b5 = both(at_x(x, B), p.XR)
    b6 = both(at_x(x, B), p.XL)
    last = [both(at_y(y, A), p.C), both(at_x(x, B), p.C)]
    a5.wait_recv()
    a7 = both(at_y(ylf, A1), p.YR)
    b5.wait_recv()
    b7 = both(at_x(p.xl, B1), p.XR)
    a6.wait_recv()
    a8 = both(at_y(yr, A2), p.YL)
    b6.wait_recv()
    b8 = both(at_x(p.xr, B2), p.XL)
    last += [both(at_y(ylf, A), p.C), both(at_x(p.xl, B), p.C)]
    last += [both(at_y(yr, A), p.C), both(at_x(p.xr, B), p.C)]
    a7.wait_recv()
    last.append(both(at_y(yo, A1), p.C))
    b7.wait_recv()
    last.append(both(at_x(p.xo, B1), p.C))
    a8.wait_recv()
    last.append(both(at_y(yo, A2), p.C))
    b8.wait_recv()
    last.append(both(at_x(p.xo, B2), p.C))
    for copy in last:
        copy.wait_recv()
    wire.drain()


def spread(src):
    width = src.shape[1]
    return remote_call(
        spread_kernel,
        "spread",
        7,
        26,
        1,
        [ANY],
        [ANY],
        (shaped((2, 2, 2, 4, 128, width)),),
    )(src)[0].reshape(32, 128, width)


def pick_kernel(sel, src, rows_out, grads_out):
    width = rows_out.shape[-1]
    tokens = jnp.concatenate([src[0, :, :width], src[1, :, :width]], axis=0)
    cot = jnp.concatenate([src[0, :, width : 2 * width], src[1, :, width : 2 * width]], axis=0)
    info = jnp.concatenate([src[0, :, 2 * width :], src[1, :, 2 * width :]], axis=0)
    table = lax.dot_general(
        sel[...], info, (((1,), (1,)), ((), ())), preferred_element_type=f32
    )
    row = lax.broadcasted_iota(i32, (2 * CAP, 256), 0)
    block = lax.broadcasted_iota(i32, (2 * CAP, 256), 1) // 128
    want = row - block * CAP
    for e in range(EXP_DEV):
        slot = jnp.broadcast_to(table[e : e + 1], (2 * CAP, 256)).astype(i32)
        hit = (slot == want) & (want >= 0) & (want < CAP)
        one = hit.astype(bf16)
        gate = jnp.sum(jnp.where(hit, table[2 + e : 3 + e], 0.0), axis=1, keepdims=True)
        rows_out[e, 0] = jnp.dot(one, tokens, preferred_element_type=f32).astype(bf16)
        grads_out[e, 0] = (jnp.dot(one, cot, preferred_element_type=f32) * gate).astype(bf16)


def pick_rows(sel, src, width):
    blocks, _, full = src.shape
    pairs = blocks // 2
    out = shaped((EXP_DEV, pairs, 2 * CAP, width))
    spec = pl.BlockSpec((EXP_DEV, 1, 2 * CAP, width), lambda i: (0, i, 0, 0))
    return pl.pallas_call(
        pick_kernel,
        name="pick_rows",
        grid=(pairs,),
        out_shape=(out, out),
        in_specs=[
            pl.BlockSpec((8, 128), lambda i: (0, 0)),
            pl.BlockSpec((2, 128, full), lambda i: (i, 0, 0)),
        ],
        out_specs=[spec, spec],
        compiler_params=pltpu.CompilerParams(vmem_limit_bytes=40 << 20),
    )(sel, src)


def fold_kernel(p0, p1, p2, p3, out, ss, rs, ls, ra, rb, rc, rd, re, rf, rg, acc_x, acc_y):
    p = Place()
    dp, yl, x = p.dp, p.yl, p.x
    greet([p.ZR, p.ZL, p.XR, p.XL, p.Y])
    wire = Wire(ss, rs)

    def added(dst, *srcs):
        total = srcs[0][...].astype(f32)
        for src in srcs[1:]:
            total = total + src[...].astype(f32)
        dst[...] = total.astype(dst.dtype)

    def loop(count, body):
        def step(i, carry):
            body(i)
            return carry

        lax.fori_loop(0, count, step, 0)

    firsts = []
    for i, part in ((2, p2), (3, p3)):
        firsts.append(wire.send(part.at[:, 1 - yl], rb.at[i - 2], p.Y))
    starts = []
    for i, part in ((0, p0), (1, p1)):
        starts.append(
            (
                wire.send(part.at[0:2, :, p.xo], ra.at[i, 0], p.XR),
                wire.send(part.at[2:4, :, p.xo], ra.at[i, 1], p.XL),
            )
        )
    seconds = []
    for i, part in ((0, p0), (1, p1)):
        one, two = starts[i]
        one.wait_recv()
        loop(2, lambda d: added(part.at[d, :, p.xr], part.at[d, :, p.xr], ra.at[i, 0, d]))
        s1 = wire.send(part.at[:, :, p.xr], rc.at[i, 0], p.XR)
        two.wait_recv()
        loop(2, lambda d: added(part.at[d + 2, :, p.xl], part.at[d + 2, :, p.xl], ra.at[i, 1, d]))
        s2 = wire.send(part.at[:, :, p.xl], rc.at[i, 1], p.XL)
        seconds.append((s1, s2))
    mids = []
    for i, part in ((2, p2), (3, p3)):
        firsts[i - 2].wait_recv()
        loop(4, lambda d: added(acc_y.at[i - 2, d], part.at[d, yl], rb.at[i - 2, d]))
        acc = acc_y.at[i - 2]
        mids.append(
            (
                wire.send(acc.at[0:2, p.xo], rd.at[i - 2, 0], p.XR),
                wire.send(acc.at[2:4, p.xo], rd.at[i - 2, 1], p.XL),
            )
        )
    yends = []
    for i, part in ((0, p0), (1, p1)):
        for s in seconds[i]:
            s.wait_recv()
        acc = acc_x.at[i]
        loop(4, lambda d: added(acc.at[d], part.at[d, :, x], rc.at[i, 0, d], rc.at[i, 1, d]))
        yends.append(wire.send(acc.at[:, 1 - yl], re.at[i], p.Y))
    xends = []
    for i in (2, 3):
        acc = acc_y.at[i - 2]
        one, two = mids[i - 2]
        one.wait_recv()
        loop(2, lambda d: added(acc.at[d, p.xr], acc.at[d, p.xr], rd.at[i - 2, 0, d]))
        s1 = wire.send(acc.at[:, p.xr], rf.at[i - 2, 0], p.XR)
        two.wait_recv()
        loop(2, lambda d: added(acc.at[d + 2, p.xl], acc.at[d + 2, p.xl], rd.at[i - 2, 1, d]))
        s2 = wire.send(acc.at[:, p.xl], rf.at[i - 2, 1], p.XL)
        xends.append((s1, s2))
    parts = []
    zs = []

    def z_first(i, acc):
        parts.append(acc)
        zs.append(
            (
                wire.send(acc.at[p.zo, 0:32], rg.at[i, 0, 0:32], p.ZR),
                wire.send(acc.at[p.zo, 32:64], rg.at[i, 1, 0:32], p.ZL),
            )
        )

    for i in (0, 1):
        yends[i].wait_recv()
        acc = acc_x.at[i]
        loop(4, lambda d: added(acc.at[d, yl], acc.at[d, yl], re.at[i, d]))
        z_first(i, acc.at[:, yl])
    for i in (2, 3):
        for s in xends[i - 2]:
            s.wait_recv()
        acc = acc_y.at[i - 2]
        loop(
            4, lambda d: added(acc.at[d, x], acc.at[d, x], rf.at[i - 2, 0, d], rf.at[i - 2, 1, d])
        )
        z_first(i, acc.at[:, x])
    ends = []
    for i in range(4):
        one, two = zs[i]
        acc = parts[i]
        one.wait_recv()
        added(acc.at[p.zr, 0:32], acc.at[p.zr, 0:32], rg.at[i, 0, 0:32])
        s1 = wire.send(acc.at[p.zr], rg.at[i, 2], p.ZR)
        two.wait_recv()
        added(acc.at[p.zl, 32:64], acc.at[p.zl, 32:64], rg.at[i, 1, 0:32])
        s2 = wire.send(acc.at[p.zl], rg.at[i, 3], p.ZL)
        ends.append((s1, s2))
    for i in range(4):
        for s in ends[i]:
            s.wait_recv()
        added(out.at[i], parts[i].at[dp], rg.at[i, 2], rg.at[i, 3])
    wire.drain()


def fold_grads(grads):
    return remote_call(
        fold_kernel,
        "fold_grads",
        8,
        36,
        1,
        [VMEM] * 4,
        [VMEM],
        (shaped((4, 64, 512), f32),),
        scratch=[
            pltpu.VMEM((2, 2, 2, 2, 64, 512), bf16),
            pltpu.VMEM((2, 4, 4, 64, 512), bf16),
            pltpu.VMEM((2, 2, 4, 2, 64, 512), bf16),
            pltpu.VMEM((2, 2, 2, 64, 512), bf16),
            pltpu.VMEM((2, 4, 64, 512), bf16),
            pltpu.VMEM((2, 2, 4, 64, 512), bf16),
            pltpu.VMEM((4, 4, 64, 512), bf16),
            pltpu.VMEM((2, 4, 2, 64, 512), bf16),
            pltpu.VMEM((2, 4, 4, 64, 512), bf16),
        ],
        vmem=48 << 20,
    )(*[g.reshape(4, 2, 4, 64, 512) for g in grads])[0]


def on_device(
    tokens,
    segment_ids,
    valid_mask,
    routes,
    attn_gain,
    w_query,
    w_key,
    w_value,
    w_out,
    query_gain,
    key_gain,
    ffn_gain,
    router,
    expert_in,
    expert_out,
    cotangent,
):
    blk = lax.axis_index("blk")
    device = lax.axis_index("head") * 8 + blk
    yl = blk // 4
    tok, width = tokens.shape
    full_in = lax.all_gather(expert_in, "dp", axis=0, tiled=True)
    full_back = lax.all_gather(expert_out, "dp", axis=0, tiled=True)

    segment, valid = segment_ids[0], valid_mask[0]
    seq_len = segment.shape[0]
    place = jnp.arange(seq_len, dtype=i32)
    query_ids = (jnp.arange(4)[:, None] * 1024 + blk * 128 + jnp.arange(128)[None]).reshape(-1)
    frequency = rope_base ** (-jnp.arange(64, dtype=f32) / 64)
    angles = query_ids.astype(f32)[:, None] * frequency[None]
    cosine, sine = jnp.cos(angles)[None], jnp.sin(angles)[None]
    half_ids = (jnp.arange(4)[:, None] * 1024 + yl * 512 + jnp.arange(512)[None]).reshape(-1)
    half_seg = lax.dynamic_index_in_dim(segment.reshape(4, 2, 512), yl, 1, keepdims=False).reshape(-1)
    key_seg = jnp.where(valid > 0, segment, -1)
    ends = half_seg.reshape(-1, QB)
    lower = jnp.sum(segment[None] < ends[:, :1], axis=1, dtype=i32) // KB
    upper = (jnp.sum(segment[None] <= ends[:, -1:], axis=1, dtype=i32) + KB - 1) // KB
    limits = jnp.stack([lower, upper])

    def rotary(values, turning):
        a, b = values[..., :64], values[..., 64:]
        turned = turning * sine
        return jnp.concatenate([a * cosine - b * turned, b * cosine + a * turned], axis=-1)

    inputs = tokens.astype(f32)
    first_inv = rms_rows(inputs)
    normed = (inputs * first_inv * attn_gain).astype(bf16)
    w_three = jnp.stack([w_query, w_key, w_value])
    gathered, out_part, normed_all = gather_weights(w_three, w_out, normed)
    full_query, full_key, full_value = (gathered[i].reshape(2048, 512) for i in range(3))
    normed_all = normed_all.reshape(512, width)

    def by_head(flat):
        return jnp.transpose(flat.reshape(512, 4, HD), (1, 0, 2))

    def flat_of(heads):
        return jnp.transpose(heads.reshape(4, 512, HD), (1, 0, 2)).reshape(512, 512)

    query_proj = by_head(jnp.dot(normed_all, full_query, preferred_element_type=f32))
    key_proj = by_head(jnp.dot(normed_all, full_key, preferred_element_type=f32))
    value_heads = by_head(jnp.dot(normed_all, full_value, preferred_element_type=f32).astype(bf16))
    query_inv = rms_rows(query_proj)
    query_unit = query_proj * query_inv
    query_heads = rotary(query_unit * query_gain, 1.0).astype(bf16)
    key_inv = rms_rows(key_proj)
    key_unit = key_proj * key_inv
    key_heads = rotary(key_unit * key_gain, 1.0).astype(bf16)

    runs = (4, 4, 128, HD)
    q, k, v, full_out = heads_over_x(
        query_heads.reshape(runs), key_heads.reshape(runs), value_heads.reshape(runs), out_part
    )
    q, k, v = q.reshape(2048, HD), k.reshape(4096, HD), v.reshape(4096, HD)
    full_out = full_out.reshape(2048, 512)
    att_low, att, inverse = attend(limits, q, k, v, half_seg, half_ids, key_seg)
    attended = back_over_x(att_low.reshape(runs))
    attended_flat = flat_of(attended)
    branch_part = jnp.einsum("qc,mc->qm", attended_flat, full_out, preferred_element_type=f32)
    middle = inputs + sum_rows(branch_part.astype(bf16), 9)
    second_inv = rms_rows(middle)
    normed_ffn = (middle * second_inv * ffn_gain).astype(bf16)
    logits = jnp.dot(normed_ffn, router, preferred_element_type=f32)
    probabilities = jax.nn.softmax(logits, axis=-1)

    expert_ids = jnp.arange(EXPERTS, dtype=i32)
    hot = jnp.sum((routes[..., None] == expert_ids).astype(f32), axis=1)
    before = (jnp.arange(tok)[:, None] > jnp.arange(tok)[None]).astype(bf16)
    slots = jnp.dot(before, hot.astype(bf16), preferred_element_type=f32)
    slot_code = jnp.where(hot > 0, slots, -1.0)
    chosen = probabilities * hot
    gate_total = jnp.sum(chosen, axis=-1, keepdims=True)
    gates = chosen / gate_total

    sent = jnp.concatenate(
        [normed_ffn, cotangent, slot_code.astype(bf16), gates.astype(bf16)], axis=1
    )
    everyone = spread(sent)
    lane = jnp.arange(128)[None]
    sel_row = jnp.arange(8)[:, None]
    sel = (
        (sel_row < 4) & (lane == (sel_row // 2) * EXPERTS + device * EXP_DEV + sel_row % 2)
    ).astype(bf16)
    expert_rows, arrived_grads = pick_rows(sel, everyone, width)
    expert_rows = expert_rows.reshape(EXP_DEV, -1, width)
    arrived_grads = arrived_grads.reshape(EXP_DEV, -1, width)

    gate_up = jnp.einsum("erd,def->erf", expert_rows, full_in, preferred_element_type=f32)
    gate_part, up_part = gate_up[..., :FF], gate_up[..., FF:]
    sigmoid_gate = jax.nn.sigmoid(gate_part)
    silu_gate = gate_part * sigmoid_gate
    hidden = (silu_gate * up_part).astype(bf16)
    expert_result = jnp.einsum(
        "erf,def->erd", hidden, full_back, preferred_element_type=f32
    ).astype(bf16)

    def home(rows):
        rows = rows.reshape(EXP_DEV, 32, CAP, width)
        moved = lax.all_to_all(rows, ("head", "blk"), split_axis=1, concat_axis=1, tiled=True)
        return moved.reshape(EXP_DEV * 32 * CAP, width)

    returned = home(expert_result)
    term_back = jnp.einsum("erc,erf->ecf", arrived_grads, hidden, preferred_element_type=f32)
    grad_hidden = jnp.einsum("erd,def->erf", arrived_grads, full_back, preferred_element_type=f32)
    grad_gate = grad_hidden * up_part * sigmoid_gate * (1.0 + gate_part * (1.0 - sigmoid_gate))
    grad_up = grad_hidden * silu_gate
    grad_gate_up = jnp.concatenate([grad_gate, grad_up], axis=-1).astype(bf16)
    grad_rows = jnp.einsum(
        "erf,def->erd", grad_gate_up, full_in, preferred_element_type=f32
    ).astype(bf16)
    back_rows = home(grad_rows)
    term_in = jnp.einsum("erc,erf->ecf", expert_rows, grad_gate_up, preferred_element_type=f32)

    def fold_dp(term):
        return lax.psum_scatter(term.astype(bf16), "dp", scatter_dimension=1, tiled=True)

    expert_out_grad = jnp.transpose(fold_dp(term_back), (1, 0, 2)).astype(f32)
    expert_in_grad = jnp.transpose(fold_dp(term_in), (1, 0, 2)).astype(f32)

    code = jnp.transpose(slot_code.reshape(tok, 32, EXP_DEV), (0, 2, 1))
    home_hot = code[..., None] == jnp.arange(CAP, dtype=f32)
    home_gate = jnp.transpose(gates.reshape(tok, 32, EXP_DEV), (0, 2, 1))[..., None]
    flat_hot = home_hot.reshape(tok, -1)
    mixture = jnp.dot(
        jnp.where(home_hot, home_gate, 0.0).astype(bf16).reshape(tok, -1),
        returned,
        preferred_element_type=f32,
    )
    output = (middle + mixture).astype(bf16)
    grad_out = cotangent.astype(f32)
    dots = jnp.einsum("td,rd->tr", cotangent, returned, preferred_element_type=f32)
    grad_gates = jnp.sum(jnp.where(flat_hot, dots, 0.0).reshape(tok, EXP_DEV, 32, CAP), axis=-1)
    grad_gates = jnp.transpose(grad_gates, (0, 2, 1)).reshape(tok, EXPERTS)
    mean_grad = jnp.sum(grad_gates * gates, axis=-1, keepdims=True)
    grad_probs = (grad_gates - mean_grad) / gate_total * hot
    grad_logits = probabilities * (
        grad_probs - jnp.sum(probabilities * grad_probs, axis=-1, keepdims=True)
    )
    router_term = jnp.dot(normed_ffn.astype(f32).T, grad_logits, precision=highest)
    grad_ffn = jnp.dot(
        flat_hot.astype(bf16), back_rows, preferred_element_type=f32
    ) + jnp.dot(grad_logits, router.astype(f32).T, precision=highest)
    ffn_gain_term = jnp.sum(grad_ffn * middle * second_inv, axis=0)
    grad_middle = grad_out + rms_back(middle, second_inv, grad_ffn * ffn_gain)
    grad_branch = grad_middle.astype(bf16)
    branch_all = gather_rows(grad_branch).reshape(512, width)
    grad_att = by_head(
        jnp.dot(branch_all, full_out, preferred_element_type=f32).astype(bf16)
    )
    grad_att = go_over_x(grad_att.reshape(runs)).reshape(2048, HD)
    delta = jnp.sum(grad_att.astype(f32) * att, axis=-1)
    dq, dk, dv = attend_back(
        limits, q, k, v, grad_att, half_seg, half_ids, key_seg, inverse[:, 0], delta
    )
    cut = (4, 2, 4, 128, HD)
    grad_query, grad_key, grad_value = grads_over_x(
        dq.reshape(runs), dk.reshape(cut), dv.reshape(cut)
    )
    heads_shape = (4, 512, HD)
    grad_query_unit = rotary(grad_query.reshape(heads_shape).astype(f32), -1.0)
    query_gain_term = jnp.sum(grad_query_unit * query_unit, axis=(0, 1))
    grad_query_flat = flat_of(
        rms_back(query_proj, query_inv, grad_query_unit * query_gain).astype(bf16)
    )
    grad_key_unit = rotary(grad_key.reshape(heads_shape).astype(f32), -1.0)
    key_gain_term = jnp.sum(grad_key_unit * key_unit, axis=(0, 1))
    grad_key_flat = flat_of(rms_back(key_proj, key_inv, grad_key_unit * key_gain).astype(bf16))
    grad_value_flat = flat_of(grad_value)
    normed_part = jnp.einsum("qc,dc->qd", grad_query_flat, full_query, preferred_element_type=f32)
    normed_part += jnp.einsum("qc,dc->qd", grad_key_flat, full_key, preferred_element_type=f32)
    normed_part += jnp.einsum("qc,dc->qd", grad_value_flat, full_value, preferred_element_type=f32)
    grad_normed = sum_rows(normed_part.astype(bf16), 10)
    attn_gain_term = jnp.sum(grad_normed * inputs * first_inv, axis=0)
    input_grad = grad_middle + rms_back(inputs, first_inv, grad_normed * attn_gain)

    def weight_grad(rows, grads):
        return jnp.einsum("qc,qf->cf", rows, grads, preferred_element_type=f32).astype(bf16)

    attn_grads = fold_grads(
        [
            weight_grad(normed_all, grad_query_flat),
            weight_grad(normed_all, grad_key_flat),
            weight_grad(normed_all, grad_value_flat),
            weight_grad(branch_all, attended_flat),
        ]
    )
    summed = lax.psum(
        (attn_gain_term, ffn_gain_term, query_gain_term, key_gain_term, router_term),
        ("dp", "head", "blk"),
    )
    return (
        output,
        input_grad,
        summed[0],
        attn_grads[0],
        attn_grads[1],
        attn_grads[2],
        attn_grads[3],
        summed[2],
        summed[3],
        summed[1],
        summed[4],
        expert_in_grad,
        expert_out_grad,
    )


def solution(mesh):
    placed = (
        P(("dp", "head", "blk"), None),
        P("dp", None),
        P("dp", None),
        P(("dp", "head", "blk"), None),
        P(),
        P(("dp", "blk"), "head"),
        P(("dp", "blk"), "head"),
        P(("dp", "blk"), "head"),
        P(("dp", "blk"), "head"),
        P(),
        P(),
        P(),
        P(),
        P("dp", ("head", "blk"), None),
        P("dp", ("head", "blk"), None),
        P(("dp", "head", "blk"), None),
    )
    return jax.shard_map(
        on_device,
        mesh=mesh,
        in_specs=placed,
        out_specs=(
            P(("dp", "head", "blk"), None),
            P(("dp", "head", "blk"), None),
            P(),
            P(("dp", "blk"), "head"),
            P(("dp", "blk"), "head"),
            P(("dp", "blk"), "head"),
            P(("dp", "blk"), "head"),
            P(),
            P(),
            P(),
            P(),
            P("dp", ("head", "blk"), None),
            P("dp", ("head", "blk"), None),
        ),
        check_vma=False,
    )
```

```python
import functools
import math

import jax
import jax.numpy as jnp
from jax import lax
from jax.experimental import pallas as pl
from jax.experimental.pallas import tpu as pltpu
from jax.sharding import PartitionSpec as P

HEADS = 16
HD = 128
FF = 1024
TOPK = 8
EXP_DEV = 2
CAP = 24
EXPERTS = 64

epsilon = 1e-06
rope_base = 50000.0
f32 = jnp.float32
bf16 = jnp.bfloat16
i32 = jnp.int32
MESH = pl.DeviceIdType.MESH
ANY = pl.BlockSpec(memory_space=pl.ANY)
VMEM = pl.BlockSpec(memory_space=pltpu.VMEM)
SMEM = pl.BlockSpec(memory_space=pltpu.SMEM)
DMA = pltpu.SemaphoreType.DMA


def rms_rows(values):
    return lax.rsqrt(jnp.mean(values * values, axis=-1, keepdims=True) + epsilon)


def rms_back(values, inverse, grad_scaled):
    inner_mean = jnp.mean(grad_scaled * values, axis=-1, keepdims=True)
    return inverse * grad_scaled - values * inverse * inverse * inverse * inner_mean


def wrap4(value):
    return lax.rem(value + 4, 4)


class Place:
    def __init__(self):
        head, blk = lax.axis_index("head"), lax.axis_index("blk")
        self.dp = lax.axis_index("dp")
        self.yh, self.co = head // 2, lax.rem(head, 2)
        self.yl, self.x = blk // 4, lax.rem(blk, 4)
        self.head = head
        self.zr, self.zl, self.zo = (wrap4(self.dp + s) for s in (1, -1, 2))
        self.xr, self.xl, self.xo = (wrap4(self.x + s) for s in (1, -1, 2))
        y = self.yh * 2 + self.yl
        self.yr, self.ylf, self.yo = (wrap4(y + s) for s in (1, -1, 2))
        self.ZR, self.ZL, self.ZO = {"dp": self.zr}, {"dp": self.zl}, {"dp": self.zo}
        self.XR, self.XL, self.XO = (self.to_x(v) for v in (self.xr, self.xl, self.xo))
        self.Y = {"blk": (1 - self.yl) * 4 + self.x}
        self.C = {"head": self.yh * 2 + (1 - self.co)}
        self.H = {"head": (1 - self.yh) * 2 + self.co}
        self.YR, self.YL = self.to_y(self.yr), self.to_y(self.ylf)

    def to_x(self, x):
        return {"blk": self.yl * 4 + x}

    def to_y(self, y):
        return {"head": (y // 2) * 2 + self.co, "blk": lax.rem(y, 2) * 4 + self.x}


def greet(devices):
    barrier = pltpu.get_barrier_semaphore()
    for device in devices:
        pl.semaphore_signal(barrier, inc=1, device_id=device, device_id_type=MESH)
    pl.semaphore_wait(barrier, len(devices))


class Wire:
    def __init__(self, send_sem, recv_sem):
        self.send_sem, self.recv_sem, self.started = send_sem, recv_sem, []

    def send(self, src, dst, device):
        at = len(self.started)
        copy = pltpu.make_async_remote_copy(
            src_ref=src,
            dst_ref=dst,
            send_sem=self.send_sem.at[at],
            recv_sem=self.recv_sem.at[at],
            device_id=device,
            device_id_type=MESH,
        )
        copy.start()
        self.started.append(copy)
        return copy

    def drain(self):
        for copy in self.started:
            copy.wait_send()


def local(src, dst, sem):
    copy = pltpu.make_async_copy(src, dst, sem)
    copy.start()
    return copy


def remote_call(body, name, cid, sends, locals_, ins, outs, out_shape, scratch=(), vmem=None):
    return pl.pallas_call(
        body,
        name=name,
        out_shape=out_shape,
        in_specs=ins,
        out_specs=outs,
        scratch_shapes=[DMA((sends,)), DMA((sends,)), DMA((max(locals_, 1),)), *scratch],
        compiler_params=pltpu.CompilerParams(
            collective_id=cid, has_side_effects=True, vmem_limit_bytes=vmem
        ),
    )


def shaped(shape, dtype=bf16):
    return jax.ShapeDtypeStruct(shape, dtype)


def weights_kernel(w, wo, n, g, go, m, ss, rs, ls):
    p = Place()
    dp, yl, x = p.dp, p.yl, p.x
    own = [
        local(w, g.at[:, dp, yl, x], ls.at[0]),
        local(n, m.at[p.head], ls.at[1]),
        local(wo, go.at[dp], ls.at[2]),
    ]
    greet([p.ZR, p.ZL, p.XR, p.XL, p.Y, p.C, p.H])
    wire = Wire(ss, rs)
    n_c = wire.send(n, m.at[p.head], p.C)
    z1 = wire.send(w, g.at[:, dp, yl, x], p.ZR)
    z2 = wire.send(w, g.at[:, dp, yl, x], p.ZL)
    n_h = wire.send(n, m.at[p.head], p.H)
    o1 = wire.send(wo, go.at[dp], p.ZR)
    o2 = wire.send(wo, go.at[dp], p.ZL)
    z1.wait_recv()
    z3 = wire.send(g.at[0:2, p.zl, yl, x], g.at[0:2, p.zl, yl, x], p.ZR)
    z2.wait_recv()
    z4 = wire.send(g.at[2, p.zr, yl, x], g.at[2, p.zr, yl, x], p.ZL)
    own[0].wait()
    z3.wait_recv()
    z4.wait_recv()
    b1 = wire.send(g.at[2, :, yl, x], g.at[2, :, yl, x], p.XR)
    b2 = wire.send(g.at[2, :, yl, x], g.at[2, :, yl, x], p.XL)
    a1 = wire.send(g.at[0:2, :, yl, x], g.at[0:2, :, yl, x], p.Y)
    c1 = wire.send(g.at[2, :, yl, x], g.at[2, :, yl, x], p.Y)
    o1.wait_recv()
    o3 = wire.send(go.at[p.zl, 0:32], go.at[p.zl, 0:32], p.ZR)
    o2.wait_recv()
    o4 = wire.send(go.at[p.zr, 32:64], go.at[p.zr, 32:64], p.ZL)
    n_h.wait_recv()
    other = (1 - p.yh) * 2 + p.co
    n_f = wire.send(m.at[other], m.at[other], p.C)
    b1.wait_recv()
    b3 = wire.send(g.at[2, 0:2, yl, p.xl], g.at[2, 0:2, yl, p.xl], p.XR)
    c2 = wire.send(g.at[2, :, yl, p.xl], g.at[2, :, yl, p.xl], p.Y)
    b2.wait_recv()
    b4 = wire.send(g.at[2, 2:4, yl, p.xr], g.at[2, 2:4, yl, p.xr], p.XL)
    c3 = wire.send(g.at[2, :, yl, p.xr], g.at[2, :, yl, p.xr], p.Y)
    a1.wait_recv()
    a2 = wire.send(g.at[0:2, :, :, x], g.at[0:2, :, :, x], p.XR)
    a3 = wire.send(g.at[0:2, :, :, x], g.at[0:2, :, :, x], p.XL)
    b3.wait_recv()
    b4.wait_recv()
    c4 = wire.send(g.at[2, :, yl, p.xo], g.at[2, :, yl, p.xo], p.Y)
    a2.wait_recv()
    a4 = wire.send(g.at[0, :, :, p.xl], g.at[0, :, :, p.xl], p.XR)
    a3.wait_recv()
    a5 = wire.send(g.at[1, :, :, p.xr], g.at[1, :, :, p.xr], p.XL)
    for copy in (n_c, n_f, o3, o4, c1, c2, c3, c4, a4, a5):
        copy.wait_recv()
    own[1].wait()
    own[2].wait()
    wire.drain()


def gather_weights(w, wo, n):
    return remote_call(
        weights_kernel,
        "gather_weights",
        1,
        24,
        3,
        [ANY] * 3,
        [ANY] * 3,
        (shaped((3, 4, 2, 4, 64, 512)), shaped((4, 64, 512)), shaped((4, 128, 2048))),
    )(w, wo, n)


def rows_kernel(n, m, ss, rs, ls):
    p = Place()
    own = local(n, m.at[p.head], ls.at[0])
    greet([p.C, p.H])
    wire = Wire(ss, rs)
    n_h = wire.send(n, m.at[p.head], p.H)
    n_c = wire.send(n, m.at[p.head], p.C)
    n_h.wait_recv()
    other = (1 - p.yh) * 2 + p.co
    n_f = wire.send(m.at[other], m.at[other], p.C)
    n_c.wait_recv()
    n_f.wait_recv()
    own.wait()
    wire.drain()


def gather_rows(n):
    return remote_call(
        rows_kernel, "gather_rows", 2, 3, 1, [ANY], [ANY], (shaped((4, 128, 2048)),)
    )(n)[0]


def sum_kernel(part, out, ss, rs, ls, got_c, got_h, half):
    p = Place()
    greet([p.C, p.H])
    wire = Wire(ss, rs)
    far = wire.send(part.at[1 - p.yh, 1 - p.co], got_c.at[0], p.C)
    near = wire.send(part.at[p.yh, 1 - p.co], got_c.at[1], p.C)
    far.wait_recv()

    def add_far(i, carry):
        rows = pl.ds(pl.multiple_of(i * 16, 16), 16)
        half[rows] = (
            part[1 - p.yh, p.co, rows].astype(f32) + got_c[0, rows].astype(f32)
        ).astype(bf16)
        return carry

    lax.fori_loop(0, 8, add_far, 0)
    over = wire.send(half, got_h, p.H)
    near.wait_recv()
    over.wait_recv()

    def add_near(i, carry):
        rows = pl.ds(pl.multiple_of(i * 16, 16), 16)
        out[rows] = (
            part[p.yh, p.co, rows].astype(f32)
            + got_c[1, rows].astype(f32)
            + got_h[rows].astype(f32)
        )
        return carry

    lax.fori_loop(0, 8, add_near, 0)
    wire.drain()


def sum_rows(part, cid):
    return remote_call(
        sum_kernel,
        "sum_rows",
        cid,
        3,
        1,
        [VMEM],
        [VMEM],
        (shaped((128, 2048), f32),),
        scratch=[
            pltpu.VMEM((2, 128, 2048), bf16),
            pltpu.VMEM((128, 2048), bf16),
            pltpu.VMEM((128, 2048), bf16),
        ],
        vmem=16 << 20,
    )(part.reshape(2, 2, 128, 2048))[0]


def heads_kernel(q, k, v, go, qd, kd, vd, gd, ss, rs, ls):
    p = Place()
    yl, x = p.yl, p.x
    own = [
        local(q.at[x], qd.at[:, x], ls.at[0]),
        local(k.at[x], kd.at[:, yl, x], ls.at[1]),
        local(v.at[x], vd.at[:, yl, x], ls.at[2]),
        local(go, gd.at[:, yl, x], ls.at[3]),
    ]
    greet([p.Y, p.XR, p.XL, p.XO])
    wire = Wire(ss, rs)
    done = [
        wire.send(k.at[x], kd.at[:, yl, x], p.Y),
        wire.send(v.at[x], vd.at[:, yl, x], p.Y),
    ]
    w1 = wire.send(go, gd.at[:, yl, x], p.Y)
    moved = []
    for there, came, device in ((p.xo, p.xo, p.XO), (p.xr, p.xl, p.XR), (p.xl, p.xr, p.XL)):
        ks = wire.send(k.at[there], kd.at[:, yl, x], device)
        vs = wire.send(v.at[there], vd.at[:, yl, x], device)
        moved.append((came, ks, vs))
    for there, device in ((p.xo, p.XO), (p.xr, p.XR), (p.xl, p.XL)):
        done.append(wire.send(q.at[there], qd.at[:, x], device))
    for came, ks, vs in moved[1:] + moved[:1]:
        ks.wait_recv()
        done.append(wire.send(kd.at[:, yl, came], kd.at[:, yl, came], p.Y))
        vs.wait_recv()
        done.append(wire.send(vd.at[:, yl, came], vd.at[:, yl, came], p.Y))
    own[3].wait()
    w1.wait_recv()
    w2 = wire.send(gd.at[:, :, x], gd.at[:, :, x], p.XR)
    w3 = wire.send(gd.at[:, :, x], gd.at[:, :, x], p.XL)
    w2.wait_recv()
    done.append(wire.send(gd.at[0:2, :, p.xl], gd.at[0:2, :, p.xl], p.XR))
    w3.wait_recv()
    done.append(wire.send(gd.at[2:4, :, p.xr], gd.at[2:4, :, p.xr], p.XL))
    for copy in done:
        copy.wait_recv()
    for copy in own[:3]:
        copy.wait()
    wire.drain()


def heads_over_x(q, k, v, go):
    return remote_call(
        heads_kernel,
        "heads_over_x",
        3,
        22,
        4,
        [ANY] * 4,
        [ANY] * 4,
        (
            shaped((4, 4, 128, 128)),
            shaped((4, 2, 4, 128, 128)),
            shaped((4, 2, 4, 128, 128)),
            shaped((4, 2, 4, 64, 512)),
        ),
    )(q, k, v, go)


def back_x_kernel(o, att, ss, rs, ls):
    p = Place()
    own = local(o.at[:, p.x], att.at[p.x], ls.at[0])
    greet([p.XR, p.XL, p.XO])
    wire = Wire(ss, rs)
    for there, device in ((p.xo, p.XO), (p.xr, p.XR), (p.xl, p.XL)):
        wire.send(o.at[:, there], att.at[p.x], device)
    for copy in wire.started:
        copy.wait_recv()
    own.wait()
    wire.drain()


def back_over_x(o):
    return remote_call(
        back_x_kernel, "back_over_x", 4, 3, 1, [ANY], [ANY], (shaped((4, 4, 128, 128)),)
    )(o)[0]


def go_x_kernel(o, d, ss, rs, ls):
    p = Place()
    own = local(o.at[p.x], d.at[:, p.x], ls.at[0])
    greet([p.XR, p.XL, p.XO])
    wire = Wire(ss, rs)
    for there, device in ((p.xo, p.XO), (p.xr, p.XR), (p.xl, p.XL)):
        wire.send(o.at[there], d.at[:, p.x], device)
    for copy in wire.started:
        copy.wait_recv()
    own.wait()
    wire.drain()


def go_over_x(o):
    return remote_call(
        go_x_kernel, "go_over_x", 5, 3, 1, [ANY], [ANY], (shaped((4, 4, 128, 128)),)
    )(o)[0]


def grads_x_kernel(dq, dk, dv, qd, kd, vd, ss, rs, ls, gk, gv, sk, sv):
    p = Place()
    x, yl = p.x, p.yl
    own = local(dq.at[:, x], qd.at[x], ls.at[0])
    greet([p.Y, p.XR, p.XL, p.XO])
    wire = Wire(ss, rs)
    order = ((p.xo, p.XO), (p.xr, p.XR), (p.xl, p.XL), (x, None))
    pairs = []
    for i, (there, device) in enumerate(order):
        pairs.append(
            (
                wire.send(dk.at[:, 1 - yl, there], gk.at[i], p.Y),
                wire.send(dv.at[:, 1 - yl, there], gv.at[i], p.Y),
            )
        )
    last = []
    for there, device in order[:3]:
        last.append(wire.send(dq.at[:, there], qd.at[x], device))
    for i, (there, device) in enumerate(order):
        for grads, got, summed, out, arrived in (
            (dk, gk, sk, kd, pairs[i][0]),
            (dv, gv, sv, vd, pairs[i][1]),
        ):
            arrived.wait_recv()
            for run in range(4):
                total = grads[run, yl, there].astype(f32) + got[i, run].astype(f32)
                if device is None:
                    out[x, run] = total.astype(bf16)
                else:
                    summed[i, run] = total.astype(bf16)
            if device is not None:
                last.append(wire.send(summed.at[i], out.at[x], device))
    for copy in last:
        copy.wait_recv()
    own.wait()
    wire.drain()


def grads_over_x(dq, dk, dv):
    return remote_call(
        grads_x_kernel,
        "grads_over_x",
        6,
        17,
        1,
        [ANY, VMEM, VMEM],
        [ANY, VMEM, VMEM],
        (shaped((4, 4, 128, 128)),) * 3,
        scratch=[
            pltpu.VMEM((4, 4, 128, 128), bf16),
            pltpu.VMEM((4, 4, 128, 128), bf16),
            pltpu.VMEM((3, 4, 128, 128), bf16),
            pltpu.VMEM((3, 4, 128, 128), bf16),
        ],
        vmem=16 << 20,
    )(dq, dk, dv)


QB = 256
KB = 512
SCALE = HD**-0.5
SCALE2 = SCALE * math.log2(math.e)


def attend_kernel(lim, q, k, v, qseg, qpos, kseg, o_low, o, linv, vext):
    rows = k.shape[0]
    ones = (lax.broadcasted_iota(i32, (KB, HD), 1) == 0).astype(bf16)

    def fill(i, carry):
        at = pl.ds(pl.multiple_of(i * KB, KB), KB)
        vext[at, :HD] = v[at]
        vext[at, HD:] = ones
        return carry

    lax.fori_loop(0, rows // KB, fill, 0)

    def one_query(b, carry):
        at = pl.ds(pl.multiple_of(b * QB, QB), QB)
        query, seg, pos = q[at], qseg[at], qpos[at]

        def one_key(j, acc):
            keys = pl.ds(pl.multiple_of(j * KB, KB), KB)
            score = lax.dot_general(
                query, k[keys], (((1,), (1,)), ((), ())), preferred_element_type=f32
            )
            key_pos = j * KB + lax.broadcasted_iota(i32, (1, KB), 1)
            allowed = (seg == kseg[:, keys]) | (pos == key_pos)
            weight = jnp.where(allowed, jnp.exp2(score * SCALE2), 0.0).astype(bf16)
            return acc + jnp.dot(weight, vext[keys], preferred_element_type=f32)

        acc = lax.fori_loop(lim[0, b], lim[1, b], one_key, jnp.zeros((QB, 2 * HD), f32))
        inverse = 1.0 / acc[:, HD : HD + 1]
        result = acc[:, :HD] * inverse
        o[at] = result
        o_low[at] = result.astype(bf16)
        linv[at] = jnp.broadcast_to(inverse, (QB, HD))
        return carry

    lax.fori_loop(0, q.shape[0] // QB, one_query, 0)


def attend(lim, q, k, v, qseg, qpos, kseg):
    n = q.shape[0]
    return pl.pallas_call(
        attend_kernel,
        name="attend",
        out_shape=(shaped((n, HD)), shaped((n, HD), f32), shaped((n, HD), f32)),
        in_specs=[SMEM] + [VMEM] * 6,
        out_specs=[VMEM] * 3,
        scratch_shapes=[pltpu.VMEM((k.shape[0], 2 * HD), bf16)],
        compiler_params=pltpu.CompilerParams(vmem_limit_bytes=32 << 20),
    )(lim, q, k, v, qseg[:, None], qpos[:, None], kseg[None])


def attend_back_kernel(
    lim, q, k, v, g, qseg, qpos, kseg, linv, delta, dq, dk, dv, kt, dk_acc, dv_acc
):
    rows = k.shape[0]

    def fill(i, carry):
        at = pl.ds(pl.multiple_of(i * KB, KB), KB)
        kt[:, at] = k[at].astype(f32).T.astype(bf16)
        dk_acc[at] = jnp.zeros((KB, HD), f32)
        dv_acc[at] = jnp.zeros((KB, HD), f32)
        return carry

    lax.fori_loop(0, rows // KB, fill, 0)
    across = (((1,), (1,)), ((), ()))

    def one_query(b, carry):
        at = pl.ds(pl.multiple_of(b * QB, QB), QB)
        query, grad = q[at], g[at]
        seg, pos, inverse, shift = qseg[:, at], qpos[:, at], linv[:, at], delta[:, at]

        def one_key(j, acc):
            keys = pl.ds(pl.multiple_of(j * KB, KB), KB)
            key = k[keys]
            score = lax.dot_general(key, query, across, preferred_element_type=f32)
            key_pos = j * KB + lax.broadcasted_iota(i32, (KB, 1), 0)
            allowed = (kseg[keys] == seg) | (key_pos == pos)
            prob = jnp.where(allowed, jnp.exp2(score * SCALE2), 0.0) * inverse
            grad_prob = lax.dot_general(v[keys], grad, across, preferred_element_type=f32)
            grad_score = (prob * (grad_prob - shift)).astype(bf16)
            dv_acc[keys] += jnp.dot(prob.astype(bf16), grad, preferred_element_type=f32)
            dk_acc[keys] += jnp.dot(grad_score, query, preferred_element_type=f32)
            return acc + jnp.dot(kt[:, keys], grad_score, preferred_element_type=f32)

        acc = lax.fori_loop(lim[0, b], lim[1, b], one_key, jnp.zeros((HD, QB), f32))
        dq[at] = (acc * SCALE).T.astype(bf16)
        return carry

    lax.fori_loop(0, q.shape[0] // QB, one_query, 0)

    def finish(i, carry):
        at = pl.ds(pl.multiple_of(i * KB, KB), KB)
        dk[at] = (dk_acc[at] * SCALE).astype(bf16)
        dv[at] = dv_acc[at].astype(bf16)
        return carry

    lax.fori_loop(0, rows // KB, finish, 0)


def attend_back(lim, q, k, v, g, qseg, qpos, kseg, linv, delta):
    n, rows = q.shape[0], k.shape[0]
    return pl.pallas_call(
        attend_back_kernel,
        name="attend_back",
        out_shape=(shaped((n, HD)), shaped((rows, HD)), shaped((rows, HD))),
        in_specs=[SMEM] + [VMEM] * 9,
        out_specs=[VMEM] * 3,
        scratch_shapes=[
            pltpu.VMEM((HD, rows), bf16),
            pltpu.VMEM((rows, HD), f32),
            pltpu.VMEM((rows, HD), f32),
        ],
        compiler_params=pltpu.CompilerParams(vmem_limit_bytes=40 << 20),
    )(lim, q, k, v, g, qseg[None], qpos[None], kseg[:, None], linv[None], delta[None])


def spread_kernel(src, dst, ss, rs, ls):
    p = Place()
    yh, co, yl, x = p.yh, p.co, p.yl, p.x
    own = local(src, dst.at[yh, co, yl, x], ls.at[0])
    greet([p.XR, p.XL, p.YR, p.YL, p.C])
    wire = Wire(ss, rs)
    A, A1, A2 = pl.ds(0, 64), pl.ds(0, 32), pl.ds(32, 32)
    B, B1, B2 = pl.ds(64, 64), pl.ds(64, 32), pl.ds(96, 32)

    def at_y(y, rows):
        return dst.at[y // 2, co, lax.rem(y, 2), :, rows]

    def at_x(xx, rows):
        return dst.at[:, co, :, xx, rows]

    def both(ref, device):
        return wire.send(ref, ref, device)

    y = yh * 2 + yl
    me = dst.at[yh, co, yl]
    a1 = wire.send(src.at[A], me.at[x, A], p.XR)
    b1 = wire.send(src.at[B], me.at[x, B], p.YR)
    a2 = wire.send(src.at[A], me.at[x, A], p.XL)
    b2 = wire.send(src.at[B], me.at[x, B], p.YL)
    a1.wait_recv()
    a3 = both(me.at[p.xl, A1], p.XR)
    a2.wait_recv()
    a4 = both(me.at[p.xr, A2], p.XL)
    yr, ylf, yo = p.yr, p.ylf, p.yo

    def block(yy, rows):
        return dst.at[yy // 2, co, lax.rem(yy, 2), x, rows]

    b1.wait_recv()
    b3 = both(block(ylf, B1), p.YR)
    b2.wait_recv()
    b4 = both(block(yr, B2), p.YL)
    own.wait()
    a3.wait_recv()
    a4.wait_recv()
    a5 = both(at_y(y, A), p.YR)
    a6 = both(at_y(y, A), p.YL)
    b3.wait_recv()
    b4.wait_recv()
    b5 = both(at_x(x, B), p.XR)
    b6 = both(at_x(x, B), p.XL)
    last = [both(at_y(y, A), p.C), both(at_x(x, B), p.C)]
    a5.wait_recv()
    a7 = both(at_y(ylf, A1), p.YR)
    b5.wait_recv()
    b7 = both(at_x(p.xl, B1), p.XR)
    a6.wait_recv()
    a8 = both(at_y(yr, A2), p.YL)
    b6.wait_recv()
    b8 = both(at_x(p.xr, B2), p.XL)
    last += [both(at_y(ylf, A), p.C), both(at_x(p.xl, B), p.C)]
    last += [both(at_y(yr, A), p.C), both(at_x(p.xr, B), p.C)]
    a7.wait_recv()
    last.append(both(at_y(yo, A1), p.C))
    b7.wait_recv()
    last.append(both(at_x(p.xo, B1), p.C))
    a8.wait_recv()
    last.append(both(at_y(yo, A2), p.C))
    b8.wait_recv()
    last.append(both(at_x(p.xo, B2), p.C))
    for copy in last:
        copy.wait_recv()
    wire.drain()


def spread(src, cid):
    width = src.shape[1]
    return remote_call(
        spread_kernel,
        "spread",
        cid,
        26,
        1,
        [ANY],
        [ANY],
        (shaped((2, 2, 2, 4, 128, width)),),
    )(src)[0].reshape(32, 128, width)


def slot_hits(table, count, rows_down):
    shape = (count * 2 * CAP, 256) if rows_down else (256, count * 2 * CAP)
    line = lax.broadcasted_iota(i32, shape, 0 if rows_down else 1)
    block = lax.broadcasted_iota(i32, shape, 1 if rows_down else 0) // 128
    expert = line // (2 * CAP)
    want = line - expert * (2 * CAP) - block * CAP

    def spread_out(first):
        value = jnp.zeros(shape, f32)
        for e in range(count):
            c = first + e
            at = table[c : c + 1] if rows_down else table[:, c : c + 1]
            value = jnp.where(expert == e, at, value)
        return value

    hit = (spread_out(0).astype(i32) == want) & (want >= 0) & (want < CAP)
    return hit, spread_out(count)


def pick_kernel(gated, sel, info, src, rows_out, *gates_out):
    tokens = jnp.concatenate([src[0], src[1]], axis=0)
    both = jnp.concatenate([info[0], info[1]], axis=0)
    table = lax.dot_general(
        sel[...], both, (((1,), (1,)), ((), ())), preferred_element_type=f32
    )
    hit, gate = slot_hits(table, EXP_DEV, True)
    rows = jnp.dot(hit.astype(bf16), tokens, preferred_element_type=f32).astype(bf16)
    for e in range(EXP_DEV):
        rows_out[e, 0] = rows[e * 2 * CAP : (e + 1) * 2 * CAP]
    if gated:
        total = jnp.sum(jnp.where(hit, gate, 0.0), axis=1, keepdims=True)
        total = jnp.broadcast_to(total, (EXP_DEV * 2 * CAP, 128))
        for e in range(EXP_DEV):
            gates_out[0][e, 0] = total[e * 2 * CAP : (e + 1) * 2 * CAP]


def pick_rows(sel, info, src, width, gated):
    pairs = src.shape[0] // 2

    def spec(lanes):
        return pl.BlockSpec((EXP_DEV, 1, 2 * CAP, lanes), lambda i: (0, i, 0, 0))

    shapes = [shaped((EXP_DEV, pairs, 2 * CAP, width)), shaped((EXP_DEV, pairs, 2 * CAP, 128), f32)]
    specs = [spec(width), spec(128)]
    return pl.pallas_call(
        functools.partial(pick_kernel, gated),
        name="pick_rows",
        grid=(pairs,),
        out_shape=shapes[: 1 + gated],
        in_specs=[
            pl.BlockSpec((8, 128), lambda i: (0, 0)),
            pl.BlockSpec((2, 128, 128), lambda i: (i, 0, 0)),
            pl.BlockSpec((2, 128, width), lambda i: (i, 0, 0)),
        ],
        out_specs=specs[: 1 + gated],
        compiler_params=pltpu.CompilerParams(vmem_limit_bytes=40 << 20),
    )(sel, info, src)


HOME_SENDS = 18


def home_scratch():
    return [
        pltpu.VMEM((2, 4, 8 * CAP, 2048), bf16),
        pltpu.VMEM((2, 2, 4, 128, 2048), bf16),
        pltpu.VMEM((2, 2, 64, 2048), bf16),
        pltpu.VMEM((2, 2, 64, 2048), bf16),
        pltpu.VMEM((2, 4, 64, 2048), bf16),
        pltpu.VMEM((2, 2, 2, 64, 2048), bf16),
        pltpu.VMEM((2, 2, 32, 2048), bf16),
        pltpu.VMEM((2, 2, 64, 2048), bf16),
    ]


def home_steps(p, wire, sems, gated, sel, info, rows, out, cat, q, a1, b1, a2, b2, c1, c2):
    yh, co, yl, x = p.yh, p.co, p.yl, p.x
    ys = [(yy // 2, lax.rem(yy, 2)) for yy in (p.yr, p.ylf, p.yo)]
    (rh, rl), (lh, ll), (oh, ol) = ys
    own, first = [], []
    for e in range(EXP_DEV):
        lines = pl.ds(e * 2 * CAP, 2 * CAP)
        there = pl.ds((2 + e) * 2 * CAP, 2 * CAP)
        first.append(wire.send(rows.at[e, :, 1 - co], cat.at[:, :, there], p.C))
        own.append(local(rows.at[e, :, co], cat.at[:, :, lines], sems.at[e]))
    yield
    for copy in own:
        copy.wait()
    for copy in first:
        copy.wait_recv()

    def place(i, carry):
        h, pair = i // 4, lax.rem(i, 4)
        block = h * 16 + co * 8 + pair * 2
        both = jnp.concatenate([info[block], info[block + 1]], axis=0)
        table = lax.dot_general(
            both, sel[...], (((1,), (1,)), ((), ())), preferred_element_type=f32
        )
        hit, gate = slot_hits(table, 4, False)
        value = jnp.where(hit, gate if gated else 1.0, 0.0).astype(bf16)
        for c in range(0, 2048, 512):
            total = jnp.dot(
                value, cat[h, pair, :, c : c + 512], preferred_element_type=f32
            ).astype(bf16)
            at = lax.rem(pair, 2) * 2
            q[h, pair // 2, at, :, c : c + 512] = total[:128]
            q[h, pair // 2, at + 1, :, c : c + 512] = total[128:]
        return carry

    lax.fori_loop(0, 8, place, 0)
    A, B = pl.ds(0, 64), pl.ds(64, 64)
    s1 = [
        wire.send(q.at[oh, ol, 0:2, A], a1.at[0], p.YR),
        wire.send(q.at[0, :, p.xo, B], b1.at[0], p.XR),
        wire.send(q.at[oh, ol, 2:4, A], a1.at[1], p.YL),
        wire.send(q.at[1, :, p.xo, B], b1.at[1], p.XL),
    ]
    yield

    def add(dst, *srcs):
        total = srcs[0][...].astype(f32)
        for src in srcs[1:]:
            total = total + src[...].astype(f32)
        dst[...] = total.astype(dst.dtype)

    def loop(count, body):
        def step(i, carry):
            body(i)
            return carry

        lax.fori_loop(0, count, step, 0)

    def plus(dst, src):
        add(dst, dst, src)

    s2 = []
    s1[0].wait_recv()
    loop(2, lambda i: plus(q.at[rh, rl, i, A], a1.at[0, i]))
    s2.append(wire.send(q.at[rh, rl, :, A], a2.at[0], p.YR))
    s1[1].wait_recv()
    loop(2, lambda i: plus(q.at[0, i, p.xr, B], b1.at[0, i]))
    s2.append(wire.send(q.at[:, :, p.xr, B], b2.at[0], p.XR))
    s1[2].wait_recv()
    loop(2, lambda i: plus(q.at[lh, ll, 2 + i, A], a1.at[1, i]))
    s2.append(wire.send(q.at[lh, ll, :, A], a2.at[1], p.YL))
    s1[3].wait_recv()
    loop(2, lambda i: plus(q.at[1, i, p.xl, B], b1.at[1, i]))
    s2.append(wire.send(q.at[:, :, p.xl, B], b2.at[1], p.XL))
    yield
    for copy in s2:
        copy.wait_recv()
    loop(4, lambda i: add(q.at[yh, yl, i, A], q.at[yh, yl, i, A], a2.at[0, i], a2.at[1, i]))
    s3 = [
        wire.send(q.at[yh, yl, p.xo, 0:32], c1.at[0, 0], p.XR),
        wire.send(q.at[yh, yl, p.xo, 32:64], c1.at[0, 1], p.XL),
    ]
    for h in range(2):
        loop(2, lambda i: add(q.at[h, i, x, B], q.at[h, i, x, B], b2.at[0, h, i], b2.at[1, h, i]))
    s3 += [
        wire.send(q.at[oh, ol, x, 64:96], c1.at[1, 0], p.YR),
        wire.send(q.at[oh, ol, x, 96:128], c1.at[1, 1], p.YL),
    ]
    yield
    s4 = []
    s3[0].wait_recv()
    plus(q.at[yh, yl, p.xr, 0:32], c1.at[0, 0])
    s4.append(wire.send(q.at[yh, yl, p.xr, A], c2.at[0, 0], p.XR))
    s3[1].wait_recv()
    plus(q.at[yh, yl, p.xl, 32:64], c1.at[0, 1])
    s4.append(wire.send(q.at[yh, yl, p.xl, A], c2.at[0, 1], p.XL))
    s3[2].wait_recv()
    plus(q.at[rh, rl, x, 64:96], c1.at[1, 0])
    s4.append(wire.send(q.at[rh, rl, x, B], c2.at[1, 0], p.YR))
    s3[3].wait_recv()
    plus(q.at[lh, ll, x, 96:128], c1.at[1, 1])
    s4.append(wire.send(q.at[lh, ll, x, B], c2.at[1, 1], p.YL))
    yield
    for copy in s4:
        copy.wait_recv()
    add(out.at[0:64], q.at[yh, yl, x, A], c2.at[0, 0], c2.at[0, 1])
    add(out.at[64:128], q.at[yh, yl, x, B], c2.at[1, 0], c2.at[1, 1])
    wire.drain()
    yield


def home_kernel(gated, sel, info, rows, out, ss, rs, ls, *scratch):
    p = Place()
    greet([p.XR, p.XL, p.YR, p.YL, p.C])
    for _ in home_steps(p, Wire(ss, rs), ls, gated, sel, info, rows, out, *scratch):
        pass


def rows_home(sel, info, rows, gated, cid):
    return remote_call(
        functools.partial(home_kernel, gated),
        "rows_home",
        cid,
        HOME_SENDS,
        2,
        [VMEM, VMEM, ANY],
        [VMEM],
        (shaped((128, 2048), f32),),
        scratch=home_scratch(),
        vmem=48 << 20,
    )(sel, info, rows.reshape(EXP_DEV, 2, 2, 4, 2 * CAP, 2048))[0]


def fold_kernel(
    p0, p1, p2, p3, small, out, whole, ss, rs, ls,
    ra, rb, rc, rd, re, rf, rg, acc_x, acc_y, sz, az, sx, ax, sy, ay, sc, ac, sh,
):
    p = Place()
    dp, yl, x = p.dp, p.yl, p.x
    greet([p.ZR, p.ZL, p.ZO, p.XR, p.XL, p.XO, p.Y, p.C, p.H])
    wire = Wire(ss, rs)
    zs_out = [
        wire.send(small.at[there], sz.at[i], device)
        for i, (there, device) in enumerate(((p.zo, p.ZO), (p.zr, p.ZR), (p.zl, p.ZL)))
    ]

    def added(dst, *srcs):
        total = srcs[0][...].astype(f32)
        for src in srcs[1:]:
            total = total + src[...].astype(f32)
        dst[...] = total.astype(dst.dtype)

    def loop(count, body):
        def step(i, carry):
            body(i)
            return carry

        lax.fori_loop(0, count, step, 0)

    firsts = []
    for i, part in ((2, p2), (3, p3)):
        firsts.append(wire.send(part.at[:, 1 - yl], rb.at[i - 2], p.Y))
    starts = []
    for i, part in ((0, p0), (1, p1)):
        starts.append(
            (
                wire.send(part.at[0:2, :, p.xo], ra.at[i, 0], p.XR),
                wire.send(part.at[2:4, :, p.xo], ra.at[i, 1], p.XL),
            )
        )
    seconds = []
    for i, part in ((0, p0), (1, p1)):
        one, two = starts[i]
        one.wait_recv()
        loop(2, lambda d: added(part.at[d, :, p.xr], part.at[d, :, p.xr], ra.at[i, 0, d]))
        s1 = wire.send(part.at[:, :, p.xr], rc.at[i, 0], p.XR)
        two.wait_recv()
        loop(2, lambda d: added(part.at[d + 2, :, p.xl], part.at[d + 2, :, p.xl], ra.at[i, 1, d]))
        s2 = wire.send(part.at[:, :, p.xl], rc.at[i, 1], p.XL)
        seconds.append((s1, s2))
    for copy in zs_out:
        copy.wait_recv()
    for half in range(2):
        az[half] = small[dp, half] + sz[0, half] + sz[1, half] + sz[2, half]
    xs_out = [
        wire.send(az.at[:, there], sx.at[i], device)
        for i, (there, device) in enumerate(((p.xo, p.XO), (p.xr, p.XR), (p.xl, p.XL)))
    ]
    mids = []
    for i, part in ((2, p2), (3, p3)):
        firsts[i - 2].wait_recv()
        loop(4, lambda d: added(acc_y.at[i - 2, d], part.at[d, yl], rb.at[i - 2, d]))
        acc = acc_y.at[i - 2]
        mids.append(
            (
                wire.send(acc.at[0:2, p.xo], rd.at[i - 2, 0], p.XR),
                wire.send(acc.at[2:4, p.xo], rd.at[i - 2, 1], p.XL),
            )
        )
    for copy in xs_out:
        copy.wait_recv()
    ax[...] = az[:, x] + sx[0] + sx[1] + sx[2]
    y_out = wire.send(ax.at[1 - yl], sy, p.Y)
    yends = []
    for i, part in ((0, p0), (1, p1)):
        for s in seconds[i]:
            s.wait_recv()
        acc = acc_x.at[i]
        loop(4, lambda d: added(acc.at[d], part.at[d, :, x], rc.at[i, 0, d], rc.at[i, 1, d]))
        yends.append(wire.send(acc.at[:, 1 - yl], re.at[i], p.Y))
    y_out.wait_recv()
    ay[...] = ax[yl] + sy[...]
    c_out = wire.send(ay, sc, p.C)
    xends = []
    for i in (2, 3):
        acc = acc_y.at[i - 2]
        one, two = mids[i - 2]
        one.wait_recv()
        loop(2, lambda d: added(acc.at[d, p.xr], acc.at[d, p.xr], rd.at[i - 2, 0, d]))
        s1 = wire.send(acc.at[:, p.xr], rf.at[i - 2, 0], p.XR)
        two.wait_recv()
        loop(2, lambda d: added(acc.at[d + 2, p.xl], acc.at[d + 2, p.xl], rd.at[i - 2, 1, d]))
        s2 = wire.send(acc.at[:, p.xl], rf.at[i - 2, 1], p.XL)
        xends.append((s1, s2))
    parts = []
    zs = []

    def z_first(i, acc):
        parts.append(acc)
        zs.append(
            (
                wire.send(acc.at[p.zo, 0:32], rg.at[i, 0, 0:32], p.ZR),
                wire.send(acc.at[p.zo, 32:64], rg.at[i, 1, 0:32], p.ZL),
            )
        )

    c_out.wait_recv()
    ac[...] = ay[...] + sc[...]
    h_out = wire.send(ac, sh, p.H)
    for i in (0, 1):
        yends[i].wait_recv()
        acc = acc_x.at[i]
        loop(4, lambda d: added(acc.at[d, yl], acc.at[d, yl], re.at[i, d]))
        z_first(i, acc.at[:, yl])
    h_out.wait_recv()
    whole[dp, yl, x] = ac[...] + sh[...]
    y_all = wire.send(whole.at[dp, yl, x], whole.at[dp, yl, x], p.Y)
    for i in (2, 3):
        for s in xends[i - 2]:
            s.wait_recv()
        acc = acc_y.at[i - 2]
        loop(
            4, lambda d: added(acc.at[d, x], acc.at[d, x], rf.at[i - 2, 0, d], rf.at[i - 2, 1, d])
        )
        z_first(i, acc.at[:, x])
    y_all.wait_recv()
    x_all = [
        wire.send(whole.at[dp, :, x], whole.at[dp, :, x], device) for device in (p.XO, p.XR, p.XL)
    ]
    ends = []
    for i in range(4):
        one, two = zs[i]
        acc = parts[i]
        one.wait_recv()
        added(acc.at[p.zr, 0:32], acc.at[p.zr, 0:32], rg.at[i, 0, 0:32])
        s1 = wire.send(acc.at[p.zr], rg.at[i, 2], p.ZR)
        two.wait_recv()
        added(acc.at[p.zl, 32:64], acc.at[p.zl, 32:64], rg.at[i, 1, 0:32])
        s2 = wire.send(acc.at[p.zl], rg.at[i, 3], p.ZL)
        ends.append((s1, s2))
    for copy in x_all:
        copy.wait_recv()
    z_all = [wire.send(whole.at[dp], whole.at[dp], device) for device in (p.ZO, p.ZR, p.ZL)]
    for i in range(4):
        for s in ends[i]:
            s.wait_recv()
        added(out.at[i], parts[i].at[dp], rg.at[i, 2], rg.at[i, 3])
    for copy in z_all:
        copy.wait_recv()
    wire.drain()


def fold_grads(grads, small):
    return remote_call(
        fold_kernel,
        "fold_grads",
        8,
        52,
        1,
        [VMEM] * 5,
        [VMEM] * 2,
        (shaped((4, 64, 512), f32), shaped((4, 2, 4, 40, 128), f32)),
        scratch=[
            pltpu.VMEM((2, 2, 2, 2, 64, 512), bf16),
            pltpu.VMEM((2, 4, 4, 64, 512), bf16),
            pltpu.VMEM((2, 2, 4, 2, 64, 512), bf16),
            pltpu.VMEM((2, 2, 2, 64, 512), bf16),
            pltpu.VMEM((2, 4, 64, 512), bf16),
            pltpu.VMEM((2, 2, 4, 64, 512), bf16),
            pltpu.VMEM((4, 4, 64, 512), bf16),
            pltpu.VMEM((2, 4, 2, 64, 512), bf16),
            pltpu.VMEM((2, 4, 4, 64, 512), bf16),
            pltpu.VMEM((3, 2, 4, 40, 128), f32),
            pltpu.VMEM((2, 4, 40, 128), f32),
            pltpu.VMEM((3, 2, 40, 128), f32),
            pltpu.VMEM((2, 40, 128), f32),
            pltpu.VMEM((40, 128), f32),
            pltpu.VMEM((40, 128), f32),
            pltpu.VMEM((40, 128), f32),
            pltpu.VMEM((40, 128), f32),
            pltpu.VMEM((40, 128), f32),
        ],
        vmem=48 << 20,
    )(*[g.reshape(4, 2, 4, 64, 512) for g in grads], small.reshape(4, 2, 4, 40, 128))


def on_device(
    tokens,
    segment_ids,
    valid_mask,
    routes,
    attn_gain,
    w_query,
    w_key,
    w_value,
    w_out,
    query_gain,
    key_gain,
    ffn_gain,
    router,
    expert_in,
    expert_out,
    cotangent,
):
    blk = lax.axis_index("blk")
    device = lax.axis_index("head") * 8 + blk
    yl = blk // 4
    tok, width = tokens.shape
    full_in = lax.all_gather(expert_in, "dp", axis=0, tiled=True)
    full_back = lax.all_gather(expert_out, "dp", axis=0, tiled=True)

    segment, valid = segment_ids[0], valid_mask[0]
    seq_len = segment.shape[0]
    place = jnp.arange(seq_len, dtype=i32)
    query_ids = (jnp.arange(4)[:, None] * 1024 + blk * 128 + jnp.arange(128)[None]).reshape(-1)
    frequency = rope_base ** (-jnp.arange(64, dtype=f32) / 64)
    angles = query_ids.astype(f32)[:, None] * frequency[None]
    cosine, sine = jnp.cos(angles)[None], jnp.sin(angles)[None]
    half_ids = (jnp.arange(4)[:, None] * 1024 + yl * 512 + jnp.arange(512)[None]).reshape(-1)
    half_seg = lax.dynamic_index_in_dim(segment.reshape(4, 2, 512), yl, 1, keepdims=False).reshape(-1)
    key_seg = jnp.where(valid > 0, segment, -1)
    ends = half_seg.reshape(-1, QB)
    lower = jnp.sum(segment[None] < ends[:, :1], axis=1, dtype=i32) // KB
    upper = (jnp.sum(segment[None] <= ends[:, -1:], axis=1, dtype=i32) + KB - 1) // KB
    limits = jnp.stack([lower, upper])

    def rotary(values, turning):
        a, b = values[..., :64], values[..., 64:]
        turned = turning * sine
        return jnp.concatenate([a * cosine - b * turned, b * cosine + a * turned], axis=-1)

    inputs = tokens.astype(f32)
    first_inv = rms_rows(inputs)
    normed = (inputs * first_inv * attn_gain).astype(bf16)
    w_three = jnp.stack([w_query, w_key, w_value])
    gathered, out_part, normed_all = gather_weights(w_three, w_out, normed)
    full_query, full_key, full_value = (gathered[i].reshape(2048, 512) for i in range(3))
    normed_all = normed_all.reshape(512, width)

    def by_head(flat):
        return jnp.transpose(flat.reshape(512, 4, HD), (1, 0, 2))

    def flat_of(heads):
        return jnp.transpose(heads.reshape(4, 512, HD), (1, 0, 2)).reshape(512, 512)

    query_proj = by_head(jnp.dot(normed_all, full_query, preferred_element_type=f32))
    key_proj = by_head(jnp.dot(normed_all, full_key, preferred_element_type=f32))
    value_heads = by_head(jnp.dot(normed_all, full_value, preferred_element_type=f32).astype(bf16))
    query_inv = rms_rows(query_proj)
    query_unit = query_proj * query_inv
    query_heads = rotary(query_unit * query_gain, 1.0).astype(bf16)
    key_inv = rms_rows(key_proj)
    key_unit = key_proj * key_inv
    key_heads = rotary(key_unit * key_gain, 1.0).astype(bf16)

    runs = (4, 4, 128, HD)
    q, k, v, full_out = heads_over_x(
        query_heads.reshape(runs), key_heads.reshape(runs), value_heads.reshape(runs), out_part
    )
    q, k, v = q.reshape(2048, HD), k.reshape(4096, HD), v.reshape(4096, HD)
    full_out = full_out.reshape(2048, 512)
    att_low, att, inverse = attend(limits, q, k, v, half_seg, half_ids, key_seg)
    attended = back_over_x(att_low.reshape(runs))
    attended_flat = flat_of(attended)
    branch_part = jnp.einsum("qc,mc->qm", attended_flat, full_out, preferred_element_type=f32)
    middle = inputs + sum_rows(branch_part.astype(bf16), 9)
    second_inv = rms_rows(middle)
    normed_ffn = (middle * second_inv * ffn_gain).astype(bf16)
    logits = jnp.dot(normed_ffn, router, preferred_element_type=f32)
    probabilities = jax.nn.softmax(logits, axis=-1)

    expert_ids = jnp.arange(EXPERTS, dtype=i32)
    hot = jnp.sum((routes[..., None] == expert_ids).astype(f32), axis=1)
    before = (jnp.arange(tok)[:, None] > jnp.arange(tok)[None]).astype(bf16)
    slots = jnp.dot(before, hot.astype(bf16), preferred_element_type=f32)
    slot_code = jnp.where(hot > 0, slots, -1.0)
    chosen = probabilities * hot
    gate_total = jnp.sum(chosen, axis=-1, keepdims=True)
    gates = chosen / gate_total

    code = jnp.transpose(slot_code.reshape(tok, 32, EXP_DEV), (0, 2, 1))
    home_hot = code[..., None] == jnp.arange(CAP, dtype=f32)
    def to_peers(rows):
        return lax.all_to_all(rows, ("head", "blk"), split_axis=1, concat_axis=1, tiled=True)

    sent = jnp.concatenate([normed_ffn, slot_code.astype(bf16), gates.astype(bf16)], axis=1)
    everyone = spread(sent, 7)
    all_cot = spread(cotangent, 11)
    lane = jnp.arange(128)[None]
    sel_row = jnp.arange(8)[:, None]
    info = everyone[:, :, width:]
    column = (sel_row // 2) * EXPERTS + device * EXP_DEV + sel_row % 2
    sel = ((sel_row < 4) & (lane == column)).astype(bf16)
    nearby = (device ^ 8) * EXP_DEV
    column = sel_row % 2 + jnp.where(sel_row // 2 % 2 == 0, device * EXP_DEV, nearby)
    sel_chip = (lane == column + (sel_row // 4) * EXPERTS).astype(bf16)
    expert_rows, row_gates = pick_rows(sel, info, everyone, width, True)
    expert_rows = expert_rows.reshape(EXP_DEV, -1, width)
    row_gates = row_gates.reshape(EXP_DEV, -1, 128)[..., :1]
    (arrived_cot,) = pick_rows(sel, info, all_cot, width, False)
    arrived_cot = arrived_cot.reshape(EXP_DEV, -1, width)

    gate_up = jnp.einsum("erd,def->erf", expert_rows, full_in, preferred_element_type=f32)
    gate_part, up_part = gate_up[..., :FF], gate_up[..., FF:]
    sigmoid_gate = jax.nn.sigmoid(gate_part)
    silu_gate = gate_part * sigmoid_gate
    hidden_full = silu_gate * up_part
    hidden = hidden_full.astype(bf16)
    scaled_hidden = (hidden_full * row_gates).astype(bf16)
    expert_result = jnp.einsum(
        "erf,def->erd", hidden, full_back, preferred_element_type=f32
    ).astype(bf16)
    row_dots = jnp.sum(expert_result.astype(f32) * arrived_cot.astype(f32), axis=-1)

    grad_hidden = row_gates * jnp.einsum(
        "erd,def->erf", arrived_cot, full_back, preferred_element_type=f32
    )
    grad_gate = grad_hidden * up_part * sigmoid_gate * (1.0 + gate_part * (1.0 - sigmoid_gate))
    grad_up = grad_hidden * silu_gate
    grad_gate_up = jnp.concatenate([grad_gate, grad_up], axis=-1).astype(bf16)
    grad_rows = jnp.einsum(
        "erf,def->erd", grad_gate_up, full_in, preferred_element_type=f32
    ).astype(bf16)
    mixture = rows_home(sel_chip, info, expert_result, True, 12)
    grad_home = rows_home(sel_chip, info, grad_rows, False, 13)
    back_dots = to_peers(row_dots.reshape(EXP_DEV, 32, CAP))
    term_back = jnp.einsum("erc,erf->ecf", arrived_cot, scaled_hidden, preferred_element_type=f32)
    term_in = jnp.einsum("erc,erf->ecf", expert_rows, grad_gate_up, preferred_element_type=f32)

    def fold_dp(term):
        return lax.psum_scatter(term.astype(bf16), "dp", scatter_dimension=1, tiled=True)

    expert_out_grad = jnp.transpose(fold_dp(term_back), (1, 0, 2)).astype(f32)
    expert_in_grad = jnp.transpose(fold_dp(term_in), (1, 0, 2)).astype(f32)

    output = (middle + mixture).astype(bf16)
    grad_out = cotangent.astype(f32)
    grad_gates = jnp.sum(jnp.where(home_hot, back_dots, 0.0), axis=-1)
    grad_gates = jnp.transpose(grad_gates, (0, 2, 1)).reshape(tok, EXPERTS)
    mean_grad = jnp.sum(grad_gates * gates, axis=-1, keepdims=True)
    grad_probs = (grad_gates - mean_grad) / gate_total * hot
    grad_logits = probabilities * (
        grad_probs - jnp.sum(probabilities * grad_probs, axis=-1, keepdims=True)
    )
    high = grad_logits.astype(bf16)
    halves = jnp.concatenate([high, (grad_logits - high.astype(f32)).astype(bf16)], axis=1)
    router_term = jnp.einsum("td,te->de", normed_ffn, halves, preferred_element_type=f32)
    router_term = router_term[:, :EXPERTS] + router_term[:, EXPERTS:]
    grad_ffn = grad_home + jnp.einsum(
        "te,de->td", halves, jnp.concatenate([router, router], axis=1), preferred_element_type=f32
    )
    ffn_gain_term = jnp.sum(grad_ffn * middle * second_inv, axis=0)
    grad_middle = grad_out + rms_back(middle, second_inv, grad_ffn * ffn_gain)
    grad_branch = grad_middle.astype(bf16)
    branch_all = gather_rows(grad_branch).reshape(512, width)
    grad_att = by_head(
        jnp.dot(branch_all, full_out, preferred_element_type=f32).astype(bf16)
    )
    grad_att = go_over_x(grad_att.reshape(runs)).reshape(2048, HD)
    delta = jnp.sum(grad_att.astype(f32) * att, axis=-1)
    dq, dk, dv = attend_back(
        limits, q, k, v, grad_att, half_seg, half_ids, key_seg, inverse[:, 0], delta
    )
    cut = (4, 2, 4, 128, HD)
    grad_query, grad_key, grad_value = grads_over_x(
        dq.reshape(runs), dk.reshape(cut), dv.reshape(cut)
    )
    heads_shape = (4, 512, HD)
    grad_query_unit = rotary(grad_query.reshape(heads_shape).astype(f32), -1.0)
    query_gain_term = jnp.sum(grad_query_unit * query_unit, axis=(0, 1))
    grad_query_flat = flat_of(
        rms_back(query_proj, query_inv, grad_query_unit * query_gain).astype(bf16)
    )
    grad_key_unit = rotary(grad_key.reshape(heads_shape).astype(f32), -1.0)
    key_gain_term = jnp.sum(grad_key_unit * key_unit, axis=(0, 1))
    grad_key_flat = flat_of(rms_back(key_proj, key_inv, grad_key_unit * key_gain).astype(bf16))
    grad_value_flat = flat_of(grad_value)
    normed_part = jnp.einsum("qc,dc->qd", grad_query_flat, full_query, preferred_element_type=f32)
    normed_part += jnp.einsum("qc,dc->qd", grad_key_flat, full_key, preferred_element_type=f32)
    normed_part += jnp.einsum("qc,dc->qd", grad_value_flat, full_value, preferred_element_type=f32)
    grad_normed = sum_rows(normed_part.astype(bf16), 10)
    attn_gain_term = jnp.sum(grad_normed * inputs * first_inv, axis=0)
    input_grad = grad_middle + rms_back(inputs, first_inv, grad_normed * attn_gain)

    def weight_grad(rows, grads):
        return jnp.einsum("qc,qf->cf", rows, grads, preferred_element_type=f32).astype(bf16)

    gains = jnp.concatenate([attn_gain_term, ffn_gain_term, query_gain_term, key_gain_term])
    gains = jnp.pad(gains, (0, 32 * 8 * 128 - gains.shape[0])).reshape(32, 8, 128)
    small = jnp.concatenate([router_term.reshape(32, 32, 128), gains], axis=1)
    attn_grads, summed = fold_grads(
        [
            weight_grad(normed_all, grad_query_flat),
            weight_grad(normed_all, grad_key_flat),
            weight_grad(normed_all, grad_value_flat),
            weight_grad(branch_all, attended_flat),
        ],
        small,
    )
    summed = summed.reshape(32, 40, 128)
    router_grad = summed[:, :32].reshape(router.shape)
    gains = summed[:, 32:].reshape(-1)
    return (
        output,
        input_grad,
        gains[:2048],
        attn_grads[0],
        attn_grads[1],
        attn_grads[2],
        attn_grads[3],
        gains[4096:4224],
        gains[4224:4352],
        gains[2048:4096],
        router_grad,
        expert_in_grad,
        expert_out_grad,
    )


def solution(mesh):
    placed = (
        P(("dp", "head", "blk"), None),
        P("dp", None),
        P("dp", None),
        P(("dp", "head", "blk"), None),
        P(),
        P(("dp", "blk"), "head"),
        P(("dp", "blk"), "head"),
        P(("dp", "blk"), "head"),
        P(("dp", "blk"), "head"),
        P(),
        P(),
        P(),
        P(),
        P("dp", ("head", "blk"), None),
        P("dp", ("head", "blk"), None),
        P(("dp", "head", "blk"), None),
    )
    return jax.shard_map(
        on_device,
        mesh=mesh,
        in_specs=placed,
        out_specs=(
            P(("dp", "head", "blk"), None),
            P(("dp", "head", "blk"), None),
            P(),
            P(("dp", "blk"), "head"),
            P(("dp", "blk"), "head"),
            P(("dp", "blk"), "head"),
            P(("dp", "blk"), "head"),
            P(),
            P(),
            P(),
            P(),
            P("dp", ("head", "blk"), None),
            P("dp", ("head", "blk"), None),
        ),
        check_vma=False,
    )
```

```python
import functools
import math

import jax
import jax.numpy as jnp
from jax import lax
from jax.experimental import pallas as pl
from jax.experimental.pallas import tpu as pltpu
from jax.sharding import PartitionSpec as P

HEADS = 16
HD = 128
FF = 1024
TOPK = 8
EXP_DEV = 2
CAP = 24
EXPERTS = 64

epsilon = 1e-06
rope_base = 50000.0
f32 = jnp.float32
bf16 = jnp.bfloat16
i32 = jnp.int32
MESH = pl.DeviceIdType.MESH
ANY = pl.BlockSpec(memory_space=pl.ANY)
VMEM = pl.BlockSpec(memory_space=pltpu.VMEM)
SMEM = pl.BlockSpec(memory_space=pltpu.SMEM)
DMA = pltpu.SemaphoreType.DMA


def rms_rows(values):
    return lax.rsqrt(jnp.mean(values * values, axis=-1, keepdims=True) + epsilon)


def rms_back(values, inverse, grad_scaled):
    inner_mean = jnp.mean(grad_scaled * values, axis=-1, keepdims=True)
    return inverse * grad_scaled - values * inverse * inverse * inverse * inner_mean


def wrap4(value):
    return lax.rem(value + 4, 4)


class Place:
    def __init__(self):
        head, blk = lax.axis_index("head"), lax.axis_index("blk")
        self.dp = lax.axis_index("dp")
        self.yh, self.co = head // 2, lax.rem(head, 2)
        self.yl, self.x = blk // 4, lax.rem(blk, 4)
        self.head = head
        self.zr, self.zl, self.zo = (wrap4(self.dp + s) for s in (1, -1, 2))
        self.xr, self.xl, self.xo = (wrap4(self.x + s) for s in (1, -1, 2))
        y = self.yh * 2 + self.yl
        self.yr, self.ylf, self.yo = (wrap4(y + s) for s in (1, -1, 2))
        self.ZR, self.ZL, self.ZO = {"dp": self.zr}, {"dp": self.zl}, {"dp": self.zo}
        self.XR, self.XL, self.XO = (self.to_x(v) for v in (self.xr, self.xl, self.xo))
        self.Y = {"blk": (1 - self.yl) * 4 + self.x}
        self.C = {"head": self.yh * 2 + (1 - self.co)}
        self.H = {"head": (1 - self.yh) * 2 + self.co}
        self.YR, self.YL = self.to_y(self.yr), self.to_y(self.ylf)

    def to_x(self, x):
        return {"blk": self.yl * 4 + x}

    def to_y(self, y):
        return {"head": (y // 2) * 2 + self.co, "blk": lax.rem(y, 2) * 4 + self.x}


def greet(devices):
    barrier = pltpu.get_barrier_semaphore()
    for device in devices:
        pl.semaphore_signal(barrier, inc=1, device_id=device, device_id_type=MESH)
    pl.semaphore_wait(barrier, len(devices))


class View:
    def __init__(self, ref, index=None):
        self.ref, self.index = ref, index

    @property
    def at(self):
        return self

    def __getitem__(self, index):
        return View(self, index)

    def get(self):
        base = self.ref.get() if isinstance(self.ref, View) else self.ref
        return base if self.index is None else base.at[self.index]

    def load(self):
        return self.get()[...]

    def store(self, value):
        ref = self.get()
        ref[...] = value.astype(ref.dtype)


def plain(ref):
    return ref.get() if isinstance(ref, View) else ref


class Sent:
    def __init__(self, make):
        self.make = make

    def wait_recv(self):
        self.make().wait_recv()

    def wait_send(self):
        self.make().wait_send()

    def wait(self):
        self.make().wait()


class Wire:
    def __init__(self, send_sem, recv_sem):
        self.send_sem, self.recv_sem, self.started = send_sem, recv_sem, []

    def send(self, src, dst, device):
        at = len(self.started)

        def make():
            return pltpu.make_async_remote_copy(
                src_ref=plain(src),
                dst_ref=plain(dst),
                send_sem=self.send_sem.at[at],
                recv_sem=self.recv_sem.at[at],
                device_id=device,
                device_id_type=MESH,
            )

        make().start()
        self.started.append(Sent(make))
        return self.started[-1]

    def drain(self):
        for copy in self.started:
            copy.wait_send()


def local(src, dst, sems, at):
    def make():
        return pltpu.make_async_copy(plain(src), plain(dst), sems.at[at])

    make().start()
    return Sent(make)


def remote_call(body, name, cid, sends, locals_, ins, outs, out_shape, scratch=(), vmem=None):
    return pl.pallas_call(
        body,
        name=name,
        out_shape=out_shape,
        in_specs=ins,
        out_specs=outs,
        scratch_shapes=[DMA((sends,)), DMA((sends,)), DMA((max(locals_, 1),)), *scratch],
        compiler_params=pltpu.CompilerParams(
            collective_id=cid, has_side_effects=True, vmem_limit_bytes=vmem
        ),
    )


def shaped(shape, dtype=bf16):
    return jax.ShapeDtypeStruct(shape, dtype)


def weights_kernel(w, wo, n, g, go, m, ss, rs, ls):
    p = Place()
    dp, yl, x = p.dp, p.yl, p.x
    own = [
        local(w, g.at[:, dp, yl, x], ls, 0),
        local(n, m.at[p.head], ls, 1),
        local(wo, go.at[dp], ls, 2),
    ]
    greet([p.ZR, p.ZL, p.XR, p.XL, p.Y, p.C, p.H])
    wire = Wire(ss, rs)
    n_c = wire.send(n, m.at[p.head], p.C)
    z1 = wire.send(w, g.at[:, dp, yl, x], p.ZR)
    z2 = wire.send(w, g.at[:, dp, yl, x], p.ZL)
    n_h = wire.send(n, m.at[p.head], p.H)
    o1 = wire.send(wo, go.at[dp], p.ZR)
    o2 = wire.send(wo, go.at[dp], p.ZL)
    z1.wait_recv()
    z3 = wire.send(g.at[0:2, p.zl, yl, x], g.at[0:2, p.zl, yl, x], p.ZR)
    z2.wait_recv()
    z4 = wire.send(g.at[2, p.zr, yl, x], g.at[2, p.zr, yl, x], p.ZL)
    own[0].wait()
    z3.wait_recv()
    z4.wait_recv()
    b1 = wire.send(g.at[2, :, yl, x], g.at[2, :, yl, x], p.XR)
    b2 = wire.send(g.at[2, :, yl, x], g.at[2, :, yl, x], p.XL)
    a1 = wire.send(g.at[0:2, :, yl, x], g.at[0:2, :, yl, x], p.Y)
    c1 = wire.send(g.at[2, :, yl, x], g.at[2, :, yl, x], p.Y)
    o1.wait_recv()
    o3 = wire.send(go.at[p.zl, 0:32], go.at[p.zl, 0:32], p.ZR)
    o2.wait_recv()
    o4 = wire.send(go.at[p.zr, 32:64], go.at[p.zr, 32:64], p.ZL)
    n_h.wait_recv()
    other = (1 - p.yh) * 2 + p.co
    n_f = wire.send(m.at[other], m.at[other], p.C)
    b1.wait_recv()
    b3 = wire.send(g.at[2, 0:2, yl, p.xl], g.at[2, 0:2, yl, p.xl], p.XR)
    c2 = wire.send(g.at[2, :, yl, p.xl], g.at[2, :, yl, p.xl], p.Y)
    b2.wait_recv()
    b4 = wire.send(g.at[2, 2:4, yl, p.xr], g.at[2, 2:4, yl, p.xr], p.XL)
    c3 = wire.send(g.at[2, :, yl, p.xr], g.at[2, :, yl, p.xr], p.Y)
    a1.wait_recv()
    a2 = wire.send(g.at[0:2, :, :, x], g.at[0:2, :, :, x], p.XR)
    a3 = wire.send(g.at[0:2, :, :, x], g.at[0:2, :, :, x], p.XL)
    b3.wait_recv()
    b4.wait_recv()
    c4 = wire.send(g.at[2, :, yl, p.xo], g.at[2, :, yl, p.xo], p.Y)
    a2.wait_recv()
    a4 = wire.send(g.at[0, :, :, p.xl], g.at[0, :, :, p.xl], p.XR)
    a3.wait_recv()
    a5 = wire.send(g.at[1, :, :, p.xr], g.at[1, :, :, p.xr], p.XL)
    for copy in (n_c, n_f, o3, o4, c1, c2, c3, c4, a4, a5):
        copy.wait_recv()
    own[1].wait()
    own[2].wait()
    wire.drain()


def gather_weights(w, wo, n):
    return remote_call(
        weights_kernel,
        "gather_weights",
        1,
        24,
        3,
        [ANY] * 3,
        [ANY] * 3,
        (shaped((3, 4, 2, 4, 64, 512)), shaped((4, 64, 512)), shaped((4, 128, 2048))),
    )(w, wo, n)


def rows_kernel(n, m, ss, rs, ls):
    p = Place()
    own = local(n, m.at[p.head], ls, 0)
    greet([p.C, p.H])
    wire = Wire(ss, rs)
    n_h = wire.send(n, m.at[p.head], p.H)
    n_c = wire.send(n, m.at[p.head], p.C)
    n_h.wait_recv()
    other = (1 - p.yh) * 2 + p.co
    n_f = wire.send(m.at[other], m.at[other], p.C)
    n_c.wait_recv()
    n_f.wait_recv()
    own.wait()
    wire.drain()


def gather_rows(n):
    return remote_call(
        rows_kernel, "gather_rows", 2, 3, 1, [ANY], [ANY], (shaped((4, 128, 2048)),)
    )(n)[0]


def sum_kernel(part, out, ss, rs, ls, got_c, got_h, half):
    p = Place()
    greet([p.C, p.H])
    wire = Wire(ss, rs)
    far = wire.send(part.at[1 - p.yh, 1 - p.co], got_c.at[0], p.C)
    near = wire.send(part.at[p.yh, 1 - p.co], got_c.at[1], p.C)
    far.wait_recv()

    def add_far(i, carry):
        rows = pl.ds(pl.multiple_of(i * 16, 16), 16)
        half[rows] = (
            part[1 - p.yh, p.co, rows].astype(f32) + got_c[0, rows].astype(f32)
        ).astype(bf16)
        return carry

    lax.fori_loop(0, 8, add_far, 0)
    over = wire.send(half, got_h, p.H)
    near.wait_recv()
    over.wait_recv()

    def add_near(i, carry):
        rows = pl.ds(pl.multiple_of(i * 16, 16), 16)
        out[rows] = (
            part[p.yh, p.co, rows].astype(f32)
            + got_c[1, rows].astype(f32)
            + got_h[rows].astype(f32)
        )
        return carry

    lax.fori_loop(0, 8, add_near, 0)
    wire.drain()


def sum_rows(part, cid):
    return remote_call(
        sum_kernel,
        "sum_rows",
        cid,
        3,
        1,
        [VMEM],
        [VMEM],
        (shaped((128, 2048), f32),),
        scratch=[
            pltpu.VMEM((2, 128, 2048), bf16),
            pltpu.VMEM((128, 2048), bf16),
            pltpu.VMEM((128, 2048), bf16),
        ],
        vmem=16 << 20,
    )(part.reshape(2, 2, 128, 2048))[0]


def heads_kernel(q, k, v, go, qd, kd, vd, gd, ss, rs, ls):
    p = Place()
    yl, x = p.yl, p.x
    own = [
        local(q.at[x], qd.at[:, x], ls, 0),
        local(k.at[x], kd.at[:, yl, x], ls, 1),
        local(v.at[x], vd.at[:, yl, x], ls, 2),
        local(go, gd.at[:, yl, x], ls, 3),
    ]
    greet([p.Y, p.XR, p.XL, p.XO])
    wire = Wire(ss, rs)
    done = [
        wire.send(k.at[x], kd.at[:, yl, x], p.Y),
        wire.send(v.at[x], vd.at[:, yl, x], p.Y),
    ]
    w1 = wire.send(go, gd.at[:, yl, x], p.Y)
    moved = []
    for there, came, device in ((p.xo, p.xo, p.XO), (p.xr, p.xl, p.XR), (p.xl, p.xr, p.XL)):
        ks = wire.send(k.at[there], kd.at[:, yl, x], device)
        vs = wire.send(v.at[there], vd.at[:, yl, x], device)
        moved.append((came, ks, vs))
    for there, device in ((p.xo, p.XO), (p.xr, p.XR), (p.xl, p.XL)):
        done.append(wire.send(q.at[there], qd.at[:, x], device))
    for came, ks, vs in moved[1:] + moved[:1]:
        ks.wait_recv()
        done.append(wire.send(kd.at[:, yl, came], kd.at[:, yl, came], p.Y))
        vs.wait_recv()
        done.append(wire.send(vd.at[:, yl, came], vd.at[:, yl, came], p.Y))
    own[3].wait()
    w1.wait_recv()
    w2 = wire.send(gd.at[:, :, x], gd.at[:, :, x], p.XR)
    w3 = wire.send(gd.at[:, :, x], gd.at[:, :, x], p.XL)
    w2.wait_recv()
    done.append(wire.send(gd.at[0:2, :, p.xl], gd.at[0:2, :, p.xl], p.XR))
    w3.wait_recv()
    done.append(wire.send(gd.at[2:4, :, p.xr], gd.at[2:4, :, p.xr], p.XL))
    for copy in done:
        copy.wait_recv()
    for copy in own[:3]:
        copy.wait()
    wire.drain()


def heads_over_x(q, k, v, go):
    return remote_call(
        heads_kernel,
        "heads_over_x",
        3,
        22,
        4,
        [ANY] * 4,
        [ANY] * 4,
        (
            shaped((4, 4, 128, 128)),
            shaped((4, 2, 4, 128, 128)),
            shaped((4, 2, 4, 128, 128)),
            shaped((4, 2, 4, 64, 512)),
        ),
    )(q, k, v, go)


def back_x_kernel(o, att, ss, rs, ls):
    p = Place()
    own = local(o.at[:, p.x], att.at[p.x], ls, 0)
    greet([p.XR, p.XL, p.XO])
    wire = Wire(ss, rs)
    for there, device in ((p.xo, p.XO), (p.xr, p.XR), (p.xl, p.XL)):
        wire.send(o.at[:, there], att.at[p.x], device)
    for copy in wire.started:
        copy.wait_recv()
    own.wait()
    wire.drain()


def back_over_x(o):
    return remote_call(
        back_x_kernel, "back_over_x", 4, 3, 1, [ANY], [ANY], (shaped((4, 4, 128, 128)),)
    )(o)[0]


def go_x_kernel(o, d, ss, rs, ls):
    p = Place()
    own = local(o.at[p.x], d.at[:, p.x], ls, 0)
    greet([p.XR, p.XL, p.XO])
    wire = Wire(ss, rs)
    for there, device in ((p.xo, p.XO), (p.xr, p.XR), (p.xl, p.XL)):
        wire.send(o.at[there], d.at[:, p.x], device)
    for copy in wire.started:
        copy.wait_recv()
    own.wait()
    wire.drain()


def go_over_x(o):
    return remote_call(
        go_x_kernel, "go_over_x", 5, 3, 1, [ANY], [ANY], (shaped((4, 4, 128, 128)),)
    )(o)[0]


def grads_x_kernel(dq, dk, dv, qd, kd, vd, ss, rs, ls, gk, gv, sk, sv):
    p = Place()
    x, yl = p.x, p.yl
    own = local(dq.at[:, x], qd.at[x], ls, 0)
    greet([p.Y, p.XR, p.XL, p.XO])
    wire = Wire(ss, rs)
    order = ((p.xo, p.XO), (p.xr, p.XR), (p.xl, p.XL), (x, None))
    pairs = []
    for i, (there, device) in enumerate(order):
        pairs.append(
            (
                wire.send(dk.at[:, 1 - yl, there], gk.at[i], p.Y),
                wire.send(dv.at[:, 1 - yl, there], gv.at[i], p.Y),
            )
        )
    last = []
    for there, device in order[:3]:
        last.append(wire.send(dq.at[:, there], qd.at[x], device))
    for i, (there, device) in enumerate(order):
        for grads, got, summed, out, arrived in (
            (dk, gk, sk, kd, pairs[i][0]),
            (dv, gv, sv, vd, pairs[i][1]),
        ):
            arrived.wait_recv()
            for run in range(4):
                total = grads[run, yl, there].astype(f32) + got[i, run].astype(f32)
                if device is None:
                    out[x, run] = total.astype(bf16)
                else:
                    summed[i, run] = total.astype(bf16)
            if device is not None:
                last.append(wire.send(summed.at[i], out.at[x], device))
    for copy in last:
        copy.wait_recv()
    own.wait()
    wire.drain()


def grads_over_x(dq, dk, dv):
    return remote_call(
        grads_x_kernel,
        "grads_over_x",
        6,
        17,
        1,
        [ANY, VMEM, VMEM],
        [ANY, VMEM, VMEM],
        (shaped((4, 4, 128, 128)),) * 3,
        scratch=[
            pltpu.VMEM((4, 4, 128, 128), bf16),
            pltpu.VMEM((4, 4, 128, 128), bf16),
            pltpu.VMEM((3, 4, 128, 128), bf16),
            pltpu.VMEM((3, 4, 128, 128), bf16),
        ],
        vmem=16 << 20,
    )(dq, dk, dv)


QB = 256
KB = 512
SCALE = HD**-0.5
SCALE2 = SCALE * math.log2(math.e)


def attend_kernel(lim, q, k, v, qseg, qpos, kseg, o_low, o, linv, vext):
    rows = k.shape[0]
    ones = (lax.broadcasted_iota(i32, (KB, HD), 1) == 0).astype(bf16)

    def fill(i, carry):
        at = pl.ds(pl.multiple_of(i * KB, KB), KB)
        vext[at, :HD] = v[at]
        vext[at, HD:] = ones
        return carry

    lax.fori_loop(0, rows // KB, fill, 0)

    def one_query(b, carry):
        at = pl.ds(pl.multiple_of(b * QB, QB), QB)
        query, seg, pos = q[at], qseg[at], qpos[at]

        def one_key(j, acc):
            keys = pl.ds(pl.multiple_of(j * KB, KB), KB)
            score = lax.dot_general(
                query, k[keys], (((1,), (1,)), ((), ())), preferred_element_type=f32
            )
            key_pos = j * KB + lax.broadcasted_iota(i32, (1, KB), 1)
            allowed = (seg == kseg[:, keys]) | (pos == key_pos)
            weight = jnp.where(allowed, jnp.exp2(score * SCALE2), 0.0).astype(bf16)
            return acc + jnp.dot(weight, vext[keys], preferred_element_type=f32)

        acc = lax.fori_loop(lim[0, b], lim[1, b], one_key, jnp.zeros((QB, 2 * HD), f32))
        inverse = 1.0 / acc[:, HD : HD + 1]
        result = acc[:, :HD] * inverse
        o[at] = result
        o_low[at] = result.astype(bf16)
        linv[at] = jnp.broadcast_to(inverse, (QB, HD))
        return carry

    lax.fori_loop(0, q.shape[0] // QB, one_query, 0)


def attend(lim, q, k, v, qseg, qpos, kseg):
    n = q.shape[0]
    return pl.pallas_call(
        attend_kernel,
        name="attend",
        out_shape=(shaped((n, HD)), shaped((n, HD), f32), shaped((n, HD), f32)),
        in_specs=[SMEM] + [VMEM] * 6,
        out_specs=[VMEM] * 3,
        scratch_shapes=[pltpu.VMEM((k.shape[0], 2 * HD), bf16)],
        compiler_params=pltpu.CompilerParams(vmem_limit_bytes=32 << 20),
    )(lim, q, k, v, qseg[:, None], qpos[:, None], kseg[None])


def attend_back_kernel(
    lim, q, k, v, g, qseg, qpos, kseg, linv, delta, dq, dk, dv, kt, dk_acc, dv_acc
):
    rows = k.shape[0]

    def fill(i, carry):
        at = pl.ds(pl.multiple_of(i * KB, KB), KB)
        kt[:, at] = k[at].astype(f32).T.astype(bf16)
        dk_acc[at] = jnp.zeros((KB, HD), f32)
        dv_acc[at] = jnp.zeros((KB, HD), f32)
        return carry

    lax.fori_loop(0, rows // KB, fill, 0)
    across = (((1,), (1,)), ((), ()))

    def one_query(b, carry):
        at = pl.ds(pl.multiple_of(b * QB, QB), QB)
        query, grad = q[at], g[at]
        seg, pos, inverse, shift = qseg[:, at], qpos[:, at], linv[:, at], delta[:, at]

        def one_key(j, acc):
            keys = pl.ds(pl.multiple_of(j * KB, KB), KB)
            key = k[keys]
            score = lax.dot_general(key, query, across, preferred_element_type=f32)
            key_pos = j * KB + lax.broadcasted_iota(i32, (KB, 1), 0)
            allowed = (kseg[keys] == seg) | (key_pos == pos)
            prob = jnp.where(allowed, jnp.exp2(score * SCALE2), 0.0) * inverse
            grad_prob = lax.dot_general(v[keys], grad, across, preferred_element_type=f32)
            grad_score = (prob * (grad_prob - shift)).astype(bf16)
            dv_acc[keys] += jnp.dot(prob.astype(bf16), grad, preferred_element_type=f32)
            dk_acc[keys] += jnp.dot(grad_score, query, preferred_element_type=f32)
            return acc + jnp.dot(kt[:, keys], grad_score, preferred_element_type=f32)

        acc = lax.fori_loop(lim[0, b], lim[1, b], one_key, jnp.zeros((HD, QB), f32))
        dq[at] = (acc * SCALE).T.astype(bf16)
        return carry

    lax.fori_loop(0, q.shape[0] // QB, one_query, 0)

    def finish(i, carry):
        at = pl.ds(pl.multiple_of(i * KB, KB), KB)
        dk[at] = (dk_acc[at] * SCALE).astype(bf16)
        dv[at] = dv_acc[at].astype(bf16)
        return carry

    lax.fori_loop(0, rows // KB, finish, 0)


def attend_back(lim, q, k, v, g, qseg, qpos, kseg, linv, delta):
    n, rows = q.shape[0], k.shape[0]
    return pl.pallas_call(
        attend_back_kernel,
        name="attend_back",
        out_shape=(shaped((n, HD)), shaped((rows, HD)), shaped((rows, HD))),
        in_specs=[SMEM] + [VMEM] * 9,
        out_specs=[VMEM] * 3,
        scratch_shapes=[
            pltpu.VMEM((HD, rows), bf16),
            pltpu.VMEM((rows, HD), f32),
            pltpu.VMEM((rows, HD), f32),
        ],
        compiler_params=pltpu.CompilerParams(vmem_limit_bytes=40 << 20),
    )(lim, q, k, v, g, qseg[None], qpos[None], kseg[:, None], linv[None], delta[None])


SPREAD_SENDS = 26


def spread_steps(p, wire, sems, src, dst):
    yh, co, yl, x = p.yh, p.co, p.yl, p.x
    (rh, rl), (lh, ll), (oh, ol) = ((y // 2, lax.rem(y, 2)) for y in (p.yr, p.ylf, p.yo))
    A, A1, A2 = pl.ds(0, 64), pl.ds(0, 32), pl.ds(32, 32)
    B, B1, B2 = pl.ds(64, 64), pl.ds(64, 32), pl.ds(96, 32)
    src, dst = View(src), View(dst)
    own = local(src, dst.at[yh, co, yl, x], sems, 0)

    def both(ref, device):
        return wire.send(ref, ref, device)

    me = dst.at[yh, co, yl]
    a1 = wire.send(src.at[A], me.at[x, A], p.XR)
    b1 = wire.send(src.at[B], me.at[x, B], p.YR)
    a2 = wire.send(src.at[A], me.at[x, A], p.XL)
    b2 = wire.send(src.at[B], me.at[x, B], p.YL)
    yield
    a1.wait_recv()
    a3 = both(me.at[p.xl, A1], p.XR)
    a2.wait_recv()
    a4 = both(me.at[p.xr, A2], p.XL)
    b1.wait_recv()
    b3 = both(dst.at[lh, co, ll, x, B1], p.YR)
    b2.wait_recv()
    b4 = both(dst.at[rh, co, rl, x, B2], p.YL)
    yield
    own.wait()
    a3.wait_recv()
    a4.wait_recv()
    a5 = both(me.at[:, A], p.YR)
    a6 = both(me.at[:, A], p.YL)
    b3.wait_recv()
    b4.wait_recv()
    b5 = both(dst.at[:, co, :, x, B], p.XR)
    b6 = both(dst.at[:, co, :, x, B], p.XL)
    last = [both(me.at[:, A], p.C), both(dst.at[:, co, :, x, B], p.C)]
    yield
    a5.wait_recv()
    a7 = both(dst.at[lh, co, ll, :, A1], p.YR)
    b5.wait_recv()
    b7 = both(dst.at[:, co, :, p.xl, B1], p.XR)
    a6.wait_recv()
    a8 = both(dst.at[rh, co, rl, :, A2], p.YL)
    b6.wait_recv()
    b8 = both(dst.at[:, co, :, p.xr, B2], p.XL)
    last += [both(dst.at[lh, co, ll, :, A], p.C), both(dst.at[:, co, :, p.xl, B], p.C)]
    last += [both(dst.at[rh, co, rl, :, A], p.C), both(dst.at[:, co, :, p.xr, B], p.C)]
    yield
    a7.wait_recv()
    last.append(both(dst.at[oh, co, ol, :, A1], p.C))
    b7.wait_recv()
    last.append(both(dst.at[:, co, :, p.xo, B1], p.C))
    a8.wait_recv()
    last.append(both(dst.at[oh, co, ol, :, A2], p.C))
    b8.wait_recv()
    last.append(both(dst.at[:, co, :, p.xo, B2], p.C))
    yield
    for copy in last:
        copy.wait_recv()
    wire.drain()
    yield


def greet_plane(p):
    greet([p.XR, p.XL, p.YR, p.YL, p.C])


def spread_kernel(src, dst, ss, rs, ls):
    p = Place()
    greet_plane(p)
    for _ in spread_steps(p, Wire(ss, rs), ls, src, dst):
        pass


def spread(src, cid):
    width = src.shape[1]
    return remote_call(
        spread_kernel,
        "spread",
        cid,
        SPREAD_SENDS,
        1,
        [ANY],
        [ANY],
        (shaped((2, 2, 2, 4, 128, width)),),
    )(src)[0].reshape(32, 128, width)


def at_step(number, *stages):
    for step, stage in stages:

        @pl.when(number == step)
        def _():
            next(stage)


def block(shape, index):
    return pl.BlockSpec(shape, index)


def nt(a, b):
    return lax.dot_general(a, b, (((1,), (1,)), ((), ())), preferred_element_type=f32)


def tn(a, b):
    return lax.dot_general(a, b, (((0,), (0,)), ((), ())), preferred_element_type=f32)


PARTS = 4


def forward_kernel(src, rows, w_in, w_out, dst, gate, up, hidden, y, ss, rs, ls):
    p = Place()
    greet_plane(p)
    moving = spread_steps(p, Wire(ss, rs), ls, src, dst)
    next(moving)
    n = rows.shape[1]
    cut = FF // PARTS

    def first(rows, w_gate, w_up, gate, up, hidden):
        at_step(pl.program_id(0) * PARTS + pl.program_id(1), (2, moving), (4, moving))
        g = jnp.dot(rows[0], w_gate[0], preferred_element_type=f32)
        u = jnp.dot(rows[0], w_up[0], preferred_element_type=f32)
        gate[0] = g.astype(bf16)
        up[0] = u.astype(bf16)
        hidden[0] = (g * jax.nn.sigmoid(g) * u).astype(bf16)

    out = block((1, n, cut), lambda e, j: (e, 0, j))
    pltpu.emit_pipeline(
        first,
        grid=(EXP_DEV, PARTS),
        in_specs=[
            block((1, n, 2048), lambda e, j: (e, 0, 0)),
            block((1, 2048, cut), lambda e, j: (e, 0, j)),
            block((1, 2048, cut), lambda e, j: (e, 0, j + PARTS)),
        ],
        out_specs=[out, out, out],
    )(rows, w_in, w_in, gate, up, hidden)

    def second(hidden, w, y):
        at_step(pl.program_id(0) * PARTS + pl.program_id(1), (3, moving))
        y[0] = nt(hidden[0], w[0]).astype(bf16)

    pltpu.emit_pipeline(
        second,
        grid=(EXP_DEV, PARTS),
        in_specs=[
            block((1, n, FF), lambda e, j: (e, 0, 0)),
            block((1, 2048 // PARTS, FF), lambda e, j: (e, j, 0)),
        ],
        out_specs=[block((1, n, 2048 // PARTS), lambda e, j: (e, 0, j))],
    )(hidden, w_out, y)
    for _ in moving:
        pass


def expert_forward(src, rows, w_in, w_out, cid):
    n, width = rows.shape[1:]
    outs = remote_call(
        forward_kernel,
        "expert_forward",
        cid,
        SPREAD_SENDS,
        1,
        [ANY] * 4,
        [ANY] * 5,
        (shaped((2, 2, 2, 4, 128, width)),)
        + (shaped((EXP_DEV, n, FF)),) * 3
        + (shaped((EXP_DEV, n, width)),),
        vmem=48 << 20,
    )(src, rows, w_in, w_out)
    return outs[0].reshape(32, 128, width), *outs[1:]


def slot_hits(table, count, rows_down):
    shape = (count * 2 * CAP, 256) if rows_down else (256, count * 2 * CAP)
    line = lax.broadcasted_iota(i32, shape, 0 if rows_down else 1)
    block = lax.broadcasted_iota(i32, shape, 1 if rows_down else 0) // 128
    expert = line // (2 * CAP)
    want = line - expert * (2 * CAP) - block * CAP

    def spread_out(first):
        value = jnp.zeros(shape, f32)
        for e in range(count):
            c = first + e
            at = table[c : c + 1] if rows_down else table[:, c : c + 1]
            value = jnp.where(expert == e, at, value)
        return value

    hit = (spread_out(0).astype(i32) == want) & (want >= 0) & (want < CAP)
    return hit, spread_out(count)


def pick_kernel(gated, sel, info, src, rows_out, *gates_out):
    tokens = jnp.concatenate([src[0], src[1]], axis=0)
    both = jnp.concatenate([info[0], info[1]], axis=0)
    table = lax.dot_general(
        sel[...], both, (((1,), (1,)), ((), ())), preferred_element_type=f32
    )
    hit, gate = slot_hits(table, EXP_DEV, True)
    rows = jnp.dot(hit.astype(bf16), tokens, preferred_element_type=f32).astype(bf16)
    for e in range(EXP_DEV):
        rows_out[e, 0] = rows[e * 2 * CAP : (e + 1) * 2 * CAP]
    if gated:
        total = jnp.sum(jnp.where(hit, gate, 0.0), axis=1, keepdims=True)
        total = jnp.broadcast_to(total, (EXP_DEV * 2 * CAP, 128))
        for e in range(EXP_DEV):
            gates_out[0][e, 0] = total[e * 2 * CAP : (e + 1) * 2 * CAP]


def pick_rows(sel, info, src, width, gated):
    pairs = src.shape[0] // 2

    def spec(lanes):
        return pl.BlockSpec((EXP_DEV, 1, 2 * CAP, lanes), lambda i: (0, i, 0, 0))

    shapes = [shaped((EXP_DEV, pairs, 2 * CAP, width)), shaped((EXP_DEV, pairs, 2 * CAP, 128), f32)]
    specs = [spec(width), spec(128)]
    return pl.pallas_call(
        functools.partial(pick_kernel, gated),
        name="pick_rows",
        grid=(pairs,),
        out_shape=shapes[: 1 + gated],
        in_specs=[
            pl.BlockSpec((8, 128), lambda i: (0, 0)),
            pl.BlockSpec((2, 128, 128), lambda i: (i, 0, 0)),
            pl.BlockSpec((2, 128, width), lambda i: (i, 0, 0)),
        ],
        out_specs=specs[: 1 + gated],
        compiler_params=pltpu.CompilerParams(vmem_limit_bytes=40 << 20),
    )(sel, info, src)


HOME_SENDS = 18


def home_scratch():
    return [
        pltpu.VMEM((2, 4, 8 * CAP, 2048), bf16),
        pltpu.VMEM((2, 2, 4, 128, 2048), bf16),
        pltpu.VMEM((2, 2, 64, 2048), bf16),
        pltpu.VMEM((2, 2, 64, 2048), bf16),
        pltpu.VMEM((2, 4, 64, 2048), bf16),
        pltpu.VMEM((2, 2, 2, 64, 2048), bf16),
        pltpu.VMEM((2, 2, 32, 2048), bf16),
        pltpu.VMEM((2, 2, 64, 2048), bf16),
    ]


def home_steps(p, wire, sems, gated, sel, info, rows, out, cat, q, a1, b1, a2, b2, c1, c2):
    yh, co, yl, x = p.yh, p.co, p.yl, p.x
    ys = [(yy // 2, lax.rem(yy, 2)) for yy in (p.yr, p.ylf, p.yo)]
    (rh, rl), (lh, ll), (oh, ol) = ys
    rows, out, whole_q, whole_cat = View(rows), View(out), q, cat
    q, cat, a1, b1, a2, b2, c1, c2 = (View(ref) for ref in (q, cat, a1, b1, a2, b2, c1, c2))
    own, first = [], []
    for e in range(EXP_DEV):
        lines = pl.ds(e * 2 * CAP, 2 * CAP)
        there = pl.ds((2 + e) * 2 * CAP, 2 * CAP)
        first.append(wire.send(rows.at[e, :, 1 - co], cat.at[:, :, there], p.C))
        own.append(local(rows.at[e, :, co], cat.at[:, :, lines], sems, e))
    yield
    for copy in own:
        copy.wait()
    for copy in first:
        copy.wait_recv()

    def place(i, carry):
        h, pair = i // 4, lax.rem(i, 4)
        block = h * 16 + co * 8 + pair * 2
        both = jnp.concatenate([info[block], info[block + 1]], axis=0)
        table = lax.dot_general(
            both, sel[...], (((1,), (1,)), ((), ())), preferred_element_type=f32
        )
        hit, gate = slot_hits(table, 4, False)
        value = jnp.where(hit, gate if gated else 1.0, 0.0).astype(bf16)
        for c in range(0, 2048, 512):
            total = jnp.dot(
                value, whole_cat[h, pair, :, c : c + 512], preferred_element_type=f32
            ).astype(bf16)
            at = lax.rem(pair, 2) * 2
            whole_q[h, pair // 2, at, :, c : c + 512] = total[:128]
            whole_q[h, pair // 2, at + 1, :, c : c + 512] = total[128:]
        return carry

    lax.fori_loop(0, 8, place, 0)
    A, B = pl.ds(0, 64), pl.ds(64, 64)
    s1 = [
        wire.send(q.at[oh, ol, 0:2, A], a1.at[0], p.YR),
        wire.send(q.at[0, :, p.xo, B], b1.at[0], p.XR),
        wire.send(q.at[oh, ol, 2:4, A], a1.at[1], p.YL),
        wire.send(q.at[1, :, p.xo, B], b1.at[1], p.XL),
    ]
    yield

    def add(dst, *srcs):
        total = srcs[0].load().astype(f32)
        for src in srcs[1:]:
            total = total + src.load().astype(f32)
        dst.store(total)

    def loop(count, body):
        def step(i, carry):
            body(i)
            return carry

        lax.fori_loop(0, count, step, 0)

    def plus(dst, src):
        add(dst, dst, src)

    s2 = []
    s1[0].wait_recv()
    loop(2, lambda i: plus(q.at[rh, rl, i, A], a1.at[0, i]))
    s2.append(wire.send(q.at[rh, rl, :, A], a2.at[0], p.YR))
    s1[1].wait_recv()
    loop(2, lambda i: plus(q.at[0, i, p.xr, B], b1.at[0, i]))
    s2.append(wire.send(q.at[:, :, p.xr, B], b2.at[0], p.XR))
    s1[2].wait_recv()
    loop(2, lambda i: plus(q.at[lh, ll, 2 + i, A], a1.at[1, i]))
    s2.append(wire.send(q.at[lh, ll, :, A], a2.at[1], p.YL))
    s1[3].wait_recv()
    loop(2, lambda i: plus(q.at[1, i, p.xl, B], b1.at[1, i]))
    s2.append(wire.send(q.at[:, :, p.xl, B], b2.at[1], p.XL))
    yield
    for copy in s2:
        copy.wait_recv()
    loop(4, lambda i: add(q.at[yh, yl, i, A], q.at[yh, yl, i, A], a2.at[0, i], a2.at[1, i]))
    s3 = [
        wire.send(q.at[yh, yl, p.xo, 0:32], c1.at[0, 0], p.XR),
        wire.send(q.at[yh, yl, p.xo, 32:64], c1.at[0, 1], p.XL),
    ]
    for h in range(2):
        loop(2, lambda i: add(q.at[h, i, x, B], q.at[h, i, x, B], b2.at[0, h, i], b2.at[1, h, i]))
    s3 += [
        wire.send(q.at[oh, ol, x, 64:96], c1.at[1, 0], p.YR),
        wire.send(q.at[oh, ol, x, 96:128], c1.at[1, 1], p.YL),
    ]
    yield
    s4 = []
    s3[0].wait_recv()
    plus(q.at[yh, yl, p.xr, 0:32], c1.at[0, 0])
    s4.append(wire.send(q.at[yh, yl, p.xr, A], c2.at[0, 0], p.XR))
    s3[1].wait_recv()
    plus(q.at[yh, yl, p.xl, 32:64], c1.at[0, 1])
    s4.append(wire.send(q.at[yh, yl, p.xl, A], c2.at[0, 1], p.XL))
    s3[2].wait_recv()
    plus(q.at[rh, rl, x, 64:96], c1.at[1, 0])
    s4.append(wire.send(q.at[rh, rl, x, B], c2.at[1, 0], p.YR))
    s3[3].wait_recv()
    plus(q.at[lh, ll, x, 96:128], c1.at[1, 1])
    s4.append(wire.send(q.at[lh, ll, x, B], c2.at[1, 1], p.YL))
    yield
    for copy in s4:
        copy.wait_recv()
    add(out.at[0:64], q.at[yh, yl, x, A], c2.at[0, 0], c2.at[0, 1])
    add(out.at[64:128], q.at[yh, yl, x, B], c2.at[1, 0], c2.at[1, 1])
    wire.drain()
    yield


def by_place(rows):
    return rows.reshape(EXP_DEV, 2, 2, 4, 2 * CAP, 2048)


def backward_kernel(
    sel, info, y_places, y, cot, gate, up, hidden, row_gates, w_in, w_out,
    mixture, dots, dgate, dup, drows, term, ss, rs, ls, *scratch,
):
    p = Place()
    greet_plane(p)
    moving = home_steps(p, Wire(ss, rs), ls, True, sel, info, y_places, mixture, *scratch)
    next(moving)
    n = cot.shape[1]
    wide, cut = 2048 // PARTS, FF // PARTS
    dots[...] = jnp.zeros_like(dots)

    def number():
        return pl.program_id(0) * PARTS + pl.program_id(1)

    def first(y, cot, hidden, row_gates, term):
        at_step(number(), (1, moving), (6, moving))
        e = pl.program_id(0)
        product = y[0].astype(f32) * cot[0].astype(f32)
        partial = product[:, :128]
        for c in range(128, wide, 128):
            partial += product[:, c : c + 128]
        dots[e] += partial
        scaled = (hidden[0].astype(f32) * row_gates[0, :, :1]).astype(bf16)
        term[0] = tn(cot[0], scaled).astype(bf16)

    part = block((1, n, wide), lambda e, j: (e, 0, j))
    whole = block((1, n, FF), lambda e, j: (e, 0, 0))
    gates = block((1, n, 128), lambda e, j: (e, 0, 0))
    pltpu.emit_pipeline(
        first,
        grid=(EXP_DEV, PARTS),
        in_specs=[part, part, whole, gates],
        out_specs=[block((1, wide, FF), lambda e, j: (e, j, 0))],
    )(y, cot, hidden, row_gates, term)

    def second(cot, w, row_gates, gate, up, dgate, dup):
        at_step(number(), (5, moving))
        dhidden = jnp.dot(cot[0], w[0], preferred_element_type=f32) * row_gates[0, :, :1]
        g, u = gate[0].astype(f32), up[0].astype(f32)
        sg = jax.nn.sigmoid(g)
        dgate[0] = (dhidden * u * sg * (1.0 + g * (1.0 - sg))).astype(bf16)
        dup[0] = (dhidden * g * sg).astype(bf16)

    out = block((1, n, cut), lambda e, j: (e, 0, j))
    pltpu.emit_pipeline(
        second,
        grid=(EXP_DEV, PARTS),
        in_specs=[
            block((1, n, 2048), lambda e, j: (e, 0, 0)),
            block((1, 2048, cut), lambda e, j: (e, 0, j)),
            gates,
            out,
            out,
        ],
        out_specs=[out, out],
    )(cot, w_out, row_gates, gate, up, dgate, dup)

    def third(dgate, dup, w, drows):
        at_step(number(), (4, moving))
        total = nt(dgate[0], w[0, :, :FF]) + nt(dup[0], w[0, :, FF:])
        drows[0] = total.astype(bf16)

    pltpu.emit_pipeline(
        third,
        grid=(EXP_DEV, PARTS),
        in_specs=[whole, whole, block((1, wide, 2 * FF), lambda e, j: (e, j, 0))],
        out_specs=[part],
    )(dgate, dup, w_in, drows)
    for _ in moving:
        pass


def expert_backward(sel, info, y, cot, gate, up, hidden, row_gates, w_in, w_out, cid):
    n = cot.shape[1]
    half = shaped((EXP_DEV, n, FF))
    return remote_call(
        backward_kernel,
        "expert_backward",
        cid,
        HOME_SENDS,
        2,
        [VMEM, VMEM] + [ANY] * 9,
        [VMEM, VMEM] + [ANY] * 4,
        (
            shaped((128, 2048), f32),
            shaped((EXP_DEV, n, 128), f32),
            half,
            half,
            shaped((EXP_DEV, n, 2048)),
            shaped((EXP_DEV, 2048, FF)),
        ),
        scratch=home_scratch(),
        vmem=58 << 20,
    )(sel, info, by_place(y), y, cot, gate, up, hidden, row_gates, w_in, w_out)


def finish_kernel(sel, info, places, rows, dgate, dup, home, term, ss, rs, ls, *scratch):
    p = Place()
    greet_plane(p)
    moving = home_steps(p, Wire(ss, rs), ls, False, sel, info, places, home, *scratch)
    next(moving)
    n = rows.shape[1]
    wide = 2048 // PARTS

    def first(rows, dgate, dup, term):
        at_step(
            pl.program_id(0) * PARTS + pl.program_id(1), (1, moving), (4, moving), (7, moving)
        )
        term[0, :, :FF] = tn(rows[0], dgate[0]).astype(bf16)
        term[0, :, FF:] = tn(rows[0], dup[0]).astype(bf16)

    whole = block((1, n, FF), lambda e, j: (e, 0, 0))
    pltpu.emit_pipeline(
        first,
        grid=(EXP_DEV, PARTS),
        in_specs=[block((1, n, wide), lambda e, j: (e, 0, j)), whole, whole],
        out_specs=[block((1, wide, 2 * FF), lambda e, j: (e, j, 0))],
    )(rows, dgate, dup, term)
    for _ in moving:
        pass


def expert_finish(sel, info, drows, rows, dgate, dup, cid):
    return remote_call(
        finish_kernel,
        "expert_finish",
        cid,
        HOME_SENDS,
        2,
        [VMEM, VMEM] + [ANY] * 4,
        [VMEM, ANY],
        (shaped((128, 2048), f32), shaped((EXP_DEV, 2048, 2 * FF))),
        scratch=home_scratch(),
        vmem=58 << 20,
    )(sel, info, by_place(drows), rows, dgate, dup)


def fold_kernel(
    p0, p1, p2, p3, small, out, whole, ss, rs, ls,
    ra, rb, rc, rd, re, rf, rg, acc_x, acc_y, sz, az, sx, ax, sy, ay, sc, ac, sh,
):
    p = Place()
    dp, yl, x = p.dp, p.yl, p.x
    greet([p.ZR, p.ZL, p.ZO, p.XR, p.XL, p.XO, p.Y, p.C, p.H])
    wire = Wire(ss, rs)
    zs_out = [
        wire.send(small.at[there], sz.at[i], device)
        for i, (there, device) in enumerate(((p.zo, p.ZO), (p.zr, p.ZR), (p.zl, p.ZL)))
    ]

    def added(dst, *srcs):
        total = srcs[0][...].astype(f32)
        for src in srcs[1:]:
            total = total + src[...].astype(f32)
        dst[...] = total.astype(dst.dtype)

    def loop(count, body):
        def step(i, carry):
            body(i)
            return carry

        lax.fori_loop(0, count, step, 0)

    firsts = []
    for i, part in ((2, p2), (3, p3)):
        firsts.append(wire.send(part.at[:, 1 - yl], rb.at[i - 2], p.Y))
    starts = []
    for i, part in ((0, p0), (1, p1)):
        starts.append(
            (
                wire.send(part.at[0:2, :, p.xo], ra.at[i, 0], p.XR),
                wire.send(part.at[2:4, :, p.xo], ra.at[i, 1], p.XL),
            )
        )
    seconds = []
    for i, part in ((0, p0), (1, p1)):
        one, two = starts[i]
        one.wait_recv()
        loop(2, lambda d: added(part.at[d, :, p.xr], part.at[d, :, p.xr], ra.at[i, 0, d]))
        s1 = wire.send(part.at[:, :, p.xr], rc.at[i, 0], p.XR)
        two.wait_recv()
        loop(2, lambda d: added(part.at[d + 2, :, p.xl], part.at[d + 2, :, p.xl], ra.at[i, 1, d]))
        s2 = wire.send(part.at[:, :, p.xl], rc.at[i, 1], p.XL)
        seconds.append((s1, s2))
    for copy in zs_out:
        copy.wait_recv()
    for half in range(2):
        az[half] = small[dp, half] + sz[0, half] + sz[1, half] + sz[2, half]
    xs_out = [
        wire.send(az.at[:, there], sx.at[i], device)
        for i, (there, device) in enumerate(((p.xo, p.XO), (p.xr, p.XR), (p.xl, p.XL)))
    ]
    mids = []
    for i, part in ((2, p2), (3, p3)):
        firsts[i - 2].wait_recv()
        loop(4, lambda d: added(acc_y.at[i - 2, d], part.at[d, yl], rb.at[i - 2, d]))
        acc = acc_y.at[i - 2]
        mids.append(
            (
                wire.send(acc.at[0:2, p.xo], rd.at[i - 2, 0], p.XR),
                wire.send(acc.at[2:4, p.xo], rd.at[i - 2, 1], p.XL),
            )
        )
    for copy in xs_out:
        copy.wait_recv()
    ax[...] = az[:, x] + sx[0] + sx[1] + sx[2]
    y_out = wire.send(ax.at[1 - yl], sy, p.Y)
    yends = []
    for i, part in ((0, p0), (1, p1)):
        for s in seconds[i]:
            s.wait_recv()
        acc = acc_x.at[i]
        loop(4, lambda d: added(acc.at[d], part.at[d, :, x], rc.at[i, 0, d], rc.at[i, 1, d]))
        yends.append(wire.send(acc.at[:, 1 - yl], re.at[i], p.Y))
    y_out.wait_recv()
    ay[...] = ax[yl] + sy[...]
    c_out = wire.send(ay, sc, p.C)
    xends = []
    for i in (2, 3):
        acc = acc_y.at[i - 2]
        one, two = mids[i - 2]
        one.wait_recv()
        loop(2, lambda d: added(acc.at[d, p.xr], acc.at[d, p.xr], rd.at[i - 2, 0, d]))
        s1 = wire.send(acc.at[:, p.xr], rf.at[i - 2, 0], p.XR)
        two.wait_recv()
        loop(2, lambda d: added(acc.at[d + 2, p.xl], acc.at[d + 2, p.xl], rd.at[i - 2, 1, d]))
        s2 = wire.send(acc.at[:, p.xl], rf.at[i - 2, 1], p.XL)
        xends.append((s1, s2))
    parts = []
    zs = []

    def z_first(i, acc):
        parts.append(acc)
        zs.append(
            (
                wire.send(acc.at[p.zo, 0:32], rg.at[i, 0, 0:32], p.ZR),
                wire.send(acc.at[p.zo, 32:64], rg.at[i, 1, 0:32], p.ZL),
            )
        )

    c_out.wait_recv()
    ac[...] = ay[...] + sc[...]
    h_out = wire.send(ac, sh, p.H)
    for i in (0, 1):
        yends[i].wait_recv()
        acc = acc_x.at[i]
        loop(4, lambda d: added(acc.at[d, yl], acc.at[d, yl], re.at[i, d]))
        z_first(i, acc.at[:, yl])
    h_out.wait_recv()
    whole[dp, yl, x] = ac[...] + sh[...]
    y_all = wire.send(whole.at[dp, yl, x], whole.at[dp, yl, x], p.Y)
    for i in (2, 3):
        for s in xends[i - 2]:
            s.wait_recv()
        acc = acc_y.at[i - 2]
        loop(
            4, lambda d: added(acc.at[d, x], acc.at[d, x], rf.at[i - 2, 0, d], rf.at[i - 2, 1, d])
        )
        z_first(i, acc.at[:, x])
    y_all.wait_recv()
    x_all = [
        wire.send(whole.at[dp, :, x], whole.at[dp, :, x], device) for device in (p.XO, p.XR, p.XL)
    ]
    ends = []
    for i in range(4):
        one, two = zs[i]
        acc = parts[i]
        one.wait_recv()
        added(acc.at[p.zr, 0:32], acc.at[p.zr, 0:32], rg.at[i, 0, 0:32])
        s1 = wire.send(acc.at[p.zr], rg.at[i, 2], p.ZR)
        two.wait_recv()
        added(acc.at[p.zl, 32:64], acc.at[p.zl, 32:64], rg.at[i, 1, 0:32])
        s2 = wire.send(acc.at[p.zl], rg.at[i, 3], p.ZL)
        ends.append((s1, s2))
    for copy in x_all:
        copy.wait_recv()
    z_all = [wire.send(whole.at[dp], whole.at[dp], device) for device in (p.ZO, p.ZR, p.ZL)]
    for i in range(4):
        for s in ends[i]:
            s.wait_recv()
        added(out.at[i], parts[i].at[dp], rg.at[i, 2], rg.at[i, 3])
    for copy in z_all:
        copy.wait_recv()
    wire.drain()


def fold_grads(grads, small):
    return remote_call(
        fold_kernel,
        "fold_grads",
        8,
        52,
        1,
        [VMEM] * 5,
        [VMEM] * 2,
        (shaped((4, 64, 512), f32), shaped((4, 2, 4, 40, 128), f32)),
        scratch=[
            pltpu.VMEM((2, 2, 2, 2, 64, 512), bf16),
            pltpu.VMEM((2, 4, 4, 64, 512), bf16),
            pltpu.VMEM((2, 2, 4, 2, 64, 512), bf16),
            pltpu.VMEM((2, 2, 2, 64, 512), bf16),
            pltpu.VMEM((2, 4, 64, 512), bf16),
            pltpu.VMEM((2, 2, 4, 64, 512), bf16),
            pltpu.VMEM((4, 4, 64, 512), bf16),
            pltpu.VMEM((2, 4, 2, 64, 512), bf16),
            pltpu.VMEM((2, 4, 4, 64, 512), bf16),
            pltpu.VMEM((3, 2, 4, 40, 128), f32),
            pltpu.VMEM((2, 4, 40, 128), f32),
            pltpu.VMEM((3, 2, 40, 128), f32),
            pltpu.VMEM((2, 40, 128), f32),
            pltpu.VMEM((40, 128), f32),
            pltpu.VMEM((40, 128), f32),
            pltpu.VMEM((40, 128), f32),
            pltpu.VMEM((40, 128), f32),
            pltpu.VMEM((40, 128), f32),
        ],
        vmem=48 << 20,
    )(*[g.reshape(4, 2, 4, 64, 512) for g in grads], small.reshape(4, 2, 4, 40, 128))


def on_device(
    tokens,
    segment_ids,
    valid_mask,
    routes,
    attn_gain,
    w_query,
    w_key,
    w_value,
    w_out,
    query_gain,
    key_gain,
    ffn_gain,
    router,
    expert_in,
    expert_out,
    cotangent,
):
    blk = lax.axis_index("blk")
    device = lax.axis_index("head") * 8 + blk
    yl = blk // 4
    tok, width = tokens.shape
    full_in = lax.all_gather(jnp.transpose(expert_in, (1, 0, 2)), "dp", axis=1, tiled=True)
    full_back = lax.all_gather(jnp.transpose(expert_out, (1, 0, 2)), "dp", axis=1, tiled=True)

    segment, valid = segment_ids[0], valid_mask[0]
    seq_len = segment.shape[0]
    place = jnp.arange(seq_len, dtype=i32)
    query_ids = (jnp.arange(4)[:, None] * 1024 + blk * 128 + jnp.arange(128)[None]).reshape(-1)
    frequency = rope_base ** (-jnp.arange(64, dtype=f32) / 64)
    angles = query_ids.astype(f32)[:, None] * frequency[None]
    cosine, sine = jnp.cos(angles)[None], jnp.sin(angles)[None]
    half_ids = (jnp.arange(4)[:, None] * 1024 + yl * 512 + jnp.arange(512)[None]).reshape(-1)
    half_seg = lax.dynamic_index_in_dim(segment.reshape(4, 2, 512), yl, 1, keepdims=False).reshape(-1)
    key_seg = jnp.where(valid > 0, segment, -1)
    ends = half_seg.reshape(-1, QB)
    lower = jnp.sum(segment[None] < ends[:, :1], axis=1, dtype=i32) // KB
    upper = (jnp.sum(segment[None] <= ends[:, -1:], axis=1, dtype=i32) + KB - 1) // KB
    limits = jnp.stack([lower, upper])

    def rotary(values, turning):
        a, b = values[..., :64], values[..., 64:]
        turned = turning * sine
        return jnp.concatenate([a * cosine - b * turned, b * cosine + a * turned], axis=-1)

    inputs = tokens.astype(f32)
    first_inv = rms_rows(inputs)
    normed = (inputs * first_inv * attn_gain).astype(bf16)
    w_three = jnp.stack([w_query, w_key, w_value])
    gathered, out_part, normed_all = gather_weights(w_three, w_out, normed)
    full_query, full_key, full_value = (gathered[i].reshape(2048, 512) for i in range(3))
    normed_all = normed_all.reshape(512, width)

    def by_head(flat):
        return jnp.transpose(flat.reshape(512, 4, HD), (1, 0, 2))

    def flat_of(heads):
        return jnp.transpose(heads.reshape(4, 512, HD), (1, 0, 2)).reshape(512, 512)

    query_proj = by_head(jnp.dot(normed_all, full_query, preferred_element_type=f32))
    key_proj = by_head(jnp.dot(normed_all, full_key, preferred_element_type=f32))
    value_heads = by_head(jnp.dot(normed_all, full_value, preferred_element_type=f32).astype(bf16))
    query_inv = rms_rows(query_proj)
    query_unit = query_proj * query_inv
    query_heads = rotary(query_unit * query_gain, 1.0).astype(bf16)
    key_inv = rms_rows(key_proj)
    key_unit = key_proj * key_inv
    key_heads = rotary(key_unit * key_gain, 1.0).astype(bf16)

    runs = (4, 4, 128, HD)
    q, k, v, full_out = heads_over_x(
        query_heads.reshape(runs), key_heads.reshape(runs), value_heads.reshape(runs), out_part
    )
    q, k, v = q.reshape(2048, HD), k.reshape(4096, HD), v.reshape(4096, HD)
    full_out = full_out.reshape(2048, 512)
    att_low, att, inverse = attend(limits, q, k, v, half_seg, half_ids, key_seg)
    attended = back_over_x(att_low.reshape(runs))
    attended_flat = flat_of(attended)
    branch_part = jnp.einsum("qc,mc->qm", attended_flat, full_out, preferred_element_type=f32)
    middle = inputs + sum_rows(branch_part.astype(bf16), 9)
    second_inv = rms_rows(middle)
    normed_ffn = (middle * second_inv * ffn_gain).astype(bf16)
    logits = jnp.dot(normed_ffn, router, preferred_element_type=f32)
    probabilities = jax.nn.softmax(logits, axis=-1)

    expert_ids = jnp.arange(EXPERTS, dtype=i32)
    hot = jnp.sum((routes[..., None] == expert_ids).astype(f32), axis=1)
    before = (jnp.arange(tok)[:, None] > jnp.arange(tok)[None]).astype(bf16)
    slots = jnp.dot(before, hot.astype(bf16), preferred_element_type=f32)
    slot_code = jnp.where(hot > 0, slots, -1.0)
    chosen = probabilities * hot
    gate_total = jnp.sum(chosen, axis=-1, keepdims=True)
    gates = chosen / gate_total

    code = jnp.transpose(slot_code.reshape(tok, 32, EXP_DEV), (0, 2, 1))
    home_hot = code[..., None] == jnp.arange(CAP, dtype=f32)
    def to_peers(rows):
        return lax.all_to_all(rows, ("head", "blk"), split_axis=1, concat_axis=1, tiled=True)

    sent = jnp.concatenate([normed_ffn, slot_code.astype(bf16), gates.astype(bf16)], axis=1)
    everyone = spread(sent, 7)
    lane = jnp.arange(128)[None]
    sel_row = jnp.arange(8)[:, None]
    info = everyone[:, :, width:]
    column = (sel_row // 2) * EXPERTS + device * EXP_DEV + sel_row % 2
    sel = ((sel_row < 4) & (lane == column)).astype(bf16)
    nearby = (device ^ 8) * EXP_DEV
    column = sel_row % 2 + jnp.where(sel_row // 2 % 2 == 0, device * EXP_DEV, nearby)
    sel_chip = (lane == column + (sel_row // 4) * EXPERTS).astype(bf16)
    expert_rows, row_gates = pick_rows(sel, info, everyone, width, True)
    expert_rows = expert_rows.reshape(EXP_DEV, -1, width)
    row_gates = row_gates.reshape(EXP_DEV, -1, 128)
    all_cot, gate_part, up_part, hidden, expert_result = expert_forward(
        cotangent, expert_rows, full_in, full_back, 11
    )
    (arrived_cot,) = pick_rows(sel, info, all_cot, width, False)
    arrived_cot = arrived_cot.reshape(EXP_DEV, -1, width)
    mixture, row_dots, grad_gate, grad_up, grad_rows, term_back = expert_backward(
        sel_chip, info, expert_result, arrived_cot, gate_part, up_part, hidden, row_gates,
        full_in, full_back, 12,
    )
    grad_home, term_in = expert_finish(
        sel_chip, info, grad_rows, expert_rows, grad_gate, grad_up, 13
    )
    back_dots = to_peers(jnp.sum(row_dots, axis=-1).reshape(EXP_DEV, 32, CAP))

    def fold_dp(term):
        return lax.psum_scatter(term.astype(bf16), "dp", scatter_dimension=1, tiled=True)

    expert_out_grad = jnp.transpose(fold_dp(term_back), (1, 0, 2)).astype(f32)
    expert_in_grad = jnp.transpose(fold_dp(term_in), (1, 0, 2)).astype(f32)

    output = (middle + mixture).astype(bf16)
    grad_out = cotangent.astype(f32)
    grad_gates = jnp.sum(jnp.where(home_hot, back_dots, 0.0), axis=-1)
    grad_gates = jnp.transpose(grad_gates, (0, 2, 1)).reshape(tok, EXPERTS)
    mean_grad = jnp.sum(grad_gates * gates, axis=-1, keepdims=True)
    grad_probs = (grad_gates - mean_grad) / gate_total * hot
    grad_logits = probabilities * (
        grad_probs - jnp.sum(probabilities * grad_probs, axis=-1, keepdims=True)
    )
    high = grad_logits.astype(bf16)
    halves = jnp.concatenate([high, (grad_logits - high.astype(f32)).astype(bf16)], axis=1)
    router_term = jnp.einsum("td,te->de", normed_ffn, halves, preferred_element_type=f32)
    router_term = router_term[:, :EXPERTS] + router_term[:, EXPERTS:]
    grad_ffn = grad_home + jnp.einsum(
        "te,de->td", halves, jnp.concatenate([router, router], axis=1), preferred_element_type=f32
    )
    ffn_gain_term = jnp.sum(grad_ffn * middle * second_inv, axis=0)
    grad_middle = grad_out + rms_back(middle, second_inv, grad_ffn * ffn_gain)
    grad_branch = grad_middle.astype(bf16)
    branch_all = gather_rows(grad_branch).reshape(512, width)
    grad_att = by_head(
        jnp.dot(branch_all, full_out, preferred_element_type=f32).astype(bf16)
    )
    grad_att = go_over_x(grad_att.reshape(runs)).reshape(2048, HD)
    delta = jnp.sum(grad_att.astype(f32) * att, axis=-1)
    dq, dk, dv = attend_back(
        limits, q, k, v, grad_att, half_seg, half_ids, key_seg, inverse[:, 0], delta
    )
    cut = (4, 2, 4, 128, HD)
    grad_query, grad_key, grad_value = grads_over_x(
        dq.reshape(runs), dk.reshape(cut), dv.reshape(cut)
    )
    heads_shape = (4, 512, HD)
    grad_query_unit = rotary(grad_query.reshape(heads_shape).astype(f32), -1.0)
    query_gain_term = jnp.sum(grad_query_unit * query_unit, axis=(0, 1))
    grad_query_flat = flat_of(
        rms_back(query_proj, query_inv, grad_query_unit * query_gain).astype(bf16)
    )
    grad_key_unit = rotary(grad_key.reshape(heads_shape).astype(f32), -1.0)
    key_gain_term = jnp.sum(grad_key_unit * key_unit, axis=(0, 1))
    grad_key_flat = flat_of(rms_back(key_proj, key_inv, grad_key_unit * key_gain).astype(bf16))
    grad_value_flat = flat_of(grad_value)
    normed_part = jnp.einsum("qc,dc->qd", grad_query_flat, full_query, preferred_element_type=f32)
    normed_part += jnp.einsum("qc,dc->qd", grad_key_flat, full_key, preferred_element_type=f32)
    normed_part += jnp.einsum("qc,dc->qd", grad_value_flat, full_value, preferred_element_type=f32)
    grad_normed = sum_rows(normed_part.astype(bf16), 10)
    attn_gain_term = jnp.sum(grad_normed * inputs * first_inv, axis=0)
    input_grad = grad_middle + rms_back(inputs, first_inv, grad_normed * attn_gain)

    def weight_grad(rows, grads):
        return jnp.einsum("qc,qf->cf", rows, grads, preferred_element_type=f32).astype(bf16)

    gains = jnp.concatenate([attn_gain_term, ffn_gain_term, query_gain_term, key_gain_term])
    gains = jnp.pad(gains, (0, 32 * 8 * 128 - gains.shape[0])).reshape(32, 8, 128)
    small = jnp.concatenate([router_term.reshape(32, 32, 128), gains], axis=1)
    attn_grads, summed = fold_grads(
        [
            weight_grad(normed_all, grad_query_flat),
            weight_grad(normed_all, grad_key_flat),
            weight_grad(normed_all, grad_value_flat),
            weight_grad(branch_all, attended_flat),
        ],
        small,
    )
    summed = summed.reshape(32, 40, 128)
    router_grad = summed[:, :32].reshape(router.shape)
    gains = summed[:, 32:].reshape(-1)
    return (
        output,
        input_grad,
        gains[:2048],
        attn_grads[0],
        attn_grads[1],
        attn_grads[2],
        attn_grads[3],
        gains[4096:4224],
        gains[4224:4352],
        gains[2048:4096],
        router_grad,
        expert_in_grad,
        expert_out_grad,
    )


def solution(mesh):
    placed = (
        P(("dp", "head", "blk"), None),
        P("dp", None),
        P("dp", None),
        P(("dp", "head", "blk"), None),
        P(),
        P(("dp", "blk"), "head"),
        P(("dp", "blk"), "head"),
        P(("dp", "blk"), "head"),
        P(("dp", "blk"), "head"),
        P(),
        P(),
        P(),
        P(),
        P("dp", ("head", "blk"), None),
        P("dp", ("head", "blk"), None),
        P(("dp", "head", "blk"), None),
    )
    return jax.shard_map(
        on_device,
        mesh=mesh,
        in_specs=placed,
        out_specs=(
            P(("dp", "head", "blk"), None),
            P(("dp", "head", "blk"), None),
            P(),
            P(("dp", "blk"), "head"),
            P(("dp", "blk"), "head"),
            P(("dp", "blk"), "head"),
            P(("dp", "blk"), "head"),
            P(),
            P(),
            P(),
            P(),
            P("dp", ("head", "blk"), None),
            P("dp", ("head", "blk"), None),
        ),
        check_vma=False,
    )
```

```python
import functools
import math

import jax
import jax.numpy as jnp
from jax import lax
from jax.experimental import pallas as pl
from jax.experimental.pallas import tpu as pltpu
from jax.sharding import PartitionSpec as P

HEADS = 16
HD = 128
FF = 1024
TOPK = 8
EXP_DEV = 2
CAP = 24
EXPERTS = 64

epsilon = 1e-06
rope_base = 50000.0
f32 = jnp.float32
bf16 = jnp.bfloat16
i32 = jnp.int32
MESH = pl.DeviceIdType.MESH
ANY = pl.BlockSpec(memory_space=pl.ANY)
VMEM = pl.BlockSpec(memory_space=pltpu.VMEM)
SMEM = pl.BlockSpec(memory_space=pltpu.SMEM)
DMA = pltpu.SemaphoreType.DMA


def rms_rows(values):
    return lax.rsqrt(jnp.mean(values * values, axis=-1, keepdims=True) + epsilon)


def rms_back(values, inverse, grad_scaled):
    inner_mean = jnp.mean(grad_scaled * values, axis=-1, keepdims=True)
    return inverse * grad_scaled - values * inverse * inverse * inverse * inner_mean


def wrap4(value):
    return lax.rem(value + 4, 4)


class Place:
    def __init__(self):
        head, blk = lax.axis_index("head"), lax.axis_index("blk")
        self.dp = lax.axis_index("dp")
        self.yh, self.co = head // 2, lax.rem(head, 2)
        self.yl, self.x = blk // 4, lax.rem(blk, 4)
        self.head = head
        self.zr, self.zl, self.zo = (wrap4(self.dp + s) for s in (1, -1, 2))
        self.xr, self.xl, self.xo = (wrap4(self.x + s) for s in (1, -1, 2))
        y = self.yh * 2 + self.yl
        self.yr, self.ylf, self.yo = (wrap4(y + s) for s in (1, -1, 2))
        self.ZR, self.ZL, self.ZO = {"dp": self.zr}, {"dp": self.zl}, {"dp": self.zo}
        self.XR, self.XL, self.XO = (self.to_x(v) for v in (self.xr, self.xl, self.xo))
        self.Y = {"blk": (1 - self.yl) * 4 + self.x}
        self.C = {"head": self.yh * 2 + (1 - self.co)}
        self.H = {"head": (1 - self.yh) * 2 + self.co}
        self.YR, self.YL = self.to_y(self.yr), self.to_y(self.ylf)

    def to_x(self, x):
        return {"blk": self.yl * 4 + x}

    def to_y(self, y):
        return {"head": (y // 2) * 2 + self.co, "blk": lax.rem(y, 2) * 4 + self.x}


def greet(devices):
    barrier = pltpu.get_barrier_semaphore()
    for device in devices:
        pl.semaphore_signal(barrier, inc=1, device_id=device, device_id_type=MESH)
    pl.semaphore_wait(barrier, len(devices))


class View:
    def __init__(self, ref, index=None):
        self.ref, self.index = ref, index

    @property
    def at(self):
        return self

    def __getitem__(self, index):
        return View(self, index)

    def get(self):
        base = self.ref.get() if isinstance(self.ref, View) else self.ref
        return base if self.index is None else base.at[self.index]

    def load(self):
        return self.get()[...]

    def store(self, value):
        ref = self.get()
        ref[...] = value.astype(ref.dtype)


def plain(ref):
    return ref.get() if isinstance(ref, View) else ref


class Sent:
    def __init__(self, make):
        self.make = make

    def wait_recv(self):
        self.make().wait_recv()

    def wait_send(self):
        self.make().wait_send()

    def wait(self):
        self.make().wait()


class Wire:
    def __init__(self, send_sem, recv_sem):
        self.send_sem, self.recv_sem, self.started = send_sem, recv_sem, []

    def send(self, src, dst, device):
        at = len(self.started)

        def make():
            return pltpu.make_async_remote_copy(
                src_ref=plain(src),
                dst_ref=plain(dst),
                send_sem=self.send_sem.at[at],
                recv_sem=self.recv_sem.at[at],
                device_id=device,
                device_id_type=MESH,
            )

        make().start()
        self.started.append(Sent(make))
        return self.started[-1]

    def drain(self):
        for copy in self.started:
            copy.wait_send()


def local(src, dst, sems, at):
    def make():
        return pltpu.make_async_copy(plain(src), plain(dst), sems.at[at])

    make().start()
    return Sent(make)


def remote_call(body, name, cid, sends, locals_, ins, outs, out_shape, scratch=(), vmem=None):
    return pl.pallas_call(
        body,
        name=name,
        out_shape=out_shape,
        in_specs=ins,
        out_specs=outs,
        scratch_shapes=[DMA((sends,)), DMA((sends,)), DMA((max(locals_, 1),)), *scratch],
        compiler_params=pltpu.CompilerParams(
            collective_id=cid, has_side_effects=True, vmem_limit_bytes=vmem
        ),
    )


def shaped(shape, dtype=bf16):
    return jax.ShapeDtypeStruct(shape, dtype)


def weights_kernel(w, wo, n, g, go, m, ss, rs, ls):
    p = Place()
    dp, yl, x = p.dp, p.yl, p.x
    own = [
        local(w, g.at[:, dp, yl, x], ls, 0),
        local(n, m.at[p.head], ls, 1),
        local(wo, go.at[dp], ls, 2),
    ]
    greet([p.ZR, p.ZL, p.XR, p.XL, p.Y, p.C, p.H])
    wire = Wire(ss, rs)
    n_c = wire.send(n, m.at[p.head], p.C)
    z1 = wire.send(w, g.at[:, dp, yl, x], p.ZR)
    z2 = wire.send(w, g.at[:, dp, yl, x], p.ZL)
    n_h = wire.send(n, m.at[p.head], p.H)
    o1 = wire.send(wo, go.at[dp], p.ZR)
    o2 = wire.send(wo, go.at[dp], p.ZL)
    z1.wait_recv()
    z3 = wire.send(g.at[0:2, p.zl, yl, x], g.at[0:2, p.zl, yl, x], p.ZR)
    z2.wait_recv()
    z4 = wire.send(g.at[2, p.zr, yl, x], g.at[2, p.zr, yl, x], p.ZL)
    own[0].wait()
    z3.wait_recv()
    z4.wait_recv()
    b1 = wire.send(g.at[2, :, yl, x], g.at[2, :, yl, x], p.XR)
    b2 = wire.send(g.at[2, :, yl, x], g.at[2, :, yl, x], p.XL)
    a1 = wire.send(g.at[0:2, :, yl, x], g.at[0:2, :, yl, x], p.Y)
    c1 = wire.send(g.at[2, :, yl, x], g.at[2, :, yl, x], p.Y)
    o1.wait_recv()
    o3 = wire.send(go.at[p.zl, 0:32], go.at[p.zl, 0:32], p.ZR)
    o2.wait_recv()
    o4 = wire.send(go.at[p.zr, 32:64], go.at[p.zr, 32:64], p.ZL)
    n_h.wait_recv()
    other = (1 - p.yh) * 2 + p.co
    n_f = wire.send(m.at[other], m.at[other], p.C)
    b1.wait_recv()
    b3 = wire.send(g.at[2, 0:2, yl, p.xl], g.at[2, 0:2, yl, p.xl], p.XR)
    c2 = wire.send(g.at[2, :, yl, p.xl], g.at[2, :, yl, p.xl], p.Y)
    b2.wait_recv()
    b4 = wire.send(g.at[2, 2:4, yl, p.xr], g.at[2, 2:4, yl, p.xr], p.XL)
    c3 = wire.send(g.at[2, :, yl, p.xr], g.at[2, :, yl, p.xr], p.Y)
    a1.wait_recv()
    a2 = wire.send(g.at[0:2, :, :, x], g.at[0:2, :, :, x], p.XR)
    a3 = wire.send(g.at[0:2, :, :, x], g.at[0:2, :, :, x], p.XL)
    b3.wait_recv()
    b4.wait_recv()
    c4 = wire.send(g.at[2, :, yl, p.xo], g.at[2, :, yl, p.xo], p.Y)
    a2.wait_recv()
    a4 = wire.send(g.at[0, :, :, p.xl], g.at[0, :, :, p.xl], p.XR)
    a3.wait_recv()
    a5 = wire.send(g.at[1, :, :, p.xr], g.at[1, :, :, p.xr], p.XL)
    for copy in (n_c, n_f, o3, o4, c1, c2, c3, c4, a4, a5):
        copy.wait_recv()
    own[1].wait()
    own[2].wait()
    wire.drain()


def gather_weights(w, wo, n):
    return remote_call(
        weights_kernel,
        "gather_weights",
        1,
        24,
        3,
        [ANY] * 3,
        [ANY] * 3,
        (shaped((3, 4, 2, 4, 64, 512)), shaped((4, 64, 512)), shaped((4, 128, 2048))),
    )(w, wo, n)


def rows_kernel(n, m, ss, rs, ls):
    p = Place()
    own = local(n, m.at[p.head], ls, 0)
    greet([p.C, p.H])
    wire = Wire(ss, rs)
    n_h = wire.send(n, m.at[p.head], p.H)
    n_c = wire.send(n, m.at[p.head], p.C)
    n_h.wait_recv()
    other = (1 - p.yh) * 2 + p.co
    n_f = wire.send(m.at[other], m.at[other], p.C)
    n_c.wait_recv()
    n_f.wait_recv()
    own.wait()
    wire.drain()


def gather_rows(n):
    return remote_call(
        rows_kernel, "gather_rows", 2, 3, 1, [ANY], [ANY], (shaped((4, 128, 2048)),)
    )(n)[0]


def sum_kernel(part, out, ss, rs, ls, got_c, got_h, half):
    p = Place()
    greet([p.C, p.H])
    wire = Wire(ss, rs)
    far = wire.send(part.at[1 - p.yh, 1 - p.co], got_c.at[0], p.C)
    near = wire.send(part.at[p.yh, 1 - p.co], got_c.at[1], p.C)
    far.wait_recv()

    def add_far(i, carry):
        rows = pl.ds(pl.multiple_of(i * 16, 16), 16)
        half[rows] = (
            part[1 - p.yh, p.co, rows].astype(f32) + got_c[0, rows].astype(f32)
        ).astype(bf16)
        return carry

    lax.fori_loop(0, 8, add_far, 0)
    over = wire.send(half, got_h, p.H)
    near.wait_recv()
    over.wait_recv()

    def add_near(i, carry):
        rows = pl.ds(pl.multiple_of(i * 16, 16), 16)
        out[rows] = (
            part[p.yh, p.co, rows].astype(f32)
            + got_c[1, rows].astype(f32)
            + got_h[rows].astype(f32)
        )
        return carry

    lax.fori_loop(0, 8, add_near, 0)
    wire.drain()


def sum_rows(part, cid):
    return remote_call(
        sum_kernel,
        "sum_rows",
        cid,
        3,
        1,
        [VMEM],
        [VMEM],
        (shaped((128, 2048), f32),),
        scratch=[
            pltpu.VMEM((2, 128, 2048), bf16),
            pltpu.VMEM((128, 2048), bf16),
            pltpu.VMEM((128, 2048), bf16),
        ],
        vmem=16 << 20,
    )(part.reshape(2, 2, 128, 2048))[0]


def heads_kernel(three, go, qd, kd, vd, gd, ss, rs, ls):
    p = Place()
    q, k, v = (three.at[i] for i in range(3))
    yl, x = p.yl, p.x
    own = [
        local(q.at[x], qd.at[:, x], ls, 0),
        local(k.at[x], kd.at[:, yl, x], ls, 1),
        local(v.at[x], vd.at[:, yl, x], ls, 2),
        local(go, gd.at[:, yl, x], ls, 3),
    ]
    greet([p.Y, p.XR, p.XL, p.XO])
    wire = Wire(ss, rs)
    done = [
        wire.send(k.at[x], kd.at[:, yl, x], p.Y),
        wire.send(v.at[x], vd.at[:, yl, x], p.Y),
    ]
    w1 = wire.send(go, gd.at[:, yl, x], p.Y)
    moved = []
    for there, came, device in ((p.xo, p.xo, p.XO), (p.xr, p.xl, p.XR), (p.xl, p.xr, p.XL)):
        ks = wire.send(k.at[there], kd.at[:, yl, x], device)
        vs = wire.send(v.at[there], vd.at[:, yl, x], device)
        moved.append((came, ks, vs))
    for there, device in ((p.xo, p.XO), (p.xr, p.XR), (p.xl, p.XL)):
        done.append(wire.send(q.at[there], qd.at[:, x], device))
    for came, ks, vs in moved[1:] + moved[:1]:
        ks.wait_recv()
        done.append(wire.send(kd.at[:, yl, came], kd.at[:, yl, came], p.Y))
        vs.wait_recv()
        done.append(wire.send(vd.at[:, yl, came], vd.at[:, yl, came], p.Y))
    own[3].wait()
    w1.wait_recv()
    w2 = wire.send(gd.at[:, :, x], gd.at[:, :, x], p.XR)
    w3 = wire.send(gd.at[:, :, x], gd.at[:, :, x], p.XL)
    w2.wait_recv()
    done.append(wire.send(gd.at[0:2, :, p.xl], gd.at[0:2, :, p.xl], p.XR))
    w3.wait_recv()
    done.append(wire.send(gd.at[2:4, :, p.xr], gd.at[2:4, :, p.xr], p.XL))
    for copy in done:
        copy.wait_recv()
    for copy in own[:3]:
        copy.wait()
    wire.drain()


def heads_over_x(three, go):
    return remote_call(
        heads_kernel,
        "heads_over_x",
        3,
        22,
        4,
        [ANY] * 2,
        [ANY] * 4,
        (
            shaped((4, 4, 128, 128)),
            shaped((4, 2, 4, 128, 128)),
            shaped((4, 2, 4, 128, 128)),
            shaped((4, 2, 4, 64, 512)),
        ),
    )(three, go)


def back_x_kernel(o, att, ss, rs, ls):
    p = Place()
    own = local(o.at[:, p.x], att.at[p.x], ls, 0)
    greet([p.XR, p.XL, p.XO])
    wire = Wire(ss, rs)
    for there, device in ((p.xo, p.XO), (p.xr, p.XR), (p.xl, p.XL)):
        wire.send(o.at[:, there], att.at[p.x], device)
    for copy in wire.started:
        copy.wait_recv()
    own.wait()
    wire.drain()


def back_over_x(o):
    return remote_call(
        back_x_kernel, "back_over_x", 4, 3, 1, [ANY], [ANY], (shaped((4, 4, 128, 128)),)
    )(o)[0]


def go_x_kernel(o, d, ss, rs, ls):
    p = Place()
    own = local(o.at[p.x], d.at[:, p.x], ls, 0)
    greet([p.XR, p.XL, p.XO])
    wire = Wire(ss, rs)
    for there, device in ((p.xo, p.XO), (p.xr, p.XR), (p.xl, p.XL)):
        wire.send(o.at[there], d.at[:, p.x], device)
    for copy in wire.started:
        copy.wait_recv()
    own.wait()
    wire.drain()


def go_over_x(o):
    return remote_call(
        go_x_kernel, "go_over_x", 5, 3, 1, [ANY], [ANY], (shaped((4, 4, 128, 128)),)
    )(o)[0]


def grads_x_kernel(dq, dk, dv, three, ss, rs, ls, gk, gv, sk, sv):
    p = Place()
    x, yl = p.x, p.yl
    qd, kd, vd = (three.at[i] for i in range(3))
    own = local(dq.at[:, x], qd.at[x], ls, 0)
    greet([p.Y, p.XR, p.XL, p.XO])
    wire = Wire(ss, rs)
    order = ((p.xo, p.XO), (p.xr, p.XR), (p.xl, p.XL), (x, None))
    pairs = []
    for i, (there, device) in enumerate(order):
        pairs.append(
            (
                wire.send(dk.at[:, 1 - yl, there], gk.at[i], p.Y),
                wire.send(dv.at[:, 1 - yl, there], gv.at[i], p.Y),
            )
        )
    last = []
    for there, device in order[:3]:
        last.append(wire.send(dq.at[:, there], qd.at[x], device))
    for i, (there, device) in enumerate(order):
        for grads, got, summed, out, arrived in (
            (dk, gk, sk, kd, pairs[i][0]),
            (dv, gv, sv, vd, pairs[i][1]),
        ):
            arrived.wait_recv()
            for run in range(4):
                total = grads[run, yl, there].astype(f32) + got[i, run].astype(f32)
                if device is None:
                    out[x, run] = total.astype(bf16)
                else:
                    summed[i, run] = total.astype(bf16)
            if device is not None:
                last.append(wire.send(summed.at[i], out.at[x], device))
    for copy in last:
        copy.wait_recv()
    own.wait()
    wire.drain()


def grads_over_x(dq, dk, dv):
    return remote_call(
        grads_x_kernel,
        "grads_over_x",
        6,
        17,
        1,
        [ANY, VMEM, VMEM],
        [VMEM],
        (shaped((3, 4, 4, 128, 128)),),
        scratch=[
            pltpu.VMEM((4, 4, 128, 128), bf16),
            pltpu.VMEM((4, 4, 128, 128), bf16),
            pltpu.VMEM((3, 4, 128, 128), bf16),
            pltpu.VMEM((3, 4, 128, 128), bf16),
        ],
        vmem=16 << 20,
    )(dq, dk, dv)[0]


def turned(values, cosine, sine):
    return values * cosine + pltpu.roll(values, 64, 1) * sine


def project_kernel(rows, w, cosine, sine, gain, heads, kept):
    flat = jnp.dot(rows[...], w[0], preferred_element_type=f32)
    step = pl.program_id(0)
    for h in range(4):
        head = flat[:, h * HD : (h + 1) * HD]

        @pl.when(step < 2)
        def _():
            kept[0, h] = head
            scaled = head * rms_rows(head) * gain[0]
            heads[0, h] = turned(scaled, cosine[...], sine[...]).astype(bf16)

        @pl.when(step == 2)
        def _():
            heads[0, h] = head.astype(bf16)


def project(rows, w, cosine, sine, gains):
    def fixed(*shape):
        return pl.BlockSpec(shape, lambda i: (0,) * len(shape))

    def two(i):
        return jnp.minimum(i, 1)

    return pl.pallas_call(
        project_kernel,
        name="project",
        grid=(3,),
        out_shape=(shaped((3, 4, 512, HD)), shaped((2, 4, 512, HD), f32)),
        in_specs=[
            fixed(512, 2048),
            pl.BlockSpec((1, 2048, 512), lambda i: (i, 0, 0)),
            fixed(512, HD),
            fixed(512, HD),
            pl.BlockSpec((1, 1, HD), lambda i: (two(i), 0, 0)),
        ],
        out_specs=[
            pl.BlockSpec((1, 4, 512, HD), lambda i: (i, 0, 0, 0)),
            pl.BlockSpec((1, 4, 512, HD), lambda i: (two(i), 0, 0, 0)),
        ],
        compiler_params=pltpu.CompilerParams(vmem_limit_bytes=60 << 20),
    )(rows, w, cosine, sine, gains)


QB = 256
KB = 512
SCALE = HD**-0.5
SCALE2 = SCALE * math.log2(math.e)


def attend_kernel(lim, q, k, v, qseg, qpos, kseg, o_low, o, linv, vext):
    rows = k.shape[0]
    ones = (lax.broadcasted_iota(i32, (KB, HD), 1) == 0).astype(bf16)

    def fill(i, carry):
        at = pl.ds(pl.multiple_of(i * KB, KB), KB)
        vext[at, :HD] = v[at]
        vext[at, HD:] = ones
        return carry

    lax.fori_loop(0, rows // KB, fill, 0)

    def one_query(b, carry):
        at = pl.ds(pl.multiple_of(b * QB, QB), QB)
        query, seg, pos = q[at], qseg[at], qpos[at]

        def one_key(j, acc):
            keys = pl.ds(pl.multiple_of(j * KB, KB), KB)
            score = lax.dot_general(
                query, k[keys], (((1,), (1,)), ((), ())), preferred_element_type=f32
            )
            key_pos = j * KB + lax.broadcasted_iota(i32, (1, KB), 1)
            allowed = (seg == kseg[:, keys]) | (pos == key_pos)
            weight = jnp.where(allowed, jnp.exp2(score * SCALE2), 0.0).astype(bf16)
            return acc + jnp.dot(weight, vext[keys], preferred_element_type=f32)

        acc = lax.fori_loop(lim[0, b], lim[1, b], one_key, jnp.zeros((QB, 2 * HD), f32))
        inverse = 1.0 / acc[:, HD : HD + 1]
        result = acc[:, :HD] * inverse
        o[at] = result
        o_low[at] = result.astype(bf16)
        linv[at] = jnp.broadcast_to(inverse, (QB, HD))
        return carry

    lax.fori_loop(0, q.shape[0] // QB, one_query, 0)


def attend(lim, q, k, v, qseg, qpos, kseg):
    n = q.shape[0]
    return pl.pallas_call(
        attend_kernel,
        name="attend",
        out_shape=(shaped((n, HD)), shaped((n, HD), f32), shaped((n, HD), f32)),
        in_specs=[SMEM] + [VMEM] * 6,
        out_specs=[VMEM] * 3,
        scratch_shapes=[pltpu.VMEM((k.shape[0], 2 * HD), bf16)],
        compiler_params=pltpu.CompilerParams(vmem_limit_bytes=32 << 20),
    )(lim, q, k, v, qseg[:, None], qpos[:, None], kseg[None])


def attend_back_kernel(
    lim, q, k, v, g, qseg, qpos, kseg, linv, delta, dq, dk, dv, kt, dk_acc, dv_acc
):
    rows = k.shape[0]

    def fill(i, carry):
        at = pl.ds(pl.multiple_of(i * KB, KB), KB)
        kt[:, at] = k[at].astype(f32).T.astype(bf16)
        dk_acc[at] = jnp.zeros((KB, HD), f32)
        dv_acc[at] = jnp.zeros((KB, HD), f32)
        return carry

    lax.fori_loop(0, rows // KB, fill, 0)
    across = (((1,), (1,)), ((), ()))

    def one_query(b, carry):
        at = pl.ds(pl.multiple_of(b * QB, QB), QB)
        query, grad = q[at], g[at]
        seg, pos, inverse, shift = qseg[:, at], qpos[:, at], linv[:, at], delta[:, at]

        def one_key(j, acc):
            keys = pl.ds(pl.multiple_of(j * KB, KB), KB)
            key = k[keys]
            score = lax.dot_general(key, query, across, preferred_element_type=f32)
            key_pos = j * KB + lax.broadcasted_iota(i32, (KB, 1), 0)
            allowed = (kseg[keys] == seg) | (key_pos == pos)
            prob = jnp.where(allowed, jnp.exp2(score * SCALE2), 0.0) * inverse
            grad_prob = lax.dot_general(v[keys], grad, across, preferred_element_type=f32)
            grad_score = (prob * (grad_prob - shift)).astype(bf16)
            dv_acc[keys] += jnp.dot(prob.astype(bf16), grad, preferred_element_type=f32)
            dk_acc[keys] += jnp.dot(grad_score, query, preferred_element_type=f32)
            return acc + jnp.dot(kt[:, keys], grad_score, preferred_element_type=f32)

        acc = lax.fori_loop(lim[0, b], lim[1, b], one_key, jnp.zeros((HD, QB), f32))
        dq[at] = (acc * SCALE).T.astype(bf16)
        return carry

    lax.fori_loop(0, q.shape[0] // QB, one_query, 0)

    def finish(i, carry):
        at = pl.ds(pl.multiple_of(i * KB, KB), KB)
        dk[at] = (dk_acc[at] * SCALE).astype(bf16)
        dv[at] = dv_acc[at].astype(bf16)
        return carry

    lax.fori_loop(0, rows // KB, finish, 0)


def attend_back(lim, q, k, v, g, qseg, qpos, kseg, linv, delta):
    n, rows = q.shape[0], k.shape[0]
    return pl.pallas_call(
        attend_back_kernel,
        name="attend_back",
        out_shape=(shaped((n, HD)), shaped((rows, HD)), shaped((rows, HD))),
        in_specs=[SMEM] + [VMEM] * 9,
        out_specs=[VMEM] * 3,
        scratch_shapes=[
            pltpu.VMEM((HD, rows), bf16),
            pltpu.VMEM((rows, HD), f32),
            pltpu.VMEM((rows, HD), f32),
        ],
        compiler_params=pltpu.CompilerParams(vmem_limit_bytes=40 << 20),
    )(lim, q, k, v, g, qseg[None], qpos[None], kseg[:, None], linv[None], delta[None])


SPREAD_SENDS = 26


def spread_steps(p, wire, sems, src, dst):
    yh, co, yl, x = p.yh, p.co, p.yl, p.x
    (rh, rl), (lh, ll), (oh, ol) = ((y // 2, lax.rem(y, 2)) for y in (p.yr, p.ylf, p.yo))
    A, A1, A2 = pl.ds(0, 64), pl.ds(0, 32), pl.ds(32, 32)
    B, B1, B2 = pl.ds(64, 64), pl.ds(64, 32), pl.ds(96, 32)
    src, dst = View(src), View(dst)
    own = local(src, dst.at[yh, co, yl, x], sems, 0)

    def both(ref, device):
        return wire.send(ref, ref, device)

    me = dst.at[yh, co, yl]
    a1 = wire.send(src.at[A], me.at[x, A], p.XR)
    b1 = wire.send(src.at[B], me.at[x, B], p.YR)
    a2 = wire.send(src.at[A], me.at[x, A], p.XL)
    b2 = wire.send(src.at[B], me.at[x, B], p.YL)
    yield
    a1.wait_recv()
    a3 = both(me.at[p.xl, A1], p.XR)
    a2.wait_recv()
    a4 = both(me.at[p.xr, A2], p.XL)
    b1.wait_recv()
    b3 = both(dst.at[lh, co, ll, x, B1], p.YR)
    b2.wait_recv()
    b4 = both(dst.at[rh, co, rl, x, B2], p.YL)
    yield
    own.wait()
    a3.wait_recv()
    a4.wait_recv()
    a5 = both(me.at[:, A], p.YR)
    a6 = both(me.at[:, A], p.YL)
    b3.wait_recv()
    b4.wait_recv()
    b5 = both(dst.at[:, co, :, x, B], p.XR)
    b6 = both(dst.at[:, co, :, x, B], p.XL)
    last = [both(me.at[:, A], p.C), both(dst.at[:, co, :, x, B], p.C)]
    yield
    a5.wait_recv()
    a7 = both(dst.at[lh, co, ll, :, A1], p.YR)
    b5.wait_recv()
    b7 = both(dst.at[:, co, :, p.xl, B1], p.XR)
    a6.wait_recv()
    a8 = both(dst.at[rh, co, rl, :, A2], p.YL)
    b6.wait_recv()
    b8 = both(dst.at[:, co, :, p.xr, B2], p.XL)
    last += [both(dst.at[lh, co, ll, :, A], p.C), both(dst.at[:, co, :, p.xl, B], p.C)]
    last += [both(dst.at[rh, co, rl, :, A], p.C), both(dst.at[:, co, :, p.xr, B], p.C)]
    yield
    a7.wait_recv()
    last.append(both(dst.at[oh, co, ol, :, A1], p.C))
    b7.wait_recv()
    last.append(both(dst.at[:, co, :, p.xo, B1], p.C))
    a8.wait_recv()
    last.append(both(dst.at[oh, co, ol, :, A2], p.C))
    b8.wait_recv()
    last.append(both(dst.at[:, co, :, p.xo, B2], p.C))
    yield
    for copy in last:
        copy.wait_recv()
    wire.drain()
    yield


def greet_plane(p):
    greet([p.XR, p.XL, p.YR, p.YL, p.C])


def spread_kernel(src, dst, ss, rs, ls):
    p = Place()
    greet_plane(p)
    for _ in spread_steps(p, Wire(ss, rs), ls, src, dst):
        pass


def spread(src, cid):
    width = src.shape[1]
    return remote_call(
        spread_kernel,
        "spread",
        cid,
        SPREAD_SENDS,
        1,
        [ANY],
        [ANY],
        (shaped((2, 2, 2, 4, 128, width)),),
    )(src)[0].reshape(32, 128, width)


def at_step(number, *stages):
    for step, stage in stages:

        @pl.when(number == step)
        def _():
            next(stage)


def block(shape, index):
    return pl.BlockSpec(shape, index)


def nt(a, b):
    return lax.dot_general(a, b, (((1,), (1,)), ((), ())), preferred_element_type=f32)


def tn(a, b):
    return lax.dot_general(a, b, (((0,), (0,)), ((), ())), preferred_element_type=f32)


PARTS = 4


def forward_kernel(src, rows, w_in, w_out, dst, gate, up, hidden, y, ss, rs, ls):
    p = Place()
    greet_plane(p)
    moving = spread_steps(p, Wire(ss, rs), ls, src, dst)
    next(moving)
    n = rows.shape[1]
    cut = FF // PARTS

    def first(rows, w_gate, w_up, gate, up, hidden):
        at_step(pl.program_id(0) * PARTS + pl.program_id(1), (2, moving), (4, moving))
        g = jnp.dot(rows[0], w_gate[0], preferred_element_type=f32)
        u = jnp.dot(rows[0], w_up[0], preferred_element_type=f32)
        gate[0] = g.astype(bf16)
        up[0] = u.astype(bf16)
        hidden[0] = (g * jax.nn.sigmoid(g) * u).astype(bf16)

    out = block((1, n, cut), lambda e, j: (e, 0, j))
    pltpu.emit_pipeline(
        first,
        grid=(EXP_DEV, PARTS),
        in_specs=[
            block((1, n, 2048), lambda e, j: (e, 0, 0)),
            block((1, 2048, cut), lambda e, j: (e, 0, j)),
            block((1, 2048, cut), lambda e, j: (e, 0, j + PARTS)),
        ],
        out_specs=[out, out, out],
    )(rows, w_in, w_in, gate, up, hidden)

    def second(hidden, w, y):
        at_step(pl.program_id(0) * PARTS + pl.program_id(1), (3, moving))
        y[0] = nt(hidden[0], w[0]).astype(bf16)

    pltpu.emit_pipeline(
        second,
        grid=(EXP_DEV, PARTS),
        in_specs=[
            block((1, n, FF), lambda e, j: (e, 0, 0)),
            block((1, 2048 // PARTS, FF), lambda e, j: (e, j, 0)),
        ],
        out_specs=[block((1, n, 2048 // PARTS), lambda e, j: (e, 0, j))],
    )(hidden, w_out, y)
    for _ in moving:
        pass


def expert_forward(src, rows, w_in, w_out, cid):
    n, width = rows.shape[1:]
    outs = remote_call(
        forward_kernel,
        "expert_forward",
        cid,
        SPREAD_SENDS,
        1,
        [ANY] * 4,
        [ANY] * 5,
        (shaped((2, 2, 2, 4, 128, width)),)
        + (shaped((EXP_DEV, n, FF)),) * 3
        + (shaped((EXP_DEV, n, width)),),
        vmem=48 << 20,
    )(src, rows, w_in, w_out)
    return outs[0].reshape(32, 128, width), *outs[1:]


def slot_hits(table, count, rows_down):
    shape = (count * 2 * CAP, 256) if rows_down else (256, count * 2 * CAP)
    line = lax.broadcasted_iota(i32, shape, 0 if rows_down else 1)
    block = lax.broadcasted_iota(i32, shape, 1 if rows_down else 0) // 128
    expert = line // (2 * CAP)
    want = line - expert * (2 * CAP) - block * CAP

    def spread_out(first):
        value = jnp.zeros(shape, f32)
        for e in range(count):
            c = first + e
            at = table[c : c + 1] if rows_down else table[:, c : c + 1]
            value = jnp.where(expert == e, at, value)
        return value

    hit = (spread_out(0).astype(i32) == want) & (want >= 0) & (want < CAP)
    return hit, spread_out(count)


def pick_kernel(gated, sel, info, src, rows_out, *gates_out):
    for pair in range(src.shape[0] // 256):
        at = slice(pair * 256, (pair + 1) * 256)
        hit, gate = slot_hits(nt(sel[...], info[at]), EXP_DEV, True)
        rows = jnp.dot(hit.astype(bf16), src[at], preferred_element_type=f32).astype(bf16)
        for e in range(EXP_DEV):
            rows_out[e, pair] = rows[e * 2 * CAP : (e + 1) * 2 * CAP]
        if gated:
            total = jnp.sum(jnp.where(hit, gate, 0.0), axis=1, keepdims=True)
            total = jnp.broadcast_to(total, (EXP_DEV * 2 * CAP, 128))
            for e in range(EXP_DEV):
                gates_out[0][e, pair] = total[e * 2 * CAP : (e + 1) * 2 * CAP]


def pick_rows(sel, info, src, width, gated):
    pairs, step = src.shape[0] // 256, 2

    def spec(lanes):
        return pl.BlockSpec((EXP_DEV, step, 2 * CAP, lanes), lambda i: (0, i, 0, 0))

    shapes = [shaped((EXP_DEV, pairs, 2 * CAP, width)), shaped((EXP_DEV, pairs, 2 * CAP, 128), f32)]
    specs = [spec(width), spec(128)]
    return pl.pallas_call(
        functools.partial(pick_kernel, gated),
        name="pick_rows",
        grid=(pairs // step,),
        out_shape=shapes[: 1 + gated],
        in_specs=[
            pl.BlockSpec((8, 128), lambda i: (0, 0)),
            pl.BlockSpec((256 * step, 128), lambda i: (i, 0)),
            pl.BlockSpec((256 * step, width), lambda i: (i, 0)),
        ],
        out_specs=specs[: 1 + gated],
        compiler_params=pltpu.CompilerParams(vmem_limit_bytes=60 << 20),
    )(sel, info, src)


HOME_SENDS = 20


def home_scratch(width):
    return [
        pltpu.VMEM((2, 4, 8 * CAP, width), bf16),
        pltpu.VMEM((2, 2, 4, 128, width), bf16),
        pltpu.VMEM((2, 2, 64, width), bf16),
        pltpu.VMEM((2, 2, 64, width), bf16),
        pltpu.VMEM((2, 4, 64, width), bf16),
        pltpu.VMEM((2, 2, 2, 64, width), bf16),
        pltpu.VMEM((2, 2, 32, width), bf16),
        pltpu.VMEM((2, 2, 64, width), bf16),
    ]


def home_steps(p, wire, sems, gated, sel, info, rows, more, out, cat, q, a1, b1, a2, b2, c1, c2):
    yh, co, yl, x = p.yh, p.co, p.yl, p.x
    ys = [(yy // 2, lax.rem(yy, 2)) for yy in (p.yr, p.ylf, p.yo)]
    (rh, rl), (lh, ll), (oh, ol) = ys
    pieces = [(View(rows), slice(0, 2048))]
    if more is not None:
        pieces.append((View(more), slice(2048, 2048 + 128)))
    rows, out, whole_q, whole_cat = View(rows), View(out), q, cat
    width = cat.shape[-1]
    q, cat, a1, b1, a2, b2, c1, c2 = (View(ref) for ref in (q, cat, a1, b1, a2, b2, c1, c2))
    own, first = [], []
    for e in range(EXP_DEV):
        lines = pl.ds(e * 2 * CAP, 2 * CAP)
        there = pl.ds((2 + e) * 2 * CAP, 2 * CAP)
        for piece, lanes in pieces:
            first.append(wire.send(piece.at[e, :, 1 - co], cat.at[:, :, there, lanes], p.C))
            own.append(local(piece.at[e, :, co], cat.at[:, :, lines, lanes], sems, len(own)))
    yield
    for copy in own:
        copy.wait()
    for copy in first:
        copy.wait_recv()

    def place(i, carry):
        h, pair = i // 4, lax.rem(i, 4)
        block = h * 16 + co * 8 + pair * 2
        both = jnp.concatenate([info[block], info[block + 1]], axis=0)
        table = lax.dot_general(
            both, sel[...], (((1,), (1,)), ((), ())), preferred_element_type=f32
        )
        hit, gate = slot_hits(table, 4, False)
        value = jnp.where(hit, gate if gated else 1.0, 0.0).astype(bf16)
        for c in range(0, width, 512):
            lanes = slice(c, min(c + 512, width))
            total = jnp.dot(
                value, whole_cat[h, pair, :, lanes], preferred_element_type=f32
            ).astype(bf16)
            at = lax.rem(pair, 2) * 2
            whole_q[h, pair // 2, at, :, lanes] = total[:128]
            whole_q[h, pair // 2, at + 1, :, lanes] = total[128:]
        return carry

    lax.fori_loop(0, 8, place, 0)
    A, B = pl.ds(0, 64), pl.ds(64, 64)
    s1 = [
        wire.send(q.at[oh, ol, 0:2, A], a1.at[0], p.YR),
        wire.send(q.at[0, :, p.xo, B], b1.at[0], p.XR),
        wire.send(q.at[oh, ol, 2:4, A], a1.at[1], p.YL),
        wire.send(q.at[1, :, p.xo, B], b1.at[1], p.XL),
    ]
    yield

    def add(dst, *srcs):
        total = srcs[0].load().astype(f32)
        for src in srcs[1:]:
            total = total + src.load().astype(f32)
        dst.store(total)

    def loop(count, body):
        def step(i, carry):
            body(i)
            return carry

        lax.fori_loop(0, count, step, 0)

    def plus(dst, src):
        add(dst, dst, src)

    s2 = []
    s1[0].wait_recv()
    loop(2, lambda i: plus(q.at[rh, rl, i, A], a1.at[0, i]))
    s2.append(wire.send(q.at[rh, rl, :, A], a2.at[0], p.YR))
    s1[1].wait_recv()
    loop(2, lambda i: plus(q.at[0, i, p.xr, B], b1.at[0, i]))
    s2.append(wire.send(q.at[:, :, p.xr, B], b2.at[0], p.XR))
    s1[2].wait_recv()
    loop(2, lambda i: plus(q.at[lh, ll, 2 + i, A], a1.at[1, i]))
    s2.append(wire.send(q.at[lh, ll, :, A], a2.at[1], p.YL))
    s1[3].wait_recv()
    loop(2, lambda i: plus(q.at[1, i, p.xl, B], b1.at[1, i]))
    s2.append(wire.send(q.at[:, :, p.xl, B], b2.at[1], p.XL))
    yield
    for copy in s2:
        copy.wait_recv()
    loop(4, lambda i: add(q.at[yh, yl, i, A], q.at[yh, yl, i, A], a2.at[0, i], a2.at[1, i]))
    s3 = [
        wire.send(q.at[yh, yl, p.xo, 0:32], c1.at[0, 0], p.XR),
        wire.send(q.at[yh, yl, p.xo, 32:64], c1.at[0, 1], p.XL),
    ]
    for h in range(2):
        loop(2, lambda i: add(q.at[h, i, x, B], q.at[h, i, x, B], b2.at[0, h, i], b2.at[1, h, i]))
    s3 += [
        wire.send(q.at[oh, ol, x, 64:96], c1.at[1, 0], p.YR),
        wire.send(q.at[oh, ol, x, 96:128], c1.at[1, 1], p.YL),
    ]
    yield
    s4 = []
    s3[0].wait_recv()
    plus(q.at[yh, yl, p.xr, 0:32], c1.at[0, 0])
    s4.append(wire.send(q.at[yh, yl, p.xr, A], c2.at[0, 0], p.XR))
    s3[1].wait_recv()
    plus(q.at[yh, yl, p.xl, 32:64], c1.at[0, 1])
    s4.append(wire.send(q.at[yh, yl, p.xl, A], c2.at[0, 1], p.XL))
    s3[2].wait_recv()
    plus(q.at[rh, rl, x, 64:96], c1.at[1, 0])
    s4.append(wire.send(q.at[rh, rl, x, B], c2.at[1, 0], p.YR))
    s3[3].wait_recv()
    plus(q.at[lh, ll, x, 96:128], c1.at[1, 1])
    s4.append(wire.send(q.at[lh, ll, x, B], c2.at[1, 1], p.YL))
    yield
    for copy in s4:
        copy.wait_recv()
    add(out.at[0:64], q.at[yh, yl, x, A], c2.at[0, 0], c2.at[0, 1])
    add(out.at[64:128], q.at[yh, yl, x, B], c2.at[1, 0], c2.at[1, 1])
    wire.drain()
    yield


def by_place(rows):
    return rows.reshape(EXP_DEV, 2, 2, 4, 2 * CAP, -1)


def backward_kernel(
    sel, info, y_places, y, cot, gate, up, hidden, row_gates, w_in, w_out,
    mixture, dots, dgate, dup, drows, term, ss, rs, ls, *scratch,
):
    p = Place()
    greet_plane(p)
    moving = home_steps(p, Wire(ss, rs), ls, True, sel, info, y_places, None, mixture, *scratch)
    next(moving)
    n = cot.shape[1]
    wide, cut = 2048 // PARTS, FF // PARTS
    dots[...] = jnp.zeros_like(dots)

    def number():
        return pl.program_id(0) * PARTS + pl.program_id(1)

    def first(y, cot, hidden, row_gates, term):
        at_step(number(), (1, moving), (6, moving))
        e = pl.program_id(0)
        product = y[0].astype(f32) * cot[0].astype(f32)
        partial = product[:, :128]
        for c in range(128, wide, 128):
            partial += product[:, c : c + 128]
        dots[e] += partial
        scaled = (hidden[0].astype(f32) * row_gates[0, :, :1]).astype(bf16)
        term[0] = tn(cot[0], scaled).astype(bf16)

    part = block((1, n, wide), lambda e, j: (e, 0, j))
    whole = block((1, n, FF), lambda e, j: (e, 0, 0))
    gates = block((1, n, 128), lambda e, j: (e, 0, 0))
    pltpu.emit_pipeline(
        first,
        grid=(EXP_DEV, PARTS),
        in_specs=[part, part, whole, gates],
        out_specs=[block((1, wide, FF), lambda e, j: (e, j, 0))],
    )(y, cot, hidden, row_gates, term)

    def second(cot, w, row_gates, gate, up, dgate, dup):
        at_step(number(), (5, moving))
        dhidden = jnp.dot(cot[0], w[0], preferred_element_type=f32) * row_gates[0, :, :1]
        g, u = gate[0].astype(f32), up[0].astype(f32)
        sg = jax.nn.sigmoid(g)
        dgate[0] = (dhidden * u * sg * (1.0 + g * (1.0 - sg))).astype(bf16)
        dup[0] = (dhidden * g * sg).astype(bf16)

    out = block((1, n, cut), lambda e, j: (e, 0, j))
    pltpu.emit_pipeline(
        second,
        grid=(EXP_DEV, PARTS),
        in_specs=[
            block((1, n, 2048), lambda e, j: (e, 0, 0)),
            block((1, 2048, cut), lambda e, j: (e, 0, j)),
            gates,
            out,
            out,
        ],
        out_specs=[out, out],
    )(cot, w_out, row_gates, gate, up, dgate, dup)

    def third(dgate, dup, w, drows):
        at_step(number(), (4, moving))
        total = nt(dgate[0], w[0, :, :FF]) + nt(dup[0], w[0, :, FF:])
        drows[0] = total.astype(bf16)

    pltpu.emit_pipeline(
        third,
        grid=(EXP_DEV, PARTS),
        in_specs=[whole, whole, block((1, wide, 2 * FF), lambda e, j: (e, j, 0))],
        out_specs=[part],
    )(dgate, dup, w_in, drows)
    for _ in moving:
        pass


def expert_backward(sel, info, y, cot, gate, up, hidden, row_gates, w_in, w_out, cid):
    n = cot.shape[1]
    half = shaped((EXP_DEV, n, FF))
    return remote_call(
        backward_kernel,
        "expert_backward",
        cid,
        HOME_SENDS,
        2,
        [VMEM, VMEM] + [ANY] * 9,
        [VMEM, VMEM] + [ANY] * 4,
        (
            shaped((128, 2048), f32),
            shaped((EXP_DEV, n, 128), f32),
            half,
            half,
            shaped((EXP_DEV, n, 2048)),
            shaped((EXP_DEV, 2048, FF)),
        ),
        scratch=home_scratch(2048),
        vmem=58 << 20,
    )(sel, info, by_place(y), y, cot, gate, up, hidden, row_gates, w_in, w_out)


def finish_kernel(sel, info, places, more, rows, dgate, dup, home, term, ss, rs, ls, *scratch):
    p = Place()
    greet_plane(p)
    moving = home_steps(p, Wire(ss, rs), ls, False, sel, info, places, more, home, *scratch)
    next(moving)
    n = rows.shape[1]
    wide = 2048 // PARTS

    def first(rows, dgate, dup, term):
        at_step(
            pl.program_id(0) * PARTS + pl.program_id(1), (1, moving), (4, moving), (7, moving)
        )
        term[0, :, :FF] = tn(rows[0], dgate[0]).astype(bf16)
        term[0, :, FF:] = tn(rows[0], dup[0]).astype(bf16)

    whole = block((1, n, FF), lambda e, j: (e, 0, 0))
    pltpu.emit_pipeline(
        first,
        grid=(EXP_DEV, PARTS),
        in_specs=[block((1, n, wide), lambda e, j: (e, 0, j)), whole, whole],
        out_specs=[block((1, wide, 2 * FF), lambda e, j: (e, j, 0))],
    )(rows, dgate, dup, term)
    for _ in moving:
        pass


def expert_finish(sel, info, drows, more, rows, dgate, dup, cid):
    return remote_call(
        finish_kernel,
        "expert_finish",
        cid,
        HOME_SENDS,
        4,
        [VMEM, VMEM] + [ANY] * 5,
        [VMEM, ANY],
        (shaped((128, 2048 + 128), f32), shaped((EXP_DEV, 2048, 2 * FF))),
        scratch=home_scratch(2048 + 128),
        vmem=58 << 20,
    )(sel, info, by_place(drows), by_place(more), rows, dgate, dup)


def unstack_kernel(grads, out, held, sems):
    e, j, steps = pl.program_id(0), pl.program_id(1), pl.num_programs(1)
    step = e * steps + j
    count = grads.shape[1]

    def copy(at):
        slot = lax.rem(at, 2)
        rows = pl.ds(pl.multiple_of(lax.rem(at, steps) * count, count), count)
        return pltpu.make_async_copy(held.at[slot], out.at[rows, at // steps], sems.at[slot])

    @pl.when(step >= 2)
    def _():
        copy(step - 2).wait()

    held[lax.rem(step, 2)] = grads[0].astype(f32)
    copy(step).start()

    @pl.when(step == EXP_DEV * steps - 1)
    def _():
        copy(step - 1).wait()
        copy(step).wait()


def unstack(grads):
    experts, rows, cols = grads.shape
    count = 128
    return pl.pallas_call(
        unstack_kernel,
        name="unstack",
        grid=(experts, rows // count),
        out_shape=shaped((rows, experts, cols), f32),
        in_specs=[pl.BlockSpec((1, count, cols), lambda e, j: (e, j, 0))],
        out_specs=ANY,
        scratch_shapes=[pltpu.VMEM((2, count, cols), f32), DMA((2,))],
        compiler_params=pltpu.CompilerParams(vmem_limit_bytes=60 << 20),
    )(grads)


def last_kernel(
    grads, kept, w, rows, cosine, sine, gain, p3, unit, small, out, normed, whole, ss, rs, ls,
    flat, total, w_grads, part, got_c, got_h, half, mine,
    ra, rb, rc, rd, re, rf, rg, acc_x, acc_y, sz, az, sx, ax, sy, ay, sc, ac, sh,
):
    p = Place()
    dp, yl, x = p.dp, p.yl, p.x
    greet([p.ZR, p.ZL, p.ZO, p.XR, p.XL, p.XO, p.Y, p.C, p.H])
    wire = Wire(ss, rs)
    p0, p1, p2 = (w_grads.at[i] for i in range(3))

    def added(dst, *srcs):
        total = srcs[0][...].astype(f32)
        for src in srcs[1:]:
            total = total + src[...].astype(f32)
        dst[...] = total.astype(dst.dtype)

    def loop(count, body):
        def step(i, carry):
            body(i)
            return carry

        lax.fori_loop(0, count, step, 0)

    def y_first(i, part):
        return wire.send(part.at[:, 1 - yl], rb.at[i - 2], p.Y)

    firsts = {3: y_first(3, p3)}
    for d in range(4):
        mine[d] = small[d]
    starts = []
    for i in range(3):
        if i < 2:
            gained = jnp.zeros((1, HD), f32)
            for h in range(4):
                grad = turned(grads[i, h].astype(f32), cosine[...], -sine[...])
                head = kept[i, h]
                inverse = rms_rows(head)
                gained += jnp.sum(grad * head * inverse, axis=0, keepdims=True)
                back = rms_back(head, inverse, grad * gain[i])
                flat[:, h * HD : (h + 1) * HD] = back.astype(bf16)
            mine[0, 1, 0, 32 + i : 33 + i] = gained
        else:
            for h in range(4):
                flat[:, h * HD : (h + 1) * HD] = grads[i, h]

        def weight_rows(c, carry):
            cols = pl.ds(pl.multiple_of(c * 512, 512), 512)
            grad = tn(rows[:, cols], flat[...]).astype(bf16)
            w_grads[i, c] = grad.reshape(2, 4, 64, 512)
            return carry

        lax.fori_loop(0, 4, weight_rows, 0)
        if i < 2:
            gradient = w_grads.at[i]
            starts.append(
                (
                    wire.send(gradient.at[0:2, :, p.xo], ra.at[i, 0], p.XR),
                    wire.send(gradient.at[2:4, :, p.xo], ra.at[i, 1], p.XL),
                )
            )
        else:
            firsts[2] = y_first(2, p2)

        def normed_cols(c, carry):
            cols = pl.ds(pl.multiple_of(c * 512, 512), 512)
            value = nt(flat[...], w[i, cols])
            if i > 0:
                value += total[:, cols]
            if i < 2:
                total[:, cols] = value
            else:
                part[:, :, cols] = value.astype(bf16).reshape(4, 128, 512)
            return carry

        lax.fori_loop(0, 4, normed_cols, 0)
    mine_head, other = p.yh * 2 + (1 - p.co), (1 - p.yh) * 2 + (1 - p.co)
    far = wire.send(part.at[other], got_c.at[0], p.C)
    near = wire.send(part.at[mine_head], got_c.at[1], p.C)
    far.wait_recv()

    def by_16(body):
        def step(i, carry):
            body(pl.ds(pl.multiple_of(i * 16, 16), 16))
            return carry

        lax.fori_loop(0, 8, step, 0)

    def add_far(at):
        away = part[(1 - p.yh) * 2 + p.co, at].astype(f32)
        half[at] = (away + got_c[0, at].astype(f32)).astype(bf16)

    by_16(add_far)
    over = wire.send(half, got_h, p.H)
    seconds = []
    for i, gradient in ((0, p0), (1, p1)):
        one, two = starts[i]
        one.wait_recv()
        loop(2, lambda d: added(gradient.at[d, :, p.xr], gradient.at[d, :, p.xr], ra.at[i, 0, d]))
        s1 = wire.send(gradient.at[:, :, p.xr], rc.at[i, 0], p.XR)
        two.wait_recv()
        loop(
            2,
            lambda d: added(gradient.at[d + 2, :, p.xl], gradient.at[d + 2, :, p.xl], ra.at[i, 1, d]),
        )
        s2 = wire.send(gradient.at[:, :, p.xl], rc.at[i, 1], p.XL)
        seconds.append((s1, s2))
    mids = {}
    for i, gradient in ((3, p3), (2, p2)):
        firsts[i].wait_recv()
        loop(4, lambda d: added(acc_y.at[i - 2, d], gradient.at[d, yl], rb.at[i - 2, d]))
        acc = acc_y.at[i - 2]
        mids[i] = (
            wire.send(acc.at[0:2, p.xo], rd.at[i - 2, 0], p.XR),
            wire.send(acc.at[2:4, p.xo], rd.at[i - 2, 1], p.XL),
        )
    near.wait_recv()
    over.wait_recv()

    def add_near(at):
        close = part[p.yh * 2 + p.co, at].astype(f32) + got_c[1, at].astype(f32)
        normed[at] = close + got_h[at].astype(f32)

    by_16(add_near)
    for c in range(16):
        cols = slice(c * 128, (c + 1) * 128)
        column = jnp.sum(normed[:, cols] * unit[:, cols], axis=0, keepdims=True)
        mine[0, 0, c // 8, 32 + c % 8 : 33 + c % 8] = column
    zs_out = [
        wire.send(mine.at[there], sz.at[i], device)
        for i, (there, device) in enumerate(((p.zo, p.ZO), (p.zr, p.ZR), (p.zl, p.ZL)))
    ]
    yends = []
    for i, gradient in ((0, p0), (1, p1)):
        for s in seconds[i]:
            s.wait_recv()
        acc = acc_x.at[i]
        loop(4, lambda d: added(acc.at[d], gradient.at[d, :, x], rc.at[i, 0, d], rc.at[i, 1, d]))
        yends.append(wire.send(acc.at[:, 1 - yl], re.at[i], p.Y))
    for copy in zs_out:
        copy.wait_recv()
    for y in range(2):
        az[y] = mine[dp, y] + sz[0, y] + sz[1, y] + sz[2, y]
    xs_out = [
        wire.send(az.at[:, there], sx.at[i], device)
        for i, (there, device) in enumerate(((p.xo, p.XO), (p.xr, p.XR), (p.xl, p.XL)))
    ]
    xends = {}
    for i in (3, 2):
        acc = acc_y.at[i - 2]
        one, two = mids[i]
        one.wait_recv()
        loop(2, lambda d: added(acc.at[d, p.xr], acc.at[d, p.xr], rd.at[i - 2, 0, d]))
        s1 = wire.send(acc.at[:, p.xr], rf.at[i - 2, 0], p.XR)
        two.wait_recv()
        loop(2, lambda d: added(acc.at[d + 2, p.xl], acc.at[d + 2, p.xl], rd.at[i - 2, 1, d]))
        s2 = wire.send(acc.at[:, p.xl], rf.at[i - 2, 1], p.XL)
        xends[i] = (s1, s2)
    for copy in xs_out:
        copy.wait_recv()
    ax[...] = az[:, x] + sx[0] + sx[1] + sx[2]
    y_out = wire.send(ax.at[1 - yl], sy, p.Y)
    parts, zs = {}, {}

    def z_first(i, acc):
        parts[i] = acc
        zs[i] = (
            wire.send(acc.at[p.zo, 0:32], rg.at[i, 0, 0:32], p.ZR),
            wire.send(acc.at[p.zo, 32:64], rg.at[i, 1, 0:32], p.ZL),
        )

    for i in (0, 1):
        yends[i].wait_recv()
        acc = acc_x.at[i]
        loop(4, lambda d: added(acc.at[d, yl], acc.at[d, yl], re.at[i, d]))
        z_first(i, acc.at[:, yl])
    y_out.wait_recv()
    ay[...] = ax[yl] + sy[...]
    c_out = wire.send(ay, sc, p.C)
    for i in (3, 2):
        for s in xends[i]:
            s.wait_recv()
        acc = acc_y.at[i - 2]
        loop(
            4, lambda d: added(acc.at[d, x], acc.at[d, x], rf.at[i - 2, 0, d], rf.at[i - 2, 1, d])
        )
        z_first(i, acc.at[:, x])
    c_out.wait_recv()
    ac[...] = ay[...] + sc[...]
    h_out = wire.send(ac, sh, p.H)
    ends = {}
    for i in (0, 1, 3, 2):
        one, two = zs[i]
        acc = parts[i]
        one.wait_recv()
        added(acc.at[p.zr, 0:32], acc.at[p.zr, 0:32], rg.at[i, 0, 0:32])
        s1 = wire.send(acc.at[p.zr], rg.at[i, 2], p.ZR)
        two.wait_recv()
        added(acc.at[p.zl, 32:64], acc.at[p.zl, 32:64], rg.at[i, 1, 0:32])
        s2 = wire.send(acc.at[p.zl], rg.at[i, 3], p.ZL)
        ends[i] = (s1, s2)
    h_out.wait_recv()
    whole[dp, yl, x] = ac[...] + sh[...]
    y_all = wire.send(whole.at[dp, yl, x], whole.at[dp, yl, x], p.Y)
    y_all.wait_recv()
    x_all = [
        wire.send(whole.at[dp, :, x], whole.at[dp, :, x], device) for device in (p.XO, p.XR, p.XL)
    ]
    for i in range(4):
        for s in ends[i]:
            s.wait_recv()
        added(out.at[i], parts[i].at[dp], rg.at[i, 2], rg.at[i, 3])
    for copy in x_all:
        copy.wait_recv()
    z_all = [wire.send(whole.at[dp], whole.at[dp], device) for device in (p.ZO, p.ZR, p.ZL)]
    for copy in z_all:
        copy.wait_recv()
    wire.drain()


def last_sums(grads, kept, w, rows, cosine, sine, gains, fourth, unit, small):
    return remote_call(
        last_kernel,
        "last_sums",
        8,
        55,
        1,
        [VMEM] * 10,
        [VMEM] * 3,
        (
            shaped((4, 64, 512), f32),
            shaped((128, 2048), f32),
            shaped((4, 2, 4, 40, 128), f32),
        ),
        scratch=[
            pltpu.VMEM((512, 512), bf16),
            pltpu.VMEM((512, 2048), f32),
            pltpu.VMEM((3, 4, 2, 4, 64, 512), bf16),
            pltpu.VMEM((4, 128, 2048), bf16),
            pltpu.VMEM((2, 128, 2048), bf16),
            pltpu.VMEM((128, 2048), bf16),
            pltpu.VMEM((128, 2048), bf16),
            pltpu.VMEM((4, 2, 4, 40, 128), f32),
            pltpu.VMEM((2, 2, 2, 2, 64, 512), bf16),
            pltpu.VMEM((2, 4, 4, 64, 512), bf16),
            pltpu.VMEM((2, 2, 4, 2, 64, 512), bf16),
            pltpu.VMEM((2, 2, 2, 64, 512), bf16),
            pltpu.VMEM((2, 4, 64, 512), bf16),
            pltpu.VMEM((2, 2, 4, 64, 512), bf16),
            pltpu.VMEM((4, 4, 64, 512), bf16),
            pltpu.VMEM((2, 4, 2, 64, 512), bf16),
            pltpu.VMEM((2, 4, 4, 64, 512), bf16),
            pltpu.VMEM((3, 2, 4, 40, 128), f32),
            pltpu.VMEM((2, 4, 40, 128), f32),
            pltpu.VMEM((3, 2, 40, 128), f32),
            pltpu.VMEM((2, 40, 128), f32),
            pltpu.VMEM((40, 128), f32),
            pltpu.VMEM((40, 128), f32),
            pltpu.VMEM((40, 128), f32),
            pltpu.VMEM((40, 128), f32),
            pltpu.VMEM((40, 128), f32),
        ],
        vmem=60 << 20,
    )(
        grads, kept, w, rows, cosine, sine, gains,
        fourth.reshape(4, 2, 4, 64, 512), unit, small.reshape(4, 2, 4, 40, 128),
    )


def on_device(
    tokens,
    segment_ids,
    valid_mask,
    routes,
    attn_gain,
    w_query,
    w_key,
    w_value,
    w_out,
    query_gain,
    key_gain,
    ffn_gain,
    router,
    expert_in,
    expert_out,
    cotangent,
):
    blk = lax.axis_index("blk")
    device = lax.axis_index("head") * 8 + blk
    yl = blk // 4
    tok, width = tokens.shape
    full_in = lax.all_gather(jnp.transpose(expert_in, (1, 0, 2)), "dp", axis=1, tiled=True)
    full_back = lax.all_gather(jnp.transpose(expert_out, (1, 0, 2)), "dp", axis=1, tiled=True)

    segment, valid = segment_ids[0], valid_mask[0]
    seq_len = segment.shape[0]
    place = jnp.arange(seq_len, dtype=i32)
    query_ids = (jnp.arange(4)[:, None] * 1024 + blk * 128 + jnp.arange(128)[None]).reshape(-1)
    frequency = rope_base ** (-jnp.arange(64, dtype=f32) / 64)
    angles = query_ids.astype(f32)[:, None] * frequency[None]
    cosine, sine = jnp.cos(angles), jnp.sin(angles)
    cosine = jnp.concatenate([cosine, cosine], axis=1)
    sine = jnp.concatenate([-sine, sine], axis=1)
    half_ids = (jnp.arange(4)[:, None] * 1024 + yl * 512 + jnp.arange(512)[None]).reshape(-1)
    half_seg = lax.dynamic_index_in_dim(segment.reshape(4, 2, 512), yl, 1, keepdims=False).reshape(-1)
    key_seg = jnp.where(valid > 0, segment, -1)
    ends = half_seg.reshape(-1, QB)
    lower = jnp.sum(segment[None] < ends[:, :1], axis=1, dtype=i32) // KB
    upper = (jnp.sum(segment[None] <= ends[:, -1:], axis=1, dtype=i32) + KB - 1) // KB
    limits = jnp.stack([lower, upper])

    inputs = tokens.astype(f32)
    first_inv = rms_rows(inputs)
    normed = (inputs * first_inv * attn_gain).astype(bf16)
    w_three = jnp.stack([w_query, w_key, w_value])
    gathered, out_part, normed_all = gather_weights(w_three, w_out, normed)
    full_three = gathered.reshape(3, 2048, 512)
    normed_all = normed_all.reshape(512, width)

    def by_head(flat):
        return jnp.transpose(flat.reshape(512, 4, HD), (1, 0, 2))

    def flat_of(heads):
        return jnp.transpose(heads.reshape(4, 512, HD), (1, 0, 2)).reshape(512, 512)

    head_gains = jnp.stack([query_gain, key_gain])[:, None]
    heads, projected = project(normed_all, full_three, cosine, sine, head_gains)
    runs = (4, 4, 128, HD)
    q, k, v, full_out = heads_over_x(heads.reshape((3,) + runs), out_part)
    q, k, v = q.reshape(2048, HD), k.reshape(4096, HD), v.reshape(4096, HD)
    full_out = full_out.reshape(2048, 512)
    att_low, att, inverse = attend(limits, q, k, v, half_seg, half_ids, key_seg)
    attended = back_over_x(att_low.reshape(runs))
    attended_flat = flat_of(attended)
    branch_part = jnp.einsum("qc,mc->qm", attended_flat, full_out, preferred_element_type=f32)
    middle = inputs + sum_rows(branch_part.astype(bf16), 9)
    second_inv = rms_rows(middle)
    normed_ffn = (middle * second_inv * ffn_gain).astype(bf16)
    logits = jnp.dot(normed_ffn, router, preferred_element_type=f32)
    probabilities = jax.nn.softmax(logits, axis=-1)

    expert_ids = jnp.arange(EXPERTS, dtype=i32)
    hot = jnp.sum((routes[..., None] == expert_ids).astype(f32), axis=1)
    before = (jnp.arange(tok)[:, None] > jnp.arange(tok)[None]).astype(bf16)
    slots = jnp.dot(before, hot.astype(bf16), preferred_element_type=f32)
    slot_code = jnp.where(hot > 0, slots, -1.0)
    chosen = probabilities * hot
    gate_total = jnp.sum(chosen, axis=-1, keepdims=True)
    gates = chosen / gate_total

    sent = jnp.concatenate([normed_ffn, slot_code.astype(bf16), gates.astype(bf16)], axis=1)
    everyone = spread(sent, 7)
    lane = jnp.arange(128)[None]
    sel_row = jnp.arange(8)[:, None]
    info = everyone[:, :, width:]
    column = (sel_row // 2) * EXPERTS + device * EXP_DEV + sel_row % 2
    sel = ((sel_row < 4) & (lane == column)).astype(bf16)
    nearby = (device ^ 8) * EXP_DEV
    column = sel_row % 2 + jnp.where(sel_row // 2 % 2 == 0, device * EXP_DEV, nearby)
    sel_chip = (lane == column + (sel_row // 4) * EXPERTS).astype(bf16)
    flat_info, flat_everyone = info.reshape(32 * tok, -1), everyone.reshape(32 * tok, -1)
    expert_rows, row_gates = pick_rows(sel, flat_info, flat_everyone, width, True)
    expert_rows = expert_rows.reshape(EXP_DEV, -1, width)
    row_gates = row_gates.reshape(EXP_DEV, -1, 128)
    all_cot, gate_part, up_part, hidden, expert_result = expert_forward(
        cotangent, expert_rows, full_in, full_back, 11
    )
    (arrived_cot,) = pick_rows(sel, flat_info, all_cot.reshape(32 * tok, width), width, False)
    arrived_cot = arrived_cot.reshape(EXP_DEV, -1, width)
    mixture, row_dots, grad_gate, grad_up, grad_rows, term_back = expert_backward(
        sel_chip, info, expert_result, arrived_cot, gate_part, up_part, hidden, row_gates,
        full_in, full_back, 12,
    )
    row_dots = jnp.sum(row_dots, axis=-1, keepdims=True)
    high = row_dots.astype(bf16)
    column = (device * EXP_DEV + jnp.arange(EXP_DEV))[:, None, None]
    low = jnp.where(lane == column + EXPERTS, (row_dots - high.astype(f32)).astype(bf16), 0)
    row_dots = jnp.where(lane == column, high, low)
    grad_home, term_in = expert_finish(
        sel_chip, info, grad_rows, row_dots, expert_rows, grad_gate, grad_up, 13
    )
    grad_gates = grad_home[:, width : width + EXPERTS] + grad_home[:, width + EXPERTS :]
    grad_home = grad_home[:, :width]

    def fold_dp(term):
        return lax.psum_scatter(term.astype(bf16), "dp", scatter_dimension=1, tiled=True)

    expert_out_grad = unstack(fold_dp(term_back))
    expert_in_grad = unstack(fold_dp(term_in))

    output = (middle + mixture).astype(bf16)
    grad_out = cotangent.astype(f32)
    mean_grad = jnp.sum(grad_gates * gates, axis=-1, keepdims=True)
    grad_probs = (grad_gates - mean_grad) / gate_total * hot
    grad_logits = probabilities * (
        grad_probs - jnp.sum(probabilities * grad_probs, axis=-1, keepdims=True)
    )
    high = grad_logits.astype(bf16)
    halves = jnp.concatenate([high, (grad_logits - high.astype(f32)).astype(bf16)], axis=1)
    router_term = jnp.einsum("td,te->de", normed_ffn, halves, preferred_element_type=f32)
    router_term = router_term[:, :EXPERTS] + router_term[:, EXPERTS:]
    grad_ffn = grad_home + jnp.einsum(
        "te,de->td", halves, jnp.concatenate([router, router], axis=1), preferred_element_type=f32
    )
    ffn_gain_term = jnp.sum(grad_ffn * middle * second_inv, axis=0)
    grad_middle = grad_out + rms_back(middle, second_inv, grad_ffn * ffn_gain)
    grad_branch = grad_middle.astype(bf16)
    branch_all = gather_rows(grad_branch).reshape(512, width)
    grad_att = by_head(
        jnp.dot(branch_all, full_out, preferred_element_type=f32).astype(bf16)
    )
    grad_att = go_over_x(grad_att.reshape(runs)).reshape(2048, HD)
    delta = jnp.sum(grad_att.astype(f32) * att, axis=-1)
    dq, dk, dv = attend_back(
        limits, q, k, v, grad_att, half_seg, half_ids, key_seg, inverse[:, 0], delta
    )
    cut = (4, 2, 4, 128, HD)
    grad_heads = grads_over_x(dq.reshape(runs), dk.reshape(cut), dv.reshape(cut))
    out_grad = jnp.einsum(
        "qc,qf->cf", branch_all, attended_flat, preferred_element_type=f32
    ).astype(bf16)
    gains = jnp.pad(ffn_gain_term, (width, 32 * 8 * 128 - 2 * width)).reshape(32, 8, 128)
    small = jnp.concatenate([router_term.reshape(32, 32, 128), gains], axis=1)
    attn_grads, grad_normed, summed = last_sums(
        grad_heads.reshape(3, 4, 512, HD), projected, full_three, normed_all, cosine, sine,
        head_gains, out_grad, inputs * first_inv, small,
    )
    input_grad = grad_middle + rms_back(inputs, first_inv, grad_normed * attn_gain)
    summed = summed.reshape(32, 40, 128)
    router_grad = summed[:, :32].reshape(router.shape)
    gains = summed[:, 32:].reshape(-1)
    return (
        output,
        input_grad,
        gains[:2048],
        attn_grads[0],
        attn_grads[1],
        attn_grads[2],
        attn_grads[3],
        gains[4096:4224],
        gains[4224:4352],
        gains[2048:4096],
        router_grad,
        expert_in_grad,
        expert_out_grad,
    )


def solution(mesh):
    placed = (
        P(("dp", "head", "blk"), None),
        P("dp", None),
        P("dp", None),
        P(("dp", "head", "blk"), None),
        P(),
        P(("dp", "blk"), "head"),
        P(("dp", "blk"), "head"),
        P(("dp", "blk"), "head"),
        P(("dp", "blk"), "head"),
        P(),
        P(),
        P(),
        P(),
        P("dp", ("head", "blk"), None),
        P("dp", ("head", "blk"), None),
        P(("dp", "head", "blk"), None),
    )
    return jax.shard_map(
        on_device,
        mesh=mesh,
        in_specs=placed,
        out_specs=(
            P(("dp", "head", "blk"), None),
            P(("dp", "head", "blk"), None),
            P(),
            P(("dp", "blk"), "head"),
            P(("dp", "blk"), "head"),
            P(("dp", "blk"), "head"),
            P(("dp", "blk"), "head"),
            P(),
            P(),
            P(),
            P(),
            P("dp", ("head", "blk"), None),
            P("dp", ("head", "blk"), None),
        ),
        check_vma=False,
    )
```

```python
import functools
import math

import jax
import jax.numpy as jnp
from jax import lax
from jax.experimental import pallas as pl
from jax.experimental.pallas import tpu as pltpu
from jax.sharding import PartitionSpec as P

HEADS = 16
HD = 128
FF = 1024
TOPK = 8
EXP_DEV = 2
CAP = 24
EXPERTS = 64

epsilon = 1e-06
rope_base = 50000.0
f32 = jnp.float32
bf16 = jnp.bfloat16
i32 = jnp.int32
MESH = pl.DeviceIdType.MESH
ANY = pl.BlockSpec(memory_space=pl.ANY)
VMEM = pl.BlockSpec(memory_space=pltpu.VMEM)
SMEM = pl.BlockSpec(memory_space=pltpu.SMEM)
DMA = pltpu.SemaphoreType.DMA


def rms_rows(values):
    return lax.rsqrt(jnp.mean(values * values, axis=-1, keepdims=True) + epsilon)


def rms_back(values, inverse, grad_scaled):
    inner_mean = jnp.mean(grad_scaled * values, axis=-1, keepdims=True)
    return inverse * grad_scaled - values * inverse * inverse * inverse * inner_mean


def wrap4(value):
    return lax.rem(value + 4, 4)


class Place:
    def __init__(self):
        head, blk = lax.axis_index("head"), lax.axis_index("blk")
        self.dp = lax.axis_index("dp")
        self.yh, self.co = head // 2, lax.rem(head, 2)
        self.yl, self.x = blk // 4, lax.rem(blk, 4)
        self.head = head
        self.zr, self.zl, self.zo = (wrap4(self.dp + s) for s in (1, -1, 2))
        self.xr, self.xl, self.xo = (wrap4(self.x + s) for s in (1, -1, 2))
        y = self.yh * 2 + self.yl
        self.yr, self.ylf, self.yo = (wrap4(y + s) for s in (1, -1, 2))
        self.ZR, self.ZL, self.ZO = {"dp": self.zr}, {"dp": self.zl}, {"dp": self.zo}
        self.XR, self.XL, self.XO = (self.to_x(v) for v in (self.xr, self.xl, self.xo))
        self.Y = {"blk": (1 - self.yl) * 4 + self.x}
        self.C = {"head": self.yh * 2 + (1 - self.co)}
        self.H = {"head": (1 - self.yh) * 2 + self.co}
        self.YR, self.YL = self.to_y(self.yr), self.to_y(self.ylf)

    def to_x(self, x):
        return {"blk": self.yl * 4 + x}

    def to_y(self, y):
        return {"head": (y // 2) * 2 + self.co, "blk": lax.rem(y, 2) * 4 + self.x}


def greet(devices):
    barrier = pltpu.get_barrier_semaphore()
    for device in devices:
        pl.semaphore_signal(barrier, inc=1, device_id=device, device_id_type=MESH)
    pl.semaphore_wait(barrier, len(devices))


class View:
    def __init__(self, ref, index=None):
        self.ref, self.index = ref, index

    @property
    def at(self):
        return self

    def __getitem__(self, index):
        return View(self, index)

    def get(self):
        base = self.ref.get() if isinstance(self.ref, View) else self.ref
        return base if self.index is None else base.at[self.index]

    def load(self):
        return self.get()[...]

    def store(self, value):
        ref = self.get()
        ref[...] = value.astype(ref.dtype)


def plain(ref):
    return ref.get() if isinstance(ref, View) else ref


class Sent:
    def __init__(self, make):
        self.make = make

    def wait_recv(self):
        self.make().wait_recv()

    def wait_send(self):
        self.make().wait_send()

    def wait(self):
        self.make().wait()


class Wire:
    def __init__(self, send_sem, recv_sem):
        self.send_sem, self.recv_sem, self.started = send_sem, recv_sem, []

    def send(self, src, dst, device):
        at = len(self.started)

        def make():
            return pltpu.make_async_remote_copy(
                src_ref=plain(src),
                dst_ref=plain(dst),
                send_sem=self.send_sem.at[at],
                recv_sem=self.recv_sem.at[at],
                device_id=device,
                device_id_type=MESH,
            )

        make().start()
        self.started.append(Sent(make))
        return self.started[-1]

    def drain(self):
        for copy in self.started:
            copy.wait_send()


def local(src, dst, sems, at):
    def make():
        return pltpu.make_async_copy(plain(src), plain(dst), sems.at[at])

    make().start()
    return Sent(make)


def remote_call(body, name, cid, sends, locals_, ins, outs, out_shape, scratch=(), vmem=None):
    return pl.pallas_call(
        body,
        name=name,
        out_shape=out_shape,
        in_specs=ins,
        out_specs=outs,
        scratch_shapes=[DMA((sends,)), DMA((sends,)), DMA((max(locals_, 1),)), *scratch],
        compiler_params=pltpu.CompilerParams(
            collective_id=cid, has_side_effects=True, vmem_limit_bytes=vmem
        ),
    )


def shaped(shape, dtype=bf16):
    return jax.ShapeDtypeStruct(shape, dtype)


def weights_kernel(w, wo, n, g, go, m, ss, rs, ls):
    p = Place()
    dp, yl, x = p.dp, p.yl, p.x
    own = [
        local(w, g.at[:, dp, yl, x], ls, 0),
        local(n, m.at[p.head], ls, 1),
        local(wo, go.at[dp], ls, 2),
    ]
    greet([p.ZR, p.ZL, p.XR, p.XL, p.Y, p.C, p.H])
    wire = Wire(ss, rs)
    n_c = wire.send(n, m.at[p.head], p.C)
    z1 = wire.send(w, g.at[:, dp, yl, x], p.ZR)
    z2 = wire.send(w, g.at[:, dp, yl, x], p.ZL)
    n_h = wire.send(n, m.at[p.head], p.H)
    o1 = wire.send(wo, go.at[dp], p.ZR)
    o2 = wire.send(wo, go.at[dp], p.ZL)
    z1.wait_recv()
    z3 = wire.send(g.at[0:2, p.zl, yl, x], g.at[0:2, p.zl, yl, x], p.ZR)
    z2.wait_recv()
    z4 = wire.send(g.at[2, p.zr, yl, x], g.at[2, p.zr, yl, x], p.ZL)
    own[0].wait()
    z3.wait_recv()
    z4.wait_recv()
    b1 = wire.send(g.at[2, :, yl, x], g.at[2, :, yl, x], p.XR)
    b2 = wire.send(g.at[2, :, yl, x], g.at[2, :, yl, x], p.XL)
    a1 = wire.send(g.at[0:2, :, yl, x], g.at[0:2, :, yl, x], p.Y)
    c1 = wire.send(g.at[2, :, yl, x], g.at[2, :, yl, x], p.Y)
    o1.wait_recv()
    o3 = wire.send(go.at[p.zl, 0:32], go.at[p.zl, 0:32], p.ZR)
    o2.wait_recv()
    o4 = wire.send(go.at[p.zr, 32:64], go.at[p.zr, 32:64], p.ZL)
    n_h.wait_recv()
    other = (1 - p.yh) * 2 + p.co
    n_f = wire.send(m.at[other], m.at[other], p.C)
    b1.wait_recv()
    b3 = wire.send(g.at[2, 0:2, yl, p.xl], g.at[2, 0:2, yl, p.xl], p.XR)
    c2 = wire.send(g.at[2, :, yl, p.xl], g.at[2, :, yl, p.xl], p.Y)
    b2.wait_recv()
    b4 = wire.send(g.at[2, 2:4, yl, p.xr], g.at[2, 2:4, yl, p.xr], p.XL)
    c3 = wire.send(g.at[2, :, yl, p.xr], g.at[2, :, yl, p.xr], p.Y)
    a1.wait_recv()
    a2 = wire.send(g.at[0:2, :, :, x], g.at[0:2, :, :, x], p.XR)
    a3 = wire.send(g.at[0:2, :, :, x], g.at[0:2, :, :, x], p.XL)
    b3.wait_recv()
    b4.wait_recv()
    c4 = wire.send(g.at[2, :, yl, p.xo], g.at[2, :, yl, p.xo], p.Y)
    a2.wait_recv()
    a4 = wire.send(g.at[0, :, :, p.xl], g.at[0, :, :, p.xl], p.XR)
    a3.wait_recv()
    a5 = wire.send(g.at[1, :, :, p.xr], g.at[1, :, :, p.xr], p.XL)
    for copy in (n_c, n_f, o3, o4, c1, c2, c3, c4, a4, a5):
        copy.wait_recv()
    own[1].wait()
    own[2].wait()
    wire.drain()


def gather_weights(w, wo, n):
    return remote_call(
        weights_kernel,
        "gather_weights",
        1,
        24,
        3,
        [ANY] * 3,
        [ANY] * 3,
        (shaped((3, 4, 2, 4, 64, 512)), shaped((4, 64, 512)), shaped((4, 128, 2048))),
    )(w, wo, n)


def rows_kernel(n, m, ss, rs, ls):
    p = Place()
    own = local(n, m.at[p.head], ls, 0)
    greet([p.C, p.H])
    wire = Wire(ss, rs)
    n_h = wire.send(n, m.at[p.head], p.H)
    n_c = wire.send(n, m.at[p.head], p.C)
    n_h.wait_recv()
    other = (1 - p.yh) * 2 + p.co
    n_f = wire.send(m.at[other], m.at[other], p.C)
    n_c.wait_recv()
    n_f.wait_recv()
    own.wait()
    wire.drain()


def gather_rows(n):
    return remote_call(
        rows_kernel, "gather_rows", 2, 3, 1, [ANY], [ANY], (shaped((4, 128, 2048)),)
    )(n)[0]


def sum_kernel(part, out, ss, rs, ls, got_c, got_h, half):
    p = Place()
    greet([p.C, p.H])
    wire = Wire(ss, rs)
    far = wire.send(part.at[1 - p.yh, 1 - p.co], got_c.at[0], p.C)
    near = wire.send(part.at[p.yh, 1 - p.co], got_c.at[1], p.C)
    far.wait_recv()

    def add_far(i, carry):
        rows = pl.ds(pl.multiple_of(i * 16, 16), 16)
        half[rows] = (
            part[1 - p.yh, p.co, rows].astype(f32) + got_c[0, rows].astype(f32)
        ).astype(bf16)
        return carry

    lax.fori_loop(0, 8, add_far, 0)
    over = wire.send(half, got_h, p.H)
    near.wait_recv()
    over.wait_recv()

    def add_near(i, carry):
        rows = pl.ds(pl.multiple_of(i * 16, 16), 16)
        out[rows] = (
            part[p.yh, p.co, rows].astype(f32)
            + got_c[1, rows].astype(f32)
            + got_h[rows].astype(f32)
        )
        return carry

    lax.fori_loop(0, 8, add_near, 0)
    wire.drain()


def sum_rows(part, cid):
    return remote_call(
        sum_kernel,
        "sum_rows",
        cid,
        3,
        1,
        [VMEM],
        [VMEM],
        (shaped((128, 2048), f32),),
        scratch=[
            pltpu.VMEM((2, 128, 2048), bf16),
            pltpu.VMEM((128, 2048), bf16),
            pltpu.VMEM((128, 2048), bf16),
        ],
        vmem=16 << 20,
    )(part.reshape(2, 2, 128, 2048))[0]


def heads_kernel(three, go, qd, kd, vd, gd, ss, rs, ls):
    p = Place()
    q, k, v = (three.at[i] for i in range(3))
    yl, x = p.yl, p.x
    own = [
        local(q.at[x], qd.at[:, x], ls, 0),
        local(k.at[x], kd.at[:, yl, x], ls, 1),
        local(v.at[x], vd.at[:, yl, x], ls, 2),
        local(go, gd.at[:, yl, x], ls, 3),
    ]
    greet([p.Y, p.XR, p.XL, p.XO])
    wire = Wire(ss, rs)
    done = [
        wire.send(k.at[x], kd.at[:, yl, x], p.Y),
        wire.send(v.at[x], vd.at[:, yl, x], p.Y),
    ]
    w1 = wire.send(go, gd.at[:, yl, x], p.Y)
    moved = []
    for there, came, device in ((p.xo, p.xo, p.XO), (p.xr, p.xl, p.XR), (p.xl, p.xr, p.XL)):
        ks = wire.send(k.at[there], kd.at[:, yl, x], device)
        vs = wire.send(v.at[there], vd.at[:, yl, x], device)
        moved.append((came, ks, vs))
    for there, device in ((p.xo, p.XO), (p.xr, p.XR), (p.xl, p.XL)):
        done.append(wire.send(q.at[there], qd.at[:, x], device))
    for came, ks, vs in moved[1:] + moved[:1]:
        ks.wait_recv()
        done.append(wire.send(kd.at[:, yl, came], kd.at[:, yl, came], p.Y))
        vs.wait_recv()
        done.append(wire.send(vd.at[:, yl, came], vd.at[:, yl, came], p.Y))
    own[3].wait()
    w1.wait_recv()
    w2 = wire.send(gd.at[:, :, x], gd.at[:, :, x], p.XR)
    w3 = wire.send(gd.at[:, :, x], gd.at[:, :, x], p.XL)
    w2.wait_recv()
    done.append(wire.send(gd.at[0:2, :, p.xl], gd.at[0:2, :, p.xl], p.XR))
    w3.wait_recv()
    done.append(wire.send(gd.at[2:4, :, p.xr], gd.at[2:4, :, p.xr], p.XL))
    for copy in done:
        copy.wait_recv()
    for copy in own[:3]:
        copy.wait()
    wire.drain()


def heads_over_x(three, go):
    return remote_call(
        heads_kernel,
        "heads_over_x",
        3,
        22,
        4,
        [ANY] * 2,
        [ANY] * 4,
        (
            shaped((4, 4, 128, 128)),
            shaped((4, 2, 4, 128, 128)),
            shaped((4, 2, 4, 128, 128)),
            shaped((4, 2, 4, 64, 512)),
        ),
    )(three, go)


def back_x_kernel(o, att, ss, rs, ls):
    p = Place()
    own = local(o.at[:, p.x], att.at[p.x], ls, 0)
    greet([p.XR, p.XL, p.XO])
    wire = Wire(ss, rs)
    for there, device in ((p.xo, p.XO), (p.xr, p.XR), (p.xl, p.XL)):
        wire.send(o.at[:, there], att.at[p.x], device)
    for copy in wire.started:
        copy.wait_recv()
    own.wait()
    wire.drain()


def back_over_x(o):
    return remote_call(
        back_x_kernel, "back_over_x", 4, 3, 1, [ANY], [ANY], (shaped((4, 4, 128, 128)),)
    )(o)[0]


def go_x_kernel(o, d, ss, rs, ls):
    p = Place()
    own = local(o.at[p.x], d.at[:, p.x], ls, 0)
    greet([p.XR, p.XL, p.XO])
    wire = Wire(ss, rs)
    for there, device in ((p.xo, p.XO), (p.xr, p.XR), (p.xl, p.XL)):
        wire.send(o.at[there], d.at[:, p.x], device)
    for copy in wire.started:
        copy.wait_recv()
    own.wait()
    wire.drain()


def go_over_x(o):
    return remote_call(
        go_x_kernel, "go_over_x", 5, 3, 1, [ANY], [ANY], (shaped((4, 4, 128, 128)),)
    )(o)[0]


def grads_x_kernel(dq, dk, dv, three, ss, rs, ls, gk, gv, sk, sv):
    p = Place()
    x, yl = p.x, p.yl
    qd, kd, vd = (three.at[i] for i in range(3))
    own = local(dq.at[:, x], qd.at[x], ls, 0)
    greet([p.Y, p.XR, p.XL, p.XO])
    wire = Wire(ss, rs)
    order = ((p.xo, p.XO), (p.xr, p.XR), (p.xl, p.XL), (x, None))
    pairs = []
    for i, (there, device) in enumerate(order):
        pairs.append(
            (
                wire.send(dk.at[:, 1 - yl, there], gk.at[i], p.Y),
                wire.send(dv.at[:, 1 - yl, there], gv.at[i], p.Y),
            )
        )
    last = []
    for there, device in order[:3]:
        last.append(wire.send(dq.at[:, there], qd.at[x], device))
    for i, (there, device) in enumerate(order):
        for grads, got, summed, out, arrived in (
            (dk, gk, sk, kd, pairs[i][0]),
            (dv, gv, sv, vd, pairs[i][1]),
        ):
            arrived.wait_recv()
            for run in range(4):
                total = grads[run, yl, there].astype(f32) + got[i, run].astype(f32)
                if device is None:
                    out[x, run] = total.astype(bf16)
                else:
                    summed[i, run] = total.astype(bf16)
            if device is not None:
                last.append(wire.send(summed.at[i], out.at[x], device))
    for copy in last:
        copy.wait_recv()
    own.wait()
    wire.drain()


def grads_over_x(dq, dk, dv):
    return remote_call(
        grads_x_kernel,
        "grads_over_x",
        6,
        17,
        1,
        [ANY, VMEM, VMEM],
        [VMEM],
        (shaped((3, 4, 4, 128, 128)),),
        scratch=[
            pltpu.VMEM((4, 4, 128, 128), bf16),
            pltpu.VMEM((4, 4, 128, 128), bf16),
            pltpu.VMEM((3, 4, 128, 128), bf16),
            pltpu.VMEM((3, 4, 128, 128), bf16),
        ],
        vmem=16 << 20,
    )(dq, dk, dv)[0]


def turned(values, cosine, sine):
    return values * cosine + pltpu.roll(values, 64, 1) * sine


def project_kernel(rows, w, cosine, sine, gain, heads, kept):
    flat = jnp.dot(rows[...], w[0], preferred_element_type=f32)
    step = pl.program_id(0)
    for h in range(4):
        head = flat[:, h * HD : (h + 1) * HD]

        @pl.when(step < 2)
        def _():
            kept[0, h] = head
            scaled = head * rms_rows(head) * gain[0]
            heads[0, h] = turned(scaled, cosine[...], sine[...]).astype(bf16)

        @pl.when(step == 2)
        def _():
            heads[0, h] = head.astype(bf16)


def project(rows, w, cosine, sine, gains):
    def fixed(*shape):
        return pl.BlockSpec(shape, lambda i: (0,) * len(shape))

    def two(i):
        return jnp.minimum(i, 1)

    return pl.pallas_call(
        project_kernel,
        name="project",
        grid=(3,),
        out_shape=(shaped((3, 4, 512, HD)), shaped((2, 4, 512, HD), f32)),
        in_specs=[
            fixed(512, 2048),
            pl.BlockSpec((1, 2048, 512), lambda i: (i, 0, 0)),
            fixed(512, HD),
            fixed(512, HD),
            pl.BlockSpec((1, 1, HD), lambda i: (two(i), 0, 0)),
        ],
        out_specs=[
            pl.BlockSpec((1, 4, 512, HD), lambda i: (i, 0, 0, 0)),
            pl.BlockSpec((1, 4, 512, HD), lambda i: (two(i), 0, 0, 0)),
        ],
        compiler_params=pltpu.CompilerParams(vmem_limit_bytes=60 << 20),
    )(rows, w, cosine, sine, gains)


QB = 256
KB = 512
SCALE = HD**-0.5
SCALE2 = SCALE * math.log2(math.e)


def attend_kernel(lim, q, k, v, qseg, qpos, kseg, o_low, o, linv, vext):
    rows = k.shape[0]
    ones = (lax.broadcasted_iota(i32, (KB, HD), 1) == 0).astype(bf16)

    def fill(i, carry):
        at = pl.ds(pl.multiple_of(i * KB, KB), KB)
        vext[at, :HD] = v[at]
        vext[at, HD:] = ones
        return carry

    lax.fori_loop(0, rows // KB, fill, 0)

    def one_query(b, carry):
        at = pl.ds(pl.multiple_of(b * QB, QB), QB)
        query, seg, pos = q[at], qseg[at], qpos[at]

        def one_key(j, acc):
            keys = pl.ds(pl.multiple_of(j * KB, KB), KB)
            score = lax.dot_general(
                query, k[keys], (((1,), (1,)), ((), ())), preferred_element_type=f32
            )
            key_pos = j * KB + lax.broadcasted_iota(i32, (1, KB), 1)
            allowed = (seg == kseg[:, keys]) | (pos == key_pos)
            weight = jnp.where(allowed, jnp.exp2(score * SCALE2), 0.0).astype(bf16)
            return acc + jnp.dot(weight, vext[keys], preferred_element_type=f32)

        acc = lax.fori_loop(lim[0, b], lim[1, b], one_key, jnp.zeros((QB, 2 * HD), f32))
        inverse = 1.0 / acc[:, HD : HD + 1]
        result = acc[:, :HD] * inverse
        o[at] = result
        o_low[at] = result.astype(bf16)
        linv[at] = jnp.broadcast_to(inverse, (QB, HD))
        return carry

    lax.fori_loop(0, q.shape[0] // QB, one_query, 0)


def attend(lim, q, k, v, qseg, qpos, kseg):
    n = q.shape[0]
    return pl.pallas_call(
        attend_kernel,
        name="attend",
        out_shape=(shaped((n, HD)), shaped((n, HD), f32), shaped((n, HD), f32)),
        in_specs=[SMEM] + [VMEM] * 6,
        out_specs=[VMEM] * 3,
        scratch_shapes=[pltpu.VMEM((k.shape[0], 2 * HD), bf16)],
        compiler_params=pltpu.CompilerParams(vmem_limit_bytes=32 << 20),
    )(lim, q, k, v, qseg[:, None], qpos[:, None], kseg[None])


def attend_back_kernel(
    lim, q, k, v, g, qseg, qpos, kseg, linv, delta, dq, dk, dv, kt, dk_acc, dv_acc
):
    rows = k.shape[0]

    def fill(i, carry):
        at = pl.ds(pl.multiple_of(i * KB, KB), KB)
        kt[:, at] = k[at].astype(f32).T.astype(bf16)
        dk_acc[at] = jnp.zeros((KB, HD), f32)
        dv_acc[at] = jnp.zeros((KB, HD), f32)
        return carry

    lax.fori_loop(0, rows // KB, fill, 0)
    across = (((1,), (1,)), ((), ()))

    def one_query(b, carry):
        at = pl.ds(pl.multiple_of(b * QB, QB), QB)
        query, grad = q[at], g[at]
        seg, pos, inverse, shift = qseg[:, at], qpos[:, at], linv[:, at], delta[:, at]

        def one_key(j, acc):
            keys = pl.ds(pl.multiple_of(j * KB, KB), KB)
            key = k[keys]
            score = lax.dot_general(key, query, across, preferred_element_type=f32)
            key_pos = j * KB + lax.broadcasted_iota(i32, (KB, 1), 0)
            allowed = (kseg[keys] == seg) | (key_pos == pos)
            prob = jnp.where(allowed, jnp.exp2(score * SCALE2), 0.0) * inverse
            grad_prob = lax.dot_general(v[keys], grad, across, preferred_element_type=f32)
            grad_score = (prob * (grad_prob - shift)).astype(bf16)
            dv_acc[keys] += jnp.dot(prob.astype(bf16), grad, preferred_element_type=f32)
            dk_acc[keys] += jnp.dot(grad_score, query, preferred_element_type=f32)
            return acc + jnp.dot(kt[:, keys], grad_score, preferred_element_type=f32)

        acc = lax.fori_loop(lim[0, b], lim[1, b], one_key, jnp.zeros((HD, QB), f32))
        dq[at] = (acc * SCALE).T.astype(bf16)
        return carry

    lax.fori_loop(0, q.shape[0] // QB, one_query, 0)

    def finish(i, carry):
        at = pl.ds(pl.multiple_of(i * KB, KB), KB)
        dk[at] = (dk_acc[at] * SCALE).astype(bf16)
        dv[at] = dv_acc[at].astype(bf16)
        return carry

    lax.fori_loop(0, rows // KB, finish, 0)


def attend_back(lim, q, k, v, g, qseg, qpos, kseg, linv, delta):
    n, rows = q.shape[0], k.shape[0]
    return pl.pallas_call(
        attend_back_kernel,
        name="attend_back",
        out_shape=(shaped((n, HD)), shaped((rows, HD)), shaped((rows, HD))),
        in_specs=[SMEM] + [VMEM] * 9,
        out_specs=[VMEM] * 3,
        scratch_shapes=[
            pltpu.VMEM((HD, rows), bf16),
            pltpu.VMEM((rows, HD), f32),
            pltpu.VMEM((rows, HD), f32),
        ],
        compiler_params=pltpu.CompilerParams(vmem_limit_bytes=40 << 20),
    )(lim, q, k, v, g, qseg[None], qpos[None], kseg[:, None], linv[None], delta[None])


SPREAD_SENDS = 26


def spread_steps(p, wire, sems, src, dst):
    yh, co, yl, x = p.yh, p.co, p.yl, p.x
    (rh, rl), (lh, ll), (oh, ol) = ((y // 2, lax.rem(y, 2)) for y in (p.yr, p.ylf, p.yo))
    A, A1, A2 = pl.ds(0, 64), pl.ds(0, 32), pl.ds(32, 32)
    B, B1, B2 = pl.ds(64, 64), pl.ds(64, 32), pl.ds(96, 32)
    src, dst = View(src), View(dst)
    own = local(src, dst.at[yh, co, yl, x], sems, 0)

    def both(ref, device):
        return wire.send(ref, ref, device)

    me = dst.at[yh, co, yl]
    a1 = wire.send(src.at[A], me.at[x, A], p.XR)
    b1 = wire.send(src.at[B], me.at[x, B], p.YR)
    a2 = wire.send(src.at[A], me.at[x, A], p.XL)
    b2 = wire.send(src.at[B], me.at[x, B], p.YL)
    yield
    a1.wait_recv()
    a3 = both(me.at[p.xl, A1], p.XR)
    a2.wait_recv()
    a4 = both(me.at[p.xr, A2], p.XL)
    b1.wait_recv()
    b3 = both(dst.at[lh, co, ll, x, B1], p.YR)
    b2.wait_recv()
    b4 = both(dst.at[rh, co, rl, x, B2], p.YL)
    yield
    own.wait()
    a3.wait_recv()
    a4.wait_recv()
    a5 = both(me.at[:, A], p.YR)
    a6 = both(me.at[:, A], p.YL)
    b3.wait_recv()
    b4.wait_recv()
    b5 = both(dst.at[:, co, :, x, B], p.XR)
    b6 = both(dst.at[:, co, :, x, B], p.XL)
    last = [both(me.at[:, A], p.C), both(dst.at[:, co, :, x, B], p.C)]
    yield
    a5.wait_recv()
    a7 = both(dst.at[lh, co, ll, :, A1], p.YR)
    b5.wait_recv()
    b7 = both(dst.at[:, co, :, p.xl, B1], p.XR)
    a6.wait_recv()
    a8 = both(dst.at[rh, co, rl, :, A2], p.YL)
    b6.wait_recv()
    b8 = both(dst.at[:, co, :, p.xr, B2], p.XL)
    last += [both(dst.at[lh, co, ll, :, A], p.C), both(dst.at[:, co, :, p.xl, B], p.C)]
    last += [both(dst.at[rh, co, rl, :, A], p.C), both(dst.at[:, co, :, p.xr, B], p.C)]
    yield
    a7.wait_recv()
    last.append(both(dst.at[oh, co, ol, :, A1], p.C))
    b7.wait_recv()
    last.append(both(dst.at[:, co, :, p.xo, B1], p.C))
    a8.wait_recv()
    last.append(both(dst.at[oh, co, ol, :, A2], p.C))
    b8.wait_recv()
    last.append(both(dst.at[:, co, :, p.xo, B2], p.C))
    yield
    for copy in last:
        copy.wait_recv()
    wire.drain()
    yield


def greet_plane(p):
    greet([p.XR, p.XL, p.YR, p.YL, p.C])


def spread_kernel(src, dst, ss, rs, ls):
    p = Place()
    greet_plane(p)
    for _ in spread_steps(p, Wire(ss, rs), ls, src, dst):
        pass


def spread(src, cid):
    width = src.shape[1]
    return remote_call(
        spread_kernel,
        "spread",
        cid,
        SPREAD_SENDS,
        1,
        [ANY],
        [ANY],
        (shaped((2, 2, 2, 4, 128, width)),),
    )(src)[0].reshape(32, 128, width)


def at_step(number, *stages):
    for step, stage in stages:

        @pl.when(number == step)
        def _():
            next(stage)


def block(shape, index):
    return pl.BlockSpec(shape, index)


def nt(a, b):
    return lax.dot_general(a, b, (((1,), (1,)), ((), ())), preferred_element_type=f32)


def tn(a, b):
    return lax.dot_general(a, b, (((0,), (0,)), ((), ())), preferred_element_type=f32)


PARTS = 4


def forward_kernel(src, rows, w_in, w_out, dst, gate, up, hidden, y, ss, rs, ls):
    p = Place()
    greet_plane(p)
    moving = spread_steps(p, Wire(ss, rs), ls, src, dst)
    next(moving)
    n = rows.shape[1]
    cut = FF // PARTS

    def first(rows, w_gate, w_up, gate, up, hidden):
        at_step(pl.program_id(0) * PARTS + pl.program_id(1), (2, moving), (4, moving))
        g = jnp.dot(rows[0], w_gate[0], preferred_element_type=f32)
        u = jnp.dot(rows[0], w_up[0], preferred_element_type=f32)
        gate[0] = g.astype(bf16)
        up[0] = u.astype(bf16)
        hidden[0] = (g * jax.nn.sigmoid(g) * u).astype(bf16)

    out = block((1, n, cut), lambda e, j: (e, 0, j))
    pltpu.emit_pipeline(
        first,
        grid=(EXP_DEV, PARTS),
        in_specs=[
            block((1, n, 2048), lambda e, j: (e, 0, 0)),
            block((1, 2048, cut), lambda e, j: (e, 0, j)),
            block((1, 2048, cut), lambda e, j: (e, 0, j + PARTS)),
        ],
        out_specs=[out, out, out],
    )(rows, w_in, w_in, gate, up, hidden)

    def second(hidden, w, y):
        at_step(pl.program_id(0) * PARTS + pl.program_id(1), (3, moving))
        y[0] = nt(hidden[0], w[0]).astype(bf16)

    pltpu.emit_pipeline(
        second,
        grid=(EXP_DEV, PARTS),
        in_specs=[
            block((1, n, FF), lambda e, j: (e, 0, 0)),
            block((1, 2048 // PARTS, FF), lambda e, j: (e, j, 0)),
        ],
        out_specs=[block((1, n, 2048 // PARTS), lambda e, j: (e, 0, j))],
    )(hidden, w_out, y)
    for _ in moving:
        pass


def expert_forward(src, rows, w_in, w_out, cid):
    n, width = rows.shape[1:]
    outs = remote_call(
        forward_kernel,
        "expert_forward",
        cid,
        SPREAD_SENDS,
        1,
        [ANY] * 4,
        [ANY] * 5,
        (shaped((2, 2, 2, 4, 128, width)),)
        + (shaped((EXP_DEV, n, FF)),) * 3
        + (shaped((EXP_DEV, n, width)),),
        vmem=48 << 20,
    )(src, rows, w_in, w_out)
    return outs[0].reshape(32, 128, width), *outs[1:]


def slot_hits(table, count, rows_down):
    shape = (count * 2 * CAP, 256) if rows_down else (256, count * 2 * CAP)
    line = lax.broadcasted_iota(i32, shape, 0 if rows_down else 1)
    block = lax.broadcasted_iota(i32, shape, 1 if rows_down else 0) // 128
    expert = line // (2 * CAP)
    want = line - expert * (2 * CAP) - block * CAP

    def spread_out(first):
        value = jnp.zeros(shape, f32)
        for e in range(count):
            c = first + e
            at = table[c : c + 1] if rows_down else table[:, c : c + 1]
            value = jnp.where(expert == e, at, value)
        return value

    hit = (spread_out(0).astype(i32) == want) & (want >= 0) & (want < CAP)
    return hit, spread_out(count)


def pick_kernel(gated, sel, info, src, rows_out, *gates_out):
    for pair in range(src.shape[0] // 256):
        at = slice(pair * 256, (pair + 1) * 256)
        hit, gate = slot_hits(nt(sel[...], info[at]), EXP_DEV, True)
        rows = jnp.dot(hit.astype(bf16), src[at], preferred_element_type=f32).astype(bf16)
        for e in range(EXP_DEV):
            rows_out[e, pair] = rows[e * 2 * CAP : (e + 1) * 2 * CAP]
        if gated:
            total = jnp.sum(jnp.where(hit, gate, 0.0), axis=1, keepdims=True)
            total = jnp.broadcast_to(total, (EXP_DEV * 2 * CAP, 128))
            for e in range(EXP_DEV):
                gates_out[0][e, pair] = total[e * 2 * CAP : (e + 1) * 2 * CAP]


def pick_rows(sel, info, src, width, gated):
    pairs, step = src.shape[0] // 256, 2

    def spec(lanes):
        return pl.BlockSpec((EXP_DEV, step, 2 * CAP, lanes), lambda i: (0, i, 0, 0))

    shapes = [shaped((EXP_DEV, pairs, 2 * CAP, width)), shaped((EXP_DEV, pairs, 2 * CAP, 128), f32)]
    specs = [spec(width), spec(128)]
    return pl.pallas_call(
        functools.partial(pick_kernel, gated),
        name="pick_rows",
        grid=(pairs // step,),
        out_shape=shapes[: 1 + gated],
        in_specs=[
            pl.BlockSpec((8, 128), lambda i: (0, 0)),
            pl.BlockSpec((256 * step, 128), lambda i: (i, 0)),
            pl.BlockSpec((256 * step, width), lambda i: (i, 0)),
        ],
        out_specs=specs[: 1 + gated],
        compiler_params=pltpu.CompilerParams(vmem_limit_bytes=60 << 20),
    )(sel, info, src)


HOME_SENDS = 20


def home_scratch(width):
    return [
        pltpu.VMEM((2, 4, 8 * CAP, width), bf16),
        pltpu.VMEM((2, 2, 4, 128, width), bf16),
        pltpu.VMEM((2, 2, 64, width), bf16),
        pltpu.VMEM((2, 2, 64, width), bf16),
        pltpu.VMEM((2, 4, 64, width), bf16),
        pltpu.VMEM((2, 2, 2, 64, width), bf16),
        pltpu.VMEM((2, 2, 32, width), bf16),
        pltpu.VMEM((2, 2, 64, width), bf16),
    ]


def home_steps(p, wire, sems, gated, sel, info, rows, more, out, cat, q, a1, b1, a2, b2, c1, c2):
    yh, co, yl, x = p.yh, p.co, p.yl, p.x
    ys = [(yy // 2, lax.rem(yy, 2)) for yy in (p.yr, p.ylf, p.yo)]
    (rh, rl), (lh, ll), (oh, ol) = ys
    pieces = [(View(rows), slice(0, 2048))]
    if more is not None:
        pieces.append((View(more), slice(2048, 2048 + 128)))
    rows, out, whole_q, whole_cat = View(rows), View(out), q, cat
    width = cat.shape[-1]
    q, cat, a1, b1, a2, b2, c1, c2 = (View(ref) for ref in (q, cat, a1, b1, a2, b2, c1, c2))
    own, first = [], []
    for e in range(EXP_DEV):
        lines = pl.ds(e * 2 * CAP, 2 * CAP)
        there = pl.ds((2 + e) * 2 * CAP, 2 * CAP)
        for piece, lanes in pieces:
            first.append(wire.send(piece.at[e, :, 1 - co], cat.at[:, :, there, lanes], p.C))
            own.append(local(piece.at[e, :, co], cat.at[:, :, lines, lanes], sems, len(own)))
    yield
    for copy in own:
        copy.wait()
    for copy in first:
        copy.wait_recv()

    def place(h, pair):
        block = h * 16 + co * 8 + pair * 2
        both = jnp.concatenate([info[block], info[block + 1]], axis=0)
        table = lax.dot_general(
            both, sel[...], (((1,), (1,)), ((), ())), preferred_element_type=f32
        )
        hit, gate = slot_hits(table, 4, False)
        value = jnp.where(hit, gate if gated else 1.0, 0.0).astype(bf16)
        for c in range(0, width, 512):
            lanes = slice(c, min(c + 512, width))
            total = jnp.dot(
                value, whole_cat[h, pair, :, lanes], preferred_element_type=f32
            ).astype(bf16)
            at = lax.rem(pair, 2) * 2
            whole_q[h, pair // 2, at, :, lanes] = total[:128]
            whole_q[h, pair // 2, at + 1, :, lanes] = total[128:]

    def far_y(k, carry):
        place(oh, ol * 2 + k)
        return carry

    def nearer(half):
        def one(k, carry):
            y = lax.rem(yh * 2 + yl + k + k // 2, 4)
            place(y // 2, lax.rem(y, 2) * 2 + half)
            return carry

        lax.fori_loop(0, 3, one, 0)

    A, B = pl.ds(0, 64), pl.ds(64, 64)
    lax.fori_loop(0, 2, far_y, 0)
    s1 = [
        wire.send(q.at[oh, ol, 0:2, A], a1.at[0], p.YR),
        wire.send(q.at[oh, ol, 2:4, A], a1.at[1], p.YL),
    ]
    nearer(p.xo // 2)
    s1.insert(1, wire.send(q.at[0, :, p.xo, B], b1.at[0], p.XR))
    s1.append(wire.send(q.at[1, :, p.xo, B], b1.at[1], p.XL))
    nearer(1 - p.xo // 2)
    yield

    def add(dst, *srcs):
        total = srcs[0].load().astype(f32)
        for src in srcs[1:]:
            total = total + src.load().astype(f32)
        dst.store(total)

    def loop(count, body):
        def step(i, carry):
            body(i)
            return carry

        lax.fori_loop(0, count, step, 0)

    def plus(dst, src):
        add(dst, dst, src)

    s2 = []
    s1[0].wait_recv()
    loop(2, lambda i: plus(q.at[rh, rl, i, A], a1.at[0, i]))
    s2.append(wire.send(q.at[rh, rl, :, A], a2.at[0], p.YR))
    s1[1].wait_recv()
    loop(2, lambda i: plus(q.at[0, i, p.xr, B], b1.at[0, i]))
    s2.append(wire.send(q.at[:, :, p.xr, B], b2.at[0], p.XR))
    s1[2].wait_recv()
    loop(2, lambda i: plus(q.at[lh, ll, 2 + i, A], a1.at[1, i]))
    s2.append(wire.send(q.at[lh, ll, :, A], a2.at[1], p.YL))
    s1[3].wait_recv()
    loop(2, lambda i: plus(q.at[1, i, p.xl, B], b1.at[1, i]))
    s2.append(wire.send(q.at[:, :, p.xl, B], b2.at[1], p.XL))
    yield
    for copy in s2:
        copy.wait_recv()
    loop(4, lambda i: add(q.at[yh, yl, i, A], q.at[yh, yl, i, A], a2.at[0, i], a2.at[1, i]))
    s3 = [
        wire.send(q.at[yh, yl, p.xo, 0:32], c1.at[0, 0], p.XR),
        wire.send(q.at[yh, yl, p.xo, 32:64], c1.at[0, 1], p.XL),
    ]
    for h in range(2):
        loop(2, lambda i: add(q.at[h, i, x, B], q.at[h, i, x, B], b2.at[0, h, i], b2.at[1, h, i]))
    s3 += [
        wire.send(q.at[oh, ol, x, 64:96], c1.at[1, 0], p.YR),
        wire.send(q.at[oh, ol, x, 96:128], c1.at[1, 1], p.YL),
    ]
    yield
    s4 = []
    s3[0].wait_recv()
    plus(q.at[yh, yl, p.xr, 0:32], c1.at[0, 0])
    s4.append(wire.send(q.at[yh, yl, p.xr, A], c2.at[0, 0], p.XR))
    s3[1].wait_recv()
    plus(q.at[yh, yl, p.xl, 32:64], c1.at[0, 1])
    s4.append(wire.send(q.at[yh, yl, p.xl, A], c2.at[0, 1], p.XL))
    s3[2].wait_recv()
    plus(q.at[rh, rl, x, 64:96], c1.at[1, 0])
    s4.append(wire.send(q.at[rh, rl, x, B], c2.at[1, 0], p.YR))
    s3[3].wait_recv()
    plus(q.at[lh, ll, x, 96:128], c1.at[1, 1])
    s4.append(wire.send(q.at[lh, ll, x, B], c2.at[1, 1], p.YL))
    yield
    for copy in s4:
        copy.wait_recv()
    add(out.at[0:64], q.at[yh, yl, x, A], c2.at[0, 0], c2.at[0, 1])
    add(out.at[64:128], q.at[yh, yl, x, B], c2.at[1, 0], c2.at[1, 1])
    wire.drain()
    yield


def by_place(rows):
    return rows.reshape(EXP_DEV, 2, 2, 4, 2 * CAP, -1)


def backward_kernel(
    sel, info, y_places, y, cot, gate, up, hidden, row_gates, w_in, w_out,
    mixture, dots, dgate, dup, drows, term, ss, rs, ls, *scratch,
):
    p = Place()
    greet_plane(p)
    moving = home_steps(p, Wire(ss, rs), ls, True, sel, info, y_places, None, mixture, *scratch)
    next(moving)
    n = cot.shape[1]
    wide, cut = 2048 // PARTS, FF // PARTS
    dots[...] = jnp.zeros_like(dots)

    def number():
        return pl.program_id(0) * PARTS + pl.program_id(1)

    def first(y, cot, hidden, row_gates, term):
        at_step(number(), (3, moving))
        e = pl.program_id(0)
        product = y[0].astype(f32) * cot[0].astype(f32)
        partial = product[:, :128]
        for c in range(128, wide, 128):
            partial += product[:, c : c + 128]
        dots[e] += partial
        scaled = (hidden[0].astype(f32) * row_gates[0, :, :1]).astype(bf16)
        term[0] = tn(cot[0], scaled).astype(bf16)

    part = block((1, n, wide), lambda e, j: (e, 0, j))
    whole = block((1, n, FF), lambda e, j: (e, 0, 0))
    gates = block((1, n, 128), lambda e, j: (e, 0, 0))
    pltpu.emit_pipeline(
        first,
        grid=(EXP_DEV, PARTS),
        in_specs=[part, part, whole, gates],
        out_specs=[block((1, wide, FF), lambda e, j: (e, j, 0))],
    )(y, cot, hidden, row_gates, term)

    def second(cot, w, row_gates, gate, up, dgate, dup):
        at_step(number(), (3, moving))
        dhidden = jnp.dot(cot[0], w[0], preferred_element_type=f32) * row_gates[0, :, :1]
        g, u = gate[0].astype(f32), up[0].astype(f32)
        sg = jax.nn.sigmoid(g)
        dgate[0] = (dhidden * u * sg * (1.0 + g * (1.0 - sg))).astype(bf16)
        dup[0] = (dhidden * g * sg).astype(bf16)

    out = block((1, n, cut), lambda e, j: (e, 0, j))
    pltpu.emit_pipeline(
        second,
        grid=(EXP_DEV, PARTS),
        in_specs=[
            block((1, n, 2048), lambda e, j: (e, 0, 0)),
            block((1, 2048, cut), lambda e, j: (e, 0, j)),
            gates,
            out,
            out,
        ],
        out_specs=[out, out],
    )(cot, w_out, row_gates, gate, up, dgate, dup)

    def third(dgate, dup, w, drows):
        at_step(number(), (5, moving), (7, moving))
        total = nt(dgate[0], w[0, :, :FF]) + nt(dup[0], w[0, :, FF:])
        drows[0] = total.astype(bf16)

    pltpu.emit_pipeline(
        third,
        grid=(EXP_DEV, PARTS),
        in_specs=[whole, whole, block((1, wide, 2 * FF), lambda e, j: (e, j, 0))],
        out_specs=[part],
    )(dgate, dup, w_in, drows)
    for _ in moving:
        pass


def expert_backward(sel, info, y, cot, gate, up, hidden, row_gates, w_in, w_out, cid):
    n = cot.shape[1]
    half = shaped((EXP_DEV, n, FF))
    return remote_call(
        backward_kernel,
        "expert_backward",
        cid,
        HOME_SENDS,
        2,
        [VMEM, VMEM] + [ANY] * 9,
        [VMEM, VMEM] + [ANY] * 4,
        (
            shaped((128, 2048), f32),
            shaped((EXP_DEV, n, 128), f32),
            half,
            half,
            shaped((EXP_DEV, n, 2048)),
            shaped((EXP_DEV, 2048, FF)),
        ),
        scratch=home_scratch(2048),
        vmem=58 << 20,
    )(sel, info, by_place(y), y, cot, gate, up, hidden, row_gates, w_in, w_out)


def finish_kernel(sel, info, places, more, rows, dgate, dup, home, term, ss, rs, ls, *scratch):
    p = Place()
    greet_plane(p)
    moving = home_steps(p, Wire(ss, rs), ls, False, sel, info, places, more, home, *scratch)
    next(moving)
    n = rows.shape[1]
    wide = 2048 // PARTS

    def first(rows, dgate, dup, term):
        at_step(
            pl.program_id(0) * PARTS + pl.program_id(1), (2, moving), (7, moving)
        )
        term[0, :, :FF] = tn(rows[0], dgate[0]).astype(bf16)
        term[0, :, FF:] = tn(rows[0], dup[0]).astype(bf16)

    whole = block((1, n, FF), lambda e, j: (e, 0, 0))
    pltpu.emit_pipeline(
        first,
        grid=(EXP_DEV, PARTS),
        in_specs=[block((1, n, wide), lambda e, j: (e, 0, j)), whole, whole],
        out_specs=[block((1, wide, 2 * FF), lambda e, j: (e, j, 0))],
    )(rows, dgate, dup, term)
    for _ in moving:
        pass


def expert_finish(sel, info, drows, more, rows, dgate, dup, cid):
    return remote_call(
        finish_kernel,
        "expert_finish",
        cid,
        HOME_SENDS,
        4,
        [VMEM, VMEM] + [ANY] * 5,
        [VMEM, ANY],
        (shaped((128, 2048 + 128), f32), shaped((EXP_DEV, 2048, 2 * FF))),
        scratch=home_scratch(2048 + 128),
        vmem=58 << 20,
    )(sel, info, by_place(drows), by_place(more), rows, dgate, dup)


def unstack_kernel(grads, out, held, sems):
    e, j, steps = pl.program_id(0), pl.program_id(1), pl.num_programs(1)
    step = e * steps + j
    count = grads.shape[1]

    def copy(at):
        slot = lax.rem(at, 2)
        rows = pl.ds(pl.multiple_of(lax.rem(at, steps) * count, count), count)
        return pltpu.make_async_copy(held.at[slot], out.at[rows, at // steps], sems.at[slot])

    @pl.when(step >= 2)
    def _():
        copy(step - 2).wait()

    held[lax.rem(step, 2)] = grads[0].astype(f32)
    copy(step).start()

    @pl.when(step == EXP_DEV * steps - 1)
    def _():
        copy(step - 1).wait()
        copy(step).wait()


def unstack(grads):
    experts, rows, cols = grads.shape
    count = 128
    return pl.pallas_call(
        unstack_kernel,
        name="unstack",
        grid=(experts, rows // count),
        out_shape=shaped((rows, experts, cols), f32),
        in_specs=[pl.BlockSpec((1, count, cols), lambda e, j: (e, j, 0))],
        out_specs=ANY,
        scratch_shapes=[pltpu.VMEM((2, count, cols), f32), DMA((2,))],
        compiler_params=pltpu.CompilerParams(vmem_limit_bytes=60 << 20),
    )(grads)


def last_kernel(
    grads, kept, w, rows, cosine, sine, gain, p3, unit, small, out, normed, whole, tiny, ss, rs, ls,
    flat, total, w_grads, part, got_c, got_h, half, mine,
    ra, rb, rc, rd, re, rf, rg, acc_x, acc_y, sz, az, sx, ax, sy, ay, sc, ac, sh,
    tz, tx, ty, tc, th,
):
    p = Place()
    dp, yl, x = p.dp, p.yl, p.x
    greet([p.ZR, p.ZL, p.ZO, p.XR, p.XL, p.XO, p.Y, p.C, p.H])
    wire = Wire(ss, rs)
    p0, p1, p2 = (w_grads.at[i] for i in range(3))

    def added(dst, *srcs):
        total = srcs[0][...].astype(f32)
        for src in srcs[1:]:
            total = total + src[...].astype(f32)
        dst[...] = total.astype(dst.dtype)

    def loop(count, body):
        def step(i, carry):
            body(i)
            return carry

        lax.fori_loop(0, count, step, 0)

    def y_first(i, part):
        return wire.send(part.at[:, 1 - yl], rb.at[i - 2], p.Y)

    firsts = {3: y_first(3, p3)}
    far_z = ((p.zo, p.ZO), (p.zr, p.ZR), (p.zl, p.ZL))
    far_x = ((p.xo, p.XO), (p.xr, p.XR), (p.xl, p.XL))
    zs_out = [wire.send(small.at[there], sz.at[i], dev) for i, (there, dev) in enumerate(far_z)]
    mine[...] = jnp.zeros_like(mine)
    starts = []
    for i in range(3):
        if i < 2:
            gained = jnp.zeros((1, HD), f32)
            for h in range(4):
                grad = turned(grads[i, h].astype(f32), cosine[...], -sine[...])
                head = kept[i, h]
                inverse = rms_rows(head)
                gained += jnp.sum(grad * head * inverse, axis=0, keepdims=True)
                back = rms_back(head, inverse, grad * gain[i])
                flat[:, h * HD : (h + 1) * HD] = back.astype(bf16)
            mine[0, 16 + i : 17 + i] = gained
        else:
            for h in range(4):
                flat[:, h * HD : (h + 1) * HD] = grads[i, h]

        def weight_rows(c, carry):
            cols = pl.ds(pl.multiple_of(c * 512, 512), 512)
            grad = tn(rows[:, cols], flat[...]).astype(bf16)
            w_grads[i, c] = grad.reshape(2, 4, 64, 512)
            return carry

        lax.fori_loop(0, 4, weight_rows, 0)
        if i < 2:
            gradient = w_grads.at[i]
            starts.append(
                (
                    wire.send(gradient.at[0:2, :, p.xo], ra.at[i, 0], p.XR),
                    wire.send(gradient.at[2:4, :, p.xo], ra.at[i, 1], p.XL),
                )
            )
        else:
            firsts[2] = y_first(2, p2)

        def normed_cols(c, carry):
            cols = pl.ds(pl.multiple_of(c * 512, 512), 512)
            value = nt(flat[...], w[i, cols])
            if i > 0:
                value += total[:, cols]
            if i < 2:
                total[:, cols] = value
            else:
                part[:, :, cols] = value.astype(bf16).reshape(4, 128, 512)
            return carry

        lax.fori_loop(0, 4, normed_cols, 0)
        if i == 0:
            for copy in zs_out:
                copy.wait_recv()
            for y in range(2):
                az[y] = small[dp, y] + sz[0, y] + sz[1, y] + sz[2, y]
            xs_out = [
                wire.send(az.at[:, there], sx.at[n], dev) for n, (there, dev) in enumerate(far_x)
            ]
        elif i == 1:
            for copy in xs_out:
                copy.wait_recv()
            ax[...] = az[:, x] + sx[0] + sx[1] + sx[2]
            y_out = wire.send(ax.at[1 - yl], sy, p.Y)
        else:
            y_out.wait_recv()
            ay[...] = ax[yl] + sy[...]
            c_out = wire.send(ay, sc, p.C)
    mine_head, other = p.yh * 2 + (1 - p.co), (1 - p.yh) * 2 + (1 - p.co)
    far = wire.send(part.at[other], got_c.at[0], p.C)
    near = wire.send(part.at[mine_head], got_c.at[1], p.C)
    far.wait_recv()

    def by_16(body):
        def step(i, carry):
            body(pl.ds(pl.multiple_of(i * 16, 16), 16))
            return carry

        lax.fori_loop(0, 8, step, 0)

    def add_far(at):
        away = part[(1 - p.yh) * 2 + p.co, at].astype(f32)
        half[at] = (away + got_c[0, at].astype(f32)).astype(bf16)

    by_16(add_far)
    over = wire.send(half, got_h, p.H)
    c_out.wait_recv()
    ac[...] = ay[...] + sc[...]
    h_out = wire.send(ac, sh, p.H)
    seconds = []
    for i, gradient in ((0, p0), (1, p1)):
        one, two = starts[i]
        one.wait_recv()
        loop(2, lambda d: added(gradient.at[d, :, p.xr], gradient.at[d, :, p.xr], ra.at[i, 0, d]))
        s1 = wire.send(gradient.at[:, :, p.xr], rc.at[i, 0], p.XR)
        two.wait_recv()
        loop(
            2,
            lambda d: added(gradient.at[d + 2, :, p.xl], gradient.at[d + 2, :, p.xl], ra.at[i, 1, d]),
        )
        s2 = wire.send(gradient.at[:, :, p.xl], rc.at[i, 1], p.XL)
        seconds.append((s1, s2))
    mids = {}
    for i, gradient in ((3, p3), (2, p2)):
        firsts[i].wait_recv()
        loop(4, lambda d: added(acc_y.at[i - 2, d], gradient.at[d, yl], rb.at[i - 2, d]))
        acc = acc_y.at[i - 2]
        mids[i] = (
            wire.send(acc.at[0:2, p.xo], rd.at[i - 2, 0], p.XR),
            wire.send(acc.at[2:4, p.xo], rd.at[i - 2, 1], p.XL),
        )
    near.wait_recv()
    over.wait_recv()

    def add_near(at):
        close = part[p.yh * 2 + p.co, at].astype(f32) + got_c[1, at].astype(f32)
        normed[at] = close + got_h[at].astype(f32)

    by_16(add_near)
    for c in range(16):
        cols = slice(c * 128, (c + 1) * 128)
        column = jnp.sum(normed[:, cols] * unit[:, cols], axis=0, keepdims=True)
        mine[0, c : c + 1] = column
    h_out.wait_recv()
    whole[dp, yl, x] = ac[...] + sh[...]
    y_all = wire.send(whole.at[dp, yl, x], whole.at[dp, yl, x], p.Y)
    tz_out = [wire.send(mine.at[0], tz.at[dp], dev) for _, dev in far_z]
    tz[dp] = mine[0]
    yends = []
    for i, gradient in ((0, p0), (1, p1)):
        for s in seconds[i]:
            s.wait_recv()
        acc = acc_x.at[i]
        loop(4, lambda d: added(acc.at[d], gradient.at[d, :, x], rc.at[i, 0, d], rc.at[i, 1, d]))
        yends.append(wire.send(acc.at[:, 1 - yl], re.at[i], p.Y))
    y_all.wait_recv()
    x_all = [wire.send(whole.at[dp, :, x], whole.at[dp, :, x], dev) for _, dev in far_x]
    for copy in tz_out:
        copy.wait_recv()
    mine[1] = tz[0] + tz[1] + tz[2] + tz[3]
    tx_out = [wire.send(mine.at[1], tx.at[x], dev) for _, dev in far_x]
    tx[x] = mine[1]
    xends = {}
    for i in (3, 2):
        acc = acc_y.at[i - 2]
        one, two = mids[i]
        one.wait_recv()
        loop(2, lambda d: added(acc.at[d, p.xr], acc.at[d, p.xr], rd.at[i - 2, 0, d]))
        s1 = wire.send(acc.at[:, p.xr], rf.at[i - 2, 0], p.XR)
        two.wait_recv()
        loop(2, lambda d: added(acc.at[d + 2, p.xl], acc.at[d + 2, p.xl], rd.at[i - 2, 1, d]))
        s2 = wire.send(acc.at[:, p.xl], rf.at[i - 2, 1], p.XL)
        xends[i] = (s1, s2)
    for copy in x_all:
        copy.wait_recv()
    z_all = [wire.send(whole.at[dp], whole.at[dp], dev) for _, dev in far_z]
    for copy in tx_out:
        copy.wait_recv()
    mine[2] = tx[0] + tx[1] + tx[2] + tx[3]
    ty_out = wire.send(mine.at[2], ty, p.Y)
    parts, zs = {}, {}

    def z_first(i, acc):
        parts[i] = acc
        zs[i] = (
            wire.send(acc.at[p.zo, 0:32], rg.at[i, 0, 0:32], p.ZR),
            wire.send(acc.at[p.zo, 32:64], rg.at[i, 1, 0:32], p.ZL),
        )

    for i in (0, 1):
        yends[i].wait_recv()
        acc = acc_x.at[i]
        loop(4, lambda d: added(acc.at[d, yl], acc.at[d, yl], re.at[i, d]))
        z_first(i, acc.at[:, yl])
    ty_out.wait_recv()
    mine[3] = mine[2] + ty[...]
    tc_out = wire.send(mine.at[3], tc, p.C)
    for i in (3, 2):
        for s in xends[i]:
            s.wait_recv()
        acc = acc_y.at[i - 2]
        loop(
            4, lambda d: added(acc.at[d, x], acc.at[d, x], rf.at[i - 2, 0, d], rf.at[i - 2, 1, d])
        )
        z_first(i, acc.at[:, x])
    tc_out.wait_recv()
    mine[4] = mine[3] + tc[...]
    th_out = wire.send(mine.at[4], th, p.H)
    ends = {}
    for i in (0, 1, 3, 2):
        one, two = zs[i]
        acc = parts[i]
        one.wait_recv()
        added(acc.at[p.zr, 0:32], acc.at[p.zr, 0:32], rg.at[i, 0, 0:32])
        s1 = wire.send(acc.at[p.zr], rg.at[i, 2], p.ZR)
        two.wait_recv()
        added(acc.at[p.zl, 32:64], acc.at[p.zl, 32:64], rg.at[i, 1, 0:32])
        s2 = wire.send(acc.at[p.zl], rg.at[i, 3], p.ZL)
        ends[i] = (s1, s2)
    th_out.wait_recv()
    tiny[...] = mine[4] + th[...]
    for i in range(4):
        for s in ends[i]:
            s.wait_recv()
        added(out.at[i], parts[i].at[dp], rg.at[i, 2], rg.at[i, 3])
    for copy in z_all:
        copy.wait_recv()
    wire.drain()


def last_sums(grads, kept, w, rows, cosine, sine, gains, fourth, unit, small):
    return remote_call(
        last_kernel,
        "last_sums",
        8,
        64,
        1,
        [VMEM] * 10,
        [VMEM] * 4,
        (
            shaped((4, 64, 512), f32),
            shaped((128, 2048), f32),
            shaped((4, 2, 4, 40, 128), f32),
            shaped((24, 128), f32),
        ),
        scratch=[
            pltpu.VMEM((512, 512), bf16),
            pltpu.VMEM((512, 2048), f32),
            pltpu.VMEM((3, 4, 2, 4, 64, 512), bf16),
            pltpu.VMEM((4, 128, 2048), bf16),
            pltpu.VMEM((2, 128, 2048), bf16),
            pltpu.VMEM((128, 2048), bf16),
            pltpu.VMEM((128, 2048), bf16),
            pltpu.VMEM((5, 24, 128), f32),
            pltpu.VMEM((2, 2, 2, 2, 64, 512), bf16),
            pltpu.VMEM((2, 4, 4, 64, 512), bf16),
            pltpu.VMEM((2, 2, 4, 2, 64, 512), bf16),
            pltpu.VMEM((2, 2, 2, 64, 512), bf16),
            pltpu.VMEM((2, 4, 64, 512), bf16),
            pltpu.VMEM((2, 2, 4, 64, 512), bf16),
            pltpu.VMEM((4, 4, 64, 512), bf16),
            pltpu.VMEM((2, 4, 2, 64, 512), bf16),
            pltpu.VMEM((2, 4, 4, 64, 512), bf16),
            pltpu.VMEM((3, 2, 4, 40, 128), f32),
            pltpu.VMEM((2, 4, 40, 128), f32),
            pltpu.VMEM((3, 2, 40, 128), f32),
            pltpu.VMEM((2, 40, 128), f32),
            pltpu.VMEM((40, 128), f32),
            pltpu.VMEM((40, 128), f32),
            pltpu.VMEM((40, 128), f32),
            pltpu.VMEM((40, 128), f32),
            pltpu.VMEM((40, 128), f32),
            pltpu.VMEM((4, 24, 128), f32),
            pltpu.VMEM((4, 24, 128), f32),
            pltpu.VMEM((24, 128), f32),
            pltpu.VMEM((24, 128), f32),
            pltpu.VMEM((24, 128), f32),
        ],
        vmem=60 << 20,
    )(
        grads, kept, w, rows, cosine, sine, gains,
        fourth.reshape(4, 2, 4, 64, 512), unit, small.reshape(4, 2, 4, 40, 128),
    )


def on_device(
    tokens,
    segment_ids,
    valid_mask,
    routes,
    attn_gain,
    w_query,
    w_key,
    w_value,
    w_out,
    query_gain,
    key_gain,
    ffn_gain,
    router,
    expert_in,
    expert_out,
    cotangent,
):
    blk = lax.axis_index("blk")
    device = lax.axis_index("head") * 8 + blk
    yl = blk // 4
    tok, width = tokens.shape
    full_in = lax.all_gather(jnp.transpose(expert_in, (1, 0, 2)), "dp", axis=1, tiled=True)
    full_back = lax.all_gather(jnp.transpose(expert_out, (1, 0, 2)), "dp", axis=1, tiled=True)

    segment, valid = segment_ids[0], valid_mask[0]
    seq_len = segment.shape[0]
    place = jnp.arange(seq_len, dtype=i32)
    query_ids = (jnp.arange(4)[:, None] * 1024 + blk * 128 + jnp.arange(128)[None]).reshape(-1)
    frequency = rope_base ** (-jnp.arange(64, dtype=f32) / 64)
    angles = query_ids.astype(f32)[:, None] * frequency[None]
    cosine, sine = jnp.cos(angles), jnp.sin(angles)
    cosine = jnp.concatenate([cosine, cosine], axis=1)
    sine = jnp.concatenate([-sine, sine], axis=1)
    half_ids = (jnp.arange(4)[:, None] * 1024 + yl * 512 + jnp.arange(512)[None]).reshape(-1)
    half_seg = lax.dynamic_index_in_dim(segment.reshape(4, 2, 512), yl, 1, keepdims=False).reshape(-1)
    key_seg = jnp.where(valid > 0, segment, -1)
    ends = half_seg.reshape(-1, QB)
    lower = jnp.sum(segment[None] < ends[:, :1], axis=1, dtype=i32) // KB
    upper = (jnp.sum(segment[None] <= ends[:, -1:], axis=1, dtype=i32) + KB - 1) // KB
    limits = jnp.stack([lower, upper])

    inputs = tokens.astype(f32)
    first_inv = rms_rows(inputs)
    normed = (inputs * first_inv * attn_gain).astype(bf16)
    w_three = jnp.stack([w_query, w_key, w_value])
    gathered, out_part, normed_all = gather_weights(w_three, w_out, normed)
    full_three = gathered.reshape(3, 2048, 512)
    normed_all = normed_all.reshape(512, width)

    def by_head(flat):
        return jnp.transpose(flat.reshape(512, 4, HD), (1, 0, 2))

    def flat_of(heads):
        return jnp.transpose(heads.reshape(4, 512, HD), (1, 0, 2)).reshape(512, 512)

    head_gains = jnp.stack([query_gain, key_gain])[:, None]
    heads, projected = project(normed_all, full_three, cosine, sine, head_gains)
    runs = (4, 4, 128, HD)
    q, k, v, full_out = heads_over_x(heads.reshape((3,) + runs), out_part)
    q, k, v = q.reshape(2048, HD), k.reshape(4096, HD), v.reshape(4096, HD)
    full_out = full_out.reshape(2048, 512)
    att_low, att, inverse = attend(limits, q, k, v, half_seg, half_ids, key_seg)
    attended = back_over_x(att_low.reshape(runs))
    attended_flat = flat_of(attended)
    branch_part = jnp.einsum("qc,mc->qm", attended_flat, full_out, preferred_element_type=f32)
    middle = inputs + sum_rows(branch_part.astype(bf16), 9)
    second_inv = rms_rows(middle)
    normed_ffn = (middle * second_inv * ffn_gain).astype(bf16)
    logits = jnp.dot(normed_ffn, router, preferred_element_type=f32)
    probabilities = jax.nn.softmax(logits, axis=-1)

    expert_ids = jnp.arange(EXPERTS, dtype=i32)
    hot = jnp.sum((routes[..., None] == expert_ids).astype(f32), axis=1)
    before = (jnp.arange(tok)[:, None] > jnp.arange(tok)[None]).astype(bf16)
    slots = jnp.dot(before, hot.astype(bf16), preferred_element_type=f32)
    slot_code = jnp.where(hot > 0, slots, -1.0)
    chosen = probabilities * hot
    gate_total = jnp.sum(chosen, axis=-1, keepdims=True)
    gates = chosen / gate_total

    sent = jnp.concatenate([normed_ffn, slot_code.astype(bf16), gates.astype(bf16)], axis=1)
    everyone = spread(sent, 7)
    lane = jnp.arange(128)[None]
    sel_row = jnp.arange(8)[:, None]
    info = everyone[:, :, width:]
    column = (sel_row // 2) * EXPERTS + device * EXP_DEV + sel_row % 2
    sel = ((sel_row < 4) & (lane == column)).astype(bf16)
    nearby = (device ^ 8) * EXP_DEV
    column = sel_row % 2 + jnp.where(sel_row // 2 % 2 == 0, device * EXP_DEV, nearby)
    sel_chip = (lane == column + (sel_row // 4) * EXPERTS).astype(bf16)
    flat_info, flat_everyone = info.reshape(32 * tok, -1), everyone.reshape(32 * tok, -1)
    expert_rows, row_gates = pick_rows(sel, flat_info, flat_everyone, width, True)
    expert_rows = expert_rows.reshape(EXP_DEV, -1, width)
    row_gates = row_gates.reshape(EXP_DEV, -1, 128)
    all_cot, gate_part, up_part, hidden, expert_result = expert_forward(
        cotangent, expert_rows, full_in, full_back, 11
    )
    (arrived_cot,) = pick_rows(sel, flat_info, all_cot.reshape(32 * tok, width), width, False)
    arrived_cot = arrived_cot.reshape(EXP_DEV, -1, width)
    mixture, row_dots, grad_gate, grad_up, grad_rows, term_back = expert_backward(
        sel_chip, info, expert_result, arrived_cot, gate_part, up_part, hidden, row_gates,
        full_in, full_back, 12,
    )
    row_dots = jnp.sum(row_dots, axis=-1, keepdims=True)
    high = row_dots.astype(bf16)
    column = (device * EXP_DEV + jnp.arange(EXP_DEV))[:, None, None]
    low = jnp.where(lane == column + EXPERTS, (row_dots - high.astype(f32)).astype(bf16), 0)
    row_dots = jnp.where(lane == column, high, low)
    grad_home, term_in = expert_finish(
        sel_chip, info, grad_rows, row_dots, expert_rows, grad_gate, grad_up, 13
    )
    grad_gates = grad_home[:, width : width + EXPERTS] + grad_home[:, width + EXPERTS :]
    grad_home = grad_home[:, :width]

    def fold_dp(term):
        return lax.psum_scatter(term.astype(bf16), "dp", scatter_dimension=1, tiled=True)

    expert_out_grad = unstack(fold_dp(term_back))
    expert_in_grad = unstack(fold_dp(term_in))

    output = (middle + mixture).astype(bf16)
    grad_out = cotangent.astype(f32)
    mean_grad = jnp.sum(grad_gates * gates, axis=-1, keepdims=True)
    grad_probs = (grad_gates - mean_grad) / gate_total * hot
    grad_logits = probabilities * (
        grad_probs - jnp.sum(probabilities * grad_probs, axis=-1, keepdims=True)
    )
    high = grad_logits.astype(bf16)
    halves = jnp.concatenate([high, (grad_logits - high.astype(f32)).astype(bf16)], axis=1)
    router_term = jnp.einsum("td,te->de", normed_ffn, halves, preferred_element_type=f32)
    router_term = router_term[:, :EXPERTS] + router_term[:, EXPERTS:]
    grad_ffn = grad_home + jnp.einsum(
        "te,de->td", halves, jnp.concatenate([router, router], axis=1), preferred_element_type=f32
    )
    ffn_gain_term = jnp.sum(grad_ffn * middle * second_inv, axis=0)
    grad_middle = grad_out + rms_back(middle, second_inv, grad_ffn * ffn_gain)
    grad_branch = grad_middle.astype(bf16)
    branch_all = gather_rows(grad_branch).reshape(512, width)
    grad_att = by_head(
        jnp.dot(branch_all, full_out, preferred_element_type=f32).astype(bf16)
    )
    grad_att = go_over_x(grad_att.reshape(runs)).reshape(2048, HD)
    delta = jnp.sum(grad_att.astype(f32) * att, axis=-1)
    dq, dk, dv = attend_back(
        limits, q, k, v, grad_att, half_seg, half_ids, key_seg, inverse[:, 0], delta
    )
    cut = (4, 2, 4, 128, HD)
    grad_heads = grads_over_x(dq.reshape(runs), dk.reshape(cut), dv.reshape(cut))
    out_grad = jnp.einsum(
        "qc,qf->cf", branch_all, attended_flat, preferred_element_type=f32
    ).astype(bf16)
    gains = jnp.pad(ffn_gain_term, (0, 32 * 8 * 128 - width)).reshape(32, 8, 128)
    small = jnp.concatenate([router_term.reshape(32, 32, 128), gains], axis=1)
    attn_grads, grad_normed, summed, tiny = last_sums(
        grad_heads.reshape(3, 4, 512, HD), projected, full_three, normed_all, cosine, sine,
        head_gains, out_grad, inputs * first_inv, small,
    )
    input_grad = grad_middle + rms_back(inputs, first_inv, grad_normed * attn_gain)
    summed = summed.reshape(32, 40, 128)
    router_grad = summed[:, :32].reshape(router.shape)
    ffn_gain_grad = summed[:, 32:].reshape(-1)[:width]
    return (
        output,
        input_grad,
        tiny[:16].reshape(-1),
        attn_grads[0],
        attn_grads[1],
        attn_grads[2],
        attn_grads[3],
        tiny[16],
        tiny[17],
        ffn_gain_grad,
        router_grad,
        expert_in_grad,
        expert_out_grad,
    )


def solution(mesh):
    placed = (
        P(("dp", "head", "blk"), None),
        P("dp", None),
        P("dp", None),
        P(("dp", "head", "blk"), None),
        P(),
        P(("dp", "blk"), "head"),
        P(("dp", "blk"), "head"),
        P(("dp", "blk"), "head"),
        P(("dp", "blk"), "head"),
        P(),
        P(),
        P(),
        P(),
        P("dp", ("head", "blk"), None),
        P("dp", ("head", "blk"), None),
        P(("dp", "head", "blk"), None),
    )
    return jax.shard_map(
        on_device,
        mesh=mesh,
        in_specs=placed,
        out_specs=(
            P(("dp", "head", "blk"), None),
            P(("dp", "head", "blk"), None),
            P(),
            P(("dp", "blk"), "head"),
            P(("dp", "blk"), "head"),
            P(("dp", "blk"), "head"),
            P(("dp", "blk"), "head"),
            P(),
            P(),
            P(),
            P(),
            P("dp", ("head", "blk"), None),
            P("dp", ("head", "blk"), None),
        ),
        check_vma=False,
    )
```

```python
import functools
import math

import jax
import jax.numpy as jnp
from jax import lax
from jax.experimental import pallas as pl
from jax.experimental.pallas import tpu as pltpu
from jax.sharding import PartitionSpec as P

HEADS = 16
HD = 128
FF = 1024
TOPK = 8
EXP_DEV = 2
CAP = 24
EXPERTS = 64

epsilon = 1e-06
rope_base = 50000.0
f32 = jnp.float32
bf16 = jnp.bfloat16
i32 = jnp.int32
MESH = pl.DeviceIdType.MESH
ANY = pl.BlockSpec(memory_space=pl.ANY)
VMEM = pl.BlockSpec(memory_space=pltpu.VMEM)
SMEM = pl.BlockSpec(memory_space=pltpu.SMEM)
DMA = pltpu.SemaphoreType.DMA


def rms_rows(values):
    return lax.rsqrt(jnp.mean(values * values, axis=-1, keepdims=True) + epsilon)


def rms_back(values, inverse, grad_scaled):
    inner_mean = jnp.mean(grad_scaled * values, axis=-1, keepdims=True)
    return inverse * grad_scaled - values * inverse * inverse * inverse * inner_mean


def wrap4(value):
    return lax.rem(value + 4, 4)


class Place:
    def __init__(self):
        head, blk = lax.axis_index("head"), lax.axis_index("blk")
        self.dp = lax.axis_index("dp")
        self.yh, self.co = head // 2, lax.rem(head, 2)
        self.yl, self.x = blk // 4, lax.rem(blk, 4)
        self.head = head
        self.zr, self.zl, self.zo = (wrap4(self.dp + s) for s in (1, -1, 2))
        self.xr, self.xl, self.xo = (wrap4(self.x + s) for s in (1, -1, 2))
        y = self.yh * 2 + self.yl
        self.yr, self.ylf, self.yo = (wrap4(y + s) for s in (1, -1, 2))
        self.ZR, self.ZL, self.ZO = {"dp": self.zr}, {"dp": self.zl}, {"dp": self.zo}
        self.XR, self.XL, self.XO = (self.to_x(v) for v in (self.xr, self.xl, self.xo))
        self.Y = {"blk": (1 - self.yl) * 4 + self.x}
        self.C = {"head": self.yh * 2 + (1 - self.co)}
        self.H = {"head": (1 - self.yh) * 2 + self.co}
        self.YR, self.YL = self.to_y(self.yr), self.to_y(self.ylf)

    def to_x(self, x):
        return {"blk": self.yl * 4 + x}

    def to_y(self, y):
        return {"head": (y // 2) * 2 + self.co, "blk": lax.rem(y, 2) * 4 + self.x}


def greet(devices):
    barrier = pltpu.get_barrier_semaphore()
    for device in devices:
        pl.semaphore_signal(barrier, inc=1, device_id=device, device_id_type=MESH)
    pl.semaphore_wait(barrier, len(devices))


class View:
    def __init__(self, ref, index=None):
        self.ref, self.index = ref, index

    @property
    def at(self):
        return self

    def __getitem__(self, index):
        return View(self, index)

    def get(self):
        base = self.ref.get() if isinstance(self.ref, View) else self.ref
        return base if self.index is None else base.at[self.index]

    def load(self):
        return self.get()[...]

    def store(self, value):
        ref = self.get()
        ref[...] = value.astype(ref.dtype)


def plain(ref):
    return ref.get() if isinstance(ref, View) else ref


class Sent:
    def __init__(self, make):
        self.make = make

    def wait_recv(self):
        self.make().wait_recv()

    def wait_send(self):
        self.make().wait_send()

    def wait(self):
        self.make().wait()


class Wire:
    def __init__(self, send_sem, recv_sem):
        self.send_sem, self.recv_sem, self.started = send_sem, recv_sem, []

    def send(self, src, dst, device):
        at = len(self.started)

        def make():
            return pltpu.make_async_remote_copy(
                src_ref=plain(src),
                dst_ref=plain(dst),
                send_sem=self.send_sem.at[at],
                recv_sem=self.recv_sem.at[at],
                device_id=device,
                device_id_type=MESH,
            )

        make().start()
        self.started.append(Sent(make))
        return self.started[-1]

    def drain(self):
        for copy in self.started:
            copy.wait_send()


def local(src, dst, sems, at):
    def make():
        return pltpu.make_async_copy(plain(src), plain(dst), sems.at[at])

    make().start()
    return Sent(make)


def remote_call(body, name, cid, sends, locals_, ins, outs, out_shape, scratch=(), vmem=None):
    return pl.pallas_call(
        body,
        name=name,
        out_shape=out_shape,
        in_specs=ins,
        out_specs=outs,
        scratch_shapes=[DMA((sends,)), DMA((sends,)), DMA((max(locals_, 1),)), *scratch],
        compiler_params=pltpu.CompilerParams(
            collective_id=cid, has_side_effects=True, vmem_limit_bytes=vmem
        ),
    )


def shaped(shape, dtype=bf16):
    return jax.ShapeDtypeStruct(shape, dtype)


def weights_kernel(w, wo, n, g, go, m, ss, rs, ls):
    p = Place()
    dp, yl, x = p.dp, p.yl, p.x
    own = [
        local(w, g.at[:, dp, yl, x], ls, 0),
        local(n, m.at[p.head], ls, 1),
        local(wo, go.at[dp], ls, 2),
    ]
    greet([p.ZR, p.ZL, p.XR, p.XL, p.Y, p.C, p.H])
    wire = Wire(ss, rs)
    n_c = wire.send(n, m.at[p.head], p.C)
    z1 = wire.send(w, g.at[:, dp, yl, x], p.ZR)
    z2 = wire.send(w, g.at[:, dp, yl, x], p.ZL)
    n_h = wire.send(n, m.at[p.head], p.H)
    o1 = wire.send(wo, go.at[dp], p.ZR)
    o2 = wire.send(wo, go.at[dp], p.ZL)
    z1.wait_recv()
    z3 = wire.send(g.at[0:2, p.zl, yl, x], g.at[0:2, p.zl, yl, x], p.ZR)
    z2.wait_recv()
    z4 = wire.send(g.at[2, p.zr, yl, x], g.at[2, p.zr, yl, x], p.ZL)
    own[0].wait()
    z3.wait_recv()
    z4.wait_recv()
    b1 = wire.send(g.at[2, :, yl, x], g.at[2, :, yl, x], p.XR)
    b2 = wire.send(g.at[2, :, yl, x], g.at[2, :, yl, x], p.XL)
    a1 = wire.send(g.at[0:2, :, yl, x], g.at[0:2, :, yl, x], p.Y)
    c1 = wire.send(g.at[2, :, yl, x], g.at[2, :, yl, x], p.Y)
    o1.wait_recv()
    o3 = wire.send(go.at[p.zl, 0:32], go.at[p.zl, 0:32], p.ZR)
    o2.wait_recv()
    o4 = wire.send(go.at[p.zr, 32:64], go.at[p.zr, 32:64], p.ZL)
    n_h.wait_recv()
    other = (1 - p.yh) * 2 + p.co
    n_f = wire.send(m.at[other], m.at[other], p.C)
    b1.wait_recv()
    b3 = wire.send(g.at[2, 0:2, yl, p.xl], g.at[2, 0:2, yl, p.xl], p.XR)
    c2 = wire.send(g.at[2, :, yl, p.xl], g.at[2, :, yl, p.xl], p.Y)
    b2.wait_recv()
    b4 = wire.send(g.at[2, 2:4, yl, p.xr], g.at[2, 2:4, yl, p.xr], p.XL)
    c3 = wire.send(g.at[2, :, yl, p.xr], g.at[2, :, yl, p.xr], p.Y)
    a1.wait_recv()
    a2 = wire.send(g.at[0:2, :, :, x], g.at[0:2, :, :, x], p.XR)
    a3 = wire.send(g.at[0:2, :, :, x], g.at[0:2, :, :, x], p.XL)
    b3.wait_recv()
    b4.wait_recv()
    c4 = wire.send(g.at[2, :, yl, p.xo], g.at[2, :, yl, p.xo], p.Y)
    a2.wait_recv()
    a4 = wire.send(g.at[0, :, :, p.xl], g.at[0, :, :, p.xl], p.XR)
    a3.wait_recv()
    a5 = wire.send(g.at[1, :, :, p.xr], g.at[1, :, :, p.xr], p.XL)
    for copy in (n_c, n_f, o3, o4, c1, c2, c3, c4, a4, a5):
        copy.wait_recv()
    own[1].wait()
    own[2].wait()
    wire.drain()


def gather_weights(w, wo, n):
    return remote_call(
        weights_kernel,
        "gather_weights",
        1,
        24,
        3,
        [ANY] * 3,
        [ANY] * 3,
        (shaped((3, 4, 2, 4, 64, 512)), shaped((4, 64, 512)), shaped((4, 128, 2048))),
    )(w, wo, n)


def heads_kernel(three, go, qd, kd, vd, gd, ss, rs, ls):
    p = Place()
    q, k, v = (three.at[i] for i in range(3))
    yl, x = p.yl, p.x
    own = [
        local(q.at[x], qd.at[:, x], ls, 0),
        local(k.at[x], kd.at[:, yl, x], ls, 1),
        local(v.at[x], vd.at[:, yl, x], ls, 2),
        local(go, gd.at[:, yl, x], ls, 3),
    ]
    greet([p.Y, p.XR, p.XL, p.XO])
    wire = Wire(ss, rs)
    done = [
        wire.send(k.at[x], kd.at[:, yl, x], p.Y),
        wire.send(v.at[x], vd.at[:, yl, x], p.Y),
    ]
    w1 = wire.send(go, gd.at[:, yl, x], p.Y)
    moved = []
    for there, came, device in ((p.xo, p.xo, p.XO), (p.xr, p.xl, p.XR), (p.xl, p.xr, p.XL)):
        ks = wire.send(k.at[there], kd.at[:, yl, x], device)
        vs = wire.send(v.at[there], vd.at[:, yl, x], device)
        moved.append((came, ks, vs))
    for there, device in ((p.xo, p.XO), (p.xr, p.XR), (p.xl, p.XL)):
        done.append(wire.send(q.at[there], qd.at[:, x], device))
    for came, ks, vs in moved[1:] + moved[:1]:
        ks.wait_recv()
        done.append(wire.send(kd.at[:, yl, came], kd.at[:, yl, came], p.Y))
        vs.wait_recv()
        done.append(wire.send(vd.at[:, yl, came], vd.at[:, yl, came], p.Y))
    own[3].wait()
    w1.wait_recv()
    w2 = wire.send(gd.at[:, :, x], gd.at[:, :, x], p.XR)
    w3 = wire.send(gd.at[:, :, x], gd.at[:, :, x], p.XL)
    w2.wait_recv()
    done.append(wire.send(gd.at[0:2, :, p.xl], gd.at[0:2, :, p.xl], p.XR))
    w3.wait_recv()
    done.append(wire.send(gd.at[2:4, :, p.xr], gd.at[2:4, :, p.xr], p.XL))
    for copy in done:
        copy.wait_recv()
    for copy in own[:3]:
        copy.wait()
    wire.drain()


def heads_over_x(three, go):
    return remote_call(
        heads_kernel,
        "heads_over_x",
        3,
        22,
        4,
        [ANY] * 2,
        [ANY] * 4,
        (
            shaped((4, 4, 128, 128)),
            shaped((4, 2, 4, 128, 128)),
            shaped((4, 2, 4, 128, 128)),
            shaped((4, 2, 4, 64, 512)),
        ),
    )(three, go)


def attended_kernel(o, w, att, out, ss, rs, ls, flat, part, got_c, got_h, half):
    p = Place()
    greet([p.C, p.H, p.XR, p.XL, p.XO])
    wire = Wire(ss, rs)
    near_c, far_c = p.yh * 2 + (1 - p.co), (1 - p.yh) * 2 + (1 - p.co)
    far = (1 - p.yh) * 2 + p.co
    order = (far_c, near_c, far, p.head)
    came = []
    for run in order:
        came.append(
            [
                wire.send(o.at[run, there], att.at[p.x, run], device)
                for there, device in ((p.xo, p.XO), (p.xr, p.XR), (p.xl, p.XL))
            ]
        )
        att[p.x, run] = o[run, p.x]

    def times(i, store):
        for copy in came[i]:
            copy.wait_recv()
        for h in range(4):
            flat[:, h * HD : (h + 1) * HD] = att[h, order[i]]
        for c in range(0, 2048, 512):
            cols = slice(c, c + 512)
            store(cols, nt(flat[...], w[cols]))

    sums = []
    for i in range(2):

        def keep(cols, value):
            part[i, :, cols] = value.astype(bf16)

        times(i, keep)
        sums.append(wire.send(part.at[i], got_c.at[i], p.C))
    sums[0].wait_recv()

    def add_far(cols, value):
        half[:, cols] = (value + got_c[0, :, cols].astype(f32)).astype(bf16)

    times(2, add_far)
    over = wire.send(half, got_h, p.H)

    def first(cols, value):
        out[:, cols] = value

    times(3, first)
    sums[1].wait_recv()
    over.wait_recv()

    def add(i, carry):
        at = pl.ds(pl.multiple_of(i * 16, 16), 16)
        out[at] += got_c[1, at].astype(f32) + got_h[at].astype(f32)
        return carry

    lax.fori_loop(0, 8, add, 0)
    wire.drain()


def attended_home(o, w):
    return remote_call(
        attended_kernel,
        "attended_home",
        4,
        15,
        1,
        [VMEM, VMEM],
        [VMEM, VMEM],
        (shaped((4, 4, 128, 128)), shaped((128, 2048), f32)),
        scratch=[
            pltpu.VMEM((128, 512), bf16),
            pltpu.VMEM((2, 128, 2048), bf16),
            pltpu.VMEM((2, 128, 2048), bf16),
            pltpu.VMEM((128, 2048), bf16),
            pltpu.VMEM((128, 2048), bf16),
        ],
        vmem=32 << 20,
    )(o, w)


def branch_kernel(n, w, m, d, ss, rs, ls, heads):
    p = Place()
    own = local(n, m.at[p.head], ls, 0)
    greet([p.C, p.H, p.XR, p.XL, p.XO])
    wire = Wire(ss, rs)
    n_h = wire.send(n, m.at[p.head], p.H)
    n_c = wire.send(n, m.at[p.head], p.C)
    sibling = p.yh * 2 + (1 - p.co)
    other, last = (1 - p.yh) * 2 + p.co, (1 - p.yh) * 2 + (1 - p.co)
    moved = []

    def out(run, at):
        value = jnp.dot(m[run], w[...], preferred_element_type=f32).astype(bf16)
        for h in range(4):
            heads[at, h] = value[:, h * HD : (h + 1) * HD]
        for there, device in ((p.xo, p.XO), (p.xr, p.XR), (p.xl, p.XL)):
            moved.append(wire.send(heads.at[at, there], d.at[run, p.x], device))
        d[run, p.x] = heads[at, p.x]

    own.wait()
    out(p.head, 0)
    n_c.wait_recv()
    out(sibling, 1)
    n_h.wait_recv()
    n_f = wire.send(m.at[other], m.at[other], p.C)
    out(other, 2)
    n_f.wait_recv()
    out(last, 3)
    for copy in moved:
        copy.wait_recv()
    wire.drain()


def branch_to_heads(n, w):
    return remote_call(
        branch_kernel,
        "branch_to_heads",
        2,
        15,
        1,
        [VMEM, VMEM],
        [VMEM, VMEM],
        (shaped((4, 128, 2048)), shaped((4, 4, 128, 128))),
        scratch=[pltpu.VMEM((4, 4, 128, 128), bf16)],
        vmem=32 << 20,
    )(n, w)


def grads_x_kernel(dq, dk, dv, three, ss, rs, ls, gk, gv, sk, sv):
    p = Place()
    x, yl = p.x, p.yl
    qd, kd, vd = (three.at[i] for i in range(3))
    own = local(dq.at[:, x], qd.at[x], ls, 0)
    greet([p.Y, p.XR, p.XL, p.XO])
    wire = Wire(ss, rs)
    order = ((p.xo, p.XO), (p.xr, p.XR), (p.xl, p.XL), (x, None))
    pairs = []
    for i, (there, device) in enumerate(order):
        pairs.append(
            (
                wire.send(dk.at[:, 1 - yl, there], gk.at[i], p.Y),
                wire.send(dv.at[:, 1 - yl, there], gv.at[i], p.Y),
            )
        )
    last = []
    for there, device in order[:3]:
        last.append(wire.send(dq.at[:, there], qd.at[x], device))
    for i, (there, device) in enumerate(order):
        for grads, got, summed, out, arrived in (
            (dk, gk, sk, kd, pairs[i][0]),
            (dv, gv, sv, vd, pairs[i][1]),
        ):
            arrived.wait_recv()
            for run in range(4):
                total = grads[run, yl, there].astype(f32) + got[i, run].astype(f32)
                if device is None:
                    out[x, run] = total.astype(bf16)
                else:
                    summed[i, run] = total.astype(bf16)
            if device is not None:
                last.append(wire.send(summed.at[i], out.at[x], device))
    for copy in last:
        copy.wait_recv()
    own.wait()
    wire.drain()


def grads_over_x(dq, dk, dv):
    return remote_call(
        grads_x_kernel,
        "grads_over_x",
        6,
        17,
        1,
        [ANY, VMEM, VMEM],
        [VMEM],
        (shaped((3, 4, 4, 128, 128)),),
        scratch=[
            pltpu.VMEM((4, 4, 128, 128), bf16),
            pltpu.VMEM((4, 4, 128, 128), bf16),
            pltpu.VMEM((3, 4, 128, 128), bf16),
            pltpu.VMEM((3, 4, 128, 128), bf16),
        ],
        vmem=16 << 20,
    )(dq, dk, dv)[0]


def turned(values, cosine, sine):
    return values * cosine + pltpu.roll(values, 64, 1) * sine


def project_kernel(rows, w, cosine, sine, gain, heads, kept):
    flat = jnp.dot(rows[...], w[0], preferred_element_type=f32)
    step = pl.program_id(0)
    for h in range(4):
        head = flat[:, h * HD : (h + 1) * HD]

        @pl.when(step < 2)
        def _():
            kept[0, h] = head
            scaled = head * rms_rows(head) * gain[0]
            heads[0, h] = turned(scaled, cosine[...], sine[...]).astype(bf16)

        @pl.when(step == 2)
        def _():
            heads[0, h] = head.astype(bf16)


def project(rows, w, cosine, sine, gains):
    def fixed(*shape):
        return pl.BlockSpec(shape, lambda i: (0,) * len(shape))

    def two(i):
        return jnp.minimum(i, 1)

    return pl.pallas_call(
        project_kernel,
        name="project",
        grid=(3,),
        out_shape=(shaped((3, 4, 512, HD)), shaped((2, 4, 512, HD), f32)),
        in_specs=[
            fixed(512, 2048),
            pl.BlockSpec((1, 2048, 512), lambda i: (i, 0, 0)),
            fixed(512, HD),
            fixed(512, HD),
            pl.BlockSpec((1, 1, HD), lambda i: (two(i), 0, 0)),
        ],
        out_specs=[
            pl.BlockSpec((1, 4, 512, HD), lambda i: (i, 0, 0, 0)),
            pl.BlockSpec((1, 4, 512, HD), lambda i: (two(i), 0, 0, 0)),
        ],
        compiler_params=pltpu.CompilerParams(vmem_limit_bytes=60 << 20),
    )(rows, w, cosine, sine, gains)


QB = 256
KB = 512
SCALE = HD**-0.5
SCALE2 = SCALE * math.log2(math.e)


def attend_kernel(lim, q, k, v, qseg, qpos, kseg, o_low, o, linv, vext):
    rows = k.shape[0]
    ones = (lax.broadcasted_iota(i32, (KB, HD), 1) == 0).astype(bf16)

    def fill(i, carry):
        at = pl.ds(pl.multiple_of(i * KB, KB), KB)
        vext[at, :HD] = v[at]
        vext[at, HD:] = ones
        return carry

    lax.fori_loop(0, rows // KB, fill, 0)

    def one_query(b, carry):
        at = pl.ds(pl.multiple_of(b * QB, QB), QB)
        query, seg, pos = q[at], qseg[at], qpos[at]

        def one_key(j, acc):
            keys = pl.ds(pl.multiple_of(j * KB, KB), KB)
            score = lax.dot_general(
                query, k[keys], (((1,), (1,)), ((), ())), preferred_element_type=f32
            )
            key_pos = j * KB + lax.broadcasted_iota(i32, (1, KB), 1)
            allowed = (seg == kseg[:, keys]) | (pos == key_pos)
            weight = jnp.where(allowed, jnp.exp2(score * SCALE2), 0.0).astype(bf16)
            return acc + jnp.dot(weight, vext[keys], preferred_element_type=f32)

        acc = lax.fori_loop(lim[0, b], lim[1, b], one_key, jnp.zeros((QB, 2 * HD), f32))
        inverse = 1.0 / acc[:, HD : HD + 1]
        result = acc[:, :HD] * inverse
        o[at] = result
        o_low[at] = result.astype(bf16)
        linv[at] = jnp.broadcast_to(inverse, (QB, HD))
        return carry

    lax.fori_loop(0, q.shape[0] // QB, one_query, 0)


def attend(lim, q, k, v, qseg, qpos, kseg):
    n = q.shape[0]
    return pl.pallas_call(
        attend_kernel,
        name="attend",
        out_shape=(shaped((n, HD)), shaped((n, HD), f32), shaped((n, HD), f32)),
        in_specs=[SMEM] + [VMEM] * 6,
        out_specs=[VMEM] * 3,
        scratch_shapes=[pltpu.VMEM((k.shape[0], 2 * HD), bf16)],
        compiler_params=pltpu.CompilerParams(vmem_limit_bytes=32 << 20),
    )(lim, q, k, v, qseg[:, None], qpos[:, None], kseg[None])


def attend_back_kernel(
    lim, q, k, v, g, qseg, qpos, kseg, linv, delta, dq, dk, dv, kt, dk_acc, dv_acc
):
    rows = k.shape[0]

    def fill(i, carry):
        at = pl.ds(pl.multiple_of(i * KB, KB), KB)
        kt[:, at] = k[at].astype(f32).T.astype(bf16)
        dk_acc[at] = jnp.zeros((KB, HD), f32)
        dv_acc[at] = jnp.zeros((KB, HD), f32)
        return carry

    lax.fori_loop(0, rows // KB, fill, 0)
    across = (((1,), (1,)), ((), ()))

    def one_query(b, carry):
        at = pl.ds(pl.multiple_of(b * QB, QB), QB)
        query, grad = q[at], g[at]
        seg, pos, inverse, shift = qseg[:, at], qpos[:, at], linv[:, at], delta[:, at]

        def one_key(j, acc):
            keys = pl.ds(pl.multiple_of(j * KB, KB), KB)
            key = k[keys]
            score = lax.dot_general(key, query, across, preferred_element_type=f32)
            key_pos = j * KB + lax.broadcasted_iota(i32, (KB, 1), 0)
            allowed = (kseg[keys] == seg) | (key_pos == pos)
            prob = jnp.where(allowed, jnp.exp2(score * SCALE2), 0.0) * inverse
            grad_prob = lax.dot_general(v[keys], grad, across, preferred_element_type=f32)
            grad_score = (prob * (grad_prob - shift)).astype(bf16)
            dv_acc[keys] += jnp.dot(prob.astype(bf16), grad, preferred_element_type=f32)
            dk_acc[keys] += jnp.dot(grad_score, query, preferred_element_type=f32)
            return acc + jnp.dot(kt[:, keys], grad_score, preferred_element_type=f32)

        acc = lax.fori_loop(lim[0, b], lim[1, b], one_key, jnp.zeros((HD, QB), f32))
        dq[at] = (acc * SCALE).T.astype(bf16)
        return carry

    lax.fori_loop(0, q.shape[0] // QB, one_query, 0)

    def finish(i, carry):
        at = pl.ds(pl.multiple_of(i * KB, KB), KB)
        dk[at] = (dk_acc[at] * SCALE).astype(bf16)
        dv[at] = dv_acc[at].astype(bf16)
        return carry

    lax.fori_loop(0, rows // KB, finish, 0)


def attend_back(lim, q, k, v, g, qseg, qpos, kseg, linv, delta):
    n, rows = q.shape[0], k.shape[0]
    return pl.pallas_call(
        attend_back_kernel,
        name="attend_back",
        out_shape=(shaped((n, HD)), shaped((rows, HD)), shaped((rows, HD))),
        in_specs=[SMEM] + [VMEM] * 9,
        out_specs=[VMEM] * 3,
        scratch_shapes=[
            pltpu.VMEM((HD, rows), bf16),
            pltpu.VMEM((rows, HD), f32),
            pltpu.VMEM((rows, HD), f32),
        ],
        compiler_params=pltpu.CompilerParams(vmem_limit_bytes=40 << 20),
    )(lim, q, k, v, g, qseg[None], qpos[None], kseg[:, None], linv[None], delta[None])


SPREAD_SENDS = 26


def spread_steps(p, wire, sems, src, dst):
    yh, co, yl, x = p.yh, p.co, p.yl, p.x
    (rh, rl), (lh, ll), (oh, ol) = ((y // 2, lax.rem(y, 2)) for y in (p.yr, p.ylf, p.yo))
    A, A1, A2 = pl.ds(0, 64), pl.ds(0, 32), pl.ds(32, 32)
    B, B1, B2 = pl.ds(64, 64), pl.ds(64, 32), pl.ds(96, 32)
    src, dst = View(src), View(dst)
    own = local(src, dst.at[yh, co, yl, x], sems, 0)

    def both(ref, device):
        return wire.send(ref, ref, device)

    me = dst.at[yh, co, yl]
    a1 = wire.send(src.at[A], me.at[x, A], p.XR)
    b1 = wire.send(src.at[B], me.at[x, B], p.YR)
    a2 = wire.send(src.at[A], me.at[x, A], p.XL)
    b2 = wire.send(src.at[B], me.at[x, B], p.YL)
    yield
    a1.wait_recv()
    a3 = both(me.at[p.xl, A1], p.XR)
    a2.wait_recv()
    a4 = both(me.at[p.xr, A2], p.XL)
    b1.wait_recv()
    b3 = both(dst.at[lh, co, ll, x, B1], p.YR)
    b2.wait_recv()
    b4 = both(dst.at[rh, co, rl, x, B2], p.YL)
    yield
    own.wait()
    a3.wait_recv()
    a4.wait_recv()
    a5 = both(me.at[:, A], p.YR)
    a6 = both(me.at[:, A], p.YL)
    b3.wait_recv()
    b4.wait_recv()
    b5 = both(dst.at[:, co, :, x, B], p.XR)
    b6 = both(dst.at[:, co, :, x, B], p.XL)
    last = [both(me.at[:, A], p.C), both(dst.at[:, co, :, x, B], p.C)]
    yield
    a5.wait_recv()
    a7 = both(dst.at[lh, co, ll, :, A1], p.YR)
    b5.wait_recv()
    b7 = both(dst.at[:, co, :, p.xl, B1], p.XR)
    a6.wait_recv()
    a8 = both(dst.at[rh, co, rl, :, A2], p.YL)
    b6.wait_recv()
    b8 = both(dst.at[:, co, :, p.xr, B2], p.XL)
    last += [both(dst.at[lh, co, ll, :, A], p.C), both(dst.at[:, co, :, p.xl, B], p.C)]
    last += [both(dst.at[rh, co, rl, :, A], p.C), both(dst.at[:, co, :, p.xr, B], p.C)]
    yield
    a7.wait_recv()
    last.append(both(dst.at[oh, co, ol, :, A1], p.C))
    b7.wait_recv()
    last.append(both(dst.at[:, co, :, p.xo, B1], p.C))
    a8.wait_recv()
    last.append(both(dst.at[oh, co, ol, :, A2], p.C))
    b8.wait_recv()
    last.append(both(dst.at[:, co, :, p.xo, B2], p.C))
    yield
    for copy in last:
        copy.wait_recv()
    wire.drain()
    yield


def greet_plane(p):
    greet([p.XR, p.XL, p.YR, p.YL, p.C])


def spread_kernel(src, dst, ss, rs, ls):
    p = Place()
    greet_plane(p)
    for _ in spread_steps(p, Wire(ss, rs), ls, src, dst):
        pass


def spread(src, cid):
    width = src.shape[1]
    return remote_call(
        spread_kernel,
        "spread",
        cid,
        SPREAD_SENDS,
        1,
        [ANY],
        [ANY],
        (shaped((2, 2, 2, 4, 128, width)),),
    )(src)[0].reshape(32, 128, width)


def at_step(number, *stages):
    for step, stage in stages:

        @pl.when(number == step)
        def _():
            next(stage)


def block(shape, index):
    return pl.BlockSpec(shape, index)


def nt(a, b):
    return lax.dot_general(a, b, (((1,), (1,)), ((), ())), preferred_element_type=f32)


def tn(a, b):
    return lax.dot_general(a, b, (((0,), (0,)), ((), ())), preferred_element_type=f32)


PARTS = 4


def forward_kernel(src, rows, w_in, w_out, dst, gate, up, hidden, y, ss, rs, ls):
    p = Place()
    greet_plane(p)
    moving = spread_steps(p, Wire(ss, rs), ls, src, dst)
    next(moving)
    n = rows.shape[1]
    cut = FF // PARTS

    def first(rows, w_gate, w_up, gate, up, hidden):
        at_step(pl.program_id(0) * PARTS + pl.program_id(1), (2, moving), (4, moving))
        g = jnp.dot(rows[0], w_gate[0], preferred_element_type=f32)
        u = jnp.dot(rows[0], w_up[0], preferred_element_type=f32)
        gate[0] = g.astype(bf16)
        up[0] = u.astype(bf16)
        hidden[0] = (g * jax.nn.sigmoid(g) * u).astype(bf16)

    out = block((1, n, cut), lambda e, j: (e, 0, j))
    pltpu.emit_pipeline(
        first,
        grid=(EXP_DEV, PARTS),
        in_specs=[
            block((1, n, 2048), lambda e, j: (e, 0, 0)),
            block((1, 2048, cut), lambda e, j: (e, 0, j)),
            block((1, 2048, cut), lambda e, j: (e, 0, j + PARTS)),
        ],
        out_specs=[out, out, out],
    )(rows, w_in, w_in, gate, up, hidden)

    def second(hidden, w, y):
        at_step(pl.program_id(0) * PARTS + pl.program_id(1), (3, moving))
        y[0] = nt(hidden[0], w[0]).astype(bf16)

    pltpu.emit_pipeline(
        second,
        grid=(EXP_DEV, PARTS),
        in_specs=[
            block((1, n, FF), lambda e, j: (e, 0, 0)),
            block((1, 2048 // PARTS, FF), lambda e, j: (e, j, 0)),
        ],
        out_specs=[block((1, n, 2048 // PARTS), lambda e, j: (e, 0, j))],
    )(hidden, w_out, y)
    for _ in moving:
        pass


def expert_forward(src, rows, w_in, w_out, cid):
    n, width = rows.shape[1:]
    outs = remote_call(
        forward_kernel,
        "expert_forward",
        cid,
        SPREAD_SENDS,
        1,
        [ANY] * 4,
        [ANY] * 5,
        (shaped((2, 2, 2, 4, 128, width)),)
        + (shaped((EXP_DEV, n, FF)),) * 3
        + (shaped((EXP_DEV, n, width)),),
        vmem=48 << 20,
    )(src, rows, w_in, w_out)
    return outs[0].reshape(32, 128, width), *outs[1:]


def slot_hits(table, count, rows_down):
    shape = (count * 2 * CAP, 256) if rows_down else (256, count * 2 * CAP)
    line = lax.broadcasted_iota(i32, shape, 0 if rows_down else 1)
    block = lax.broadcasted_iota(i32, shape, 1 if rows_down else 0) // 128
    expert = line // (2 * CAP)
    want = line - expert * (2 * CAP) - block * CAP

    def spread_out(first):
        value = jnp.zeros(shape, f32)
        for e in range(count):
            c = first + e
            at = table[c : c + 1] if rows_down else table[:, c : c + 1]
            value = jnp.where(expert == e, at, value)
        return value

    hit = (spread_out(0).astype(i32) == want) & (want >= 0) & (want < CAP)
    return hit, spread_out(count)


def pick_kernel(gated, sel, info, src, rows_out, *gates_out):
    for pair in range(src.shape[0] // 256):
        at = slice(pair * 256, (pair + 1) * 256)
        hit, gate = slot_hits(nt(sel[...], info[at]), EXP_DEV, True)
        rows = jnp.dot(hit.astype(bf16), src[at], preferred_element_type=f32).astype(bf16)
        for e in range(EXP_DEV):
            rows_out[e, pair] = rows[e * 2 * CAP : (e + 1) * 2 * CAP]
        if gated:
            total = jnp.sum(jnp.where(hit, gate, 0.0), axis=1, keepdims=True)
            total = jnp.broadcast_to(total, (EXP_DEV * 2 * CAP, 128))
            for e in range(EXP_DEV):
                gates_out[0][e, pair] = total[e * 2 * CAP : (e + 1) * 2 * CAP]


def pick_rows(sel, info, src, width, gated):
    pairs, step = src.shape[0] // 256, 2

    def spec(lanes):
        return pl.BlockSpec((EXP_DEV, step, 2 * CAP, lanes), lambda i: (0, i, 0, 0))

    shapes = [shaped((EXP_DEV, pairs, 2 * CAP, width)), shaped((EXP_DEV, pairs, 2 * CAP, 128), f32)]
    specs = [spec(width), spec(128)]
    return pl.pallas_call(
        functools.partial(pick_kernel, gated),
        name="pick_rows",
        grid=(pairs // step,),
        out_shape=shapes[: 1 + gated],
        in_specs=[
            pl.BlockSpec((8, 128), lambda i: (0, 0)),
            pl.BlockSpec((256 * step, 128), lambda i: (i, 0)),
            pl.BlockSpec((256 * step, width), lambda i: (i, 0)),
        ],
        out_specs=specs[: 1 + gated],
        compiler_params=pltpu.CompilerParams(vmem_limit_bytes=60 << 20),
    )(sel, info, src)


HOME_SENDS = 20


def home_scratch(width):
    return [
        pltpu.VMEM((2, 4, 8 * CAP, width), bf16),
        pltpu.VMEM((2, 2, 4, 128, width), bf16),
        pltpu.VMEM((2, 2, 64, width), bf16),
        pltpu.VMEM((2, 2, 64, width), bf16),
        pltpu.VMEM((2, 4, 64, width), bf16),
        pltpu.VMEM((2, 2, 2, 64, width), bf16),
        pltpu.VMEM((2, 2, 32, width), bf16),
        pltpu.VMEM((2, 2, 64, width), bf16),
    ]


def home_steps(p, wire, sems, gated, sel, info, rows, more, out, cat, q, a1, b1, a2, b2, c1, c2):
    yh, co, yl, x = p.yh, p.co, p.yl, p.x
    ys = [(yy // 2, lax.rem(yy, 2)) for yy in (p.yr, p.ylf, p.yo)]
    (rh, rl), (lh, ll), (oh, ol) = ys
    pieces = [(View(rows), slice(0, 2048))]
    if more is not None:
        pieces.append((View(more), slice(2048, 2048 + 128)))
    rows, out, whole_q, whole_cat = View(rows), View(out), q, cat
    width = cat.shape[-1]
    q, cat, a1, b1, a2, b2, c1, c2 = (View(ref) for ref in (q, cat, a1, b1, a2, b2, c1, c2))
    own, first = [], []
    for e in range(EXP_DEV):
        lines = pl.ds(e * 2 * CAP, 2 * CAP)
        there = pl.ds((2 + e) * 2 * CAP, 2 * CAP)
        for piece, lanes in pieces:
            first.append(wire.send(piece.at[e, :, 1 - co], cat.at[:, :, there, lanes], p.C))
            own.append(local(piece.at[e, :, co], cat.at[:, :, lines, lanes], sems, len(own)))
    yield
    for copy in own:
        copy.wait()
    for copy in first:
        copy.wait_recv()

    def place(h, pair):
        block = h * 16 + co * 8 + pair * 2
        both = jnp.concatenate([info[block], info[block + 1]], axis=0)
        table = lax.dot_general(
            both, sel[...], (((1,), (1,)), ((), ())), preferred_element_type=f32
        )
        hit, gate = slot_hits(table, 4, False)
        value = jnp.where(hit, gate if gated else 1.0, 0.0).astype(bf16)
        for c in range(0, width, 512):
            lanes = slice(c, min(c + 512, width))
            total = jnp.dot(
                value, whole_cat[h, pair, :, lanes], preferred_element_type=f32
            ).astype(bf16)
            at = lax.rem(pair, 2) * 2
            whole_q[h, pair // 2, at, :, lanes] = total[:128]
            whole_q[h, pair // 2, at + 1, :, lanes] = total[128:]

    def far_y(k, carry):
        place(oh, ol * 2 + k)
        return carry

    def nearer(half):
        def one(k, carry):
            y = lax.rem(yh * 2 + yl + k + k // 2, 4)
            place(y // 2, lax.rem(y, 2) * 2 + half)
            return carry

        lax.fori_loop(0, 3, one, 0)

    A, B = pl.ds(0, 64), pl.ds(64, 64)
    lax.fori_loop(0, 2, far_y, 0)
    s1 = [
        wire.send(q.at[oh, ol, 0:2, A], a1.at[0], p.YR),
        wire.send(q.at[oh, ol, 2:4, A], a1.at[1], p.YL),
    ]
    nearer(p.xo // 2)
    s1.insert(1, wire.send(q.at[0, :, p.xo, B], b1.at[0], p.XR))
    s1.append(wire.send(q.at[1, :, p.xo, B], b1.at[1], p.XL))
    nearer(1 - p.xo // 2)
    yield

    def add(dst, *srcs):
        total = srcs[0].load().astype(f32)
        for src in srcs[1:]:
            total = total + src.load().astype(f32)
        dst.store(total)

    def loop(count, body):
        def step(i, carry):
            body(i)
            return carry

        lax.fori_loop(0, count, step, 0)

    def plus(dst, src):
        add(dst, dst, src)

    s2 = []
    s1[0].wait_recv()
    loop(2, lambda i: plus(q.at[rh, rl, i, A], a1.at[0, i]))
    s2.append(wire.send(q.at[rh, rl, :, A], a2.at[0], p.YR))
    s1[1].wait_recv()
    loop(2, lambda i: plus(q.at[0, i, p.xr, B], b1.at[0, i]))
    s2.append(wire.send(q.at[:, :, p.xr, B], b2.at[0], p.XR))
    s1[2].wait_recv()
    loop(2, lambda i: plus(q.at[lh, ll, 2 + i, A], a1.at[1, i]))
    s2.append(wire.send(q.at[lh, ll, :, A], a2.at[1], p.YL))
    s1[3].wait_recv()
    loop(2, lambda i: plus(q.at[1, i, p.xl, B], b1.at[1, i]))
    s2.append(wire.send(q.at[:, :, p.xl, B], b2.at[1], p.XL))
    yield
    for copy in s2:
        copy.wait_recv()
    loop(4, lambda i: add(q.at[yh, yl, i, A], q.at[yh, yl, i, A], a2.at[0, i], a2.at[1, i]))
    s3 = [
        wire.send(q.at[yh, yl, p.xo, 0:32], c1.at[0, 0], p.XR),
        wire.send(q.at[yh, yl, p.xo, 32:64], c1.at[0, 1], p.XL),
    ]
    for h in range(2):
        loop(2, lambda i: add(q.at[h, i, x, B], q.at[h, i, x, B], b2.at[0, h, i], b2.at[1, h, i]))
    s3 += [
        wire.send(q.at[oh, ol, x, 64:96], c1.at[1, 0], p.YR),
        wire.send(q.at[oh, ol, x, 96:128], c1.at[1, 1], p.YL),
    ]
    yield
    s4 = []
    s3[0].wait_recv()
    plus(q.at[yh, yl, p.xr, 0:32], c1.at[0, 0])
    s4.append(wire.send(q.at[yh, yl, p.xr, A], c2.at[0, 0], p.XR))
    s3[1].wait_recv()
    plus(q.at[yh, yl, p.xl, 32:64], c1.at[0, 1])
    s4.append(wire.send(q.at[yh, yl, p.xl, A], c2.at[0, 1], p.XL))
    s3[2].wait_recv()
    plus(q.at[rh, rl, x, 64:96], c1.at[1, 0])
    s4.append(wire.send(q.at[rh, rl, x, B], c2.at[1, 0], p.YR))
    s3[3].wait_recv()
    plus(q.at[lh, ll, x, 96:128], c1.at[1, 1])
    s4.append(wire.send(q.at[lh, ll, x, B], c2.at[1, 1], p.YL))
    yield
    for copy in s4:
        copy.wait_recv()
    add(out.at[0:64], q.at[yh, yl, x, A], c2.at[0, 0], c2.at[0, 1])
    add(out.at[64:128], q.at[yh, yl, x, B], c2.at[1, 0], c2.at[1, 1])
    wire.drain()
    yield


def by_place(rows):
    return rows.reshape(EXP_DEV, 2, 2, 4, 2 * CAP, -1)


def backward_kernel(
    sel, info, y_places, y, cot, gate, up, hidden, row_gates, w_in, w_out,
    mixture, dots, dgate, dup, drows, term, ss, rs, ls, *scratch,
):
    p = Place()
    greet_plane(p)
    moving = home_steps(p, Wire(ss, rs), ls, True, sel, info, y_places, None, mixture, *scratch)
    next(moving)
    n = cot.shape[1]
    wide, cut = 2048 // PARTS, FF // PARTS
    dots[...] = jnp.zeros_like(dots)

    def number():
        return pl.program_id(0) * PARTS + pl.program_id(1)

    def first(y, cot, hidden, row_gates, term):
        at_step(number(), (3, moving))
        e = pl.program_id(0)
        product = y[0].astype(f32) * cot[0].astype(f32)
        partial = product[:, :128]
        for c in range(128, wide, 128):
            partial += product[:, c : c + 128]
        dots[e] += partial
        scaled = (hidden[0].astype(f32) * row_gates[0, :, :1]).astype(bf16)
        term[0] = tn(cot[0], scaled).astype(bf16)

    part = block((1, n, wide), lambda e, j: (e, 0, j))
    whole = block((1, n, FF), lambda e, j: (e, 0, 0))
    gates = block((1, n, 128), lambda e, j: (e, 0, 0))
    pltpu.emit_pipeline(
        first,
        grid=(EXP_DEV, PARTS),
        in_specs=[part, part, whole, gates],
        out_specs=[block((1, wide, FF), lambda e, j: (e, j, 0))],
    )(y, cot, hidden, row_gates, term)

    def second(cot, w, row_gates, gate, up, dgate, dup):
        at_step(number(), (3, moving))
        dhidden = jnp.dot(cot[0], w[0], preferred_element_type=f32) * row_gates[0, :, :1]
        g, u = gate[0].astype(f32), up[0].astype(f32)
        sg = jax.nn.sigmoid(g)
        dgate[0] = (dhidden * u * sg * (1.0 + g * (1.0 - sg))).astype(bf16)
        dup[0] = (dhidden * g * sg).astype(bf16)

    out = block((1, n, cut), lambda e, j: (e, 0, j))
    pltpu.emit_pipeline(
        second,
        grid=(EXP_DEV, PARTS),
        in_specs=[
            block((1, n, 2048), lambda e, j: (e, 0, 0)),
            block((1, 2048, cut), lambda e, j: (e, 0, j)),
            gates,
            out,
            out,
        ],
        out_specs=[out, out],
    )(cot, w_out, row_gates, gate, up, dgate, dup)

    def third(dgate, dup, w, drows):
        at_step(number(), (5, moving), (7, moving))
        total = nt(dgate[0], w[0, :, :FF]) + nt(dup[0], w[0, :, FF:])
        drows[0] = total.astype(bf16)

    pltpu.emit_pipeline(
        third,
        grid=(EXP_DEV, PARTS),
        in_specs=[whole, whole, block((1, wide, 2 * FF), lambda e, j: (e, j, 0))],
        out_specs=[part],
    )(dgate, dup, w_in, drows)
    for _ in moving:
        pass


def expert_backward(sel, info, y, cot, gate, up, hidden, row_gates, w_in, w_out, cid):
    n = cot.shape[1]
    half = shaped((EXP_DEV, n, FF))
    return remote_call(
        backward_kernel,
        "expert_backward",
        cid,
        HOME_SENDS,
        2,
        [VMEM, VMEM] + [ANY] * 9,
        [VMEM, VMEM] + [ANY] * 4,
        (
            shaped((128, 2048), f32),
            shaped((EXP_DEV, n, 128), f32),
            half,
            half,
            shaped((EXP_DEV, n, 2048)),
            shaped((EXP_DEV, 2048, FF)),
        ),
        scratch=home_scratch(2048),
        vmem=58 << 20,
    )(sel, info, by_place(y), y, cot, gate, up, hidden, row_gates, w_in, w_out)


def finish_kernel(sel, info, places, more, rows, dgate, dup, home, term, ss, rs, ls, *scratch):
    p = Place()
    greet_plane(p)
    moving = home_steps(p, Wire(ss, rs), ls, False, sel, info, places, more, home, *scratch)
    next(moving)
    n = rows.shape[1]
    wide = 2048 // PARTS

    def first(rows, dgate, dup, term):
        at_step(
            pl.program_id(0) * PARTS + pl.program_id(1), (2, moving), (7, moving)
        )
        term[0, :, :FF] = tn(rows[0], dgate[0]).astype(bf16)
        term[0, :, FF:] = tn(rows[0], dup[0]).astype(bf16)

    whole = block((1, n, FF), lambda e, j: (e, 0, 0))
    pltpu.emit_pipeline(
        first,
        grid=(EXP_DEV, PARTS),
        in_specs=[block((1, n, wide), lambda e, j: (e, 0, j)), whole, whole],
        out_specs=[block((1, wide, 2 * FF), lambda e, j: (e, j, 0))],
    )(rows, dgate, dup, term)
    for _ in moving:
        pass


def expert_finish(sel, info, drows, more, rows, dgate, dup, cid):
    return remote_call(
        finish_kernel,
        "expert_finish",
        cid,
        HOME_SENDS,
        4,
        [VMEM, VMEM] + [ANY] * 5,
        [VMEM, ANY],
        (shaped((128, 2048 + 128), f32), shaped((EXP_DEV, 2048, 2 * FF))),
        scratch=home_scratch(2048 + 128),
        vmem=58 << 20,
    )(sel, info, by_place(drows), by_place(more), rows, dgate, dup)


def unstack_kernel(grads, out, held, sems):
    e, j, steps = pl.program_id(0), pl.program_id(1), pl.num_programs(1)
    step = e * steps + j
    count = grads.shape[1]

    def copy(at):
        slot = lax.rem(at, 2)
        rows = pl.ds(pl.multiple_of(lax.rem(at, steps) * count, count), count)
        return pltpu.make_async_copy(held.at[slot], out.at[rows, at // steps], sems.at[slot])

    @pl.when(step >= 2)
    def _():
        copy(step - 2).wait()

    held[lax.rem(step, 2)] = grads[0].astype(f32)
    copy(step).start()

    @pl.when(step == EXP_DEV * steps - 1)
    def _():
        copy(step - 1).wait()
        copy(step).wait()


def unstack(grads):
    experts, rows, cols = grads.shape
    count = 128
    return pl.pallas_call(
        unstack_kernel,
        name="unstack",
        grid=(experts, rows // count),
        out_shape=shaped((rows, experts, cols), f32),
        in_specs=[pl.BlockSpec((1, count, cols), lambda e, j: (e, j, 0))],
        out_specs=ANY,
        scratch_shapes=[pltpu.VMEM((2, count, cols), f32), DMA((2,))],
        compiler_params=pltpu.CompilerParams(vmem_limit_bytes=60 << 20),
    )(grads)


def last_kernel(
    grads, kept, w, rows, cosine, sine, gain, p3, unit, small, out, normed, whole, tiny, ss, rs, ls,
    flat, total, w_grads, part, got_c, got_h, half, mine,
    ra, rb, rc, rd, re, rf, rg, acc_x, acc_y, sz, az, sx, ax, sy, ay, sc, ac, sh,
    tz, tx, ty, tc, th,
):
    p = Place()
    dp, yl, x = p.dp, p.yl, p.x
    greet([p.ZR, p.ZL, p.ZO, p.XR, p.XL, p.XO, p.Y, p.C, p.H])
    wire = Wire(ss, rs)
    p0, p1, p2 = (w_grads.at[i] for i in range(3))

    def added(dst, *srcs):
        total = srcs[0][...].astype(f32)
        for src in srcs[1:]:
            total = total + src[...].astype(f32)
        dst[...] = total.astype(dst.dtype)

    def loop(count, body):
        def step(i, carry):
            body(i)
            return carry

        lax.fori_loop(0, count, step, 0)

    def y_first(i, part):
        return wire.send(part.at[:, 1 - yl], rb.at[i - 2], p.Y)

    firsts = {3: y_first(3, p3)}
    far_z = ((p.zo, p.ZO), (p.zr, p.ZR), (p.zl, p.ZL))
    far_x = ((p.xo, p.XO), (p.xr, p.XR), (p.xl, p.XL))
    zs_out = [wire.send(small.at[there], sz.at[i], dev) for i, (there, dev) in enumerate(far_z)]
    mine[...] = jnp.zeros_like(mine)
    starts = []
    for i in range(3):
        if i < 2:
            gained = jnp.zeros((1, HD), f32)
            for h in range(4):
                grad = turned(grads[i, h].astype(f32), cosine[...], -sine[...])
                head = kept[i, h]
                inverse = rms_rows(head)
                gained += jnp.sum(grad * head * inverse, axis=0, keepdims=True)
                back = rms_back(head, inverse, grad * gain[i])
                flat[:, h * HD : (h + 1) * HD] = back.astype(bf16)
            mine[0, 16 + i : 17 + i] = gained
        else:
            for h in range(4):
                flat[:, h * HD : (h + 1) * HD] = grads[i, h]

        def weight_rows(c, carry):
            cols = pl.ds(pl.multiple_of(c * 512, 512), 512)
            grad = tn(rows[:, cols], flat[...]).astype(bf16)
            w_grads[i, c] = grad.reshape(2, 4, 64, 512)
            return carry

        lax.fori_loop(0, 4, weight_rows, 0)
        if i < 2:
            gradient = w_grads.at[i]
            starts.append(
                (
                    wire.send(gradient.at[0:2, :, p.xo], ra.at[i, 0], p.XR),
                    wire.send(gradient.at[2:4, :, p.xo], ra.at[i, 1], p.XL),
                )
            )
        else:
            firsts[2] = y_first(2, p2)

        def normed_cols(c, carry):
            cols = pl.ds(pl.multiple_of(c * 512, 512), 512)
            value = nt(flat[...], w[i, cols])
            if i > 0:
                value += total[:, cols]
            if i < 2:
                total[:, cols] = value
            else:
                part[:, :, cols] = value.astype(bf16).reshape(4, 128, 512)
            return carry

        lax.fori_loop(0, 4, normed_cols, 0)
        if i == 0:
            for copy in zs_out:
                copy.wait_recv()
            for y in range(2):
                az[y] = small[dp, y] + sz[0, y] + sz[1, y] + sz[2, y]
            xs_out = [
                wire.send(az.at[:, there], sx.at[n], dev) for n, (there, dev) in enumerate(far_x)
            ]
        elif i == 1:
            for copy in xs_out:
                copy.wait_recv()
            ax[...] = az[:, x] + sx[0] + sx[1] + sx[2]
            y_out = wire.send(ax.at[1 - yl], sy, p.Y)
        else:
            y_out.wait_recv()
            ay[...] = ax[yl] + sy[...]
            c_out = wire.send(ay, sc, p.C)
    mine_head, other = p.yh * 2 + (1 - p.co), (1 - p.yh) * 2 + (1 - p.co)
    far = wire.send(part.at[other], got_c.at[0], p.C)
    near = wire.send(part.at[mine_head], got_c.at[1], p.C)
    far.wait_recv()

    def by_16(body):
        def step(i, carry):
            body(pl.ds(pl.multiple_of(i * 16, 16), 16))
            return carry

        lax.fori_loop(0, 8, step, 0)

    def add_far(at):
        away = part[(1 - p.yh) * 2 + p.co, at].astype(f32)
        half[at] = (away + got_c[0, at].astype(f32)).astype(bf16)

    by_16(add_far)
    over = wire.send(half, got_h, p.H)
    c_out.wait_recv()
    ac[...] = ay[...] + sc[...]
    h_out = wire.send(ac, sh, p.H)
    seconds = []
    for i, gradient in ((0, p0), (1, p1)):
        one, two = starts[i]
        one.wait_recv()
        loop(2, lambda d: added(gradient.at[d, :, p.xr], gradient.at[d, :, p.xr], ra.at[i, 0, d]))
        s1 = wire.send(gradient.at[:, :, p.xr], rc.at[i, 0], p.XR)
        two.wait_recv()
        loop(
            2,
            lambda d: added(gradient.at[d + 2, :, p.xl], gradient.at[d + 2, :, p.xl], ra.at[i, 1, d]),
        )
        s2 = wire.send(gradient.at[:, :, p.xl], rc.at[i, 1], p.XL)
        seconds.append((s1, s2))
    mids = {}
    for i, gradient in ((3, p3), (2, p2)):
        firsts[i].wait_recv()
        loop(4, lambda d: added(acc_y.at[i - 2, d], gradient.at[d, yl], rb.at[i - 2, d]))
        acc = acc_y.at[i - 2]
        mids[i] = (
            wire.send(acc.at[0:2, p.xo], rd.at[i - 2, 0], p.XR),
            wire.send(acc.at[2:4, p.xo], rd.at[i - 2, 1], p.XL),
        )
    near.wait_recv()
    over.wait_recv()

    def add_near(at):
        close = part[p.yh * 2 + p.co, at].astype(f32) + got_c[1, at].astype(f32)
        normed[at] = close + got_h[at].astype(f32)

    by_16(add_near)
    for c in range(16):
        cols = slice(c * 128, (c + 1) * 128)
        column = jnp.sum(normed[:, cols] * unit[:, cols], axis=0, keepdims=True)
        mine[0, c : c + 1] = column
    h_out.wait_recv()
    whole[dp, yl, x] = ac[...] + sh[...]
    y_all = wire.send(whole.at[dp, yl, x], whole.at[dp, yl, x], p.Y)
    tz_out = [wire.send(mine.at[0], tz.at[dp], dev) for _, dev in far_z]
    tz[dp] = mine[0]
    yends = []
    for i, gradient in ((0, p0), (1, p1)):
        for s in seconds[i]:
            s.wait_recv()
        acc = acc_x.at[i]
        loop(4, lambda d: added(acc.at[d], gradient.at[d, :, x], rc.at[i, 0, d], rc.at[i, 1, d]))
        yends.append(wire.send(acc.at[:, 1 - yl], re.at[i], p.Y))
    y_all.wait_recv()
    x_all = [wire.send(whole.at[dp, :, x], whole.at[dp, :, x], dev) for _, dev in far_x]
    for copy in tz_out:
        copy.wait_recv()
    mine[1] = tz[0] + tz[1] + tz[2] + tz[3]
    tx_out = [wire.send(mine.at[1], tx.at[x], dev) for _, dev in far_x]
    tx[x] = mine[1]
    xends = {}
    for i in (3, 2):
        acc = acc_y.at[i - 2]
        one, two = mids[i]
        one.wait_recv()
        loop(2, lambda d: added(acc.at[d, p.xr], acc.at[d, p.xr], rd.at[i - 2, 0, d]))
        s1 = wire.send(acc.at[:, p.xr], rf.at[i - 2, 0], p.XR)
        two.wait_recv()
        loop(2, lambda d: added(acc.at[d + 2, p.xl], acc.at[d + 2, p.xl], rd.at[i - 2, 1, d]))
        s2 = wire.send(acc.at[:, p.xl], rf.at[i - 2, 1], p.XL)
        xends[i] = (s1, s2)
    for copy in x_all:
        copy.wait_recv()
    z_all = [wire.send(whole.at[dp], whole.at[dp], dev) for _, dev in far_z]
    for copy in tx_out:
        copy.wait_recv()
    mine[2] = tx[0] + tx[1] + tx[2] + tx[3]
    ty_out = wire.send(mine.at[2], ty, p.Y)
    parts, zs = {}, {}

    def z_first(i, acc):
        parts[i] = acc
        zs[i] = (
            wire.send(acc.at[p.zo, 0:32], rg.at[i, 0, 0:32], p.ZR),
            wire.send(acc.at[p.zo, 32:64], rg.at[i, 1, 0:32], p.ZL),
        )

    for i in (0, 1):
        yends[i].wait_recv()
        acc = acc_x.at[i]
        loop(4, lambda d: added(acc.at[d, yl], acc.at[d, yl], re.at[i, d]))
        z_first(i, acc.at[:, yl])
    ty_out.wait_recv()
    mine[3] = mine[2] + ty[...]
    tc_out = wire.send(mine.at[3], tc, p.C)
    for i in (3, 2):
        for s in xends[i]:
            s.wait_recv()
        acc = acc_y.at[i - 2]
        loop(
            4, lambda d: added(acc.at[d, x], acc.at[d, x], rf.at[i - 2, 0, d], rf.at[i - 2, 1, d])
        )
        z_first(i, acc.at[:, x])
    tc_out.wait_recv()
    mine[4] = mine[3] + tc[...]
    th_out = wire.send(mine.at[4], th, p.H)
    ends = {}
    for i in (0, 1, 3, 2):
        one, two = zs[i]
        acc = parts[i]
        one.wait_recv()
        added(acc.at[p.zr, 0:32], acc.at[p.zr, 0:32], rg.at[i, 0, 0:32])
        s1 = wire.send(acc.at[p.zr], rg.at[i, 2], p.ZR)
        two.wait_recv()
        added(acc.at[p.zl, 32:64], acc.at[p.zl, 32:64], rg.at[i, 1, 0:32])
        s2 = wire.send(acc.at[p.zl], rg.at[i, 3], p.ZL)
        ends[i] = (s1, s2)
    th_out.wait_recv()
    tiny[...] = mine[4] + th[...]
    for i in range(4):
        for s in ends[i]:
            s.wait_recv()
        added(out.at[i], parts[i].at[dp], rg.at[i, 2], rg.at[i, 3])
    for copy in z_all:
        copy.wait_recv()
    wire.drain()


def last_sums(grads, kept, w, rows, cosine, sine, gains, fourth, unit, small):
    return remote_call(
        last_kernel,
        "last_sums",
        8,
        64,
        1,
        [VMEM] * 10,
        [VMEM] * 4,
        (
            shaped((4, 64, 512), f32),
            shaped((128, 2048), f32),
            shaped((4, 2, 4, 40, 128), f32),
            shaped((24, 128), f32),
        ),
        scratch=[
            pltpu.VMEM((512, 512), bf16),
            pltpu.VMEM((512, 2048), f32),
            pltpu.VMEM((3, 4, 2, 4, 64, 512), bf16),
            pltpu.VMEM((4, 128, 2048), bf16),
            pltpu.VMEM((2, 128, 2048), bf16),
            pltpu.VMEM((128, 2048), bf16),
            pltpu.VMEM((128, 2048), bf16),
            pltpu.VMEM((5, 24, 128), f32),
            pltpu.VMEM((2, 2, 2, 2, 64, 512), bf16),
            pltpu.VMEM((2, 4, 4, 64, 512), bf16),
            pltpu.VMEM((2, 2, 4, 2, 64, 512), bf16),
            pltpu.VMEM((2, 2, 2, 64, 512), bf16),
            pltpu.VMEM((2, 4, 64, 512), bf16),
            pltpu.VMEM((2, 2, 4, 64, 512), bf16),
            pltpu.VMEM((4, 4, 64, 512), bf16),
            pltpu.VMEM((2, 4, 2, 64, 512), bf16),
            pltpu.VMEM((2, 4, 4, 64, 512), bf16),
            pltpu.VMEM((3, 2, 4, 40, 128), f32),
            pltpu.VMEM((2, 4, 40, 128), f32),
            pltpu.VMEM((3, 2, 40, 128), f32),
            pltpu.VMEM((2, 40, 128), f32),
            pltpu.VMEM((40, 128), f32),
            pltpu.VMEM((40, 128), f32),
            pltpu.VMEM((40, 128), f32),
            pltpu.VMEM((40, 128), f32),
            pltpu.VMEM((40, 128), f32),
            pltpu.VMEM((4, 24, 128), f32),
            pltpu.VMEM((4, 24, 128), f32),
            pltpu.VMEM((24, 128), f32),
            pltpu.VMEM((24, 128), f32),
            pltpu.VMEM((24, 128), f32),
        ],
        vmem=60 << 20,
    )(
        grads, kept, w, rows, cosine, sine, gains,
        fourth.reshape(4, 2, 4, 64, 512), unit, small.reshape(4, 2, 4, 40, 128),
    )


def on_device(
    tokens,
    segment_ids,
    valid_mask,
    routes,
    attn_gain,
    w_query,
    w_key,
    w_value,
    w_out,
    query_gain,
    key_gain,
    ffn_gain,
    router,
    expert_in,
    expert_out,
    cotangent,
):
    blk = lax.axis_index("blk")
    device = lax.axis_index("head") * 8 + blk
    yl = blk // 4
    tok, width = tokens.shape
    full_in = lax.all_gather(jnp.transpose(expert_in, (1, 0, 2)), "dp", axis=1, tiled=True)
    full_back = lax.all_gather(jnp.transpose(expert_out, (1, 0, 2)), "dp", axis=1, tiled=True)

    segment, valid = segment_ids[0], valid_mask[0]
    seq_len = segment.shape[0]
    place = jnp.arange(seq_len, dtype=i32)
    query_ids = (jnp.arange(4)[:, None] * 1024 + blk * 128 + jnp.arange(128)[None]).reshape(-1)
    frequency = rope_base ** (-jnp.arange(64, dtype=f32) / 64)
    angles = query_ids.astype(f32)[:, None] * frequency[None]
    cosine, sine = jnp.cos(angles), jnp.sin(angles)
    cosine = jnp.concatenate([cosine, cosine], axis=1)
    sine = jnp.concatenate([-sine, sine], axis=1)
    half_ids = (jnp.arange(4)[:, None] * 1024 + yl * 512 + jnp.arange(512)[None]).reshape(-1)
    half_seg = lax.dynamic_index_in_dim(segment.reshape(4, 2, 512), yl, 1, keepdims=False).reshape(-1)
    key_seg = jnp.where(valid > 0, segment, -1)
    ends = half_seg.reshape(-1, QB)
    lower = jnp.sum(segment[None] < ends[:, :1], axis=1, dtype=i32) // KB
    upper = (jnp.sum(segment[None] <= ends[:, -1:], axis=1, dtype=i32) + KB - 1) // KB
    limits = jnp.stack([lower, upper])

    inputs = tokens.astype(f32)
    first_inv = rms_rows(inputs)
    normed = (inputs * first_inv * attn_gain).astype(bf16)
    w_three = jnp.stack([w_query, w_key, w_value])
    gathered, out_part, normed_all = gather_weights(w_three, w_out, normed)
    full_three = gathered.reshape(3, 2048, 512)
    normed_all = normed_all.reshape(512, width)

    def flat_of(heads):
        return jnp.transpose(heads.reshape(4, 512, HD), (1, 0, 2)).reshape(512, 512)

    head_gains = jnp.stack([query_gain, key_gain])[:, None]
    heads, projected = project(normed_all, full_three, cosine, sine, head_gains)
    runs = (4, 4, 128, HD)
    q, k, v, full_out = heads_over_x(heads.reshape((3,) + runs), out_part)
    q, k, v = q.reshape(2048, HD), k.reshape(4096, HD), v.reshape(4096, HD)
    full_out = full_out.reshape(2048, 512)
    att_low, att, inverse = attend(limits, q, k, v, half_seg, half_ids, key_seg)
    attended, branch = attended_home(att_low.reshape(runs), full_out)
    attended_flat = flat_of(attended)
    middle = inputs + branch
    second_inv = rms_rows(middle)
    normed_ffn = (middle * second_inv * ffn_gain).astype(bf16)
    logits = jnp.dot(normed_ffn, router, preferred_element_type=f32)
    probabilities = jax.nn.softmax(logits, axis=-1)

    expert_ids = jnp.arange(EXPERTS, dtype=i32)
    hot = jnp.sum((routes[..., None] == expert_ids).astype(f32), axis=1)
    before = (jnp.arange(tok)[:, None] > jnp.arange(tok)[None]).astype(bf16)
    slots = jnp.dot(before, hot.astype(bf16), preferred_element_type=f32)
    slot_code = jnp.where(hot > 0, slots, -1.0)
    chosen = probabilities * hot
    gate_total = jnp.sum(chosen, axis=-1, keepdims=True)
    gates = chosen / gate_total

    sent = jnp.concatenate([normed_ffn, slot_code.astype(bf16), gates.astype(bf16)], axis=1)
    everyone = spread(sent, 7)
    lane = jnp.arange(128)[None]
    sel_row = jnp.arange(8)[:, None]
    info = everyone[:, :, width:]
    column = (sel_row // 2) * EXPERTS + device * EXP_DEV + sel_row % 2
    sel = ((sel_row < 4) & (lane == column)).astype(bf16)
    nearby = (device ^ 8) * EXP_DEV
    column = sel_row % 2 + jnp.where(sel_row // 2 % 2 == 0, device * EXP_DEV, nearby)
    sel_chip = (lane == column + (sel_row // 4) * EXPERTS).astype(bf16)
    flat_info, flat_everyone = info.reshape(32 * tok, -1), everyone.reshape(32 * tok, -1)
    expert_rows, row_gates = pick_rows(sel, flat_info, flat_everyone, width, True)
    expert_rows = expert_rows.reshape(EXP_DEV, -1, width)
    row_gates = row_gates.reshape(EXP_DEV, -1, 128)
    all_cot, gate_part, up_part, hidden, expert_result = expert_forward(
        cotangent, expert_rows, full_in, full_back, 11
    )
    (arrived_cot,) = pick_rows(sel, flat_info, all_cot.reshape(32 * tok, width), width, False)
    arrived_cot = arrived_cot.reshape(EXP_DEV, -1, width)
    mixture, row_dots, grad_gate, grad_up, grad_rows, term_back = expert_backward(
        sel_chip, info, expert_result, arrived_cot, gate_part, up_part, hidden, row_gates,
        full_in, full_back, 12,
    )
    row_dots = jnp.sum(row_dots, axis=-1, keepdims=True)
    high = row_dots.astype(bf16)
    column = (device * EXP_DEV + jnp.arange(EXP_DEV))[:, None, None]
    low = jnp.where(lane == column + EXPERTS, (row_dots - high.astype(f32)).astype(bf16), 0)
    row_dots = jnp.where(lane == column, high, low)
    grad_home, term_in = expert_finish(
        sel_chip, info, grad_rows, row_dots, expert_rows, grad_gate, grad_up, 13
    )
    grad_gates = grad_home[:, width : width + EXPERTS] + grad_home[:, width + EXPERTS :]
    grad_home = grad_home[:, :width]

    def fold_dp(term):
        return lax.psum_scatter(term.astype(bf16), "dp", scatter_dimension=1, tiled=True)

    expert_out_grad = unstack(fold_dp(term_back))
    expert_in_grad = unstack(fold_dp(term_in))

    output = (middle + mixture).astype(bf16)
    grad_out = cotangent.astype(f32)
    mean_grad = jnp.sum(grad_gates * gates, axis=-1, keepdims=True)
    grad_probs = (grad_gates - mean_grad) / gate_total * hot
    grad_logits = probabilities * (
        grad_probs - jnp.sum(probabilities * grad_probs, axis=-1, keepdims=True)
    )
    high = grad_logits.astype(bf16)
    halves = jnp.concatenate([high, (grad_logits - high.astype(f32)).astype(bf16)], axis=1)
    router_term = jnp.einsum("td,te->de", normed_ffn, halves, preferred_element_type=f32)
    router_term = router_term[:, :EXPERTS] + router_term[:, EXPERTS:]
    grad_ffn = grad_home + jnp.einsum(
        "te,de->td", halves, jnp.concatenate([router, router], axis=1), preferred_element_type=f32
    )
    ffn_gain_term = jnp.sum(grad_ffn * middle * second_inv, axis=0)
    grad_middle = grad_out + rms_back(middle, second_inv, grad_ffn * ffn_gain)
    grad_branch = grad_middle.astype(bf16)
    branch_all, grad_att = branch_to_heads(grad_branch, full_out)
    branch_all, grad_att = branch_all.reshape(512, width), grad_att.reshape(2048, HD)
    delta = jnp.sum(grad_att.astype(f32) * att, axis=-1)
    dq, dk, dv = attend_back(
        limits, q, k, v, grad_att, half_seg, half_ids, key_seg, inverse[:, 0], delta
    )
    cut = (4, 2, 4, 128, HD)
    grad_heads = grads_over_x(dq.reshape(runs), dk.reshape(cut), dv.reshape(cut))
    out_grad = jnp.einsum(
        "qc,qf->cf", branch_all, attended_flat, preferred_element_type=f32
    ).astype(bf16)
    gains = jnp.pad(ffn_gain_term, (0, 32 * 8 * 128 - width)).reshape(32, 8, 128)
    small = jnp.concatenate([router_term.reshape(32, 32, 128), gains], axis=1)
    attn_grads, grad_normed, summed, tiny = last_sums(
        grad_heads.reshape(3, 4, 512, HD), projected, full_three, normed_all, cosine, sine,
        head_gains, out_grad, inputs * first_inv, small,
    )
    input_grad = grad_middle + rms_back(inputs, first_inv, grad_normed * attn_gain)
    summed = summed.reshape(32, 40, 128)
    router_grad = summed[:, :32].reshape(router.shape)
    ffn_gain_grad = summed[:, 32:].reshape(-1)[:width]
    return (
        output,
        input_grad,
        tiny[:16].reshape(-1),
        attn_grads[0],
        attn_grads[1],
        attn_grads[2],
        attn_grads[3],
        tiny[16],
        tiny[17],
        ffn_gain_grad,
        router_grad,
        expert_in_grad,
        expert_out_grad,
    )


def solution(mesh):
    placed = (
        P(("dp", "head", "blk"), None),
        P("dp", None),
        P("dp", None),
        P(("dp", "head", "blk"), None),
        P(),
        P(("dp", "blk"), "head"),
        P(("dp", "blk"), "head"),
        P(("dp", "blk"), "head"),
        P(("dp", "blk"), "head"),
        P(),
        P(),
        P(),
        P(),
        P("dp", ("head", "blk"), None),
        P("dp", ("head", "blk"), None),
        P(("dp", "head", "blk"), None),
    )
    return jax.shard_map(
        on_device,
        mesh=mesh,
        in_specs=placed,
        out_specs=(
            P(("dp", "head", "blk"), None),
            P(("dp", "head", "blk"), None),
            P(),
            P(("dp", "blk"), "head"),
            P(("dp", "blk"), "head"),
            P(("dp", "blk"), "head"),
            P(("dp", "blk"), "head"),
            P(),
            P(),
            P(),
            P(),
            P("dp", ("head", "blk"), None),
            P("dp", ("head", "blk"), None),
        ),
        check_vma=False,
    )
```

```python
import functools
import math

import jax
import jax.numpy as jnp
from jax import lax
from jax.experimental import pallas as pl
from jax.experimental.pallas import tpu as pltpu
from jax.sharding import PartitionSpec as P

HEADS = 16
HD = 128
FF = 1024
TOPK = 8
EXP_DEV = 2
CAP = 24
EXPERTS = 64

epsilon = 1e-06
rope_base = 50000.0
f32 = jnp.float32
bf16 = jnp.bfloat16
i32 = jnp.int32
MESH = pl.DeviceIdType.MESH
ANY = pl.BlockSpec(memory_space=pl.ANY)
VMEM = pl.BlockSpec(memory_space=pltpu.VMEM)
SMEM = pl.BlockSpec(memory_space=pltpu.SMEM)
DMA = pltpu.SemaphoreType.DMA


def rms_rows(values):
    return lax.rsqrt(jnp.mean(values * values, axis=-1, keepdims=True) + epsilon)


def rms_back(values, inverse, grad_scaled):
    inner_mean = jnp.mean(grad_scaled * values, axis=-1, keepdims=True)
    return inverse * grad_scaled - values * inverse * inverse * inverse * inner_mean


def wrap4(value):
    return lax.rem(value + 4, 4)


class Place:
    def __init__(self):
        head, blk = lax.axis_index("head"), lax.axis_index("blk")
        self.dp = lax.axis_index("dp")
        self.yh, self.co = head // 2, lax.rem(head, 2)
        self.yl, self.x = blk // 4, lax.rem(blk, 4)
        self.head = head
        self.zr, self.zl, self.zo = (wrap4(self.dp + s) for s in (1, -1, 2))
        self.xr, self.xl, self.xo = (wrap4(self.x + s) for s in (1, -1, 2))
        y = self.yh * 2 + self.yl
        self.yr, self.ylf, self.yo = (wrap4(y + s) for s in (1, -1, 2))
        self.ZR, self.ZL, self.ZO = {"dp": self.zr}, {"dp": self.zl}, {"dp": self.zo}
        self.XR, self.XL, self.XO = (self.to_x(v) for v in (self.xr, self.xl, self.xo))
        self.Y = {"blk": (1 - self.yl) * 4 + self.x}
        self.C = {"head": self.yh * 2 + (1 - self.co)}
        self.H = {"head": (1 - self.yh) * 2 + self.co}
        self.YR, self.YL = self.to_y(self.yr), self.to_y(self.ylf)

    def to_x(self, x):
        return {"blk": self.yl * 4 + x}

    def to_y(self, y):
        return {"head": (y // 2) * 2 + self.co, "blk": lax.rem(y, 2) * 4 + self.x}


def greet(devices):
    barrier = pltpu.get_barrier_semaphore()
    for device in devices:
        pl.semaphore_signal(barrier, inc=1, device_id=device, device_id_type=MESH)
    pl.semaphore_wait(barrier, len(devices))


class View:
    def __init__(self, ref, index=None):
        self.ref, self.index = ref, index

    @property
    def at(self):
        return self

    def __getitem__(self, index):
        return View(self, index)

    def get(self):
        base = self.ref.get() if isinstance(self.ref, View) else self.ref
        return base if self.index is None else base.at[self.index]

    def load(self):
        return self.get()[...]

    def store(self, value):
        ref = self.get()
        ref[...] = value.astype(ref.dtype)


def plain(ref):
    return ref.get() if isinstance(ref, View) else ref


class Sent:
    def __init__(self, make):
        self.make = make

    def wait_recv(self):
        self.make().wait_recv()

    def wait_send(self):
        self.make().wait_send()

    def wait(self):
        self.make().wait()


class Wire:
    def __init__(self, send_sem, recv_sem):
        self.send_sem, self.recv_sem, self.started = send_sem, recv_sem, []

    def send(self, src, dst, device):
        at = len(self.started)

        def make():
            return pltpu.make_async_remote_copy(
                src_ref=plain(src),
                dst_ref=plain(dst),
                send_sem=self.send_sem.at[at],
                recv_sem=self.recv_sem.at[at],
                device_id=device,
                device_id_type=MESH,
            )

        make().start()
        self.started.append(Sent(make))
        return self.started[-1]

    def drain(self):
        for copy in self.started:
            copy.wait_send()


def local(src, dst, sems, at):
    def make():
        return pltpu.make_async_copy(plain(src), plain(dst), sems.at[at])

    make().start()
    return Sent(make)


def remote_call(body, name, cid, sends, locals_, ins, outs, out_shape, scratch=(), vmem=None):
    return pl.pallas_call(
        body,
        name=name,
        out_shape=out_shape,
        in_specs=ins,
        out_specs=outs,
        scratch_shapes=[DMA((sends,)), DMA((sends,)), DMA((max(locals_, 1),)), *scratch],
        compiler_params=pltpu.CompilerParams(
            collective_id=cid, has_side_effects=True, vmem_limit_bytes=vmem
        ),
    )


def shaped(shape, dtype=bf16):
    return jax.ShapeDtypeStruct(shape, dtype)


def weights_kernel(w, wo, n, g, go, m, ss, rs, ls):
    p = Place()
    dp, yl, x = p.dp, p.yl, p.x
    own = [
        local(w, g.at[:, dp, yl, x], ls, 0),
        local(n, m.at[p.head], ls, 1),
        local(wo, go.at[dp], ls, 2),
    ]
    greet([p.ZR, p.ZL, p.XR, p.XL, p.Y, p.C, p.H])
    wire = Wire(ss, rs)
    n_c = wire.send(n, m.at[p.head], p.C)
    z1 = wire.send(w, g.at[:, dp, yl, x], p.ZR)
    z2 = wire.send(w, g.at[:, dp, yl, x], p.ZL)
    n_h = wire.send(n, m.at[p.head], p.H)
    o1 = wire.send(wo, go.at[dp], p.ZR)
    o2 = wire.send(wo, go.at[dp], p.ZL)
    z1.wait_recv()
    z3 = wire.send(g.at[0:2, p.zl, yl, x], g.at[0:2, p.zl, yl, x], p.ZR)
    z2.wait_recv()
    z4 = wire.send(g.at[2, p.zr, yl, x], g.at[2, p.zr, yl, x], p.ZL)
    own[0].wait()
    z3.wait_recv()
    z4.wait_recv()
    b1 = wire.send(g.at[2, :, yl, x], g.at[2, :, yl, x], p.XR)
    b2 = wire.send(g.at[2, :, yl, x], g.at[2, :, yl, x], p.XL)
    a1 = wire.send(g.at[0:2, :, yl, x], g.at[0:2, :, yl, x], p.Y)
    c1 = wire.send(g.at[2, :, yl, x], g.at[2, :, yl, x], p.Y)
    o1.wait_recv()
    o3 = wire.send(go.at[p.zl, 0:32], go.at[p.zl, 0:32], p.ZR)
    o2.wait_recv()
    o4 = wire.send(go.at[p.zr, 32:64], go.at[p.zr, 32:64], p.ZL)
    n_h.wait_recv()
    other = (1 - p.yh) * 2 + p.co
    n_f = wire.send(m.at[other], m.at[other], p.C)
    b1.wait_recv()
    b3 = wire.send(g.at[2, 0:2, yl, p.xl], g.at[2, 0:2, yl, p.xl], p.XR)
    c2 = wire.send(g.at[2, :, yl, p.xl], g.at[2, :, yl, p.xl], p.Y)
    b2.wait_recv()
    b4 = wire.send(g.at[2, 2:4, yl, p.xr], g.at[2, 2:4, yl, p.xr], p.XL)
    c3 = wire.send(g.at[2, :, yl, p.xr], g.at[2, :, yl, p.xr], p.Y)
    a1.wait_recv()
    a2 = wire.send(g.at[0:2, :, :, x], g.at[0:2, :, :, x], p.XR)
    a3 = wire.send(g.at[0:2, :, :, x], g.at[0:2, :, :, x], p.XL)
    b3.wait_recv()
    b4.wait_recv()
    c4 = wire.send(g.at[2, :, yl, p.xo], g.at[2, :, yl, p.xo], p.Y)
    a2.wait_recv()
    a4 = wire.send(g.at[0, :, :, p.xl], g.at[0, :, :, p.xl], p.XR)
    a3.wait_recv()
    a5 = wire.send(g.at[1, :, :, p.xr], g.at[1, :, :, p.xr], p.XL)
    for copy in (n_c, n_f, o3, o4, c1, c2, c3, c4, a4, a5):
        copy.wait_recv()
    own[1].wait()
    own[2].wait()
    wire.drain()


def gather_weights(w, wo, n):
    return remote_call(
        weights_kernel,
        "gather_weights",
        1,
        24,
        3,
        [ANY] * 3,
        [ANY] * 3,
        (shaped((3, 4, 2, 4, 64, 512)), shaped((4, 64, 512)), shaped((4, 128, 2048))),
    )(w, wo, n)


def heads_kernel(three, go, qd, kd, vd, gd, ss, rs, ls):
    p = Place()
    q, k, v = (three.at[i] for i in range(3))
    yl, x = p.yl, p.x
    own = [
        local(q.at[x], qd.at[:, x], ls, 0),
        local(k.at[x], kd.at[:, yl, x], ls, 1),
        local(v.at[x], vd.at[:, yl, x], ls, 2),
        local(go, gd.at[:, yl, x], ls, 3),
    ]
    greet([p.Y, p.XR, p.XL, p.XO])
    wire = Wire(ss, rs)
    done = [
        wire.send(k.at[x], kd.at[:, yl, x], p.Y),
        wire.send(v.at[x], vd.at[:, yl, x], p.Y),
    ]
    w1 = wire.send(go, gd.at[:, yl, x], p.Y)
    moved = []
    for there, came, device in ((p.xo, p.xo, p.XO), (p.xr, p.xl, p.XR), (p.xl, p.xr, p.XL)):
        ks = wire.send(k.at[there], kd.at[:, yl, x], device)
        vs = wire.send(v.at[there], vd.at[:, yl, x], device)
        moved.append((came, ks, vs))
    for there, device in ((p.xo, p.XO), (p.xr, p.XR), (p.xl, p.XL)):
        done.append(wire.send(q.at[there], qd.at[:, x], device))
    for came, ks, vs in moved[1:] + moved[:1]:
        ks.wait_recv()
        done.append(wire.send(kd.at[:, yl, came], kd.at[:, yl, came], p.Y))
        vs.wait_recv()
        done.append(wire.send(vd.at[:, yl, came], vd.at[:, yl, came], p.Y))
    own[3].wait()
    w1.wait_recv()
    w2 = wire.send(gd.at[:, :, x], gd.at[:, :, x], p.XR)
    w3 = wire.send(gd.at[:, :, x], gd.at[:, :, x], p.XL)
    w2.wait_recv()
    done.append(wire.send(gd.at[0:2, :, p.xl], gd.at[0:2, :, p.xl], p.XR))
    w3.wait_recv()
    done.append(wire.send(gd.at[2:4, :, p.xr], gd.at[2:4, :, p.xr], p.XL))
    for copy in done:
        copy.wait_recv()
    for copy in own[:3]:
        copy.wait()
    wire.drain()


def heads_over_x(three, go):
    return remote_call(
        heads_kernel,
        "heads_over_x",
        3,
        22,
        4,
        [ANY] * 2,
        [ANY] * 4,
        (
            shaped((4, 4, 128, 128)),
            shaped((4, 2, 4, 128, 128)),
            shaped((4, 2, 4, 128, 128)),
            shaped((4, 2, 4, 64, 512)),
        ),
    )(three, go)


def attended_kernel(o, w, att, out, ss, rs, ls, flat, part, got_c, got_h, half):
    p = Place()
    greet([p.C, p.H, p.XR, p.XL, p.XO])
    wire = Wire(ss, rs)
    near_c, far_c = p.yh * 2 + (1 - p.co), (1 - p.yh) * 2 + (1 - p.co)
    far = (1 - p.yh) * 2 + p.co
    order = (far_c, near_c, far, p.head)
    came = []
    for run in order:
        came.append(
            [
                wire.send(o.at[run, there], att.at[p.x, run], device)
                for there, device in ((p.xo, p.XO), (p.xr, p.XR), (p.xl, p.XL))
            ]
        )
        att[p.x, run] = o[run, p.x]

    def times(i, store):
        for copy in came[i]:
            copy.wait_recv()
        for h in range(4):
            flat[:, h * HD : (h + 1) * HD] = att[h, order[i]]
        for c in range(0, 2048, 512):
            cols = slice(c, c + 512)
            store(cols, nt(flat[...], w[cols]))

    sums = []
    for i in range(2):

        def keep(cols, value):
            part[i, :, cols] = value.astype(bf16)

        times(i, keep)
        sums.append(wire.send(part.at[i], got_c.at[i], p.C))
    sums[0].wait_recv()

    def add_far(cols, value):
        half[:, cols] = (value + got_c[0, :, cols].astype(f32)).astype(bf16)

    times(2, add_far)
    over = wire.send(half, got_h, p.H)

    def first(cols, value):
        out[:, cols] = value

    times(3, first)
    sums[1].wait_recv()
    over.wait_recv()

    def add(i, carry):
        at = pl.ds(pl.multiple_of(i * 16, 16), 16)
        out[at] += got_c[1, at].astype(f32) + got_h[at].astype(f32)
        return carry

    lax.fori_loop(0, 8, add, 0)
    wire.drain()


def attended_home(o, w):
    return remote_call(
        attended_kernel,
        "attended_home",
        4,
        15,
        1,
        [VMEM, VMEM],
        [VMEM, VMEM],
        (shaped((4, 4, 128, 128)), shaped((128, 2048), f32)),
        scratch=[
            pltpu.VMEM((128, 512), bf16),
            pltpu.VMEM((2, 128, 2048), bf16),
            pltpu.VMEM((2, 128, 2048), bf16),
            pltpu.VMEM((128, 2048), bf16),
            pltpu.VMEM((128, 2048), bf16),
        ],
        vmem=32 << 20,
    )(o, w)


def branch_kernel(n, w, m, d, ss, rs, ls, heads):
    p = Place()
    own = local(n, m.at[p.head], ls, 0)
    greet([p.C, p.H, p.XR, p.XL, p.XO])
    wire = Wire(ss, rs)
    n_h = wire.send(n, m.at[p.head], p.H)
    n_c = wire.send(n, m.at[p.head], p.C)
    sibling = p.yh * 2 + (1 - p.co)
    other, last = (1 - p.yh) * 2 + p.co, (1 - p.yh) * 2 + (1 - p.co)
    moved = []

    def out(run, at):
        value = jnp.dot(m[run], w[...], preferred_element_type=f32).astype(bf16)
        for h in range(4):
            heads[at, h] = value[:, h * HD : (h + 1) * HD]
        for there, device in ((p.xo, p.XO), (p.xr, p.XR), (p.xl, p.XL)):
            moved.append(wire.send(heads.at[at, there], d.at[run, p.x], device))
        d[run, p.x] = heads[at, p.x]

    own.wait()
    out(p.head, 0)
    n_c.wait_recv()
    out(sibling, 1)
    n_h.wait_recv()
    n_f = wire.send(m.at[other], m.at[other], p.C)
    out(other, 2)
    n_f.wait_recv()
    out(last, 3)
    for copy in moved:
        copy.wait_recv()
    wire.drain()


def branch_to_heads(n, w):
    return remote_call(
        branch_kernel,
        "branch_to_heads",
        2,
        15,
        1,
        [VMEM, VMEM],
        [VMEM, VMEM],
        (shaped((4, 128, 2048)), shaped((4, 4, 128, 128))),
        scratch=[pltpu.VMEM((4, 4, 128, 128), bf16)],
        vmem=32 << 20,
    )(n, w)


def grads_x_kernel(dq, dk, dv, three, ss, rs, ls, gk, gv, sk, sv):
    p = Place()
    x, yl = p.x, p.yl
    qd, kd, vd = (three.at[i] for i in range(3))
    own = local(dq.at[:, x], qd.at[x], ls, 0)
    greet([p.Y, p.XR, p.XL, p.XO])
    wire = Wire(ss, rs)
    order = ((p.xo, p.XO), (p.xr, p.XR), (p.xl, p.XL), (x, None))
    pairs = []
    for i, (there, device) in enumerate(order):
        pairs.append(
            (
                wire.send(dk.at[:, 1 - yl, there], gk.at[i], p.Y),
                wire.send(dv.at[:, 1 - yl, there], gv.at[i], p.Y),
            )
        )
    last = []
    for there, device in order[:3]:
        last.append(wire.send(dq.at[:, there], qd.at[x], device))
    for i, (there, device) in enumerate(order):
        for grads, got, summed, out, arrived in (
            (dk, gk, sk, kd, pairs[i][0]),
            (dv, gv, sv, vd, pairs[i][1]),
        ):
            arrived.wait_recv()
            for run in range(4):
                total = grads[run, yl, there].astype(f32) + got[i, run].astype(f32)
                if device is None:
                    out[x, run] = total.astype(bf16)
                else:
                    summed[i, run] = total.astype(bf16)
            if device is not None:
                last.append(wire.send(summed.at[i], out.at[x], device))
    for copy in last:
        copy.wait_recv()
    own.wait()
    wire.drain()


def grads_over_x(dq, dk, dv):
    return remote_call(
        grads_x_kernel,
        "grads_over_x",
        6,
        17,
        1,
        [ANY, VMEM, VMEM],
        [VMEM],
        (shaped((3, 4, 4, 128, 128)),),
        scratch=[
            pltpu.VMEM((4, 4, 128, 128), bf16),
            pltpu.VMEM((4, 4, 128, 128), bf16),
            pltpu.VMEM((3, 4, 128, 128), bf16),
            pltpu.VMEM((3, 4, 128, 128), bf16),
        ],
        vmem=16 << 20,
    )(dq, dk, dv)[0]


def turned(values, cosine, sine):
    return values * cosine + pltpu.roll(values, 64, 1) * sine


def project_kernel(rows, w, cosine, sine, gain, heads, kept):
    flat = jnp.dot(rows[...], w[0], preferred_element_type=f32)
    step = pl.program_id(0)
    for h in range(4):
        head = flat[:, h * HD : (h + 1) * HD]

        @pl.when(step < 2)
        def _():
            kept[0, h] = head
            scaled = head * rms_rows(head) * gain[0]
            heads[0, h] = turned(scaled, cosine[...], sine[...]).astype(bf16)

        @pl.when(step == 2)
        def _():
            heads[0, h] = head.astype(bf16)


def project(rows, w, cosine, sine, gains):
    def fixed(*shape):
        return pl.BlockSpec(shape, lambda i: (0,) * len(shape))

    def two(i):
        return jnp.minimum(i, 1)

    return pl.pallas_call(
        project_kernel,
        name="project",
        grid=(3,),
        out_shape=(shaped((3, 4, 512, HD)), shaped((2, 4, 512, HD), f32)),
        in_specs=[
            fixed(512, 2048),
            pl.BlockSpec((1, 2048, 512), lambda i: (i, 0, 0)),
            fixed(512, HD),
            fixed(512, HD),
            pl.BlockSpec((1, 1, HD), lambda i: (two(i), 0, 0)),
        ],
        out_specs=[
            pl.BlockSpec((1, 4, 512, HD), lambda i: (i, 0, 0, 0)),
            pl.BlockSpec((1, 4, 512, HD), lambda i: (two(i), 0, 0, 0)),
        ],
        compiler_params=pltpu.CompilerParams(vmem_limit_bytes=60 << 20),
    )(rows, w, cosine, sine, gains)


QB = 256
KB = 512
SCALE = HD**-0.5
SCALE2 = SCALE * math.log2(math.e)


def attend_kernel(lim, q, k, v, qseg, qpos, kseg, o_low, o, linv, vext):
    rows = k.shape[0]
    ones = (lax.broadcasted_iota(i32, (KB, HD), 1) == 0).astype(bf16)

    def fill(i, carry):
        at = pl.ds(pl.multiple_of(i * KB, KB), KB)
        vext[at, :HD] = v[at]
        vext[at, HD:] = ones
        return carry

    lax.fori_loop(0, rows // KB, fill, 0)

    def one_query(b, carry):
        at = pl.ds(pl.multiple_of(b * QB, QB), QB)
        query, seg, pos = q[at], qseg[at], qpos[at]

        def one_key(j, acc):
            keys = pl.ds(pl.multiple_of(j * KB, KB), KB)
            score = lax.dot_general(
                query, k[keys], (((1,), (1,)), ((), ())), preferred_element_type=f32
            )
            key_pos = j * KB + lax.broadcasted_iota(i32, (1, KB), 1)
            allowed = (seg == kseg[:, keys]) | (pos == key_pos)
            weight = jnp.where(allowed, jnp.exp2(score * SCALE2), 0.0).astype(bf16)
            return acc + jnp.dot(weight, vext[keys], preferred_element_type=f32)

        acc = lax.fori_loop(lim[0, b], lim[1, b], one_key, jnp.zeros((QB, 2 * HD), f32))
        inverse = 1.0 / acc[:, HD : HD + 1]
        result = acc[:, :HD] * inverse
        o[at] = result
        o_low[at] = result.astype(bf16)
        linv[at] = jnp.broadcast_to(inverse, (QB, HD))
        return carry

    lax.fori_loop(0, q.shape[0] // QB, one_query, 0)


def attend(lim, q, k, v, qseg, qpos, kseg):
    n = q.shape[0]
    return pl.pallas_call(
        attend_kernel,
        name="attend",
        out_shape=(shaped((n, HD)), shaped((n, HD), f32), shaped((n, HD), f32)),
        in_specs=[SMEM] + [VMEM] * 6,
        out_specs=[VMEM] * 3,
        scratch_shapes=[pltpu.VMEM((k.shape[0], 2 * HD), bf16)],
        compiler_params=pltpu.CompilerParams(vmem_limit_bytes=32 << 20),
    )(lim, q, k, v, qseg[:, None], qpos[:, None], kseg[None])


def attend_back_kernel(
    lim, q, k, v, g, qseg, qpos, kseg, linv, delta, dq, dk, dv, kt, dk_acc, dv_acc
):
    rows = k.shape[0]

    def fill(i, carry):
        at = pl.ds(pl.multiple_of(i * KB, KB), KB)
        kt[:, at] = k[at].astype(f32).T.astype(bf16)
        dk_acc[at] = jnp.zeros((KB, HD), f32)
        dv_acc[at] = jnp.zeros((KB, HD), f32)
        return carry

    lax.fori_loop(0, rows // KB, fill, 0)
    across = (((1,), (1,)), ((), ()))

    def one_query(b, carry):
        at = pl.ds(pl.multiple_of(b * QB, QB), QB)
        query, grad = q[at], g[at]
        seg, pos, inverse, shift = qseg[:, at], qpos[:, at], linv[:, at], delta[:, at]

        def one_key(j, acc):
            keys = pl.ds(pl.multiple_of(j * KB, KB), KB)
            key = k[keys]
            score = lax.dot_general(key, query, across, preferred_element_type=f32)
            key_pos = j * KB + lax.broadcasted_iota(i32, (KB, 1), 0)
            allowed = (kseg[keys] == seg) | (key_pos == pos)
            prob = jnp.where(allowed, jnp.exp2(score * SCALE2), 0.0) * inverse
            grad_prob = lax.dot_general(v[keys], grad, across, preferred_element_type=f32)
            grad_score = (prob * (grad_prob - shift)).astype(bf16)
            dv_acc[keys] += jnp.dot(prob.astype(bf16), grad, preferred_element_type=f32)
            dk_acc[keys] += jnp.dot(grad_score, query, preferred_element_type=f32)
            return acc + jnp.dot(kt[:, keys], grad_score, preferred_element_type=f32)

        acc = lax.fori_loop(lim[0, b], lim[1, b], one_key, jnp.zeros((HD, QB), f32))
        dq[at] = (acc * SCALE).T.astype(bf16)
        return carry

    lax.fori_loop(0, q.shape[0] // QB, one_query, 0)

    def finish(i, carry):
        at = pl.ds(pl.multiple_of(i * KB, KB), KB)
        dk[at] = (dk_acc[at] * SCALE).astype(bf16)
        dv[at] = dv_acc[at].astype(bf16)
        return carry

    lax.fori_loop(0, rows // KB, finish, 0)


def attend_back(lim, q, k, v, g, qseg, qpos, kseg, linv, delta):
    n, rows = q.shape[0], k.shape[0]
    return pl.pallas_call(
        attend_back_kernel,
        name="attend_back",
        out_shape=(shaped((n, HD)), shaped((rows, HD)), shaped((rows, HD))),
        in_specs=[SMEM] + [VMEM] * 9,
        out_specs=[VMEM] * 3,
        scratch_shapes=[
            pltpu.VMEM((HD, rows), bf16),
            pltpu.VMEM((rows, HD), f32),
            pltpu.VMEM((rows, HD), f32),
        ],
        compiler_params=pltpu.CompilerParams(vmem_limit_bytes=40 << 20),
    )(lim, q, k, v, g, qseg[None], qpos[None], kseg[:, None], linv[None], delta[None])


SPREAD_SENDS = 26


def spread_steps(p, wire, sems, src, dst):
    yh, co, yl, x = p.yh, p.co, p.yl, p.x
    (rh, rl), (lh, ll), (oh, ol) = ((y // 2, lax.rem(y, 2)) for y in (p.yr, p.ylf, p.yo))
    A, A1, A2 = pl.ds(0, 64), pl.ds(0, 32), pl.ds(32, 32)
    B, B1, B2 = pl.ds(64, 64), pl.ds(64, 32), pl.ds(96, 32)
    src, dst = View(src), View(dst)
    own = local(src, dst.at[yh, co, yl, x], sems, 0)

    def both(ref, device):
        return wire.send(ref, ref, device)

    me = dst.at[yh, co, yl]
    a1 = wire.send(src.at[A], me.at[x, A], p.XR)
    b1 = wire.send(src.at[B], me.at[x, B], p.YR)
    a2 = wire.send(src.at[A], me.at[x, A], p.XL)
    b2 = wire.send(src.at[B], me.at[x, B], p.YL)
    yield
    a1.wait_recv()
    a3 = both(me.at[p.xl, A1], p.XR)
    a2.wait_recv()
    a4 = both(me.at[p.xr, A2], p.XL)
    b1.wait_recv()
    b3 = both(dst.at[lh, co, ll, x, B1], p.YR)
    b2.wait_recv()
    b4 = both(dst.at[rh, co, rl, x, B2], p.YL)
    yield
    own.wait()
    a3.wait_recv()
    a4.wait_recv()
    a5 = both(me.at[:, A], p.YR)
    a6 = both(me.at[:, A], p.YL)
    b3.wait_recv()
    b4.wait_recv()
    b5 = both(dst.at[:, co, :, x, B], p.XR)
    b6 = both(dst.at[:, co, :, x, B], p.XL)
    last = [both(me.at[:, A], p.C), both(dst.at[:, co, :, x, B], p.C)]
    yield
    a5.wait_recv()
    a7 = both(dst.at[lh, co, ll, :, A1], p.YR)
    b5.wait_recv()
    b7 = both(dst.at[:, co, :, p.xl, B1], p.XR)
    a6.wait_recv()
    a8 = both(dst.at[rh, co, rl, :, A2], p.YL)
    b6.wait_recv()
    b8 = both(dst.at[:, co, :, p.xr, B2], p.XL)
    last += [both(dst.at[lh, co, ll, :, A], p.C), both(dst.at[:, co, :, p.xl, B], p.C)]
    last += [both(dst.at[rh, co, rl, :, A], p.C), both(dst.at[:, co, :, p.xr, B], p.C)]
    yield
    a7.wait_recv()
    last.append(both(dst.at[oh, co, ol, :, A1], p.C))
    b7.wait_recv()
    last.append(both(dst.at[:, co, :, p.xo, B1], p.C))
    a8.wait_recv()
    last.append(both(dst.at[oh, co, ol, :, A2], p.C))
    b8.wait_recv()
    last.append(both(dst.at[:, co, :, p.xo, B2], p.C))
    yield
    for copy in last:
        copy.wait_recv()
    wire.drain()
    yield


def greet_plane(p):
    greet([p.XR, p.XL, p.YR, p.YL, p.C])


def spread_kernel(src, dst, ss, rs, ls):
    p = Place()
    greet_plane(p)
    for _ in spread_steps(p, Wire(ss, rs), ls, src, dst):
        pass


def spread(src, cid):
    width = src.shape[1]
    return remote_call(
        spread_kernel,
        "spread",
        cid,
        SPREAD_SENDS,
        1,
        [ANY],
        [ANY],
        (shaped((2, 2, 2, 4, 128, width)),),
    )(src)[0].reshape(32, 128, width)


def at_step(number, *stages):
    for step, stage in stages:

        @pl.when(number == step)
        def _():
            next(stage)


def block(shape, index):
    return pl.BlockSpec(shape, index)


def nt(a, b):
    return lax.dot_general(a, b, (((1,), (1,)), ((), ())), preferred_element_type=f32)


def tn(a, b):
    return lax.dot_general(a, b, (((0,), (0,)), ((), ())), preferred_element_type=f32)


PARTS = 4


def forward_kernel(src, rows, w_in, w_out, dst, gate, up, hidden, y, ss, rs, ls):
    p = Place()
    greet_plane(p)
    moving = spread_steps(p, Wire(ss, rs), ls, src, dst)
    next(moving)
    n = rows.shape[1]
    cut = FF // PARTS

    def first(rows, w_gate, w_up, gate, up, hidden):
        at_step(pl.program_id(0) * PARTS + pl.program_id(1), (2, moving), (4, moving))
        g = jnp.dot(rows[0], w_gate[0], preferred_element_type=f32)
        u = jnp.dot(rows[0], w_up[0], preferred_element_type=f32)
        gate[0] = g.astype(bf16)
        up[0] = u.astype(bf16)
        hidden[0] = (g * jax.nn.sigmoid(g) * u).astype(bf16)

    out = block((1, n, cut), lambda e, j: (e, 0, j))
    pltpu.emit_pipeline(
        first,
        grid=(EXP_DEV, PARTS),
        in_specs=[
            block((1, n, 2048), lambda e, j: (e, 0, 0)),
            block((1, 2048, cut), lambda e, j: (e, 0, j)),
            block((1, 2048, cut), lambda e, j: (e, 0, j + PARTS)),
        ],
        out_specs=[out, out, out],
    )(rows, w_in, w_in, gate, up, hidden)

    def second(hidden, w, y):
        at_step(pl.program_id(0) * PARTS + pl.program_id(1), (3, moving))
        y[0] = nt(hidden[0], w[0]).astype(bf16)

    pltpu.emit_pipeline(
        second,
        grid=(EXP_DEV, PARTS),
        in_specs=[
            block((1, n, FF), lambda e, j: (e, 0, 0)),
            block((1, 2048 // PARTS, FF), lambda e, j: (e, j, 0)),
        ],
        out_specs=[block((1, n, 2048 // PARTS), lambda e, j: (e, 0, j))],
    )(hidden, w_out, y)
    for _ in moving:
        pass


def expert_forward(src, rows, w_in, w_out, cid):
    n, width = rows.shape[1:]
    outs = remote_call(
        forward_kernel,
        "expert_forward",
        cid,
        SPREAD_SENDS,
        1,
        [ANY] * 4,
        [ANY] * 5,
        (shaped((2, 2, 2, 4, 128, width)),)
        + (shaped((EXP_DEV, n, FF)),) * 3
        + (shaped((EXP_DEV, n, width)),),
        vmem=48 << 20,
    )(src, rows, w_in, w_out)
    return outs[0].reshape(32, 128, width), *outs[1:]


def slot_hits(table, count, rows_down):
    shape = (count * 2 * CAP, 256) if rows_down else (256, count * 2 * CAP)
    line = lax.broadcasted_iota(i32, shape, 0 if rows_down else 1)
    block = lax.broadcasted_iota(i32, shape, 1 if rows_down else 0) // 128
    expert = line // (2 * CAP)
    want = line - expert * (2 * CAP) - block * CAP

    def spread_out(first):
        value = jnp.zeros(shape, f32)
        for e in range(count):
            c = first + e
            at = table[c : c + 1] if rows_down else table[:, c : c + 1]
            value = jnp.where(expert == e, at, value)
        return value

    hit = (spread_out(0).astype(i32) == want) & (want >= 0) & (want < CAP)
    return hit, spread_out(count)


def pick_kernel(gated, sel, info, src, rows_out, *gates_out):
    for pair in range(src.shape[0] // 256):
        at = slice(pair * 256, (pair + 1) * 256)
        hit, gate = slot_hits(nt(sel[...], info[at]), EXP_DEV, True)
        rows = jnp.dot(hit.astype(bf16), src[at], preferred_element_type=f32).astype(bf16)
        for e in range(EXP_DEV):
            rows_out[e, pair] = rows[e * 2 * CAP : (e + 1) * 2 * CAP]
        if gated:
            total = jnp.sum(jnp.where(hit, gate, 0.0), axis=1, keepdims=True)
            total = jnp.broadcast_to(total, (EXP_DEV * 2 * CAP, 128))
            for e in range(EXP_DEV):
                gates_out[0][e, pair] = total[e * 2 * CAP : (e + 1) * 2 * CAP]


def pick_rows(sel, info, src, width, gated):
    pairs, step = src.shape[0] // 256, 2

    def spec(lanes):
        return pl.BlockSpec((EXP_DEV, step, 2 * CAP, lanes), lambda i: (0, i, 0, 0))

    shapes = [shaped((EXP_DEV, pairs, 2 * CAP, width)), shaped((EXP_DEV, pairs, 2 * CAP, 128), f32)]
    specs = [spec(width), spec(128)]
    return pl.pallas_call(
        functools.partial(pick_kernel, gated),
        name="pick_rows",
        grid=(pairs // step,),
        out_shape=shapes[: 1 + gated],
        in_specs=[
            pl.BlockSpec((8, 128), lambda i: (0, 0)),
            pl.BlockSpec((256 * step, 128), lambda i: (i, 0)),
            pl.BlockSpec((256 * step, width), lambda i: (i, 0)),
        ],
        out_specs=specs[: 1 + gated],
        compiler_params=pltpu.CompilerParams(vmem_limit_bytes=60 << 20),
    )(sel, info, src)


HOME_SENDS = 20


def home_scratch(width):
    return [
        pltpu.VMEM((2, 4, 8 * CAP, width), bf16),
        pltpu.VMEM((2, 2, 4, 128, width), bf16),
        pltpu.VMEM((2, 2, 64, width), bf16),
        pltpu.VMEM((2, 2, 64, width), bf16),
        pltpu.VMEM((2, 4, 64, width), bf16),
        pltpu.VMEM((2, 2, 2, 64, width), bf16),
        pltpu.VMEM((2, 2, 32, width), bf16),
        pltpu.VMEM((2, 2, 64, width), bf16),
    ]


def home_steps(p, wire, sems, gated, sel, info, rows, more, out, cat, q, a1, b1, a2, b2, c1, c2):
    yh, co, yl, x = p.yh, p.co, p.yl, p.x
    ys = [(yy // 2, lax.rem(yy, 2)) for yy in (p.yr, p.ylf, p.yo)]
    (rh, rl), (lh, ll), (oh, ol) = ys
    pieces = [(View(rows), slice(0, 2048))]
    if more is not None:
        pieces.append((View(more), slice(2048, 2048 + 128)))
    rows, out, whole_q, whole_cat = View(rows), View(out), q, cat
    width = cat.shape[-1]
    q, cat, a1, b1, a2, b2, c1, c2 = (View(ref) for ref in (q, cat, a1, b1, a2, b2, c1, c2))
    own, first = [], []
    for e in range(EXP_DEV):
        lines = pl.ds(e * 2 * CAP, 2 * CAP)
        there = pl.ds((2 + e) * 2 * CAP, 2 * CAP)
        for piece, lanes in pieces:
            first.append(wire.send(piece.at[e, :, 1 - co], cat.at[:, :, there, lanes], p.C))
            own.append(local(piece.at[e, :, co], cat.at[:, :, lines, lanes], sems, len(own)))
    yield
    for copy in own:
        copy.wait()
    for copy in first:
        copy.wait_recv()

    def place(h, pair):
        block = h * 16 + co * 8 + pair * 2
        both = jnp.concatenate([info[block], info[block + 1]], axis=0)
        table = lax.dot_general(
            both, sel[...], (((1,), (1,)), ((), ())), preferred_element_type=f32
        )
        hit, gate = slot_hits(table, 4, False)
        value = jnp.where(hit, gate if gated else 1.0, 0.0).astype(bf16)
        for c in range(0, width, 512):
            lanes = slice(c, min(c + 512, width))
            total = jnp.dot(
                value, whole_cat[h, pair, :, lanes], preferred_element_type=f32
            ).astype(bf16)
            at = lax.rem(pair, 2) * 2
            whole_q[h, pair // 2, at, :, lanes] = total[:128]
            whole_q[h, pair // 2, at + 1, :, lanes] = total[128:]

    def far_y(k, carry):
        place(oh, ol * 2 + k)
        return carry

    def nearer(half):
        def one(k, carry):
            y = lax.rem(yh * 2 + yl + k + k // 2, 4)
            place(y // 2, lax.rem(y, 2) * 2 + half)
            return carry

        lax.fori_loop(0, 3, one, 0)

    A, B = pl.ds(0, 64), pl.ds(64, 64)
    lax.fori_loop(0, 2, far_y, 0)
    s1 = [
        wire.send(q.at[oh, ol, 0:2, A], a1.at[0], p.YR),
        wire.send(q.at[oh, ol, 2:4, A], a1.at[1], p.YL),
    ]
    nearer(p.xo // 2)
    s1.insert(1, wire.send(q.at[0, :, p.xo, B], b1.at[0], p.XR))
    s1.append(wire.send(q.at[1, :, p.xo, B], b1.at[1], p.XL))
    nearer(1 - p.xo // 2)
    yield

    def add(dst, *srcs):
        total = srcs[0].load().astype(f32)
        for src in srcs[1:]:
            total = total + src.load().astype(f32)
        dst.store(total)

    def loop(count, body):
        def step(i, carry):
            body(i)
            return carry

        lax.fori_loop(0, count, step, 0)

    def plus(dst, src):
        add(dst, dst, src)

    s2 = []
    s1[0].wait_recv()
    loop(2, lambda i: plus(q.at[rh, rl, i, A], a1.at[0, i]))
    s2.append(wire.send(q.at[rh, rl, :, A], a2.at[0], p.YR))
    s1[1].wait_recv()
    loop(2, lambda i: plus(q.at[0, i, p.xr, B], b1.at[0, i]))
    s2.append(wire.send(q.at[:, :, p.xr, B], b2.at[0], p.XR))
    s1[2].wait_recv()
    loop(2, lambda i: plus(q.at[lh, ll, 2 + i, A], a1.at[1, i]))
    s2.append(wire.send(q.at[lh, ll, :, A], a2.at[1], p.YL))
    s1[3].wait_recv()
    loop(2, lambda i: plus(q.at[1, i, p.xl, B], b1.at[1, i]))
    s2.append(wire.send(q.at[:, :, p.xl, B], b2.at[1], p.XL))
    yield
    for copy in s2:
        copy.wait_recv()
    loop(4, lambda i: add(q.at[yh, yl, i, A], q.at[yh, yl, i, A], a2.at[0, i], a2.at[1, i]))
    s3 = [
        wire.send(q.at[yh, yl, p.xo, 0:32], c1.at[0, 0], p.XR),
        wire.send(q.at[yh, yl, p.xo, 32:64], c1.at[0, 1], p.XL),
    ]
    for h in range(2):
        loop(2, lambda i: add(q.at[h, i, x, B], q.at[h, i, x, B], b2.at[0, h, i], b2.at[1, h, i]))
    s3 += [
        wire.send(q.at[oh, ol, x, 64:96], c1.at[1, 0], p.YR),
        wire.send(q.at[oh, ol, x, 96:128], c1.at[1, 1], p.YL),
    ]
    yield
    s4 = []
    s3[0].wait_recv()
    plus(q.at[yh, yl, p.xr, 0:32], c1.at[0, 0])
    s4.append(wire.send(q.at[yh, yl, p.xr, A], c2.at[0, 0], p.XR))
    s3[1].wait_recv()
    plus(q.at[yh, yl, p.xl, 32:64], c1.at[0, 1])
    s4.append(wire.send(q.at[yh, yl, p.xl, A], c2.at[0, 1], p.XL))
    s3[2].wait_recv()
    plus(q.at[rh, rl, x, 64:96], c1.at[1, 0])
    s4.append(wire.send(q.at[rh, rl, x, B], c2.at[1, 0], p.YR))
    s3[3].wait_recv()
    plus(q.at[lh, ll, x, 96:128], c1.at[1, 1])
    s4.append(wire.send(q.at[lh, ll, x, B], c2.at[1, 1], p.YL))
    yield
    for copy in s4:
        copy.wait_recv()
    add(out.at[0:64], q.at[yh, yl, x, A], c2.at[0, 0], c2.at[0, 1])
    add(out.at[64:128], q.at[yh, yl, x, B], c2.at[1, 0], c2.at[1, 1])
    wire.drain()
    yield


def by_place(rows):
    return rows.reshape(EXP_DEV, 2, 2, 4, 2 * CAP, -1)


def backward_kernel(
    sel, info, y_places, y, cot, gate, up, hidden, row_gates, w_in, w_out,
    mixture, dots, dgate, dup, drows, term, ss, rs, ls, *scratch,
):
    p = Place()
    greet_plane(p)
    moving = home_steps(p, Wire(ss, rs), ls, True, sel, info, y_places, None, mixture, *scratch)
    next(moving)
    n = cot.shape[1]
    wide, cut = 2048 // PARTS, FF // PARTS
    dots[...] = jnp.zeros_like(dots)

    def number():
        return pl.program_id(0) * PARTS + pl.program_id(1)

    def first(y, cot, hidden, row_gates, term):
        at_step(number(), (3, moving))
        e = pl.program_id(0)
        product = y[0].astype(f32) * cot[0].astype(f32)
        partial = product[:, :128]
        for c in range(128, wide, 128):
            partial += product[:, c : c + 128]
        dots[e] += partial
        scaled = (hidden[0].astype(f32) * row_gates[0, :, :1]).astype(bf16)
        term[0] = tn(cot[0], scaled).astype(bf16)

    part = block((1, n, wide), lambda e, j: (e, 0, j))
    whole = block((1, n, FF), lambda e, j: (e, 0, 0))
    gates = block((1, n, 128), lambda e, j: (e, 0, 0))
    pltpu.emit_pipeline(
        first,
        grid=(EXP_DEV, PARTS),
        in_specs=[part, part, whole, gates],
        out_specs=[block((1, wide, FF), lambda e, j: (e, j, 0))],
    )(y, cot, hidden, row_gates, term)

    def second(cot, w, row_gates, gate, up, dgate, dup):
        at_step(number(), (3, moving))
        dhidden = jnp.dot(cot[0], w[0], preferred_element_type=f32) * row_gates[0, :, :1]
        g, u = gate[0].astype(f32), up[0].astype(f32)
        sg = jax.nn.sigmoid(g)
        dgate[0] = (dhidden * u * sg * (1.0 + g * (1.0 - sg))).astype(bf16)
        dup[0] = (dhidden * g * sg).astype(bf16)

    out = block((1, n, cut), lambda e, j: (e, 0, j))
    pltpu.emit_pipeline(
        second,
        grid=(EXP_DEV, PARTS),
        in_specs=[
            block((1, n, 2048), lambda e, j: (e, 0, 0)),
            block((1, 2048, cut), lambda e, j: (e, 0, j)),
            gates,
            out,
            out,
        ],
        out_specs=[out, out],
    )(cot, w_out, row_gates, gate, up, dgate, dup)

    def third(dgate, dup, w, drows):
        at_step(number(), (5, moving), (7, moving))
        total = nt(dgate[0], w[0, :, :FF]) + nt(dup[0], w[0, :, FF:])
        drows[0] = total.astype(bf16)

    pltpu.emit_pipeline(
        third,
        grid=(EXP_DEV, PARTS),
        in_specs=[whole, whole, block((1, wide, 2 * FF), lambda e, j: (e, j, 0))],
        out_specs=[part],
    )(dgate, dup, w_in, drows)
    for _ in moving:
        pass


def expert_backward(sel, info, y, cot, gate, up, hidden, row_gates, w_in, w_out, cid):
    n = cot.shape[1]
    half = shaped((EXP_DEV, n, FF))
    return remote_call(
        backward_kernel,
        "expert_backward",
        cid,
        HOME_SENDS,
        2,
        [VMEM, VMEM] + [ANY] * 9,
        [VMEM, VMEM] + [ANY] * 4,
        (
            shaped((128, 2048), f32),
            shaped((EXP_DEV, n, 128), f32),
            half,
            half,
            shaped((EXP_DEV, n, 2048)),
            shaped((EXP_DEV, 2048, FF)),
        ),
        scratch=home_scratch(2048),
        vmem=58 << 20,
    )(sel, info, by_place(y), y, cot, gate, up, hidden, row_gates, w_in, w_out)


def finish_kernel(sel, info, places, more, rows, dgate, dup, home, term, ss, rs, ls, *scratch):
    p = Place()
    greet_plane(p)
    moving = home_steps(p, Wire(ss, rs), ls, False, sel, info, places, more, home, *scratch)
    next(moving)
    n = rows.shape[1]
    wide = 2048 // PARTS

    def first(rows, dgate, dup, term):
        at_step(
            pl.program_id(0) * PARTS + pl.program_id(1), (2, moving), (7, moving)
        )
        term[0, :, :FF] = tn(rows[0], dgate[0]).astype(bf16)
        term[0, :, FF:] = tn(rows[0], dup[0]).astype(bf16)

    whole = block((1, n, FF), lambda e, j: (e, 0, 0))
    pltpu.emit_pipeline(
        first,
        grid=(EXP_DEV, PARTS),
        in_specs=[block((1, n, wide), lambda e, j: (e, 0, j)), whole, whole],
        out_specs=[block((1, wide, 2 * FF), lambda e, j: (e, j, 0))],
    )(rows, dgate, dup, term)
    for _ in moving:
        pass


def expert_finish(sel, info, drows, more, rows, dgate, dup, cid):
    return remote_call(
        finish_kernel,
        "expert_finish",
        cid,
        HOME_SENDS,
        4,
        [VMEM, VMEM] + [ANY] * 5,
        [VMEM, ANY],
        (shaped((128, 2048 + 128), f32), shaped((EXP_DEV, 2048, 2 * FF))),
        scratch=home_scratch(2048 + 128),
        vmem=58 << 20,
    )(sel, info, by_place(drows), by_place(more), rows, dgate, dup)


def unstack_kernel(first, second, first_out, second_out, held, held_two, sems):
    e, j, steps = pl.program_id(0), pl.program_id(1), pl.num_programs(1)
    step = e * steps + j
    count = first.shape[1]

    def copies(at):
        slot = lax.rem(at, 2)
        rows = pl.ds(pl.multiple_of(lax.rem(at, steps) * count, count), count)
        return [
            pltpu.make_async_copy(buffer.at[slot], out.at[rows, at // steps], sems.at[i, slot])
            for i, (buffer, out) in enumerate(((held, first_out), (held_two, second_out)))
        ]

    def wait(at):
        for copy in copies(at):
            copy.wait()

    @pl.when(step >= 2)
    def _():
        wait(step - 2)

    held[lax.rem(step, 2)] = first[0].astype(f32)
    held_two[lax.rem(step, 2)] = second[0].astype(f32)
    for copy in copies(step):
        copy.start()

    @pl.when(step == EXP_DEV * steps - 1)
    def _():
        wait(step - 1)
        wait(step)


def unstack(first, second):
    experts, rows = first.shape[:2]
    count = 128
    wide = (first.shape[2], second.shape[2])
    return pl.pallas_call(
        unstack_kernel,
        name="unstack",
        grid=(experts, rows // count),
        out_shape=tuple(shaped((rows, experts, cols), f32) for cols in wide),
        in_specs=[pl.BlockSpec((1, count, cols), lambda e, j: (e, j, 0)) for cols in wide],
        out_specs=[ANY, ANY],
        scratch_shapes=[pltpu.VMEM((2, count, cols), f32) for cols in wide] + [DMA((2, 2))],
        compiler_params=pltpu.CompilerParams(vmem_limit_bytes=60 << 20),
    )(first, second)


def last_kernel(
    grads, kept, w, rows, cosine, sine, gain, p3, unit, small, out, normed, whole, tiny, ss, rs, ls,
    flat, total, w_grads, part, got_c, got_h, half, mine,
    ra, rb, rc, rd, re, rf, rg, acc_x, acc_y, sz, az, sx, ax, sy, ay, sc, ac, sh,
    tz, tx, ty, tc, th,
):
    p = Place()
    dp, yl, x = p.dp, p.yl, p.x
    greet([p.ZR, p.ZL, p.ZO, p.XR, p.XL, p.XO, p.Y, p.C, p.H])
    wire = Wire(ss, rs)
    p0, p1, p2 = (w_grads.at[i] for i in range(3))

    def added(dst, *srcs):
        total = srcs[0][...].astype(f32)
        for src in srcs[1:]:
            total = total + src[...].astype(f32)
        dst[...] = total.astype(dst.dtype)

    def loop(count, body):
        def step(i, carry):
            body(i)
            return carry

        lax.fori_loop(0, count, step, 0)

    def y_first(i, part):
        return wire.send(part.at[:, 1 - yl], rb.at[i - 2], p.Y)

    firsts = {3: y_first(3, p3)}
    far_z = ((p.zo, p.ZO), (p.zr, p.ZR), (p.zl, p.ZL))
    far_x = ((p.xo, p.XO), (p.xr, p.XR), (p.xl, p.XL))
    zs_out = [wire.send(small.at[there], sz.at[i], dev) for i, (there, dev) in enumerate(far_z)]
    mine[...] = jnp.zeros_like(mine)
    starts = []
    for i in range(3):
        if i < 2:
            gained = jnp.zeros((1, HD), f32)
            for h in range(4):
                grad = turned(grads[i, h].astype(f32), cosine[...], -sine[...])
                head = kept[i, h]
                inverse = rms_rows(head)
                gained += jnp.sum(grad * head * inverse, axis=0, keepdims=True)
                back = rms_back(head, inverse, grad * gain[i])
                flat[:, h * HD : (h + 1) * HD] = back.astype(bf16)
            mine[0, 16 + i : 17 + i] = gained
        else:
            for h in range(4):
                flat[:, h * HD : (h + 1) * HD] = grads[i, h]

        def weight_rows(c, carry):
            cols = pl.ds(pl.multiple_of(c * 512, 512), 512)
            grad = tn(rows[:, cols], flat[...]).astype(bf16)
            w_grads[i, c] = grad.reshape(2, 4, 64, 512)
            return carry

        lax.fori_loop(0, 4, weight_rows, 0)
        if i < 2:
            gradient = w_grads.at[i]
            starts.append(
                (
                    wire.send(gradient.at[0:2, :, p.xo], ra.at[i, 0], p.XR),
                    wire.send(gradient.at[2:4, :, p.xo], ra.at[i, 1], p.XL),
                )
            )
        else:
            firsts[2] = y_first(2, p2)

        def normed_cols(c, carry):
            cols = pl.ds(pl.multiple_of(c * 512, 512), 512)
            value = nt(flat[...], w[i, cols])
            if i > 0:
                value += total[:, cols]
            if i < 2:
                total[:, cols] = value
            else:
                part[:, :, cols] = value.astype(bf16).reshape(4, 128, 512)
            return carry

        lax.fori_loop(0, 4, normed_cols, 0)
        if i == 0:
            for copy in zs_out:
                copy.wait_recv()
            for y in range(2):
                az[y] = small[dp, y] + sz[0, y] + sz[1, y] + sz[2, y]
            xs_out = [
                wire.send(az.at[:, there], sx.at[n], dev) for n, (there, dev) in enumerate(far_x)
            ]
        elif i == 1:
            for copy in xs_out:
                copy.wait_recv()
            ax[...] = az[:, x] + sx[0] + sx[1] + sx[2]
            y_out = wire.send(ax.at[1 - yl], sy, p.Y)
        else:
            y_out.wait_recv()
            ay[...] = ax[yl] + sy[...]
            c_out = wire.send(ay, sc, p.C)
    mine_head, other = p.yh * 2 + (1 - p.co), (1 - p.yh) * 2 + (1 - p.co)
    far = wire.send(part.at[other], got_c.at[0], p.C)
    near = wire.send(part.at[mine_head], got_c.at[1], p.C)
    far.wait_recv()

    def by_16(body):
        def step(i, carry):
            body(pl.ds(pl.multiple_of(i * 16, 16), 16))
            return carry

        lax.fori_loop(0, 8, step, 0)

    def add_far(at):
        away = part[(1 - p.yh) * 2 + p.co, at].astype(f32)
        half[at] = (away + got_c[0, at].astype(f32)).astype(bf16)

    by_16(add_far)
    over = wire.send(half, got_h, p.H)
    c_out.wait_recv()
    ac[...] = ay[...] + sc[...]
    h_out = wire.send(ac, sh, p.H)
    seconds = []
    for i, gradient in ((0, p0), (1, p1)):
        one, two = starts[i]
        one.wait_recv()
        loop(2, lambda d: added(gradient.at[d, :, p.xr], gradient.at[d, :, p.xr], ra.at[i, 0, d]))
        s1 = wire.send(gradient.at[:, :, p.xr], rc.at[i, 0], p.XR)
        two.wait_recv()
        loop(
            2,
            lambda d: added(gradient.at[d + 2, :, p.xl], gradient.at[d + 2, :, p.xl], ra.at[i, 1, d]),
        )
        s2 = wire.send(gradient.at[:, :, p.xl], rc.at[i, 1], p.XL)
        seconds.append((s1, s2))
    mids = {}
    for i, gradient in ((3, p3), (2, p2)):
        firsts[i].wait_recv()
        loop(4, lambda d: added(acc_y.at[i - 2, d], gradient.at[d, yl], rb.at[i - 2, d]))
        acc = acc_y.at[i - 2]
        mids[i] = (
            wire.send(acc.at[0:2, p.xo], rd.at[i - 2, 0], p.XR),
            wire.send(acc.at[2:4, p.xo], rd.at[i - 2, 1], p.XL),
        )
    near.wait_recv()
    over.wait_recv()

    def add_near(at):
        close = part[p.yh * 2 + p.co, at].astype(f32) + got_c[1, at].astype(f32)
        normed[at] = close + got_h[at].astype(f32)

    by_16(add_near)
    for c in range(16):
        cols = slice(c * 128, (c + 1) * 128)
        column = jnp.sum(normed[:, cols] * unit[:, cols], axis=0, keepdims=True)
        mine[0, c : c + 1] = column
    h_out.wait_recv()
    whole[dp, yl, x] = ac[...] + sh[...]
    y_all = wire.send(whole.at[dp, yl, x], whole.at[dp, yl, x], p.Y)
    tz_out = [wire.send(mine.at[0], tz.at[dp], dev) for _, dev in far_z]
    tz[dp] = mine[0]
    yends = []
    for i, gradient in ((0, p0), (1, p1)):
        for s in seconds[i]:
            s.wait_recv()
        acc = acc_x.at[i]
        loop(4, lambda d: added(acc.at[d], gradient.at[d, :, x], rc.at[i, 0, d], rc.at[i, 1, d]))
        yends.append(wire.send(acc.at[:, 1 - yl], re.at[i], p.Y))
    y_all.wait_recv()
    x_all = [wire.send(whole.at[dp, :, x], whole.at[dp, :, x], dev) for _, dev in far_x]
    for copy in tz_out:
        copy.wait_recv()
    mine[1] = tz[0] + tz[1] + tz[2] + tz[3]
    tx_out = [wire.send(mine.at[1], tx.at[x], dev) for _, dev in far_x]
    tx[x] = mine[1]
    xends = {}
    for i in (3, 2):
        acc = acc_y.at[i - 2]
        one, two = mids[i]
        one.wait_recv()
        loop(2, lambda d: added(acc.at[d, p.xr], acc.at[d, p.xr], rd.at[i - 2, 0, d]))
        s1 = wire.send(acc.at[:, p.xr], rf.at[i - 2, 0], p.XR)
        two.wait_recv()
        loop(2, lambda d: added(acc.at[d + 2, p.xl], acc.at[d + 2, p.xl], rd.at[i - 2, 1, d]))
        s2 = wire.send(acc.at[:, p.xl], rf.at[i - 2, 1], p.XL)
        xends[i] = (s1, s2)
    for copy in x_all:
        copy.wait_recv()
    z_all = [wire.send(whole.at[dp], whole.at[dp], dev) for _, dev in far_z]
    for copy in tx_out:
        copy.wait_recv()
    mine[2] = tx[0] + tx[1] + tx[2] + tx[3]
    ty_out = wire.send(mine.at[2], ty, p.Y)
    parts, zs = {}, {}

    def z_first(i, acc):
        parts[i] = acc
        zs[i] = (
            wire.send(acc.at[p.zo, 0:32], rg.at[i, 0, 0:32], p.ZR),
            wire.send(acc.at[p.zo, 32:64], rg.at[i, 1, 0:32], p.ZL),
        )

    for i in (0, 1):
        yends[i].wait_recv()
        acc = acc_x.at[i]
        loop(4, lambda d: added(acc.at[d, yl], acc.at[d, yl], re.at[i, d]))
        z_first(i, acc.at[:, yl])
    ty_out.wait_recv()
    mine[3] = mine[2] + ty[...]
    tc_out = wire.send(mine.at[3], tc, p.C)
    for i in (3, 2):
        for s in xends[i]:
            s.wait_recv()
        acc = acc_y.at[i - 2]
        loop(
            4, lambda d: added(acc.at[d, x], acc.at[d, x], rf.at[i - 2, 0, d], rf.at[i - 2, 1, d])
        )
        z_first(i, acc.at[:, x])
    tc_out.wait_recv()
    mine[4] = mine[3] + tc[...]
    th_out = wire.send(mine.at[4], th, p.H)
    ends = {}
    for i in (0, 1, 3, 2):
        one, two = zs[i]
        acc = parts[i]
        one.wait_recv()
        added(acc.at[p.zr, 0:32], acc.at[p.zr, 0:32], rg.at[i, 0, 0:32])
        s1 = wire.send(acc.at[p.zr], rg.at[i, 2], p.ZR)
        two.wait_recv()
        added(acc.at[p.zl, 32:64], acc.at[p.zl, 32:64], rg.at[i, 1, 0:32])
        s2 = wire.send(acc.at[p.zl], rg.at[i, 3], p.ZL)
        ends[i] = (s1, s2)
    th_out.wait_recv()
    tiny[...] = mine[4] + th[...]
    for i in range(4):
        for s in ends[i]:
            s.wait_recv()
        added(out.at[i], parts[i].at[dp], rg.at[i, 2], rg.at[i, 3])
    for copy in z_all:
        copy.wait_recv()
    wire.drain()


def last_sums(grads, kept, w, rows, cosine, sine, gains, fourth, unit, small):
    return remote_call(
        last_kernel,
        "last_sums",
        8,
        64,
        1,
        [VMEM] * 10,
        [VMEM] * 4,
        (
            shaped((4, 64, 512), f32),
            shaped((128, 2048), f32),
            shaped((4, 2, 4, 40, 128), f32),
            shaped((24, 128), f32),
        ),
        scratch=[
            pltpu.VMEM((512, 512), bf16),
            pltpu.VMEM((512, 2048), f32),
            pltpu.VMEM((3, 4, 2, 4, 64, 512), bf16),
            pltpu.VMEM((4, 128, 2048), bf16),
            pltpu.VMEM((2, 128, 2048), bf16),
            pltpu.VMEM((128, 2048), bf16),
            pltpu.VMEM((128, 2048), bf16),
            pltpu.VMEM((5, 24, 128), f32),
            pltpu.VMEM((2, 2, 2, 2, 64, 512), bf16),
            pltpu.VMEM((2, 4, 4, 64, 512), bf16),
            pltpu.VMEM((2, 2, 4, 2, 64, 512), bf16),
            pltpu.VMEM((2, 2, 2, 64, 512), bf16),
            pltpu.VMEM((2, 4, 64, 512), bf16),
            pltpu.VMEM((2, 2, 4, 64, 512), bf16),
            pltpu.VMEM((4, 4, 64, 512), bf16),
            pltpu.VMEM((2, 4, 2, 64, 512), bf16),
            pltpu.VMEM((2, 4, 4, 64, 512), bf16),
            pltpu.VMEM((3, 2, 4, 40, 128), f32),
            pltpu.VMEM((2, 4, 40, 128), f32),
            pltpu.VMEM((3, 2, 40, 128), f32),
            pltpu.VMEM((2, 40, 128), f32),
            pltpu.VMEM((40, 128), f32),
            pltpu.VMEM((40, 128), f32),
            pltpu.VMEM((40, 128), f32),
            pltpu.VMEM((40, 128), f32),
            pltpu.VMEM((40, 128), f32),
            pltpu.VMEM((4, 24, 128), f32),
            pltpu.VMEM((4, 24, 128), f32),
            pltpu.VMEM((24, 128), f32),
            pltpu.VMEM((24, 128), f32),
            pltpu.VMEM((24, 128), f32),
        ],
        vmem=60 << 20,
    )(
        grads, kept, w, rows, cosine, sine, gains,
        fourth.reshape(4, 2, 4, 64, 512), unit, small.reshape(4, 2, 4, 40, 128),
    )


def on_device(
    tokens,
    segment_ids,
    valid_mask,
    routes,
    attn_gain,
    w_query,
    w_key,
    w_value,
    w_out,
    query_gain,
    key_gain,
    ffn_gain,
    router,
    expert_in,
    expert_out,
    cotangent,
):
    blk = lax.axis_index("blk")
    device = lax.axis_index("head") * 8 + blk
    yl = blk // 4
    tok, width = tokens.shape
    full_in = lax.all_gather(jnp.transpose(expert_in, (1, 0, 2)), "dp", axis=1, tiled=True)
    full_back = lax.all_gather(jnp.transpose(expert_out, (1, 0, 2)), "dp", axis=1, tiled=True)

    segment, valid = segment_ids[0], valid_mask[0]
    seq_len = segment.shape[0]
    place = jnp.arange(seq_len, dtype=i32)
    query_ids = (jnp.arange(4)[:, None] * 1024 + blk * 128 + jnp.arange(128)[None]).reshape(-1)
    frequency = rope_base ** (-jnp.arange(64, dtype=f32) / 64)
    angles = query_ids.astype(f32)[:, None] * frequency[None]
    cosine, sine = jnp.cos(angles), jnp.sin(angles)
    cosine = jnp.concatenate([cosine, cosine], axis=1)
    sine = jnp.concatenate([-sine, sine], axis=1)
    half_ids = (jnp.arange(4)[:, None] * 1024 + yl * 512 + jnp.arange(512)[None]).reshape(-1)
    half_seg = lax.dynamic_index_in_dim(segment.reshape(4, 2, 512), yl, 1, keepdims=False).reshape(-1)
    key_seg = jnp.where(valid > 0, segment, -1)
    ends = half_seg.reshape(-1, QB)
    lower = jnp.sum(segment[None] < ends[:, :1], axis=1, dtype=i32) // KB
    upper = (jnp.sum(segment[None] <= ends[:, -1:], axis=1, dtype=i32) + KB - 1) // KB
    limits = jnp.stack([lower, upper])

    inputs = tokens.astype(f32)
    first_inv = rms_rows(inputs)
    normed = (inputs * first_inv * attn_gain).astype(bf16)
    w_three = jnp.stack([w_query, w_key, w_value])
    gathered, out_part, normed_all = gather_weights(w_three, w_out, normed)
    full_three = gathered.reshape(3, 2048, 512)
    normed_all = normed_all.reshape(512, width)

    def flat_of(heads):
        return jnp.transpose(heads.reshape(4, 512, HD), (1, 0, 2)).reshape(512, 512)

    head_gains = jnp.stack([query_gain, key_gain])[:, None]
    heads, projected = project(normed_all, full_three, cosine, sine, head_gains)
    runs = (4, 4, 128, HD)
    q, k, v, full_out = heads_over_x(heads.reshape((3,) + runs), out_part)
    q, k, v = q.reshape(2048, HD), k.reshape(4096, HD), v.reshape(4096, HD)
    full_out = full_out.reshape(2048, 512)
    att_low, att, inverse = attend(limits, q, k, v, half_seg, half_ids, key_seg)
    attended, branch = attended_home(att_low.reshape(runs), full_out)
    attended_flat = flat_of(attended)
    middle = inputs + branch
    second_inv = rms_rows(middle)
    normed_ffn = (middle * second_inv * ffn_gain).astype(bf16)
    logits = jnp.dot(normed_ffn, router, preferred_element_type=f32)
    probabilities = jax.nn.softmax(logits, axis=-1)

    expert_ids = jnp.arange(EXPERTS, dtype=i32)
    hot = jnp.sum((routes[..., None] == expert_ids).astype(f32), axis=1)
    before = (jnp.arange(tok)[:, None] > jnp.arange(tok)[None]).astype(bf16)
    slots = jnp.dot(before, hot.astype(bf16), preferred_element_type=f32)
    slot_code = jnp.where(hot > 0, slots, -1.0)
    chosen = probabilities * hot
    gate_total = jnp.sum(chosen, axis=-1, keepdims=True)
    gates = chosen / gate_total

    sent = jnp.concatenate([normed_ffn, slot_code.astype(bf16), gates.astype(bf16)], axis=1)
    everyone = spread(sent, 7)
    lane = jnp.arange(128)[None]
    sel_row = jnp.arange(8)[:, None]
    info = everyone[:, :, width:]
    column = (sel_row // 2) * EXPERTS + device * EXP_DEV + sel_row % 2
    sel = ((sel_row < 4) & (lane == column)).astype(bf16)
    nearby = (device ^ 8) * EXP_DEV
    column = sel_row % 2 + jnp.where(sel_row // 2 % 2 == 0, device * EXP_DEV, nearby)
    sel_chip = (lane == column + (sel_row // 4) * EXPERTS).astype(bf16)
    flat_info, flat_everyone = info.reshape(32 * tok, -1), everyone.reshape(32 * tok, -1)
    expert_rows, row_gates = pick_rows(sel, flat_info, flat_everyone, width, True)
    expert_rows = expert_rows.reshape(EXP_DEV, -1, width)
    row_gates = row_gates.reshape(EXP_DEV, -1, 128)
    all_cot, gate_part, up_part, hidden, expert_result = expert_forward(
        cotangent, expert_rows, full_in, full_back, 11
    )
    (arrived_cot,) = pick_rows(sel, flat_info, all_cot.reshape(32 * tok, width), width, False)
    arrived_cot = arrived_cot.reshape(EXP_DEV, -1, width)
    mixture, row_dots, grad_gate, grad_up, grad_rows, term_back = expert_backward(
        sel_chip, info, expert_result, arrived_cot, gate_part, up_part, hidden, row_gates,
        full_in, full_back, 12,
    )
    row_dots = jnp.sum(row_dots, axis=-1, keepdims=True)
    high = row_dots.astype(bf16)
    column = (device * EXP_DEV + jnp.arange(EXP_DEV))[:, None, None]
    low = jnp.where(lane == column + EXPERTS, (row_dots - high.astype(f32)).astype(bf16), 0)
    row_dots = jnp.where(lane == column, high, low)
    grad_home, term_in = expert_finish(
        sel_chip, info, grad_rows, row_dots, expert_rows, grad_gate, grad_up, 13
    )
    grad_gates = grad_home[:, width : width + EXPERTS] + grad_home[:, width + EXPERTS :]
    grad_home = grad_home[:, :width]

    def fold_dp(term):
        return lax.psum_scatter(term.astype(bf16), "dp", scatter_dimension=1, tiled=True)

    expert_in_grad, expert_out_grad = unstack(fold_dp(term_in), fold_dp(term_back))

    output = (middle + mixture).astype(bf16)
    grad_out = cotangent.astype(f32)
    mean_grad = jnp.sum(grad_gates * gates, axis=-1, keepdims=True)
    grad_probs = (grad_gates - mean_grad) / gate_total * hot
    grad_logits = probabilities * (
        grad_probs - jnp.sum(probabilities * grad_probs, axis=-1, keepdims=True)
    )
    high = grad_logits.astype(bf16)
    halves = jnp.concatenate([high, (grad_logits - high.astype(f32)).astype(bf16)], axis=1)
    router_term = jnp.einsum("td,te->de", normed_ffn, halves, preferred_element_type=f32)
    router_term = router_term[:, :EXPERTS] + router_term[:, EXPERTS:]
    grad_ffn = grad_home + jnp.einsum(
        "te,de->td", halves, jnp.concatenate([router, router], axis=1), preferred_element_type=f32
    )
    ffn_gain_term = jnp.sum(grad_ffn * middle * second_inv, axis=0)
    grad_middle = grad_out + rms_back(middle, second_inv, grad_ffn * ffn_gain)
    grad_branch = grad_middle.astype(bf16)
    branch_all, grad_att = branch_to_heads(grad_branch, full_out)
    branch_all, grad_att = branch_all.reshape(512, width), grad_att.reshape(2048, HD)
    delta = jnp.sum(grad_att.astype(f32) * att, axis=-1)
    dq, dk, dv = attend_back(
        limits, q, k, v, grad_att, half_seg, half_ids, key_seg, inverse[:, 0], delta
    )
    cut = (4, 2, 4, 128, HD)
    grad_heads = grads_over_x(dq.reshape(runs), dk.reshape(cut), dv.reshape(cut))
    out_grad = jnp.einsum(
        "qc,qf->cf", branch_all, attended_flat, preferred_element_type=f32
    ).astype(bf16)
    gains = jnp.pad(ffn_gain_term, (0, 32 * 8 * 128 - width)).reshape(32, 8, 128)
    small = jnp.concatenate([router_term.reshape(32, 32, 128), gains], axis=1)
    attn_grads, grad_normed, summed, tiny = last_sums(
        grad_heads.reshape(3, 4, 512, HD), projected, full_three, normed_all, cosine, sine,
        head_gains, out_grad, inputs * first_inv, small,
    )
    input_grad = grad_middle + rms_back(inputs, first_inv, grad_normed * attn_gain)
    summed = summed.reshape(32, 40, 128)
    router_grad = summed[:, :32].reshape(router.shape)
    ffn_gain_grad = summed[:, 32:].reshape(-1)[:width]
    return (
        output,
        input_grad,
        tiny[:16].reshape(-1),
        attn_grads[0],
        attn_grads[1],
        attn_grads[2],
        attn_grads[3],
        tiny[16],
        tiny[17],
        ffn_gain_grad,
        router_grad,
        expert_in_grad,
        expert_out_grad,
    )


def solution(mesh):
    placed = (
        P(("dp", "head", "blk"), None),
        P("dp", None),
        P("dp", None),
        P(("dp", "head", "blk"), None),
        P(),
        P(("dp", "blk"), "head"),
        P(("dp", "blk"), "head"),
        P(("dp", "blk"), "head"),
        P(("dp", "blk"), "head"),
        P(),
        P(),
        P(),
        P(),
        P("dp", ("head", "blk"), None),
        P("dp", ("head", "blk"), None),
        P(("dp", "head", "blk"), None),
    )
    return jax.shard_map(
        on_device,
        mesh=mesh,
        in_specs=placed,
        out_specs=(
            P(("dp", "head", "blk"), None),
            P(("dp", "head", "blk"), None),
            P(),
            P(("dp", "blk"), "head"),
            P(("dp", "blk"), "head"),
            P(("dp", "blk"), "head"),
            P(("dp", "blk"), "head"),
            P(),
            P(),
            P(),
            P(),
            P("dp", ("head", "blk"), None),
            P("dp", ("head", "blk"), None),
        ),
        check_vma=False,
    )
```
